32 devices in a mesh: memory: 4 (over z), group: 8 (over y, x, core).
Axes of the slice: x: 2, y: 2, z: 4, core: 2. Of those that a mesh axis runs over, the one named last changes fastest.
Arguments:
- queries: bfloat16 [8, 32, 32, 128], P('group', 'memory')
- positives: bfloat16 [8, 32, 128, 128], P('group', 'memory'), may hold values from -6 to 6
- memory: bfloat16 [8, 512, 128, 128], P('group', 'memory'), may hold values from -6 to 6
- candidates: int32 [8, 32, 64], P('group', 'memory'), may hold values from 0 to 511, as said below
- counts: int32 [8, 32], P('group', 'memory'), may hold values from 16 to 32
Outputs:
- batch_scores: float32 [8, 32, 64], P('group', 'memory')
- memory_scores: float32 [8, 32, 64], P('group', 'memory')
- loss: float32 [8, 32], P('group', 'memory')
The draws below stay inside these ranges and needn't reach their ends.
Inputs may be any that keep to these rules, and one draw needn't show every extreme that they name: `candidates`: passage id r of a column lies on memory index r // 128. Among the valid slots of the queries of one device (queries[g, m * 8 to (m + 1) * 8 - 1]), at most 96 name passages of any one memory index, and some memory index is named by exactly 96 of them. Ids may repeat.
All inputs are finite; a program needn't handle non-finite values.
Results may differ from the reference program's by a relative error of at most 0.0003.
Values may be sent and summed in bfloat16 or wider, within the bound.
No kernel may reach another device: no remote copies, remote signals or barrier semaphores. Data moves between devices by JAX's collectives and lax.ppermute only.
A program may use at most 128 MiB of HBM per device.

```python
import jax
import jax.numpy as jnp
from jax import lax

D = 128
QT = 32
S = 128
C = 64
Q_DEV = 8
P_DEV = 128
GROUPS = 8
Q_COL = 32
P_COL = 512
CAP = 96
N_GROUP = 8


def draw_queries(key, part):
    values = jax.random.normal(key, (GROUPS, Q_COL, QT, D), jnp.float32) * D ** (-0.5)
    return values.astype(jnp.bfloat16)


def block_ids(key):
    shards = P_COL // P_DEV
    total = Q_DEV * C
    live = C // 2 * Q_DEV - CAP
    first, second, third, fourth = jax.random.split(key, 4)
    hottest = jax.random.randint(first, (), 0, shards)
    shuffled = jax.random.permutation(second, live).astype(jnp.int32)
    offsets = jnp.concatenate([jnp.zeros((CAP,), jnp.int32), 1 + shuffled % (shards - 1), jax.random.randint(third, (total - CAP - live,), 1, shards)])
    owners = (hottest + offsets) % shards
    local_rows = jax.random.randint(fourth, (total,), 0, P_DEV)
    ids = owners * P_DEV + local_rows
    return ids.reshape(C, Q_DEV).T


def draw_candidates(key, part):
    keys = jax.random.split(key, GROUPS * (Q_COL // Q_DEV))
    blocks = jax.vmap(block_ids)(keys)
    return blocks.reshape(GROUPS, Q_COL, C).astype(jnp.int32)


def place_ends(drawn, stream_key, smallest, top_value):
    spot = [jax.random.randint(jax.random.fold_in(stream_key, axis), (), 0, length) for axis, length in enumerate(drawn.shape)]
    longest = drawn.shape.index(max(drawn.shape))
    neighbour = spot[:longest] + [(spot[longest] + 1) % drawn.shape[longest]] + spot[longest + 1:]
    return drawn.at[tuple(spot)].set(smallest).at[tuple(neighbour)].set(top_value)


def shard_levels(stream_key, dims, cuts, low, top_value):
    factor_of = 1.0
    for dim, shards_of in cuts:
        steps = jax.random.uniform(jax.random.fold_in(jax.random.fold_in(stream_key, 6), dim), (shards_of,), jnp.float32, low / len(cuts), top_value / len(cuts))
        factor_of = factor_of * jnp.repeat(jnp.exp(steps), dims[dim] // shards_of).reshape((-1,) + (1,) * (len(dims) - 1 - dim))
    return factor_of


def centred(own_key, extent, spread, most, pieces=(), held_as=jnp.bfloat16):
    gain = shard_levels(own_key, extent, pieces, -0.22, 0.18) if pieces else 1.0
    entries = jax.random.normal(own_key, extent, jnp.float32) * spread * gain
    return jnp.minimum(jnp.maximum(entries, -most), most).astype(held_as)


def setup_inputs(seed: int = 0) -> dict:
    splits = jax.random.split(jax.random.key(seed), 6)
    queries = draw_queries(jax.random.fold_in(splits[5], 71), 0)
    positives = centred(splits[1], (GROUPS, Q_COL, S, D), 1.0, 6.0, ((0, 8), (1, 4)))
    memory = centred(splits[2], (GROUPS, P_COL, S, D), 1.0, 6.0, ((0, 8), (1, 4)))
    candidates = draw_candidates(jax.random.fold_in(splits[5], 71), 0)
    counts = place_ends(jax.random.randint(splits[4], (GROUPS, Q_COL), C // 4, C // 2 + 1), jax.random.fold_in(splits[4], 1), C // 4, (C // 2 + 1) - 1).astype(jnp.int32)
    return dict(queries=queries, positives=positives, memory=memory, candidates=candidates, counts=counts)


def maxsim(query_tokens, passages):
    product = jnp.einsum("qd,nsd->nqs", query_tokens.astype(jnp.float32), passages.astype(jnp.float32))
    return jnp.sum(jnp.max(product, axis=2), axis=1)


def reference(queries, positives, memory, candidates, counts):
    flat_queries = queries.reshape(GROUPS * Q_COL, QT, D)
    flat_candidates = candidates.reshape(GROUPS * Q_COL, C)
    flat_counts = counts.reshape(GROUPS * Q_COL)
    slot_iota = jnp.arange(C, dtype=jnp.int32)
    batch_iota = jnp.arange(N_GROUP * Q_DEV, dtype=jnp.int32)

    def one_query(flat_index):
        group_index = flat_index // Q_COL
        inner = flat_index % Q_COL
        block = inner // Q_DEV
        query_tokens = flat_queries[flat_index]
        block_pos = lax.dynamic_slice_in_dim(positives, (block * Q_DEV).astype(jnp.int32), Q_DEV, 1)
        block_pos = block_pos.reshape(N_GROUP * Q_DEV, S, D)
        batch_row = maxsim(query_tokens, block_pos)
        column = memory[group_index]
        chosen = column[flat_candidates[flat_index]]
        valid = slot_iota < flat_counts[flat_index]
        raw = maxsim(query_tokens, chosen)
        memory_row = jnp.where(valid, raw, jnp.float32(0.0))
        top = jnp.maximum(jnp.max(batch_row), jnp.max(jnp.where(valid, raw, -jnp.inf)))
        total = jnp.sum(jnp.exp(batch_row - top)) + jnp.sum(jnp.where(valid, jnp.exp(raw - top), jnp.float32(0.0)))
        own_index = group_index * Q_DEV + inner % Q_DEV
        target = jnp.sum(jnp.where(batch_iota == own_index, batch_row, jnp.float32(0.0)))
        return batch_row, memory_row, top + jnp.log(total) - target

    batch_rows, memory_rows, losses = lax.map(one_query, jnp.arange(GROUPS * Q_COL, dtype=jnp.int32))
    return (batch_rows.reshape(GROUPS, Q_COL, N_GROUP * Q_DEV), memory_rows.reshape(GROUPS, Q_COL, C), losses.reshape(GROUPS, Q_COL))
```

```python
import functools

import jax
import jax.numpy as jnp
from jax import lax
from jax.experimental import pallas as pl
from jax.experimental.pallas import tpu as pltpu
from jax.sharding import PartitionSpec as P

LANES = 128
DOT_PASSAGES = 4
VMEM_BYTES = 32 * 1024 * 1024


def token_max(passages, tokens):
    count, width, depth = passages.shape
    product = lax.dot_general(
        passages.reshape(count * width, depth),
        tokens,
        (((1,), (1,)), ((), ())),
        preferred_element_type=jnp.float32,
    )
    return jnp.max(product.reshape(count, width, tokens.shape[0]), axis=1)


def token_sum(best, queries):
    tokens = best.shape[1]
    per_query = tokens // queries
    row = lax.broadcasted_iota(jnp.int32, (queries, tokens), 0)
    col = lax.broadcasted_iota(jnp.int32, (queries, tokens), 1)
    own = (col // per_query == row).astype(jnp.float32)
    return lax.dot_general(
        own,
        best,
        (((1,), (1,)), ((), ())),
        precision=lax.Precision.HIGHEST,
        preferred_element_type=jnp.float32,
    )


def memory_kernel(query_ref, passage_ref, out_ref, best_ref):
    step = pl.program_id(0)
    _, queries, per_query, depth = query_ref.shape
    tokens = query_ref[0].reshape(queries * per_query, depth)
    block = passage_ref.shape[1]
    rows = []
    for start in range(0, block, DOT_PASSAGES):
        size = min(DOT_PASSAGES, block - start)
        rows.append(token_max(passage_ref[0, start : start + size], tokens))
    first = pl.multiple_of(step * block, block)
    best_ref[pl.ds(first, block), :] = jnp.concatenate(rows, axis=0)

    @pl.when(step == pl.num_programs(0) - 1)
    def _():
        out_ref[...] = token_sum(best_ref[...], queries)


def score_memory(queries, memory):
    _, q_count, q_tokens, depth = queries.shape
    _, p_count, p_tokens, _ = memory.shape
    block = min(16, p_count)
    return pl.pallas_call(
        memory_kernel,
        grid=(p_count // block,),
        in_specs=[
            pl.BlockSpec((1, q_count, q_tokens, depth), lambda i: (0, 0, 0, 0)),
            pl.BlockSpec((1, block, p_tokens, depth), lambda i: (0, i, 0, 0)),
        ],
        out_specs=pl.BlockSpec((q_count, p_count), lambda i: (0, 0)),
        out_shape=jax.ShapeDtypeStruct((q_count, p_count), jnp.float32),
        scratch_shapes=[pltpu.VMEM((p_count, q_count * q_tokens), jnp.float32)],
        compiler_params=pltpu.CompilerParams(vmem_limit_bytes=VMEM_BYTES),
        cost_estimate=pl.CostEstimate(
            flops=2 * q_count * q_tokens * p_count * p_tokens * depth,
            bytes_accessed=2 * p_count * p_tokens * depth,
            transcendentals=0,
        ),
        name="score_memory",
    )(queries, memory)


def batch_kernel(peers, *refs):
    query_refs = refs[:peers]
    own_ref, mate_ref = refs[peers : peers + 2]
    out_refs = refs[peers + 2 :]
    for query_ref, out_ref in zip(query_refs, out_refs):
        _, queries, per_query, depth = query_ref.shape
        tokens = query_ref[0].reshape(queries * per_query, depth)
        best = jnp.concatenate(
            [token_max(own_ref[0], tokens), token_max(mate_ref[0], tokens)], axis=0
        )
        out_ref[...] = token_sum(best, queries)


def score_batch(query_list, own_positives, mate_positives):
    _, q_count, q_tokens, depth = query_list[0].shape
    _, p_count, p_tokens, _ = own_positives.shape
    peers = len(query_list)
    return pl.pallas_call(
        functools.partial(batch_kernel, peers),
        out_shape=[jax.ShapeDtypeStruct((q_count, 2 * p_count), jnp.float32)] * peers,
        compiler_params=pltpu.CompilerParams(vmem_limit_bytes=VMEM_BYTES),
        cost_estimate=pl.CostEstimate(
            flops=4 * peers * q_count * q_tokens * p_count * p_tokens * depth,
            bytes_accessed=4 * p_count * p_tokens * depth,
            transcendentals=0,
        ),
        name="score_batch",
    )(*query_list, own_positives, mate_positives)


def loss_kernel(chips, shards, place_ref, *refs):
    batch_refs = refs[:chips]
    memory_refs = refs[chips : chips + shards]
    candidate_ref, count_ref, batch_ref, memory_ref, loss_ref = refs[chips + shards :]
    group, shard = place_ref[0], place_ref[1]
    chip, core = group // 2, group % 2
    _, q_count, slots = candidate_ref.shape
    p_count = memory_refs[0].shape[1]
    pair = batch_refs[0].shape[1]
    half = pair // 2

    parts = []
    for target in range(chips):
        part = jnp.zeros((q_count, pair), jnp.float32)
        for step in range(chips):
            part = jnp.where(chip == target ^ step, batch_refs[step][...], part)
        swapped = jnp.concatenate([part[:, half:], part[:, :half]], axis=1)
        parts.append(jnp.where(core == 0, part, swapped))
    batch = jnp.concatenate(parts, axis=1)
    batch_ref[0] = batch

    ids = candidate_ref[0]
    padded = jnp.concatenate([ids, jnp.zeros((q_count, p_count - slots), jnp.int32)], axis=1)
    holder, local = padded // p_count, padded % p_count
    picked = jnp.zeros((q_count, p_count), jnp.float32)
    for step in range(shards):
        found = jnp.take_along_axis(memory_refs[step][...], local, axis=1)
        picked = jnp.where(holder == (shard ^ step), found, picked)

    square = (q_count, q_count)
    diagonal = lax.broadcasted_iota(jnp.int32, square, 0) == lax.broadcasted_iota(
        jnp.int32, square, 1
    )
    counts = jnp.sum(
        jnp.where(diagonal, jnp.broadcast_to(count_ref[...], square), 0), axis=1, keepdims=True
    )
    valid = lax.broadcasted_iota(jnp.int32, (q_count, p_count), 1) < counts
    memory_ref[0] = jnp.where(valid, picked, 0.0)[:, :slots]

    top = jnp.maximum(
        jnp.max(batch, axis=1, keepdims=True),
        jnp.max(jnp.where(valid, picked, -jnp.inf), axis=1, keepdims=True),
    )
    total = jnp.sum(jnp.exp(batch - top), axis=1, keepdims=True) + jnp.sum(
        jnp.where(valid, jnp.exp(picked - top), 0.0), axis=1, keepdims=True
    )
    column = lax.broadcasted_iota(jnp.int32, batch.shape, 1)
    own = group * q_count + lax.broadcasted_iota(jnp.int32, batch.shape, 0)
    target_score = jnp.sum(jnp.where(column == own, batch, 0.0), axis=1, keepdims=True)
    loss = top + jnp.log(total) - target_score
    loss_ref[...] = jnp.sum(
        jnp.where(diagonal, jnp.broadcast_to(loss, square), 0.0), axis=0, keepdims=True
    )


def finish(batch_parts, memory_parts, candidates, counts, place):
    _, q_count, slots = candidates.shape
    chips, shards = len(batch_parts), len(memory_parts)
    columns = chips * batch_parts[0].shape[1]
    vmem = pl.BlockSpec(memory_space=pltpu.VMEM)
    return pl.pallas_call(
        functools.partial(loss_kernel, chips, shards),
        in_specs=[pl.BlockSpec(memory_space=pltpu.SMEM)] + [vmem] * (chips + shards + 2),
        out_shape=[
            jax.ShapeDtypeStruct((1, q_count, columns), jnp.float32),
            jax.ShapeDtypeStruct((1, q_count, slots), jnp.float32),
            jax.ShapeDtypeStruct((1, q_count), jnp.float32),
        ],
        name="finish",
    )(place, *batch_parts, *memory_parts, candidates, counts)


def body(queries, positives, memory, candidates, counts):
    shards = lax.axis_size("memory")
    groups = lax.axis_size("group")
    chips = groups // 2

    def to_shard(array, step):
        return lax.ppermute(array, "memory", [(i, i ^ step) for i in range(shards)])

    def to_chip(array, step):
        return lax.ppermute(array, "group", [(i, i ^ (2 * step)) for i in range(groups)])

    memory_queries = [queries] + [to_shard(queries, step) for step in range(1, shards)]
    mate_positives = lax.ppermute(positives, "group", [(i, i ^ 1) for i in range(groups)])
    batch_queries = [queries] + [to_chip(queries, step) for step in range(1, chips)]

    memory_scores = [score_memory(q, memory) for q in memory_queries]
    batch_scores = score_batch(batch_queries, positives, mate_positives)

    memory_parts = memory_scores[:1] + [
        to_shard(memory_scores[step], step) for step in range(1, shards)
    ]
    batch_parts = list(batch_scores[:1]) + [
        to_chip(batch_scores[step], step) for step in range(1, chips)
    ]
    place = jnp.stack([lax.axis_index("group"), lax.axis_index("memory")]).astype(jnp.int32)
    return finish(batch_parts, memory_parts, candidates, counts, place)


def solution(mesh):
    in_specs = (
        P("group", "memory", None, None),
        P("group", "memory", None, None),
        P("group", "memory", None, None),
        P("group", "memory", None),
        P("group", "memory"),
    )
    out_specs = (P("group", "memory", None), P("group", "memory", None), P("group", "memory"))
    return jax.shard_map(body, mesh=mesh, in_specs=in_specs, out_specs=out_specs, check_vma=False)
```

```python
import jax
import jax.numpy as jnp
from jax import lax
from jax.experimental import pallas as pl
from jax.experimental.pallas import tpu as pltpu
from jax.sharding import PartitionSpec as P

LANES = 128
DOT_PASSAGES = 4
VMEM_BYTES = 32 * 1024 * 1024


def token_max(passages, tokens):
    count, width, depth = passages.shape
    product = lax.dot_general(
        passages.reshape(count * width, depth),
        tokens,
        (((1,), (1,)), ((), ())),
        preferred_element_type=jnp.float32,
    )
    return jnp.max(product.reshape(count, width, tokens.shape[0]), axis=1)


def token_sum(best, queries):
    tokens = best.shape[1]
    per_query = tokens // queries
    row = lax.broadcasted_iota(jnp.int32, (queries, tokens), 0)
    col = lax.broadcasted_iota(jnp.int32, (queries, tokens), 1)
    own = (col // per_query == row).astype(jnp.float32)
    return lax.dot_general(
        own,
        best,
        (((1,), (1,)), ((), ())),
        precision=lax.Precision.HIGHEST,
        preferred_element_type=jnp.float32,
    )


def memory_kernel(place_ref, query_ref, passage_ref, out_ref, best_ref):
    step, steps = pl.program_id(1), pl.num_programs(1)
    _, queries, per_query, depth = query_ref.shape
    tokens = query_ref[0].reshape(queries * per_query, depth)
    block = passage_ref.shape[1]
    rows = []
    for start in range(0, block, DOT_PASSAGES):
        size = min(DOT_PASSAGES, block - start)
        rows.append(token_max(passage_ref[0, start : start + size], tokens))
    first = pl.multiple_of(step * block, block)
    best_ref[pl.ds(first, block), :] = jnp.concatenate(rows, axis=0)

    @pl.when(step == steps - 1)
    def _():
        out_ref[0] = token_sum(best_ref[...], queries)


def score_memory(queries, memory, place, others):
    askers, q_count, q_tokens, depth = queries.shape
    _, p_count, p_tokens, _ = memory.shape
    block = min(32, p_count)
    rounds = askers - 1 if others else 1

    def asker(index, place):
        return (place[1] + index + 1) % askers if others else 0

    return pl.pallas_call(
        memory_kernel,
        grid_spec=pltpu.PrefetchScalarGridSpec(
            num_scalar_prefetch=1,
            grid=(rounds, p_count // block),
            in_specs=[
                pl.BlockSpec(
                    (1, q_count, q_tokens, depth), lambda j, i, p: (asker(j, p), 0, 0, 0)
                ),
                pl.BlockSpec((1, block, p_tokens, depth), lambda j, i, p: (0, i, 0, 0)),
            ],
            out_specs=pl.BlockSpec((1, q_count, p_count), lambda j, i, p: (asker(j, p), 0, 0)),
            scratch_shapes=[pltpu.VMEM((p_count, q_count * q_tokens), jnp.float32)],
        ),
        out_shape=jax.ShapeDtypeStruct((askers, q_count, p_count), jnp.float32),
        compiler_params=pltpu.CompilerParams(vmem_limit_bytes=VMEM_BYTES),
        cost_estimate=pl.CostEstimate(
            flops=2 * rounds * q_count * q_tokens * p_count * p_tokens * depth,
            bytes_accessed=2 * rounds * p_count * p_tokens * depth,
            transcendentals=0,
        ),
        name="score_memory",
    )(place, queries, memory)


def batch_kernel(query_ref, own_ref, mate_ref, out_ref):
    peers, queries, per_query, depth = query_ref.shape
    for peer in range(peers):
        tokens = query_ref[peer].reshape(queries * per_query, depth)
        best = jnp.concatenate(
            [token_max(own_ref[0], tokens), token_max(mate_ref[0], tokens)], axis=0
        )
        out_ref[peer] = token_sum(best, queries)


def score_batch(queries, own_positives, mate_positives):
    peers, q_count, q_tokens, depth = queries.shape
    _, p_count, p_tokens, _ = own_positives.shape
    return pl.pallas_call(
        batch_kernel,
        out_shape=jax.ShapeDtypeStruct((peers, q_count, 2 * p_count), jnp.float32),
        compiler_params=pltpu.CompilerParams(vmem_limit_bytes=VMEM_BYTES),
        cost_estimate=pl.CostEstimate(
            flops=4 * peers * q_count * q_tokens * p_count * p_tokens * depth,
            bytes_accessed=4 * p_count * p_tokens * depth,
            transcendentals=0,
        ),
        name="score_batch",
    )(queries, own_positives, mate_positives)


def loss_kernel(place_ref, batch_parts, own_ref, memory_parts, candidate_ref, count_ref, *out_refs):
    batch_ref, memory_ref, loss_ref = out_refs
    group, shard = place_ref[0], place_ref[1]
    core = group % 2
    _, q_count, slots = candidate_ref.shape
    chips, _, pair = batch_parts.shape
    shards, _, p_count = memory_parts.shape
    half = pair // 2

    parts = []
    for chip in range(chips):
        part = batch_parts[chip]
        swapped = jnp.concatenate([part[:, half:], part[:, :half]], axis=1)
        parts.append(jnp.where(core == 0, part, swapped))
    batch = jnp.concatenate(parts, axis=1)
    batch_ref[0] = batch

    ids = candidate_ref[0]
    padded = jnp.concatenate([ids, jnp.zeros((q_count, p_count - slots), jnp.int32)], axis=1)
    holder, local = padded // p_count, padded % p_count
    picked = jnp.take_along_axis(own_ref[0], local, axis=1)
    for index in range(shards):
        found = jnp.take_along_axis(memory_parts[index], local, axis=1)
        picked = jnp.where((holder == index) & (shard != index), found, picked)

    square = (q_count, q_count)
    diagonal = lax.broadcasted_iota(jnp.int32, square, 0) == lax.broadcasted_iota(
        jnp.int32, square, 1
    )
    counts = jnp.sum(
        jnp.where(diagonal, jnp.broadcast_to(count_ref[...], square), 0), axis=1, keepdims=True
    )
    valid = lax.broadcasted_iota(jnp.int32, (q_count, p_count), 1) < counts
    memory_ref[0] = jnp.where(valid, picked, 0.0)[:, :slots]

    top = jnp.maximum(
        jnp.max(batch, axis=1, keepdims=True),
        jnp.max(jnp.where(valid, picked, -jnp.inf), axis=1, keepdims=True),
    )
    total = jnp.sum(jnp.exp(batch - top), axis=1, keepdims=True) + jnp.sum(
        jnp.where(valid, jnp.exp(picked - top), 0.0), axis=1, keepdims=True
    )
    column = lax.broadcasted_iota(jnp.int32, batch.shape, 1)
    own = group * q_count + lax.broadcasted_iota(jnp.int32, batch.shape, 0)
    target_score = jnp.sum(jnp.where(column == own, batch, 0.0), axis=1, keepdims=True)
    loss = top + jnp.log(total) - target_score
    loss_ref[...] = jnp.sum(
        jnp.where(diagonal, jnp.broadcast_to(loss, square), 0.0), axis=0, keepdims=True
    )


def finish(batch_parts, own_scores, memory_parts, candidates, counts, place):
    _, q_count, slots = candidates.shape
    columns = batch_parts.shape[0] * batch_parts.shape[2]
    vmem = pl.BlockSpec(memory_space=pltpu.VMEM)
    return pl.pallas_call(
        loss_kernel,
        in_specs=[pl.BlockSpec(memory_space=pltpu.SMEM)] + [vmem] * 5,
        out_shape=[
            jax.ShapeDtypeStruct((1, q_count, columns), jnp.float32),
            jax.ShapeDtypeStruct((1, q_count, slots), jnp.float32),
            jax.ShapeDtypeStruct((1, q_count), jnp.float32),
        ],
        name="finish",
    )(place, batch_parts, own_scores, memory_parts, candidates, counts)


def body(queries, positives, memory, candidates, counts):
    groups = lax.axis_size("group")
    chips = groups // 2
    same_core = [list(range(core, groups, 2)) for core in range(2)]
    place = jnp.stack([lax.axis_index("group"), lax.axis_index("memory")]).astype(jnp.int32)

    column = lax.all_gather(queries, "memory", axis=0, tiled=True)
    mate_positives = lax.ppermute(positives, "group", [(i, i ^ 1) for i in range(groups)])
    row = lax.all_to_all(
        jnp.broadcast_to(queries, (chips,) + queries.shape[1:]),
        "group",
        split_axis=0,
        concat_axis=0,
        axis_index_groups=same_core,
        tiled=True,
    )
    own_scores = score_memory(queries, memory, place, False)
    batch_scores = score_batch(row, positives, mate_positives)
    memory_scores = score_memory(column, memory, place, True)

    batch_parts = lax.all_to_all(
        batch_scores,
        "group",
        split_axis=0,
        concat_axis=0,
        axis_index_groups=same_core,
        tiled=True,
    )
    memory_parts = lax.all_to_all(
        memory_scores, "memory", split_axis=0, concat_axis=0, tiled=True
    )
    return finish(batch_parts, own_scores, memory_parts, candidates, counts, place)


def solution(mesh):
    in_specs = (
        P("group", "memory", None, None),
        P("group", "memory", None, None),
        P("group", "memory", None, None),
        P("group", "memory", None),
        P("group", "memory"),
    )
    out_specs = (P("group", "memory", None), P("group", "memory", None), P("group", "memory"))
    return jax.shard_map(body, mesh=mesh, in_specs=in_specs, out_specs=out_specs, check_vma=False)
```

```python
import functools

import jax
import jax.numpy as jnp
from jax import lax
from jax.experimental import pallas as pl
from jax.experimental.pallas import tpu as pltpu
from jax.sharding import PartitionSpec as P

LANES = 128
CHUNK = 8
DOT_PASSAGES = 4


def token_max(passages, tokens):
    count, width, depth = passages.shape
    product = jnp.dot(
        passages.reshape(count * width, depth), tokens, preferred_element_type=jnp.float32
    )
    return jnp.max(product.reshape(count, width, tokens.shape[1]), axis=1)


def token_sum(best, queries):
    tokens = best.shape[1]
    per_query = tokens // queries
    row = lax.broadcasted_iota(jnp.int32, (queries, tokens), 0)
    col = lax.broadcasted_iota(jnp.int32, (queries, tokens), 1)
    own = (col // per_query == row).astype(jnp.float32)
    return lax.dot_general(
        own,
        best,
        (((1,), (1,)), ((), ())),
        precision=lax.Precision.HIGHEST,
        preferred_element_type=jnp.float32,
    )


def flat_tokens(query_ref):
    _, queries, per_query, depth = query_ref.shape
    return query_ref[0].reshape(queries * per_query, depth).T


def best_rows(passage_ref, first, tokens):
    rows = [
        token_max(passage_ref[0, pl.ds(first + start, DOT_PASSAGES)], tokens)
        for start in range(0, CHUNK, DOT_PASSAGES)
    ]
    return jnp.concatenate(rows, axis=0)


def memory_kernel(askers, *refs):
    query_refs, passage_ref = refs[:askers], refs[askers]
    out_refs = refs[askers + 1 : 2 * askers + 1]
    token_ref, best_ref = refs[2 * askers + 1 :]
    step, steps = pl.program_id(0), pl.num_programs(0)
    queries = query_refs[0].shape[1]
    block = passage_ref.shape[1]

    @pl.when(step == 0)
    def _():
        for index, query_ref in enumerate(query_refs):
            token_ref[index] = flat_tokens(query_ref)

    @pl.loop(0, block // CHUNK)
    def _(chunk):
        first = pl.multiple_of(chunk * CHUNK, CHUNK)
        row = pl.multiple_of(step * block + first, CHUNK)
        for index in range(askers):
            best_ref[index, pl.ds(row, CHUNK), :] = best_rows(
                passage_ref, first, token_ref[index]
            )

    @pl.when(step == steps - 1)
    def _():
        for index, out_ref in enumerate(out_refs):
            out_ref[...] = token_sum(best_ref[index], queries)


def score_memory(query_list, memory):
    askers = len(query_list)
    _, q_count, q_tokens, depth = query_list[0].shape
    _, p_count, p_tokens, _ = memory.shape
    block = min(32, p_count)
    tokens = q_count * q_tokens
    whole = pl.BlockSpec((1, q_count, q_tokens, depth), lambda i: (0, 0, 0, 0))
    return pl.pallas_call(
        functools.partial(memory_kernel, askers),
        grid=(p_count // block,),
        in_specs=[whole] * askers
        + [pl.BlockSpec((1, block, p_tokens, depth), lambda i: (0, i, 0, 0))],
        out_specs=[pl.BlockSpec((q_count, p_count), lambda i: (0, 0))] * askers,
        out_shape=[jax.ShapeDtypeStruct((q_count, p_count), jnp.float32)] * askers,
        scratch_shapes=[
            pltpu.VMEM((askers, depth, tokens), jnp.bfloat16),
            pltpu.VMEM((askers, p_count, tokens), jnp.float32),
        ],
        cost_estimate=pl.CostEstimate(
            flops=2 * askers * tokens * p_count * p_tokens * depth,
            bytes_accessed=2 * p_count * p_tokens * depth,
            transcendentals=0,
        ),
        name="score_memory",
    )(*query_list, memory)


def batch_kernel(chips, *refs):
    query_refs, passage_refs = refs[:2], refs[2 : 2 + chips]
    out_refs, best_ref = refs[2 + chips : 4 + chips], refs[4 + chips]
    queries = query_refs[0].shape[1]
    count = passage_refs[0].shape[1]
    best_ref[...] = jnp.zeros_like(best_ref)
    for query_ref, out_ref in zip(query_refs, out_refs):
        tokens = flat_tokens(query_ref)
        for chip, passage_ref in enumerate(passage_refs):
            for first in range(0, count, CHUNK):
                row = chip * count + first
                best_ref[row : row + CHUNK, :] = best_rows(passage_ref, first, tokens)
        out_ref[...] = token_sum(best_ref[...], queries)


def score_batch(queries, mate_queries, positives):
    _, q_count, q_tokens, depth = queries.shape
    _, p_count, p_tokens, _ = positives[0].shape
    chips = len(positives)
    lanes = -(-chips * p_count // LANES) * LANES
    return pl.pallas_call(
        functools.partial(batch_kernel, chips),
        out_shape=[jax.ShapeDtypeStruct((q_count, lanes), jnp.float32)] * 2,
        scratch_shapes=[pltpu.VMEM((lanes, q_count * q_tokens), jnp.float32)],
        cost_estimate=pl.CostEstimate(
            flops=4 * chips * q_count * q_tokens * p_count * p_tokens * depth,
            bytes_accessed=2 * chips * p_count * p_tokens * depth,
            transcendentals=0,
        ),
        name="score_batch",
    )(queries, mate_queries, *positives)


def loss_kernel(shards, place_ref, own_batch, mate_batch, own_ref, *refs):
    memory_refs = refs[: shards - 1]
    candidate_ref, count_ref, batch_ref, memory_ref, loss_ref = refs[shards - 1 :]
    group, shard = place_ref[0], place_ref[1]
    chip, core = group // 2, group % 2
    _, q_count, slots = candidate_ref.shape
    p_count = own_ref.shape[1]
    columns = batch_ref.shape[2]

    parts = []
    for first in range(0, columns, LANES):
        lane = lax.broadcasted_iota(jnp.int32, (q_count, LANES), 1) + first
        owner = lane // q_count
        source = ((owner // 2) ^ chip) * q_count + lane % q_count
        source = source % LANES
        own = jnp.take_along_axis(own_batch[...], source, axis=1)
        mate = jnp.take_along_axis(mate_batch[...], source, axis=1)
        parts.append(jnp.where(owner % 2 == core, own, mate))
    batch = jnp.concatenate(parts, axis=1)[:, :columns]
    batch_ref[0] = batch

    ids = candidate_ref[0]
    padded = jnp.concatenate([ids, jnp.zeros((q_count, p_count - slots), jnp.int32)], axis=1)
    holder, local = padded // p_count, padded % p_count
    picked = jnp.take_along_axis(own_ref[...], local, axis=1)
    for step in range(1, shards):
        found = jnp.take_along_axis(memory_refs[step - 1][...], local, axis=1)
        picked = jnp.where(holder == (shard ^ step), found, picked)

    square = (q_count, q_count)
    diagonal = lax.broadcasted_iota(jnp.int32, square, 0) == lax.broadcasted_iota(
        jnp.int32, square, 1
    )
    counts = jnp.sum(
        jnp.where(diagonal, jnp.broadcast_to(count_ref[...], square), 0), axis=1, keepdims=True
    )
    valid = lax.broadcasted_iota(jnp.int32, (q_count, p_count), 1) < counts
    memory_ref[0] = jnp.where(valid, picked, 0.0)[:, :slots]

    top = jnp.maximum(
        jnp.max(batch, axis=1, keepdims=True),
        jnp.max(jnp.where(valid, picked, -jnp.inf), axis=1, keepdims=True),
    )
    total = jnp.sum(jnp.exp(batch - top), axis=1, keepdims=True) + jnp.sum(
        jnp.where(valid, jnp.exp(picked - top), 0.0), axis=1, keepdims=True
    )
    column = lax.broadcasted_iota(jnp.int32, batch.shape, 1)
    own = group * q_count + lax.broadcasted_iota(jnp.int32, batch.shape, 0)
    target_score = jnp.sum(jnp.where(column == own, batch, 0.0), axis=1, keepdims=True)
    loss = top + jnp.log(total) - target_score
    loss_ref[...] = jnp.sum(
        jnp.where(diagonal, jnp.broadcast_to(loss, square), 0.0), axis=0, keepdims=True
    )


def finish(own_batch, mate_batch, own_scores, memory_parts, candidates, counts, place, columns):
    _, q_count, slots = candidates.shape
    shards = len(memory_parts) + 1
    vmem = pl.BlockSpec(memory_space=pltpu.VMEM)
    return pl.pallas_call(
        functools.partial(loss_kernel, shards),
        in_specs=[pl.BlockSpec(memory_space=pltpu.SMEM)] + [vmem] * (shards + 4),
        out_shape=[
            jax.ShapeDtypeStruct((1, q_count, columns), jnp.float32),
            jax.ShapeDtypeStruct((1, q_count, slots), jnp.float32),
            jax.ShapeDtypeStruct((1, q_count), jnp.float32),
        ],
        name="finish",
    )(place, own_batch, mate_batch, own_scores, *memory_parts, candidates, counts)


def body(queries, positives, memory, candidates, counts):
    shards = lax.axis_size("memory")
    groups = lax.axis_size("group")
    chips = groups // 2
    q_count = queries.shape[1]

    def to_shard(array, step):
        return lax.ppermute(array, "memory", [(i, i ^ step) for i in range(shards)])

    def to_group(array, step):
        return lax.ppermute(array, "group", [(i, i ^ step) for i in range(groups)])

    place = jnp.stack([lax.axis_index("group"), lax.axis_index("memory")]).astype(jnp.int32)
    askers = [to_shard(queries, step) for step in range(1, shards)]
    mate_queries = to_group(queries, 1)
    row = [positives] + [to_group(positives, 2 * step) for step in range(1, chips)]

    other_scores = score_memory(askers, memory)
    memory_parts = [to_shard(other_scores[step - 1], step) for step in range(1, shards)]
    queries, mate_queries, _ = lax.optimization_barrier((queries, mate_queries, other_scores))
    own_batch, mate_batch = score_batch(queries, mate_queries, row)
    mate_batch = to_group(mate_batch, 1)
    queries, _ = lax.optimization_barrier((queries, own_batch))
    (own_scores,) = score_memory([queries], memory)
    columns = groups * q_count
    return finish(
        own_batch, mate_batch, own_scores, memory_parts, candidates, counts, place, columns
    )


def solution(mesh):
    in_specs = (
        P("group", "memory", None, None),
        P("group", "memory", None, None),
        P("group", "memory", None, None),
        P("group", "memory", None),
        P("group", "memory"),
    )
    out_specs = (P("group", "memory", None), P("group", "memory", None), P("group", "memory"))
    return jax.shard_map(body, mesh=mesh, in_specs=in_specs, out_specs=out_specs, check_vma=False)
```

```python
import functools

import jax
import jax.numpy as jnp
from jax import lax
from jax.experimental import pallas as pl
from jax.experimental.pallas import tpu as pltpu
from jax.sharding import PartitionSpec as P

LANES = 128
MIB = 1024 * 1024
SLOTS = 8
CHUNK = 32
LIST_ROWS = 16


def token_max(passages, tokens):
    count, width, depth = passages.shape
    product = lax.dot_general(
        passages.reshape(count * width, depth),
        tokens,
        (((1,), (1,)), ((), ())),
        preferred_element_type=jnp.float32,
    )
    return jnp.max(product.reshape(count, width, tokens.shape[0]), axis=1)


def token_sum(best, queries):
    tokens = best.shape[1]
    per_query = tokens // queries
    row = lax.broadcasted_iota(jnp.int32, (queries, tokens), 0)
    col = lax.broadcasted_iota(jnp.int32, (queries, tokens), 1)
    own = (col // per_query == row).astype(jnp.float32)
    return lax.dot_general(
        own,
        best,
        (((1,), (1,)), ((), ())),
        precision=lax.Precision.HIGHEST,
        preferred_element_type=jnp.float32,
    )


def column_of(row):
    size = row.shape[1]
    square = (size, size)
    diagonal = lax.broadcasted_iota(jnp.int32, square, 0) == lax.broadcasted_iota(
        jnp.int32, square, 1
    )
    return jnp.sum(jnp.where(diagonal, jnp.broadcast_to(row, square), 0), axis=1, keepdims=True)


def row_of(column):
    size = column.shape[0]
    square = (size, size)
    diagonal = lax.broadcasted_iota(jnp.int32, square, 0) == lax.broadcasted_iota(
        jnp.int32, square, 1
    )
    return jnp.sum(jnp.where(diagonal, jnp.broadcast_to(column, square), 0), axis=0, keepdims=True)


def pack_kernel(p_count, query_ref, candidate_ref, count_ref, out_ref):
    _, q_count, slots = candidate_ref.shape
    _, _, q_tokens, depth = query_ref.shape
    out_ref[0, :q_count] = query_ref[0]
    ids = candidate_ref[0]
    valid = lax.broadcasted_iota(jnp.int32, ids.shape, 1) < column_of(count_ref[...])
    holder = jnp.where(valid, ids // p_count, -1)
    planes = jnp.concatenate([ids % p_count, holder], axis=0).astype(jnp.float32)
    planes = jnp.concatenate(
        [planes, jnp.zeros((2 * q_count, depth - slots), jnp.float32)], axis=1
    )
    rest = jnp.zeros((q_tokens - 2 * q_count, depth), jnp.float32)
    out_ref[0, q_count] = jnp.concatenate([planes, rest], axis=0).astype(out_ref.dtype)


def pack(queries, candidates, counts, p_count):
    _, q_count, q_tokens, depth = queries.shape
    return pl.pallas_call(
        functools.partial(pack_kernel, p_count),
        out_shape=jax.ShapeDtypeStruct((1, q_count + 1, q_tokens, depth), queries.dtype),
        compiler_params=pltpu.CompilerParams(vmem_limit_bytes=4 * MIB),
        name="pack",
    )(queries, candidates, counts)


def memory_kernel(shards, slots, *refs):
    packed_refs, memory_ref = refs[:shards], refs[shards]
    out_refs = refs[shards + 1 : 2 * shards + 1]
    passage_ref, query_ref, rank_ref, best_ref, list_ref, scalar_ref, copy_sems, list_sem = refs[
        2 * shards + 1 :
    ]
    q_count = out_refs[0].shape[0]
    p_count = passage_ref.shape[0]
    total = shards * q_count
    chunks = p_count // CHUNK

    def fetch(chunk):
        rows = pl.ds(pl.multiple_of(chunk * CHUNK, CHUNK), CHUNK)
        return pltpu.make_async_copy(
            memory_ref.at[0, rows], passage_ref.at[rows], copy_sems.at[chunk]
        )

    for chunk in range(chunks):
        fetch(chunk).start()

    me = lax.axis_index("memory").astype(jnp.float32)
    keys = []
    for index, packed_ref in enumerate(packed_refs):
        query_ref[index * q_count : (index + 1) * q_count] = packed_ref[0, :q_count]
        planes = packed_ref[0, q_count].astype(jnp.float32)
        local, holder = planes[:q_count], planes[q_count : 2 * q_count]
        keys.append(jnp.where(holder == me, local, -1.0))
    keys = jnp.concatenate(keys, axis=0)
    passage = lax.broadcasted_iota(jnp.int32, (total, p_count), 1).astype(jnp.float32)
    named = jnp.zeros((total, p_count), jnp.float32)
    for slot in range(slots):
        named = jnp.where(keys[:, slot : slot + 1] == passage, 1.0, named)

    square = (total, total)
    earlier = lax.broadcasted_iota(jnp.int32, square, 1) < lax.broadcasted_iota(
        jnp.int32, square, 0
    )
    before = jnp.dot(earlier.astype(jnp.float32), named, preferred_element_type=jnp.float32)
    rank_ref[...] = jnp.where(named > 0.0, before, -1.0)
    counts = jnp.sum(named, axis=0, keepdims=True)
    most = jnp.broadcast_to(jnp.max(counts, axis=1, keepdims=True), counts.shape)
    rest = jnp.zeros((LIST_ROWS - SLOTS - 2, p_count), jnp.float32)

    def write_list(first):
        asker = lax.broadcasted_iota(jnp.int32, (total, p_count), 0).astype(jnp.float32)
        rank = rank_ref[...] - first
        rows = [
            jnp.sum(jnp.where(rank == float(slot), asker, 0.0), axis=0, keepdims=True)
            for slot in range(SLOTS)
        ]
        list_ref[...] = jnp.concatenate(rows + [counts, most, rest], axis=0).astype(jnp.int32)
        copy = pltpu.make_async_copy(list_ref, scalar_ref, list_sem)
        copy.start()
        copy.wait()

    def unit(index):
        tokens = [query_ref[scalar_ref[slot, index]] for slot in range(SLOTS)]
        return token_max(passage_ref[pl.ds(index, 1)], jnp.concatenate(tokens, axis=0))

    def add_scores(first):
        sums = token_sum(best_ref[...], SLOTS)
        for index, out_ref in enumerate(out_refs):
            rank = rank_ref[index * q_count : (index + 1) * q_count] - first
            for slot in range(SLOTS):
                out_ref[...] = jnp.where(rank == float(slot), sums[slot : slot + 1], out_ref[...])

    for out_ref in out_refs:
        out_ref[...] = jnp.zeros_like(out_ref)
    write_list(0.0)

    @pl.loop(0, chunks)
    def _(chunk):
        fetch(chunk).wait()
        for start in range(0, CHUNK, 8):
            first = pl.multiple_of(chunk * CHUNK + start, 8)
            rows = [unit(first + offset) for offset in range(8)]
            best_ref[pl.ds(first, 8), :] = jnp.concatenate(rows, axis=0)

    add_scores(0.0)

    @pl.loop(1, (scalar_ref[SLOTS + 1, 0] + SLOTS - 1) // SLOTS)
    def _(turn):
        done = turn * SLOTS
        write_list(done.astype(jnp.float32))

        @pl.loop(0, p_count)
        def _(index):
            @pl.when(scalar_ref[SLOTS, index] > done)
            def _():
                best_ref[pl.ds(index, 1), :] = unit(index)

        add_scores(done.astype(jnp.float32))


def score_memory(packed, memory, slots):
    shards = len(packed)
    _, blocks, q_tokens, depth = packed[0].shape
    q_count = blocks - 1
    _, p_count, p_tokens, _ = memory.shape
    total = shards * q_count
    vmem = pl.BlockSpec(memory_space=pltpu.VMEM)
    return pl.pallas_call(
        functools.partial(memory_kernel, shards, slots),
        in_specs=[vmem] * shards + [pl.BlockSpec(memory_space=pltpu.HBM)],
        out_specs=[vmem] * shards,
        out_shape=[jax.ShapeDtypeStruct((q_count, p_count), jnp.float32)] * shards,
        scratch_shapes=[
            pltpu.VMEM((p_count, p_tokens, depth), memory.dtype),
            pltpu.VMEM((total, q_tokens, depth), memory.dtype),
            pltpu.VMEM((total, p_count), jnp.float32),
            pltpu.VMEM((p_count, SLOTS * q_tokens), jnp.float32),
            pltpu.VMEM((LIST_ROWS, p_count), jnp.int32),
            pltpu.SMEM((LIST_ROWS, p_count), jnp.int32),
            pltpu.SemaphoreType.DMA((p_count // CHUNK,)),
            pltpu.SemaphoreType.DMA,
        ],
        compiler_params=pltpu.CompilerParams(vmem_limit_bytes=60 * MIB),
        cost_estimate=pl.CostEstimate(
            flops=2 * SLOTS * q_tokens * p_count * p_tokens * depth,
            bytes_accessed=2 * p_count * p_tokens * depth,
            transcendentals=0,
        ),
        name="score_memory",
    )(*packed, memory)


def batch_kernel(chips, *refs):
    query_refs, passage_refs = refs[:2], refs[2 : 2 + chips]
    out_refs, best_ref = refs[2 + chips : 4 + chips], refs[4 + chips]
    _, queries, q_tokens, depth = query_refs[0].shape
    count = passage_refs[0].shape[1]
    if chips * count < best_ref.shape[0]:
        best_ref[...] = jnp.zeros_like(best_ref)
    for query_ref, out_ref in zip(query_refs, out_refs):
        tokens = query_ref[0].reshape(queries * q_tokens, depth)
        for chip, passage_ref in enumerate(passage_refs):
            best_ref[chip * count : (chip + 1) * count, :] = token_max(passage_ref[0], tokens)
        out_ref[...] = token_sum(best_ref[...], queries)


def score_batch(queries, mate_queries, positives):
    _, q_count, q_tokens, depth = queries.shape
    _, p_count, p_tokens, _ = positives[0].shape
    chips = len(positives)
    lanes = -(-chips * p_count // LANES) * LANES
    return pl.pallas_call(
        functools.partial(batch_kernel, chips),
        out_shape=[jax.ShapeDtypeStruct((q_count, lanes), jnp.float32)] * 2,
        scratch_shapes=[pltpu.VMEM((lanes, q_count * q_tokens), jnp.float32)],
        compiler_params=pltpu.CompilerParams(vmem_limit_bytes=16 * MIB),
        cost_estimate=pl.CostEstimate(
            flops=4 * chips * q_count * q_tokens * p_count * p_tokens * depth,
            bytes_accessed=2 * chips * p_count * p_tokens * depth,
            transcendentals=0,
        ),
        name="score_batch",
    )(queries, mate_queries, *positives)


def loss_kernel(shards, own_batch, mate_batch, *refs):
    memory_refs = refs[:shards]
    candidate_ref, count_ref, batch_ref, memory_ref, loss_ref = refs[shards:]
    group, shard = lax.axis_index("group"), lax.axis_index("memory")
    chip, core = group // 2, group % 2
    _, q_count, slots = candidate_ref.shape
    p_count = memory_refs[0].shape[1]
    columns = batch_ref.shape[2]

    parts = []
    for first in range(0, columns, LANES):
        lane = lax.broadcasted_iota(jnp.int32, (q_count, LANES), 1) + first
        owner = lane // q_count
        source = (((owner // 2) ^ chip) * q_count + lane % q_count) % LANES
        own = jnp.take_along_axis(own_batch[...], source, axis=1)
        mate = jnp.take_along_axis(mate_batch[...], source, axis=1)
        parts.append(jnp.where(owner % 2 == core, own, mate))
    batch = jnp.concatenate(parts, axis=1)[:, :columns]
    batch_ref[0] = batch

    ids = candidate_ref[0]
    padded = jnp.concatenate([ids, jnp.zeros((q_count, p_count - slots), jnp.int32)], axis=1)
    holder, local = padded // p_count, padded % p_count
    picked = jnp.zeros((q_count, p_count), jnp.float32)
    for step in range(shards):
        found = jnp.take_along_axis(memory_refs[step][...], local, axis=1)
        picked = jnp.where(holder == (shard ^ step), found, picked)

    valid = lax.broadcasted_iota(jnp.int32, (q_count, p_count), 1) < column_of(count_ref[...])
    memory_ref[0] = jnp.where(valid, picked, 0.0)[:, :slots]

    top = jnp.maximum(
        jnp.max(batch, axis=1, keepdims=True),
        jnp.max(jnp.where(valid, picked, -jnp.inf), axis=1, keepdims=True),
    )
    total = jnp.sum(jnp.exp(batch - top), axis=1, keepdims=True) + jnp.sum(
        jnp.where(valid, jnp.exp(picked - top), 0.0), axis=1, keepdims=True
    )
    column = lax.broadcasted_iota(jnp.int32, batch.shape, 1)
    own = group * q_count + lax.broadcasted_iota(jnp.int32, batch.shape, 0)
    target_score = jnp.sum(jnp.where(column == own, batch, 0.0), axis=1, keepdims=True)
    loss_ref[...] = row_of(top + jnp.log(total) - target_score)


def finish(own_batch, mate_batch, memory_parts, candidates, counts, columns):
    _, q_count, slots = candidates.shape
    return pl.pallas_call(
        functools.partial(loss_kernel, len(memory_parts)),
        out_shape=[
            jax.ShapeDtypeStruct((1, q_count, columns), jnp.float32),
            jax.ShapeDtypeStruct((1, q_count, slots), jnp.float32),
            jax.ShapeDtypeStruct((1, q_count), jnp.float32),
        ],
        compiler_params=pltpu.CompilerParams(vmem_limit_bytes=4 * MIB),
        name="finish",
    )(own_batch, mate_batch, *memory_parts, candidates, counts)


def body(queries, positives, memory, candidates, counts):
    shards = lax.axis_size("memory")
    groups = lax.axis_size("group")
    chips = groups // 2
    q_count = queries.shape[1]
    slots = candidates.shape[2] // 2

    def to_shard(array, step):
        return lax.ppermute(array, "memory", [(i, i ^ step) for i in range(shards)])

    def to_group(array, step):
        return lax.ppermute(array, "group", [(i, i ^ step) for i in range(groups)])

    own = pack(queries, candidates, counts, memory.shape[1])
    packed = [own] + [to_shard(own, step) for step in range(1, shards)]
    mate_queries = to_group(queries, 1)
    row = [positives] + [to_group(positives, 2 * step) for step in range(1, chips)]

    scores = score_memory(packed, memory, slots)
    memory_parts = [scores[0]] + [to_shard(scores[step], step) for step in range(1, shards)]
    queries, mate_queries, _ = lax.optimization_barrier((queries, mate_queries, scores[0]))
    own_batch, mate_batch = score_batch(queries, mate_queries, row)
    mate_batch = to_group(mate_batch, 1)
    return finish(own_batch, mate_batch, memory_parts, candidates, counts, groups * q_count)


def solution(mesh):
    in_specs = (
        P("group", "memory", None, None),
        P("group", "memory", None, None),
        P("group", "memory", None, None),
        P("group", "memory", None),
        P("group", "memory"),
    )
    out_specs = (P("group", "memory", None), P("group", "memory", None), P("group", "memory"))
    return jax.shard_map(body, mesh=mesh, in_specs=in_specs, out_specs=out_specs, check_vma=False)
```

```python
import functools

import jax
import jax.numpy as jnp
from jax import lax
from jax.experimental import pallas as pl
from jax.experimental.pallas import tpu as pltpu
from jax.sharding import PartitionSpec as P

LANES = 128
MIB = 1024 * 1024
SLOTS = 8
CHUNK = 32
LIST_ROWS = 16


def token_max(passages, tokens):
    count, width, depth = passages.shape
    product = lax.dot_general(
        passages.reshape(count * width, depth),
        tokens,
        (((1,), (1,)), ((), ())),
        preferred_element_type=jnp.float32,
    )
    return jnp.max(product.reshape(count, width, tokens.shape[0]), axis=1)


def token_sum(best, queries):
    tokens = best.shape[1]
    per_query = tokens // queries
    row = lax.broadcasted_iota(jnp.int32, (queries, tokens), 0)
    col = lax.broadcasted_iota(jnp.int32, (queries, tokens), 1)
    own = (col // per_query == row).astype(jnp.float32)
    return lax.dot_general(
        own,
        best,
        (((1,), (1,)), ((), ())),
        precision=lax.Precision.HIGHEST,
        preferred_element_type=jnp.float32,
    )


def column_of(row):
    size = row.shape[1]
    square = (size, size)
    diagonal = lax.broadcasted_iota(jnp.int32, square, 0) == lax.broadcasted_iota(
        jnp.int32, square, 1
    )
    return jnp.sum(jnp.where(diagonal, jnp.broadcast_to(row, square), 0), axis=1, keepdims=True)


def row_of(column):
    size = column.shape[0]
    square = (size, size)
    diagonal = lax.broadcasted_iota(jnp.int32, square, 0) == lax.broadcasted_iota(
        jnp.int32, square, 1
    )
    return jnp.sum(jnp.where(diagonal, jnp.broadcast_to(column, square), 0), axis=0, keepdims=True)


def pack_kernel(p_count, query_ref, candidate_ref, count_ref, out_ref):
    _, q_count, slots = candidate_ref.shape
    _, _, q_tokens, depth = query_ref.shape
    out_ref[0, :q_count] = query_ref[0]
    ids = candidate_ref[0]
    row = lax.broadcasted_iota(jnp.int32, ids.shape, 0)
    valid_count = jnp.zeros(ids.shape, jnp.int32)
    for index in range(q_count):
        valid_count = jnp.where(row == index, count_ref[0, index], valid_count)
    valid = lax.broadcasted_iota(jnp.int32, ids.shape, 1) < valid_count
    holder = jnp.where(valid, ids // p_count, -1)
    planes = jnp.concatenate([ids % p_count, holder], axis=0).astype(jnp.float32)
    planes = jnp.concatenate(
        [planes, jnp.zeros((2 * q_count, depth - slots), jnp.float32)], axis=1
    )
    rest = jnp.zeros((q_tokens - 2 * q_count, depth), jnp.float32)
    out_ref[0, q_count] = jnp.concatenate([planes, rest], axis=0).astype(out_ref.dtype)


def pack(queries, candidates, counts, p_count):
    _, q_count, q_tokens, depth = queries.shape
    vmem = pl.BlockSpec(memory_space=pltpu.VMEM)
    return pl.pallas_call(
        functools.partial(pack_kernel, p_count),
        in_specs=[vmem, vmem, pl.BlockSpec(memory_space=pltpu.SMEM)],
        out_shape=jax.ShapeDtypeStruct((1, q_count + 1, q_tokens, depth), queries.dtype),
        compiler_params=pltpu.CompilerParams(vmem_limit_bytes=4 * MIB),
        name="pack",
    )(queries, candidates, counts)


def memory_kernel(shards, slots, *refs):
    packed_refs, memory_ref = refs[:shards], refs[shards]
    out_refs = refs[shards + 1 : 2 * shards + 1]
    passage_ref, query_ref, rank_ref, best_ref, list_ref, scalar_ref, copy_sems, list_sem = refs[
        2 * shards + 1 :
    ]
    q_count = out_refs[0].shape[0]
    p_count = passage_ref.shape[0]
    total = shards * q_count
    chunks = p_count // CHUNK

    def fetch(chunk):
        rows = pl.ds(pl.multiple_of(chunk * CHUNK, CHUNK), CHUNK)
        return pltpu.make_async_copy(
            memory_ref.at[0, rows], passage_ref.at[rows], copy_sems.at[chunk]
        )

    for chunk in range(chunks):
        fetch(chunk).start()

    me = lax.axis_index("memory").astype(jnp.float32)
    keys = []
    for index, packed_ref in enumerate(packed_refs):
        query_ref[index * q_count : (index + 1) * q_count] = packed_ref[0, :q_count]
        planes = packed_ref[0, q_count].astype(jnp.float32)
        local, holder = planes[:q_count], planes[q_count : 2 * q_count]
        keys.append(jnp.where(holder == me, local, -1.0))
    keys = jnp.concatenate(keys, axis=0)
    passage = lax.broadcasted_iota(jnp.int32, (total, p_count), 1).astype(jnp.float32)
    named = jnp.zeros((total, p_count), jnp.float32)
    for slot in range(slots):
        named = jnp.where(keys[:, slot : slot + 1] == passage, 1.0, named)

    square = (total, total)
    earlier = lax.broadcasted_iota(jnp.int32, square, 1) < lax.broadcasted_iota(
        jnp.int32, square, 0
    )
    before = jnp.dot(earlier.astype(jnp.float32), named, preferred_element_type=jnp.float32)
    rank_ref[...] = jnp.where(named > 0.0, before, -1.0)
    counts = jnp.sum(named, axis=0, keepdims=True)
    most = jnp.broadcast_to(jnp.max(counts, axis=1, keepdims=True), counts.shape)
    rest = jnp.zeros((LIST_ROWS - SLOTS - 2, p_count), jnp.float32)

    def write_list(first):
        asker = lax.broadcasted_iota(jnp.int32, (total, p_count), 0).astype(jnp.float32)
        rank = rank_ref[...] - first
        rows = [
            jnp.sum(jnp.where(rank == float(slot), asker, 0.0), axis=0, keepdims=True)
            for slot in range(SLOTS)
        ]
        list_ref[...] = jnp.concatenate(rows + [counts, most, rest], axis=0).astype(jnp.int32)
        copy = pltpu.make_async_copy(list_ref, scalar_ref, list_sem)
        copy.start()
        copy.wait()

    def unit(index):
        tokens = [query_ref[scalar_ref[slot, index]] for slot in range(SLOTS)]
        return token_max(passage_ref[pl.ds(index, 1)], jnp.concatenate(tokens, axis=0))

    def add_scores(first):
        sums = token_sum(best_ref[...], SLOTS)
        for index, out_ref in enumerate(out_refs):
            rank = rank_ref[index * q_count : (index + 1) * q_count] - first
            for slot in range(SLOTS):
                out_ref[...] = jnp.where(rank == float(slot), sums[slot : slot + 1], out_ref[...])

    for out_ref in out_refs:
        out_ref[...] = jnp.zeros_like(out_ref)
    write_list(0.0)

    @pl.loop(0, chunks)
    def _(chunk):
        fetch(chunk).wait()
        for start in range(0, CHUNK, 8):
            first = pl.multiple_of(chunk * CHUNK + start, 8)
            rows = [unit(first + offset) for offset in range(8)]
            best_ref[pl.ds(first, 8), :] = jnp.concatenate(rows, axis=0)

    add_scores(0.0)

    @pl.loop(1, (scalar_ref[SLOTS + 1, 0] + SLOTS - 1) // SLOTS)
    def _(turn):
        done = turn * SLOTS
        write_list(done.astype(jnp.float32))

        @pl.loop(0, p_count)
        def _(index):
            @pl.when(scalar_ref[SLOTS, index] > done)
            def _():
                best_ref[pl.ds(index, 1), :] = unit(index)

        add_scores(done.astype(jnp.float32))


def score_memory(packed, memory, slots):
    shards = len(packed)
    _, blocks, q_tokens, depth = packed[0].shape
    q_count = blocks - 1
    _, p_count, p_tokens, _ = memory.shape
    total = shards * q_count
    vmem = pl.BlockSpec(memory_space=pltpu.VMEM)
    return pl.pallas_call(
        functools.partial(memory_kernel, shards, slots),
        in_specs=[vmem] * shards + [pl.BlockSpec(memory_space=pltpu.HBM)],
        out_specs=[vmem] * shards,
        out_shape=[jax.ShapeDtypeStruct((q_count, p_count), jnp.float32)] * shards,
        scratch_shapes=[
            pltpu.VMEM((p_count, p_tokens, depth), memory.dtype),
            pltpu.VMEM((total, q_tokens, depth), memory.dtype),
            pltpu.VMEM((total, p_count), jnp.float32),
            pltpu.VMEM((p_count, SLOTS * q_tokens), jnp.float32),
            pltpu.VMEM((LIST_ROWS, p_count), jnp.int32),
            pltpu.SMEM((LIST_ROWS, p_count), jnp.int32),
            pltpu.SemaphoreType.DMA((p_count // CHUNK,)),
            pltpu.SemaphoreType.DMA,
        ],
        compiler_params=pltpu.CompilerParams(vmem_limit_bytes=57 * MIB),
        cost_estimate=pl.CostEstimate(
            flops=2 * SLOTS * q_tokens * p_count * p_tokens * depth,
            bytes_accessed=2 * p_count * p_tokens * depth,
            transcendentals=0,
        ),
        name="score_memory",
    )(*packed, memory)


def batch_kernel(chips, *refs):
    query_refs, passage_refs = refs[:2], refs[2 : 2 + chips]
    out_refs, best_ref = refs[2 + chips : 4 + chips], refs[4 + chips]
    _, queries, q_tokens, depth = query_refs[0].shape
    count = passage_refs[0].shape[1]
    if chips * count < best_ref.shape[0]:
        best_ref[...] = jnp.zeros_like(best_ref)
    for query_ref, out_ref in zip(query_refs, out_refs):
        tokens = query_ref[0].reshape(queries * q_tokens, depth)
        for chip, passage_ref in enumerate(passage_refs):
            best_ref[chip * count : (chip + 1) * count, :] = token_max(passage_ref[0], tokens)
        out_ref[...] = token_sum(best_ref[...], queries)


def score_batch(queries, mate_queries, positives):
    _, q_count, q_tokens, depth = queries.shape
    _, p_count, p_tokens, _ = positives[0].shape
    chips = len(positives)
    lanes = -(-chips * p_count // LANES) * LANES
    return pl.pallas_call(
        functools.partial(batch_kernel, chips),
        out_shape=[jax.ShapeDtypeStruct((q_count, lanes), jnp.float32)] * 2,
        scratch_shapes=[pltpu.VMEM((lanes, q_count * q_tokens), jnp.float32)],
        compiler_params=pltpu.CompilerParams(vmem_limit_bytes=16 * MIB),
        cost_estimate=pl.CostEstimate(
            flops=4 * chips * q_count * q_tokens * p_count * p_tokens * depth,
            bytes_accessed=2 * chips * p_count * p_tokens * depth,
            transcendentals=0,
        ),
        name="score_batch",
    )(queries, mate_queries, *positives)


def loss_kernel(shards, own_batch, mate_batch, *refs):
    memory_refs = refs[:shards]
    candidate_ref, count_ref, batch_ref, memory_ref, loss_ref = refs[shards:]
    group, shard = lax.axis_index("group"), lax.axis_index("memory")
    chip, core = group // 2, group % 2
    _, q_count, slots = candidate_ref.shape
    p_count = memory_refs[0].shape[1]
    columns = batch_ref.shape[2]

    parts = []
    for first in range(0, columns, LANES):
        lane = lax.broadcasted_iota(jnp.int32, (q_count, LANES), 1) + first
        owner = lane // q_count
        source = (((owner // 2) ^ chip) * q_count + lane % q_count) % LANES
        own = jnp.take_along_axis(own_batch[...], source, axis=1)
        mate = jnp.take_along_axis(mate_batch[...], source, axis=1)
        parts.append(jnp.where(owner % 2 == core, own, mate))
    batch = jnp.concatenate(parts, axis=1)[:, :columns]
    batch_ref[0] = batch

    ids = candidate_ref[0]
    padded = jnp.concatenate([ids, jnp.zeros((q_count, p_count - slots), jnp.int32)], axis=1)
    holder, local = padded // p_count, padded % p_count
    picked = jnp.zeros((q_count, p_count), jnp.float32)
    for step in range(shards):
        found = jnp.take_along_axis(memory_refs[step][...], local, axis=1)
        picked = jnp.where(holder == (shard ^ step), found, picked)

    valid = lax.broadcasted_iota(jnp.int32, (q_count, p_count), 1) < column_of(count_ref[...])
    memory_ref[0] = jnp.where(valid, picked, 0.0)[:, :slots]

    top = jnp.maximum(
        jnp.max(batch, axis=1, keepdims=True),
        jnp.max(jnp.where(valid, picked, -jnp.inf), axis=1, keepdims=True),
    )
    total = jnp.sum(jnp.exp(batch - top), axis=1, keepdims=True) + jnp.sum(
        jnp.where(valid, jnp.exp(picked - top), 0.0), axis=1, keepdims=True
    )
    column = lax.broadcasted_iota(jnp.int32, batch.shape, 1)
    own = group * q_count + lax.broadcasted_iota(jnp.int32, batch.shape, 0)
    target_score = jnp.sum(jnp.where(column == own, batch, 0.0), axis=1, keepdims=True)
    loss_ref[...] = row_of(top + jnp.log(total) - target_score)


def finish(own_batch, mate_batch, memory_parts, candidates, counts, columns):
    _, q_count, slots = candidates.shape
    return pl.pallas_call(
        functools.partial(loss_kernel, len(memory_parts)),
        out_shape=[
            jax.ShapeDtypeStruct((1, q_count, columns), jnp.float32),
            jax.ShapeDtypeStruct((1, q_count, slots), jnp.float32),
            jax.ShapeDtypeStruct((1, q_count), jnp.float32),
        ],
        compiler_params=pltpu.CompilerParams(vmem_limit_bytes=4 * MIB),
        name="finish",
    )(own_batch, mate_batch, *memory_parts, candidates, counts)


def body(queries, positives, memory, candidates, counts):
    shards = lax.axis_size("memory")
    groups = lax.axis_size("group")
    chips = groups // 2
    q_count = queries.shape[1]
    slots = candidates.shape[2] // 2

    def to_shard(array, step):
        return lax.ppermute(array, "memory", [(i, i ^ step) for i in range(shards)])

    def to_group(array, step):
        return lax.ppermute(array, "group", [(i, i ^ step) for i in range(groups)])

    own = pack(queries, candidates, counts, memory.shape[1])
    packed = [own] + [to_shard(own, step) for step in range(1, shards)]
    early, _ = lax.optimization_barrier((positives, own))
    late, late_queries, _ = lax.optimization_barrier((positives, queries, packed[1]))
    row = [positives]
    for step in range(1, chips):
        near = step & (step - 1) == 0
        row.append(to_group(early if near else late, 2 * step))
    mate_queries = to_group(late_queries, 1)

    scores = score_memory(packed, memory, slots)
    memory_parts = [scores[0]] + [to_shard(scores[step], step) for step in range(1, shards)]
    queries, mate_queries, _ = lax.optimization_barrier((queries, mate_queries, scores[0]))
    own_batch, mate_batch = score_batch(queries, mate_queries, row)
    mate_batch = to_group(mate_batch, 1)
    return finish(own_batch, mate_batch, memory_parts, candidates, counts, groups * q_count)


def solution(mesh):
    in_specs = (
        P("group", "memory", None, None),
        P("group", "memory", None, None),
        P("group", "memory", None, None),
        P("group", "memory", None),
        P("group", "memory"),
    )
    out_specs = (P("group", "memory", None), P("group", "memory", None), P("group", "memory"))
    return jax.shard_map(body, mesh=mesh, in_specs=in_specs, out_specs=out_specs, check_vma=False)
```

```python
import functools

import jax
import jax.numpy as jnp
from jax import lax
from jax.experimental import pallas as pl
from jax.experimental.pallas import tpu as pltpu
from jax.sharding import PartitionSpec as P

LANES = 128
MIB = 1024 * 1024
SLOTS = 8
CHUNK = 32
LIST_ROWS = 16


def token_max(passages, tokens):
    count, width, depth = passages.shape
    product = lax.dot_general(
        passages.reshape(count * width, depth),
        tokens,
        (((1,), (1,)), ((), ())),
        preferred_element_type=jnp.float32,
    )
    return jnp.max(product.reshape(count, width, tokens.shape[0]), axis=1)


def token_sum(best, queries):
    tokens = best.shape[1]
    per_query = tokens // queries
    row = lax.broadcasted_iota(jnp.int32, (queries, tokens), 0)
    col = lax.broadcasted_iota(jnp.int32, (queries, tokens), 1)
    own = (col // per_query == row).astype(jnp.float32)
    return lax.dot_general(
        own,
        best,
        (((1,), (1,)), ((), ())),
        precision=lax.Precision.HIGHEST,
        preferred_element_type=jnp.float32,
    )


def column_of(row):
    size = row.shape[1]
    square = (size, size)
    diagonal = lax.broadcasted_iota(jnp.int32, square, 0) == lax.broadcasted_iota(
        jnp.int32, square, 1
    )
    return jnp.sum(jnp.where(diagonal, jnp.broadcast_to(row, square), 0), axis=1, keepdims=True)


def row_of(column):
    size = column.shape[0]
    square = (size, size)
    diagonal = lax.broadcasted_iota(jnp.int32, square, 0) == lax.broadcasted_iota(
        jnp.int32, square, 1
    )
    return jnp.sum(jnp.where(diagonal, jnp.broadcast_to(column, square), 0), axis=0, keepdims=True)


def pack_kernel(p_count, query_ref, candidate_ref, count_ref, out_ref):
    _, q_count, slots = candidate_ref.shape
    _, _, q_tokens, depth = query_ref.shape
    out_ref[0, :q_count] = query_ref[0]
    ids = candidate_ref[0]
    row = lax.broadcasted_iota(jnp.int32, ids.shape, 0)
    valid_count = jnp.zeros(ids.shape, jnp.int32)
    for index in range(q_count):
        valid_count = jnp.where(row == index, count_ref[0, index], valid_count)
    valid = lax.broadcasted_iota(jnp.int32, ids.shape, 1) < valid_count
    holder = jnp.where(valid, ids // p_count, -1)
    planes = jnp.concatenate([ids % p_count, holder], axis=0).astype(jnp.float32)
    planes = jnp.concatenate(
        [planes, jnp.zeros((2 * q_count, depth - slots), jnp.float32)], axis=1
    )
    rest = jnp.zeros((q_tokens - 2 * q_count, depth), jnp.float32)
    out_ref[0, q_count] = jnp.concatenate([planes, rest], axis=0).astype(out_ref.dtype)


def pack(queries, candidates, counts, p_count):
    _, q_count, q_tokens, depth = queries.shape
    vmem = pl.BlockSpec(memory_space=pltpu.VMEM)
    return pl.pallas_call(
        functools.partial(pack_kernel, p_count),
        in_specs=[vmem, vmem, pl.BlockSpec(memory_space=pltpu.SMEM)],
        out_shape=jax.ShapeDtypeStruct((1, q_count + 1, q_tokens, depth), queries.dtype),
        compiler_params=pltpu.CompilerParams(vmem_limit_bytes=56 * MIB),
        name="pack",
    )(queries, candidates, counts)


def memory_kernel(shards, slots, *refs):
    packed_refs, memory_ref = refs[:shards], refs[shards]
    out_refs = refs[shards + 1 : 2 * shards + 1]
    passage_ref, query_ref, rank_ref, best_ref, list_ref, scalar_ref, copy_sems, list_sem = refs[
        2 * shards + 1 :
    ]
    q_count = out_refs[0].shape[0]
    p_count = passage_ref.shape[0]
    total = shards * q_count
    chunks = p_count // CHUNK

    def fetch(chunk):
        rows = pl.ds(pl.multiple_of(chunk * CHUNK, CHUNK), CHUNK)
        return pltpu.make_async_copy(
            memory_ref.at[0, rows], passage_ref.at[rows], copy_sems.at[chunk]
        )

    for chunk in range(chunks):
        fetch(chunk).start()

    me = lax.axis_index("memory").astype(jnp.float32)
    keys = []
    for index, packed_ref in enumerate(packed_refs):
        query_ref[index * q_count : (index + 1) * q_count] = packed_ref[0, :q_count]
        planes = packed_ref[0, q_count].astype(jnp.float32)
        local, holder = planes[:q_count], planes[q_count : 2 * q_count]
        keys.append(jnp.where(holder == me, local, -1.0))
    keys = jnp.concatenate(keys, axis=0)
    passage = lax.broadcasted_iota(jnp.int32, (total, p_count), 1).astype(jnp.float32)
    named = jnp.zeros((total, p_count), jnp.float32)
    for slot in range(slots):
        named = jnp.where(keys[:, slot : slot + 1] == passage, 1.0, named)

    square = (total, total)
    earlier = lax.broadcasted_iota(jnp.int32, square, 1) < lax.broadcasted_iota(
        jnp.int32, square, 0
    )
    before = jnp.dot(earlier.astype(jnp.float32), named, preferred_element_type=jnp.float32)
    rank_ref[...] = jnp.where(named > 0.0, before, -1.0)
    counts = jnp.sum(named, axis=0, keepdims=True)
    most = jnp.broadcast_to(jnp.max(counts, axis=1, keepdims=True), counts.shape)
    rest = jnp.zeros((LIST_ROWS - SLOTS - 2, p_count), jnp.float32)

    def write_list(first):
        asker = lax.broadcasted_iota(jnp.int32, (total, p_count), 0).astype(jnp.float32)
        rank = rank_ref[...] - first
        rows = [
            jnp.sum(jnp.where(rank == float(slot), asker, 0.0), axis=0, keepdims=True)
            for slot in range(SLOTS)
        ]
        list_ref[...] = jnp.concatenate(rows + [counts, most, rest], axis=0).astype(jnp.int32)
        copy = pltpu.make_async_copy(list_ref, scalar_ref, list_sem)
        copy.start()
        copy.wait()

    def unit(index):
        tokens = [query_ref[scalar_ref[slot, index]] for slot in range(SLOTS)]
        return token_max(passage_ref[pl.ds(index, 1)], jnp.concatenate(tokens, axis=0))

    def add_scores(first):
        sums = token_sum(best_ref[...], SLOTS)
        for index, out_ref in enumerate(out_refs):
            rank = rank_ref[index * q_count : (index + 1) * q_count] - first
            for slot in range(SLOTS):
                out_ref[...] = jnp.where(rank == float(slot), sums[slot : slot + 1], out_ref[...])

    for out_ref in out_refs:
        out_ref[...] = jnp.zeros_like(out_ref)
    write_list(0.0)

    @pl.loop(0, chunks)
    def _(chunk):
        fetch(chunk).wait()
        for start in range(0, CHUNK, 8):
            first = pl.multiple_of(chunk * CHUNK + start, 8)
            rows = [unit(first + offset) for offset in range(8)]
            best_ref[pl.ds(first, 8), :] = jnp.concatenate(rows, axis=0)

    add_scores(0.0)

    @pl.loop(1, (scalar_ref[SLOTS + 1, 0] + SLOTS - 1) // SLOTS)
    def _(turn):
        done = turn * SLOTS
        write_list(done.astype(jnp.float32))

        @pl.loop(0, p_count)
        def _(index):
            @pl.when(scalar_ref[SLOTS, index] > done)
            def _():
                best_ref[pl.ds(index, 1), :] = unit(index)

        add_scores(done.astype(jnp.float32))


def score_memory(packed, memory, slots):
    shards = len(packed)
    _, blocks, q_tokens, depth = packed[0].shape
    q_count = blocks - 1
    _, p_count, p_tokens, _ = memory.shape
    total = shards * q_count
    vmem = pl.BlockSpec(memory_space=pltpu.VMEM)
    return pl.pallas_call(
        functools.partial(memory_kernel, shards, slots),
        in_specs=[vmem] * shards + [pl.BlockSpec(memory_space=pltpu.HBM)],
        out_specs=[vmem] * shards,
        out_shape=[jax.ShapeDtypeStruct((q_count, p_count), jnp.float32)] * shards,
        scratch_shapes=[
            pltpu.VMEM((p_count, p_tokens, depth), memory.dtype),
            pltpu.VMEM((total, q_tokens, depth), memory.dtype),
            pltpu.VMEM((total, p_count), jnp.float32),
            pltpu.VMEM((p_count, SLOTS * q_tokens), jnp.float32),
            pltpu.VMEM((LIST_ROWS, p_count), jnp.int32),
            pltpu.SMEM((LIST_ROWS, p_count), jnp.int32),
            pltpu.SemaphoreType.DMA((p_count // CHUNK,)),
            pltpu.SemaphoreType.DMA,
        ],
        compiler_params=pltpu.CompilerParams(vmem_limit_bytes=52 * MIB),
        cost_estimate=pl.CostEstimate(
            flops=2 * SLOTS * q_tokens * p_count * p_tokens * depth,
            bytes_accessed=2 * p_count * p_tokens * depth,
            transcendentals=0,
        ),
        name="score_memory",
    )(*packed, memory)


def batch_kernel(chips, *refs):
    query_refs, passage_refs = refs[:2], refs[2 : 2 + chips]
    out_refs, best_ref = refs[2 + chips : 4 + chips], refs[4 + chips]
    _, queries, q_tokens, depth = query_refs[0].shape
    count = passage_refs[0].shape[1]
    if chips * count < best_ref.shape[0]:
        best_ref[...] = jnp.zeros_like(best_ref)
    for query_ref, out_ref in zip(query_refs, out_refs):
        tokens = query_ref[0].reshape(queries * q_tokens, depth)
        for chip, passage_ref in enumerate(passage_refs):
            best_ref[chip * count : (chip + 1) * count, :] = token_max(passage_ref[0], tokens)
        out_ref[...] = token_sum(best_ref[...], queries)


def score_batch(queries, mate_queries, positives):
    _, q_count, q_tokens, depth = queries.shape
    _, p_count, p_tokens, _ = positives[0].shape
    chips = len(positives)
    lanes = -(-chips * p_count // LANES) * LANES
    return pl.pallas_call(
        functools.partial(batch_kernel, chips),
        out_shape=[jax.ShapeDtypeStruct((q_count, lanes), jnp.float32)] * 2,
        scratch_shapes=[pltpu.VMEM((lanes, q_count * q_tokens), jnp.float32)],
        compiler_params=pltpu.CompilerParams(vmem_limit_bytes=16 * MIB),
        cost_estimate=pl.CostEstimate(
            flops=4 * chips * q_count * q_tokens * p_count * p_tokens * depth,
            bytes_accessed=2 * chips * p_count * p_tokens * depth,
            transcendentals=0,
        ),
        name="score_batch",
    )(queries, mate_queries, *positives)


def loss_kernel(shards, own_batch, mate_batch, *refs):
    memory_refs = refs[:shards]
    candidate_ref, count_ref, batch_ref, memory_ref, loss_ref = refs[shards:]
    group, shard = lax.axis_index("group"), lax.axis_index("memory")
    chip, core = group // 2, group % 2
    _, q_count, slots = candidate_ref.shape
    p_count = memory_refs[0].shape[1]
    columns = batch_ref.shape[2]

    parts = []
    for first in range(0, columns, LANES):
        lane = lax.broadcasted_iota(jnp.int32, (q_count, LANES), 1) + first
        owner = lane // q_count
        source = (((owner // 2) ^ chip) * q_count + lane % q_count) % LANES
        own = jnp.take_along_axis(own_batch[...], source, axis=1)
        mate = jnp.take_along_axis(mate_batch[...], source, axis=1)
        parts.append(jnp.where(owner % 2 == core, own, mate))
    batch = jnp.concatenate(parts, axis=1)[:, :columns]
    batch_ref[0] = batch

    ids = candidate_ref[0]
    padded = jnp.concatenate([ids, jnp.zeros((q_count, p_count - slots), jnp.int32)], axis=1)
    holder, local = padded // p_count, padded % p_count
    picked = jnp.zeros((q_count, p_count), jnp.float32)
    for step in range(shards):
        found = jnp.take_along_axis(memory_refs[step][...], local, axis=1)
        picked = jnp.where(holder == (shard ^ step), found, picked)

    valid = lax.broadcasted_iota(jnp.int32, (q_count, p_count), 1) < column_of(count_ref[...])
    memory_ref[0] = jnp.where(valid, picked, 0.0)[:, :slots]

    top = jnp.maximum(
        jnp.max(batch, axis=1, keepdims=True),
        jnp.max(jnp.where(valid, picked, -jnp.inf), axis=1, keepdims=True),
    )
    total = jnp.sum(jnp.exp(batch - top), axis=1, keepdims=True) + jnp.sum(
        jnp.where(valid, jnp.exp(picked - top), 0.0), axis=1, keepdims=True
    )
    column = lax.broadcasted_iota(jnp.int32, batch.shape, 1)
    own = group * q_count + lax.broadcasted_iota(jnp.int32, batch.shape, 0)
    target_score = jnp.sum(jnp.where(column == own, batch, 0.0), axis=1, keepdims=True)
    loss_ref[...] = row_of(top + jnp.log(total) - target_score)


def finish(own_batch, mate_batch, memory_parts, candidates, counts, columns):
    _, q_count, slots = candidates.shape
    return pl.pallas_call(
        functools.partial(loss_kernel, len(memory_parts)),
        out_shape=[
            jax.ShapeDtypeStruct((1, q_count, columns), jnp.float32),
            jax.ShapeDtypeStruct((1, q_count, slots), jnp.float32),
            jax.ShapeDtypeStruct((1, q_count), jnp.float32),
        ],
        compiler_params=pltpu.CompilerParams(vmem_limit_bytes=4 * MIB),
        name="finish",
    )(own_batch, mate_batch, *memory_parts, candidates, counts)


def body(queries, positives, memory, candidates, counts):
    shards = lax.axis_size("memory")
    groups = lax.axis_size("group")
    chips = groups // 2
    q_count = queries.shape[1]
    slots = candidates.shape[2] // 2

    def to_shard(array, step):
        return lax.ppermute(array, "memory", [(i, i ^ step) for i in range(shards)])

    def to_group(array, step):
        return lax.ppermute(array, "group", [(i, i ^ step) for i in range(groups)])

    own = pack(queries, candidates, counts, memory.shape[1])
    packed = [own] + [to_shard(own, step) for step in range(1, shards)]
    sent_positives, _ = lax.optimization_barrier((positives, packed[1]))
    sent_queries, _ = lax.optimization_barrier((queries, packed[-1]))
    row = [positives] + [to_group(sent_positives, 2 * step) for step in range(1, chips)]
    mate_queries = to_group(sent_queries, 1)

    scores = score_memory(packed, memory, slots)
    memory_parts = [scores[0]] + [to_shard(scores[step], step) for step in range(1, shards)]
    queries, mate_queries, _ = lax.optimization_barrier((queries, mate_queries, scores[0]))
    own_batch, mate_batch = score_batch(queries, mate_queries, row)
    mate_batch = to_group(mate_batch, 1)
    return finish(own_batch, mate_batch, memory_parts, candidates, counts, groups * q_count)


def solution(mesh):
    in_specs = (
        P("group", "memory", None, None),
        P("group", "memory", None, None),
        P("group", "memory", None, None),
        P("group", "memory", None),
        P("group", "memory"),
    )
    out_specs = (P("group", "memory", None), P("group", "memory", None), P("group", "memory"))
    return jax.shard_map(body, mesh=mesh, in_specs=in_specs, out_specs=out_specs, check_vma=False)
```

```python
import functools

import jax
import jax.numpy as jnp
from jax import lax
from jax.experimental import pallas as pl
from jax.experimental.pallas import tpu as pltpu
from jax.sharding import PartitionSpec as P

LANES = 128
MIB = 1024 * 1024
SLOTS = 8
CHUNK = 32
LIST_ROWS = 16


def in_hbm(array):
    return pltpu.with_memory_space_constraint(array, pltpu.HBM)


def token_max(passages, tokens):
    count, width, depth = passages.shape
    product = lax.dot_general(
        passages.reshape(count * width, depth),
        tokens,
        (((1,), (1,)), ((), ())),
        preferred_element_type=jnp.float32,
    )
    return jnp.max(product.reshape(count, width, tokens.shape[0]), axis=1)


def token_sum(best, queries):
    tokens = best.shape[1]
    per_query = tokens // queries
    row = lax.broadcasted_iota(jnp.int32, (queries, tokens), 0)
    col = lax.broadcasted_iota(jnp.int32, (queries, tokens), 1)
    own = (col // per_query == row).astype(jnp.float32)
    return lax.dot_general(
        own,
        best,
        (((1,), (1,)), ((), ())),
        precision=lax.Precision.HIGHEST,
        preferred_element_type=jnp.float32,
    )


def column_of(row):
    size = row.shape[1]
    square = (size, size)
    diagonal = lax.broadcasted_iota(jnp.int32, square, 0) == lax.broadcasted_iota(
        jnp.int32, square, 1
    )
    return jnp.sum(jnp.where(diagonal, jnp.broadcast_to(row, square), 0), axis=1, keepdims=True)


def row_of(column):
    size = column.shape[0]
    square = (size, size)
    diagonal = lax.broadcasted_iota(jnp.int32, square, 0) == lax.broadcasted_iota(
        jnp.int32, square, 1
    )
    return jnp.sum(jnp.where(diagonal, jnp.broadcast_to(column, square), 0), axis=0, keepdims=True)


def split_ids(p_count, candidate_ref, count_ref):
    ids = candidate_ref[0]
    row = lax.broadcasted_iota(jnp.int32, ids.shape, 0)
    valid_count = jnp.zeros(ids.shape, jnp.int32)
    for index in range(ids.shape[0]):
        valid_count = jnp.where(row == index, count_ref[0, index], valid_count)
    valid = lax.broadcasted_iota(jnp.int32, ids.shape, 1) < valid_count
    holder = jnp.where(valid, ids // p_count, -1)
    return (ids % p_count).astype(jnp.float32), holder.astype(jnp.float32)


def pack_kernel(p_count, query_ref, candidate_ref, count_ref, out_ref):
    _, q_count, slots = candidate_ref.shape
    _, _, q_tokens, depth = query_ref.shape
    out_ref[0, :q_count] = query_ref[0]
    planes = jnp.concatenate(split_ids(p_count, candidate_ref, count_ref), axis=0)
    planes = jnp.concatenate(
        [planes, jnp.zeros((2 * q_count, depth - slots), jnp.float32)], axis=1
    )
    rest = jnp.zeros((q_tokens - 2 * q_count, depth), jnp.float32)
    out_ref[0, q_count] = jnp.concatenate([planes, rest], axis=0).astype(out_ref.dtype)


def pack(queries, candidates, counts, p_count):
    _, q_count, q_tokens, depth = queries.shape
    vmem = pl.BlockSpec(memory_space=pltpu.VMEM)
    return pl.pallas_call(
        functools.partial(pack_kernel, p_count),
        in_specs=[vmem, vmem, pl.BlockSpec(memory_space=pltpu.SMEM)],
        out_shape=jax.ShapeDtypeStruct((1, q_count + 1, q_tokens, depth), queries.dtype),
        compiler_params=pltpu.CompilerParams(vmem_limit_bytes=4 * MIB),
        name="pack",
    )(in_hbm(queries), in_hbm(candidates), in_hbm(counts))


def memory_kernel(shards, slots, *refs):
    packed_refs, memory_ref = refs[:shards], refs[shards]
    out_refs = refs[shards + 1 : 2 * shards + 1]
    passage_ref, query_ref, rank_ref, best_ref, list_ref, scalar_ref, copy_sems, list_sem = refs[
        2 * shards + 1 :
    ]
    q_count = out_refs[0].shape[0]
    p_count = passage_ref.shape[0]
    total = shards * q_count
    chunks = p_count // CHUNK

    def fetch(chunk):
        rows = pl.ds(pl.multiple_of(chunk * CHUNK, CHUNK), CHUNK)
        return pltpu.make_async_copy(
            memory_ref.at[0, rows], passage_ref.at[rows], copy_sems.at[chunk]
        )

    for chunk in range(chunks):
        fetch(chunk).start()

    me = lax.axis_index("memory").astype(jnp.float32)
    keys = []
    for index, packed_ref in enumerate(packed_refs):
        query_ref[index * q_count : (index + 1) * q_count] = packed_ref[0, :q_count]
        planes = packed_ref[0, q_count].astype(jnp.float32)
        local, holder = planes[:q_count], planes[q_count : 2 * q_count]
        keys.append(jnp.where(holder == me, local, -1.0))
    keys = jnp.concatenate(keys, axis=0)
    passage = lax.broadcasted_iota(jnp.int32, (total, p_count), 1).astype(jnp.float32)
    named = jnp.zeros((total, p_count), jnp.float32)
    for slot in range(slots):
        named = jnp.where(keys[:, slot : slot + 1] == passage, 1.0, named)

    square = (total, total)
    earlier = lax.broadcasted_iota(jnp.int32, square, 1) < lax.broadcasted_iota(
        jnp.int32, square, 0
    )
    before = jnp.dot(earlier.astype(jnp.float32), named, preferred_element_type=jnp.float32)
    rank_ref[...] = jnp.where(named > 0.0, before, -1.0)
    counts = jnp.sum(named, axis=0, keepdims=True)
    most = jnp.broadcast_to(jnp.max(counts, axis=1, keepdims=True), counts.shape)
    rest = jnp.zeros((LIST_ROWS - SLOTS - 2, p_count), jnp.float32)

    def write_list(first):
        asker = lax.broadcasted_iota(jnp.int32, (total, p_count), 0).astype(jnp.float32)
        rank = rank_ref[...] - first
        rows = [
            jnp.sum(jnp.where(rank == float(slot), asker, 0.0), axis=0, keepdims=True)
            for slot in range(SLOTS)
        ]
        list_ref[...] = jnp.concatenate(rows + [counts, most, rest], axis=0).astype(jnp.int32)
        copy = pltpu.make_async_copy(list_ref, scalar_ref, list_sem)
        copy.start()
        copy.wait()

    def unit(index):
        tokens = [query_ref[scalar_ref[slot, index]] for slot in range(SLOTS)]
        return token_max(passage_ref[pl.ds(index, 1)], jnp.concatenate(tokens, axis=0))

    def add_scores(first):
        sums = token_sum(best_ref[...], SLOTS)
        for index, out_ref in enumerate(out_refs):
            rank = rank_ref[index * q_count : (index + 1) * q_count] - first
            for slot in range(SLOTS):
                out_ref[...] = jnp.where(rank == float(slot), sums[slot : slot + 1], out_ref[...])

    for out_ref in out_refs:
        out_ref[...] = jnp.zeros_like(out_ref)
    write_list(0.0)

    @pl.loop(0, chunks)
    def _(chunk):
        fetch(chunk).wait()
        for start in range(0, CHUNK, 8):
            first = pl.multiple_of(chunk * CHUNK + start, 8)
            rows = [unit(first + offset) for offset in range(8)]
            best_ref[pl.ds(first, 8), :] = jnp.concatenate(rows, axis=0)

    add_scores(0.0)

    @pl.loop(1, (scalar_ref[SLOTS + 1, 0] + SLOTS - 1) // SLOTS)
    def _(turn):
        done = turn * SLOTS
        write_list(done.astype(jnp.float32))

        @pl.loop(0, p_count)
        def _(index):
            @pl.when(scalar_ref[SLOTS, index] > done)
            def _():
                best_ref[pl.ds(index, 1), :] = unit(index)

        add_scores(done.astype(jnp.float32))


def score_memory(packed, memory, slots):
    shards = len(packed)
    _, blocks, q_tokens, depth = packed[0].shape
    q_count = blocks - 1
    _, p_count, p_tokens, _ = memory.shape
    total = shards * q_count
    vmem = pl.BlockSpec(memory_space=pltpu.VMEM)
    return pl.pallas_call(
        functools.partial(memory_kernel, shards, slots),
        in_specs=[vmem] * shards + [pl.BlockSpec(memory_space=pltpu.HBM)],
        out_specs=[vmem] * shards,
        out_shape=[jax.ShapeDtypeStruct((q_count, p_count), jnp.float32)] * shards,
        scratch_shapes=[
            pltpu.VMEM((p_count, p_tokens, depth), memory.dtype),
            pltpu.VMEM((total, q_tokens, depth), memory.dtype),
            pltpu.VMEM((total, p_count), jnp.float32),
            pltpu.VMEM((p_count, SLOTS * q_tokens), jnp.float32),
            pltpu.VMEM((LIST_ROWS, p_count), jnp.int32),
            pltpu.SMEM((LIST_ROWS, p_count), jnp.int32),
            pltpu.SemaphoreType.DMA((p_count // CHUNK,)),
            pltpu.SemaphoreType.DMA,
        ],
        compiler_params=pltpu.CompilerParams(vmem_limit_bytes=16 * MIB),
        cost_estimate=pl.CostEstimate(
            flops=2 * total * q_tokens * p_count * p_tokens * depth,
            bytes_accessed=2 * p_count * p_tokens * depth,
            transcendentals=0,
        ),
        name="score_memory",
    )(*packed, in_hbm(memory))


def batch_kernel(chips, *refs):
    query_refs, passage_refs = refs[:2], refs[2 : 2 + chips]
    out_refs, best_ref = refs[2 + chips : 4 + chips], refs[4 + chips]
    _, queries, q_tokens, depth = query_refs[0].shape
    count = passage_refs[0].shape[1]
    if chips * count < best_ref.shape[0]:
        best_ref[...] = jnp.zeros_like(best_ref)
    for query_ref, out_ref in zip(query_refs, out_refs):
        tokens = query_ref[0].reshape(queries * q_tokens, depth)
        for chip, passage_ref in enumerate(passage_refs):
            best_ref[chip * count : (chip + 1) * count, :] = token_max(passage_ref[0], tokens)
        out_ref[...] = token_sum(best_ref[...], queries)


def score_batch(queries, mate_queries, positives):
    _, q_count, q_tokens, depth = queries.shape
    _, p_count, p_tokens, _ = positives[0].shape
    chips = len(positives)
    lanes = -(-chips * p_count // LANES) * LANES
    return pl.pallas_call(
        functools.partial(batch_kernel, chips),
        out_shape=[jax.ShapeDtypeStruct((q_count, lanes), jnp.float32)] * 2,
        scratch_shapes=[pltpu.VMEM((lanes, q_count * q_tokens), jnp.float32)],
        compiler_params=pltpu.CompilerParams(vmem_limit_bytes=16 * MIB),
        cost_estimate=pl.CostEstimate(
            flops=4 * chips * q_count * q_tokens * p_count * p_tokens * depth,
            bytes_accessed=2 * chips * p_count * p_tokens * depth,
            transcendentals=0,
        ),
        name="score_batch",
    )(queries, mate_queries, *positives)


def loss_kernel(shards, own_batch, mate_batch, *refs):
    memory_refs = refs[:shards]
    candidate_ref, count_ref, batch_ref, memory_ref, loss_ref = refs[shards:]
    group, shard = lax.axis_index("group"), lax.axis_index("memory")
    chip, core = group // 2, group % 2
    _, q_count, slots = candidate_ref.shape
    p_count = memory_refs[0].shape[1]
    columns = batch_ref.shape[2]

    parts = []
    for first in range(0, columns, LANES):
        lane = lax.broadcasted_iota(jnp.int32, (q_count, LANES), 1) + first
        owner = lane // q_count
        source = (((owner // 2) ^ chip) * q_count + lane % q_count) % LANES
        own = jnp.take_along_axis(own_batch[...], source, axis=1)
        mate = jnp.take_along_axis(mate_batch[...], source, axis=1)
        parts.append(jnp.where(owner % 2 == core, own, mate))
    batch = jnp.concatenate(parts, axis=1)[:, :columns]
    batch_ref[0] = batch

    ids = candidate_ref[0]
    padded = jnp.concatenate([ids, jnp.zeros((q_count, p_count - slots), jnp.int32)], axis=1)
    holder, local = padded // p_count, padded % p_count
    picked = jnp.zeros((q_count, p_count), jnp.float32)
    for step in range(shards):
        found = jnp.take_along_axis(memory_refs[step][...], local, axis=1)
        picked = jnp.where(holder == (shard ^ step), found, picked)

    valid = lax.broadcasted_iota(jnp.int32, (q_count, p_count), 1) < column_of(count_ref[...])
    memory_ref[0] = jnp.where(valid, picked, 0.0)[:, :slots]

    top = jnp.maximum(
        jnp.max(batch, axis=1, keepdims=True),
        jnp.max(jnp.where(valid, picked, -jnp.inf), axis=1, keepdims=True),
    )
    total = jnp.sum(jnp.exp(batch - top), axis=1, keepdims=True) + jnp.sum(
        jnp.where(valid, jnp.exp(picked - top), 0.0), axis=1, keepdims=True
    )
    column = lax.broadcasted_iota(jnp.int32, batch.shape, 1)
    own = group * q_count + lax.broadcasted_iota(jnp.int32, batch.shape, 0)
    target_score = jnp.sum(jnp.where(column == own, batch, 0.0), axis=1, keepdims=True)
    loss_ref[...] = row_of(top + jnp.log(total) - target_score)


def finish(own_batch, mate_batch, memory_parts, candidates, counts, columns):
    _, q_count, slots = candidates.shape
    return pl.pallas_call(
        functools.partial(loss_kernel, len(memory_parts)),
        out_shape=[
            jax.ShapeDtypeStruct((1, q_count, columns), jnp.float32),
            jax.ShapeDtypeStruct((1, q_count, slots), jnp.float32),
            jax.ShapeDtypeStruct((1, q_count), jnp.float32),
        ],
        compiler_params=pltpu.CompilerParams(vmem_limit_bytes=4 * MIB),
        name="finish",
    )(own_batch, mate_batch, *memory_parts, candidates, counts)


def body(queries, positives, memory, candidates, counts):
    shards = lax.axis_size("memory")
    groups = lax.axis_size("group")
    chips = groups // 2
    q_count = queries.shape[1]
    slots = candidates.shape[2] // 2

    def to_shard(array, step):
        return lax.ppermute(array, "memory", [(i, i ^ step) for i in range(shards)])

    def to_group(array, step):
        return lax.ppermute(array, "group", [(i, i ^ step) for i in range(groups)])

    own = pack(queries, candidates, counts, memory.shape[1])
    packed = [own] + [to_shard(own, step) for step in range(1, shards)]
    sent_positives, sent_queries, _ = lax.optimization_barrier((positives, queries, own))
    row = [positives] + [to_group(sent_positives, 2 * step) for step in range(1, chips)]
    mate_queries = to_group(sent_queries, 1)

    scores = list(score_memory(packed, memory, slots))
    own_queries, mate_queries, _ = lax.optimization_barrier((queries, mate_queries, scores[0]))
    own_batch, mate_batch = score_batch(own_queries, mate_queries, row)
    scores[1], mate_batch = lax.optimization_barrier((scores[1], mate_batch))
    mate_batch = to_group(mate_batch, 1)
    memory_parts = [scores[0]] + [to_shard(scores[step], step) for step in range(1, shards)]
    return finish(own_batch, mate_batch, memory_parts, candidates, counts, groups * q_count)


def solution(mesh):
    in_specs = (
        P("group", "memory", None, None),
        P("group", "memory", None, None),
        P("group", "memory", None, None),
        P("group", "memory", None),
        P("group", "memory"),
    )
    out_specs = (P("group", "memory", None), P("group", "memory", None), P("group", "memory"))
    return jax.shard_map(body, mesh=mesh, in_specs=in_specs, out_specs=out_specs, check_vma=False)
```

```python
import functools

import jax
import jax.numpy as jnp
from jax import lax
from jax.experimental import pallas as pl
from jax.experimental.pallas import tpu as pltpu
from jax.sharding import PartitionSpec as P

LANES = 128
MIB = 1024 * 1024
SLOTS = 8
CHUNK = 32
LIST_ROWS = 16


def in_hbm(array):
    return pltpu.with_memory_space_constraint(array, pltpu.HBM)


def token_max(passages, tokens):
    count, width, depth = passages.shape
    product = lax.dot_general(
        passages.reshape(count * width, depth),
        tokens,
        (((1,), (1,)), ((), ())),
        preferred_element_type=jnp.float32,
    )
    return jnp.max(product.reshape(count, width, tokens.shape[0]), axis=1)


def token_sum(best, queries):
    tokens = best.shape[1]
    per_query = tokens // queries
    row = lax.broadcasted_iota(jnp.int32, (queries, tokens), 0)
    col = lax.broadcasted_iota(jnp.int32, (queries, tokens), 1)
    own = (col // per_query == row).astype(jnp.float32)
    return lax.dot_general(
        own,
        best,
        (((1,), (1,)), ((), ())),
        precision=lax.Precision.HIGHEST,
        preferred_element_type=jnp.float32,
    )


def column_of(row):
    size = row.shape[1]
    square = (size, size)
    diagonal = lax.broadcasted_iota(jnp.int32, square, 0) == lax.broadcasted_iota(
        jnp.int32, square, 1
    )
    return jnp.sum(jnp.where(diagonal, jnp.broadcast_to(row, square), 0), axis=1, keepdims=True)


def row_of(column):
    size = column.shape[0]
    square = (size, size)
    diagonal = lax.broadcasted_iota(jnp.int32, square, 0) == lax.broadcasted_iota(
        jnp.int32, square, 1
    )
    return jnp.sum(jnp.where(diagonal, jnp.broadcast_to(column, square), 0), axis=0, keepdims=True)


def split_ids(p_count, candidate_ref, count_ref):
    ids = candidate_ref[0]
    row = lax.broadcasted_iota(jnp.int32, ids.shape, 0)
    valid_count = jnp.zeros(ids.shape, jnp.int32)
    for index in range(ids.shape[0]):
        valid_count = jnp.where(row == index, count_ref[0, index], valid_count)
    valid = lax.broadcasted_iota(jnp.int32, ids.shape, 1) < valid_count
    holder = jnp.where(valid, ids // p_count, -1)
    return (ids % p_count).astype(jnp.float32), holder.astype(jnp.float32)


def pack_kernel(p_count, query_ref, candidate_ref, count_ref, out_ref):
    _, q_count, slots = candidate_ref.shape
    _, _, q_tokens, depth = query_ref.shape
    out_ref[0, :q_count] = query_ref[0]
    planes = jnp.concatenate(split_ids(p_count, candidate_ref, count_ref), axis=0)
    planes = jnp.concatenate(
        [planes, jnp.zeros((2 * q_count, depth - slots), jnp.float32)], axis=1
    )
    rest = jnp.zeros((q_tokens - 2 * q_count, depth), jnp.float32)
    out_ref[0, q_count] = jnp.concatenate([planes, rest], axis=0).astype(out_ref.dtype)


def pack(queries, candidates, counts, p_count):
    _, q_count, q_tokens, depth = queries.shape
    vmem = pl.BlockSpec(memory_space=pltpu.VMEM)
    return pl.pallas_call(
        functools.partial(pack_kernel, p_count),
        in_specs=[vmem, vmem, pl.BlockSpec(memory_space=pltpu.SMEM)],
        out_shape=jax.ShapeDtypeStruct((1, q_count + 1, q_tokens, depth), queries.dtype),
        compiler_params=pltpu.CompilerParams(vmem_limit_bytes=4 * MIB),
        name="pack",
    )(in_hbm(queries), in_hbm(candidates), in_hbm(counts))


def memory_kernel(shards, slots, *refs):
    packed_refs, memory_ref = refs[:shards], refs[shards]
    out_refs = refs[shards + 1 : 2 * shards + 1]
    passage_ref, query_ref, rank_ref, best_ref, list_ref, scalar_ref, copy_sems, list_sem = refs[
        2 * shards + 1 :
    ]
    q_count = out_refs[0].shape[0]
    p_count = passage_ref.shape[0]
    total = shards * q_count
    chunks = p_count // CHUNK

    def fetch(chunk):
        rows = pl.ds(pl.multiple_of(chunk * CHUNK, CHUNK), CHUNK)
        return pltpu.make_async_copy(
            memory_ref.at[0, rows], passage_ref.at[rows], copy_sems.at[chunk]
        )

    for chunk in range(chunks):
        fetch(chunk).start()

    me = lax.axis_index("memory").astype(jnp.float32)
    keys = []
    for index, packed_ref in enumerate(packed_refs):
        query_ref[index * q_count : (index + 1) * q_count] = packed_ref[0, :q_count]
        planes = packed_ref[0, q_count].astype(jnp.float32)
        local, holder = planes[:q_count], planes[q_count : 2 * q_count]
        keys.append(jnp.where(holder == me, local, -1.0))
    keys = jnp.concatenate(keys, axis=0)
    passage = lax.broadcasted_iota(jnp.int32, (total, p_count), 1).astype(jnp.float32)
    named = jnp.zeros((total, p_count), jnp.float32)
    for slot in range(slots):
        named = jnp.where(keys[:, slot : slot + 1] == passage, 1.0, named)

    square = (total, total)
    earlier = lax.broadcasted_iota(jnp.int32, square, 1) < lax.broadcasted_iota(
        jnp.int32, square, 0
    )
    before = jnp.dot(earlier.astype(jnp.float32), named, preferred_element_type=jnp.float32)
    rank_ref[...] = jnp.where(named > 0.0, before, -1.0)
    counts = jnp.sum(named, axis=0, keepdims=True)
    most = jnp.broadcast_to(jnp.max(counts, axis=1, keepdims=True), counts.shape)
    rest = jnp.zeros((LIST_ROWS - SLOTS - 2, p_count), jnp.float32)

    def write_list(first):
        asker = lax.broadcasted_iota(jnp.int32, (total, p_count), 0).astype(jnp.float32)
        rank = rank_ref[...] - first
        rows = [
            jnp.sum(jnp.where(rank == float(slot), asker, 0.0), axis=0, keepdims=True)
            for slot in range(SLOTS)
        ]
        list_ref[...] = jnp.concatenate(rows + [counts, most, rest], axis=0).astype(jnp.int32)
        copy = pltpu.make_async_copy(list_ref, scalar_ref, list_sem)
        copy.start()
        copy.wait()

    def unit(index):
        tokens = [query_ref[scalar_ref[slot, index]] for slot in range(SLOTS)]
        return token_max(passage_ref[pl.ds(index, 1)], jnp.concatenate(tokens, axis=0))

    def add_scores(first):
        sums = token_sum(best_ref[...], SLOTS)
        for index, out_ref in enumerate(out_refs):
            rank = rank_ref[index * q_count : (index + 1) * q_count] - first
            for slot in range(SLOTS):
                out_ref[...] = jnp.where(rank == float(slot), sums[slot : slot + 1], out_ref[...])

    for out_ref in out_refs:
        out_ref[...] = jnp.zeros_like(out_ref)
    write_list(0.0)

    @pl.loop(0, chunks)
    def _(chunk):
        fetch(chunk).wait()
        for start in range(0, CHUNK, 8):
            first = pl.multiple_of(chunk * CHUNK + start, 8)
            rows = [unit(first + offset) for offset in range(8)]
            best_ref[pl.ds(first, 8), :] = jnp.concatenate(rows, axis=0)

    add_scores(0.0)

    @pl.loop(1, (scalar_ref[SLOTS + 1, 0] + SLOTS - 1) // SLOTS)
    def _(turn):
        done = turn * SLOTS
        write_list(done.astype(jnp.float32))

        @pl.loop(0, p_count)
        def _(index):
            @pl.when(scalar_ref[SLOTS, index] > done)
            def _():
                best_ref[pl.ds(index, 1), :] = unit(index)

        add_scores(done.astype(jnp.float32))


def score_memory(packed, memory, slots):
    shards = len(packed)
    _, blocks, q_tokens, depth = packed[0].shape
    q_count = blocks - 1
    _, p_count, p_tokens, _ = memory.shape
    total = shards * q_count
    vmem = pl.BlockSpec(memory_space=pltpu.VMEM)
    return pl.pallas_call(
        functools.partial(memory_kernel, shards, slots),
        in_specs=[vmem] * shards + [pl.BlockSpec(memory_space=pltpu.HBM)],
        out_specs=[vmem] * shards,
        out_shape=[jax.ShapeDtypeStruct((q_count, p_count), jnp.float32)] * shards,
        scratch_shapes=[
            pltpu.VMEM((p_count, p_tokens, depth), memory.dtype),
            pltpu.VMEM((total, q_tokens, depth), memory.dtype),
            pltpu.VMEM((total, p_count), jnp.float32),
            pltpu.VMEM((p_count, SLOTS * q_tokens), jnp.float32),
            pltpu.VMEM((LIST_ROWS, p_count), jnp.int32),
            pltpu.SMEM((LIST_ROWS, p_count), jnp.int32),
            pltpu.SemaphoreType.DMA((p_count // CHUNK,)),
            pltpu.SemaphoreType.DMA,
        ],
        compiler_params=pltpu.CompilerParams(vmem_limit_bytes=16 * MIB),
        cost_estimate=pl.CostEstimate(
            flops=2 * total * q_tokens * p_count * p_tokens * depth,
            bytes_accessed=2 * p_count * p_tokens * depth,
            transcendentals=0,
        ),
        name="score_memory",
    )(*packed, in_hbm(memory))


def batch_kernel(query_ref, *refs):
    passage_refs, (out_ref, best_ref) = refs[:-2], refs[-2:]
    _, queries, q_tokens, depth = query_ref.shape
    count = passage_refs[0].shape[1]
    if len(passage_refs) * count < best_ref.shape[0]:
        best_ref[...] = jnp.zeros_like(best_ref)
    tokens = query_ref[0].reshape(queries * q_tokens, depth)
    for chip, passage_ref in enumerate(passage_refs):
        best_ref[chip * count : (chip + 1) * count, :] = token_max(passage_ref[0], tokens)
    out_ref[...] = token_sum(best_ref[...], queries)


def score_batch(queries, positives):
    _, q_count, q_tokens, depth = queries.shape
    _, p_count, p_tokens, _ = positives[0].shape
    chips = len(positives)
    lanes = -(-chips * p_count // LANES) * LANES
    return pl.pallas_call(
        batch_kernel,
        out_shape=jax.ShapeDtypeStruct((q_count, lanes), jnp.float32),
        scratch_shapes=[pltpu.VMEM((lanes, q_count * q_tokens), jnp.float32)],
        compiler_params=pltpu.CompilerParams(vmem_limit_bytes=16 * MIB),
        cost_estimate=pl.CostEstimate(
            flops=2 * chips * q_count * q_tokens * p_count * p_tokens * depth,
            bytes_accessed=2 * chips * p_count * p_tokens * depth,
            transcendentals=0,
        ),
        name="score_batch",
    )(queries, *positives)


def loss_kernel(shards, own_batch, mate_batch, *refs):
    memory_refs = refs[:shards]
    candidate_ref, count_ref, batch_ref, memory_ref, loss_ref = refs[shards:]
    group, shard = lax.axis_index("group"), lax.axis_index("memory")
    chip, core = group // 2, group % 2
    _, q_count, slots = candidate_ref.shape
    p_count = memory_refs[0].shape[1]
    columns = batch_ref.shape[2]

    parts = []
    for first in range(0, columns, LANES):
        lane = lax.broadcasted_iota(jnp.int32, (q_count, LANES), 1) + first
        owner = lane // q_count
        source = (((owner // 2) ^ chip) * q_count + lane % q_count) % LANES
        own = jnp.take_along_axis(own_batch[...], source, axis=1)
        mate = jnp.take_along_axis(mate_batch[...], source, axis=1)
        parts.append(jnp.where(owner % 2 == core, own, mate))
    batch = jnp.concatenate(parts, axis=1)[:, :columns]
    batch_ref[0] = batch

    ids = candidate_ref[0]
    padded = jnp.concatenate([ids, jnp.zeros((q_count, p_count - slots), jnp.int32)], axis=1)
    holder, local = padded // p_count, padded % p_count
    picked = jnp.zeros((q_count, p_count), jnp.float32)
    for step in range(shards):
        found = jnp.take_along_axis(memory_refs[-step][...], local, axis=1)
        picked = jnp.where(holder == (shard ^ step), found, picked)

    valid = lax.broadcasted_iota(jnp.int32, (q_count, p_count), 1) < column_of(count_ref[...])
    memory_ref[0] = jnp.where(valid, picked, 0.0)[:, :slots]

    top = jnp.maximum(
        jnp.max(batch, axis=1, keepdims=True),
        jnp.max(jnp.where(valid, picked, -jnp.inf), axis=1, keepdims=True),
    )
    total = jnp.sum(jnp.exp(batch - top), axis=1, keepdims=True) + jnp.sum(
        jnp.where(valid, jnp.exp(picked - top), 0.0), axis=1, keepdims=True
    )
    column = lax.broadcasted_iota(jnp.int32, batch.shape, 1)
    own = group * q_count + lax.broadcasted_iota(jnp.int32, batch.shape, 0)
    target_score = jnp.sum(jnp.where(column == own, batch, 0.0), axis=1, keepdims=True)
    loss_ref[...] = row_of(top + jnp.log(total) - target_score)


def finish(own_batch, mate_batch, memory_parts, candidates, counts, columns):
    _, q_count, slots = candidates.shape
    return pl.pallas_call(
        functools.partial(loss_kernel, len(memory_parts)),
        out_shape=[
            jax.ShapeDtypeStruct((1, q_count, columns), jnp.float32),
            jax.ShapeDtypeStruct((1, q_count, slots), jnp.float32),
            jax.ShapeDtypeStruct((1, q_count), jnp.float32),
        ],
        compiler_params=pltpu.CompilerParams(vmem_limit_bytes=4 * MIB),
        name="finish",
    )(own_batch, mate_batch, *memory_parts, candidates, counts)


def body(queries, positives, memory, candidates, counts):
    shards = lax.axis_size("memory")
    groups = lax.axis_size("group")
    chips = groups // 2
    q_count = queries.shape[1]
    slots = candidates.shape[2] // 2

    def to_shard(array, step):
        return lax.ppermute(array, "memory", [(i, i ^ step) for i in range(shards)])

    def to_group(array, step):
        return lax.ppermute(array, "group", [(i, i ^ step) for i in range(groups)])

    own = pack(queries, candidates, counts, memory.shape[1])
    packed = [own] + [to_shard(own, step) for step in range(1, shards)]
    sent_positives, sent_queries, _ = lax.optimization_barrier((positives, queries, own))
    row = [positives] + [to_group(sent_positives, 2 * step) for step in range(1, chips)]
    mate_queries = to_group(sent_queries, 1)

    scores = list(score_memory(packed, memory, slots))
    returned = {step: to_shard(scores[step], step) for step in range(shards - 1, 0, -1)}
    memory_parts = [scores[0]] + list(returned.values())
    mate_queries, _ = lax.optimization_barrier((mate_queries, scores[0]))
    mate_scores = score_batch(mate_queries, row)
    mate_batch = to_group(mate_scores, 1)
    own_queries, _ = lax.optimization_barrier((queries, mate_scores))
    own_batch = score_batch(own_queries, row)
    return finish(own_batch, mate_batch, memory_parts, candidates, counts, groups * q_count)


def solution(mesh):
    in_specs = (
        P("group", "memory", None, None),
        P("group", "memory", None, None),
        P("group", "memory", None, None),
        P("group", "memory", None),
        P("group", "memory"),
    )
    out_specs = (P("group", "memory", None), P("group", "memory", None), P("group", "memory"))
    return jax.shard_map(body, mesh=mesh, in_specs=in_specs, out_specs=out_specs, check_vma=False)
```

```python
import functools

import jax
import jax.numpy as jnp
from jax import lax
from jax.experimental import pallas as pl
from jax.experimental.pallas import tpu as pltpu
from jax.sharding import PartitionSpec as P

LANES = 128
MIB = 1024 * 1024
SLOTS = 8
CHUNK = 64
LIST_ROWS = 16


def in_hbm(array):
    return pltpu.with_memory_space_constraint(array, pltpu.HBM)


def token_max(passages, tokens):
    count, width, depth = passages.shape
    product = lax.dot_general(
        passages.reshape(count * width, depth),
        tokens,
        (((1,), (1,)), ((), ())),
        preferred_element_type=jnp.float32,
    )
    return jnp.max(product.reshape(count, width, tokens.shape[0]), axis=1)


def token_sum(best, queries):
    tokens = best.shape[1]
    per_query = tokens // queries
    row = lax.broadcasted_iota(jnp.int32, (queries, tokens), 0)
    col = lax.broadcasted_iota(jnp.int32, (queries, tokens), 1)
    own = (col // per_query == row).astype(jnp.float32)
    return lax.dot_general(
        own,
        best,
        (((1,), (1,)), ((), ())),
        precision=lax.Precision.HIGHEST,
        preferred_element_type=jnp.float32,
    )


def column_of(row):
    size = row.shape[1]
    square = (size, size)
    diagonal = lax.broadcasted_iota(jnp.int32, square, 0) == lax.broadcasted_iota(
        jnp.int32, square, 1
    )
    return jnp.sum(jnp.where(diagonal, jnp.broadcast_to(row, square), 0), axis=1, keepdims=True)


def row_of(column):
    size = column.shape[0]
    square = (size, size)
    diagonal = lax.broadcasted_iota(jnp.int32, square, 0) == lax.broadcasted_iota(
        jnp.int32, square, 1
    )
    return jnp.sum(jnp.where(diagonal, jnp.broadcast_to(column, square), 0), axis=0, keepdims=True)


def split_ids(p_count, candidate_ref, count_ref):
    ids = candidate_ref[0]
    row = lax.broadcasted_iota(jnp.int32, ids.shape, 0)
    valid_count = jnp.zeros(ids.shape, jnp.int32)
    for index in range(ids.shape[0]):
        valid_count = jnp.where(row == index, count_ref[0, index], valid_count)
    valid = lax.broadcasted_iota(jnp.int32, ids.shape, 1) < valid_count
    holder = jnp.where(valid, ids // p_count, -1)
    return (ids % p_count).astype(jnp.float32), holder.astype(jnp.float32)


def pack_kernel(p_count, query_ref, candidate_ref, count_ref, out_ref):
    _, q_count, slots = candidate_ref.shape
    _, _, q_tokens, depth = query_ref.shape
    out_ref[0, :q_count] = query_ref[0]
    planes = jnp.concatenate(split_ids(p_count, candidate_ref, count_ref), axis=0)
    planes = jnp.concatenate(
        [planes, jnp.zeros((2 * q_count, depth - slots), jnp.float32)], axis=1
    )
    rest = jnp.zeros((q_tokens - 2 * q_count, depth), jnp.float32)
    out_ref[0, q_count] = jnp.concatenate([planes, rest], axis=0).astype(out_ref.dtype)


def pack(queries, candidates, counts, p_count):
    _, q_count, q_tokens, depth = queries.shape
    vmem = pl.BlockSpec(memory_space=pltpu.VMEM)
    return pl.pallas_call(
        functools.partial(pack_kernel, p_count),
        in_specs=[vmem, vmem, pl.BlockSpec(memory_space=pltpu.SMEM)],
        out_shape=jax.ShapeDtypeStruct((1, q_count + 1, q_tokens, depth), queries.dtype),
        compiler_params=pltpu.CompilerParams(vmem_limit_bytes=4 * MIB),
        name="pack",
    )(in_hbm(queries), in_hbm(candidates), in_hbm(counts))


def memory_kernel(shards, slots, *refs):
    packed_refs, memory_ref = refs[shards - 1 :: -1], refs[shards]
    pairs = shards // 2
    pair_refs = refs[shards + pairs : shards : -1]
    passage_ref, query_ref, rank_ref, best_ref, list_ref, scalar_ref, copy_sems, list_sem = refs[
        shards + 1 + pairs :
    ]
    out_refs = [pair_ref.at[index] for pair_ref in pair_refs for index in range(2)]
    q_count = pair_refs[0].shape[1]
    p_count = passage_ref.shape[0]
    total = shards * q_count
    chunks = p_count // CHUNK

    def fetch(chunk):
        rows = pl.ds(pl.multiple_of(chunk * CHUNK, CHUNK), CHUNK)
        return pltpu.make_async_copy(
            memory_ref.at[0, rows], passage_ref.at[rows], copy_sems.at[chunk]
        )

    for chunk in range(chunks):
        fetch(chunk).start()

    me = lax.axis_index("memory").astype(jnp.float32)
    keys = []
    for index, packed_ref in enumerate(packed_refs):
        query_ref[index * q_count : (index + 1) * q_count] = packed_ref[0, :q_count]
        planes = packed_ref[0, q_count].astype(jnp.float32)
        local, holder = planes[:q_count], planes[q_count : 2 * q_count]
        keys.append(jnp.where(holder == me, local, -1.0))
    keys = jnp.concatenate(keys, axis=0)
    passage = lax.broadcasted_iota(jnp.int32, (total, p_count), 1).astype(jnp.float32)
    named = jnp.zeros((total, p_count), jnp.float32)
    for slot in range(slots):
        named = jnp.where(keys[:, slot : slot + 1] == passage, 1.0, named)

    square = (total, total)
    earlier = lax.broadcasted_iota(jnp.int32, square, 1) < lax.broadcasted_iota(
        jnp.int32, square, 0
    )
    before = jnp.dot(earlier.astype(jnp.float32), named, preferred_element_type=jnp.float32)
    rank_ref[...] = jnp.where(named > 0.0, before, -1.0)
    counts = jnp.sum(named, axis=0, keepdims=True)
    most = jnp.broadcast_to(jnp.max(counts, axis=1, keepdims=True), counts.shape)

    def left_over(first):
        left = jnp.where(rank_ref[...] == first, 1.0, 0.0)
        left = jnp.sum(left, axis=0, keepdims=True)
        square = (p_count, p_count)
        row = lax.broadcasted_iota(jnp.int32, square, 0).astype(jnp.float32)
        column = lax.broadcasted_iota(jnp.int32, square, 1).astype(jnp.float32)
        place = jnp.dot(left, (row < column).astype(jnp.float32), preferred_element_type=jnp.float32)
        mine = jnp.where((place == row) & (left > 0.0), column, 0.0)
        index = jnp.sum(mine, axis=1, keepdims=True)
        index = jnp.sum(jnp.where(row == column, index, 0.0), axis=0, keepdims=True)
        return [index, jnp.broadcast_to(jnp.sum(left, axis=1, keepdims=True), left.shape)]

    def write_list(first, extra):
        asker = lax.broadcasted_iota(jnp.int32, (total, p_count), 0).astype(jnp.float32)
        rank = rank_ref[...] - first
        rows = [
            jnp.sum(jnp.where(rank == float(slot), asker, 0.0), axis=0, keepdims=True)
            for slot in range(SLOTS)
        ]
        rest = jnp.zeros((LIST_ROWS - SLOTS - len(extra), p_count), jnp.float32)
        list_ref[...] = jnp.concatenate(rows + extra + [rest], axis=0).astype(jnp.int32)
        copy = pltpu.make_async_copy(list_ref, scalar_ref, list_sem)
        copy.start()
        copy.wait()

    def unit(index):
        tokens = [query_ref[scalar_ref[slot, index]] for slot in range(SLOTS)]
        return token_max(passage_ref[pl.ds(index, 1)], jnp.concatenate(tokens, axis=0))

    def add_scores(first):
        sums = token_sum(best_ref[...], SLOTS)
        for index, out_ref in enumerate(out_refs):
            rank = rank_ref[index * q_count : (index + 1) * q_count] - first
            for slot in range(SLOTS):
                out_ref[...] = jnp.where(rank == float(slot), sums[slot : slot + 1], out_ref[...])

    for out_ref in out_refs:
        out_ref[...] = jnp.zeros_like(out_ref)
    write_list(0.0, [most])
    rounds = (scalar_ref[SLOTS, 0] + SLOTS - 1) // SLOTS

    @pl.loop(0, chunks)
    def _(chunk):
        fetch(chunk).wait()
        for start in range(0, CHUNK, 8):
            first = pl.multiple_of(chunk * CHUNK + start, 8)
            rows = [unit(first + offset) for offset in range(8)]
            best_ref[pl.ds(first, 8), :] = jnp.concatenate(rows, axis=0)

    add_scores(0.0)

    @pl.loop(1, rounds)
    def _(turn):
        done = (turn * SLOTS).astype(jnp.float32)
        write_list(done, left_over(done))

        @pl.loop(0, scalar_ref[SLOTS + 1, 0])
        def _(place):
            index = scalar_ref[SLOTS, place]
            best_ref[pl.ds(index, 1), :] = unit(index)

        add_scores(done)


def score_memory(packed, memory, slots):
    shards = len(packed)
    _, blocks, q_tokens, depth = packed[0].shape
    q_count = blocks - 1
    _, p_count, p_tokens, _ = memory.shape
    total = shards * q_count
    vmem = pl.BlockSpec(memory_space=pltpu.VMEM)
    return pl.pallas_call(
        functools.partial(memory_kernel, shards, slots),
        in_specs=[vmem] * shards + [pl.BlockSpec(memory_space=pltpu.HBM)],
        out_specs=[vmem] * (shards // 2),
        out_shape=[jax.ShapeDtypeStruct((2, q_count, p_count), jnp.float32)] * (shards // 2),
        scratch_shapes=[
            pltpu.VMEM((p_count, p_tokens, depth), memory.dtype),
            pltpu.VMEM((total, q_tokens, depth), memory.dtype),
            pltpu.VMEM((total, p_count), jnp.float32),
            pltpu.VMEM((p_count, SLOTS * q_tokens), jnp.float32),
            pltpu.VMEM((LIST_ROWS, p_count), jnp.int32),
            pltpu.SMEM((LIST_ROWS, p_count), jnp.int32),
            pltpu.SemaphoreType.DMA((p_count // CHUNK,)),
            pltpu.SemaphoreType.DMA,
        ],
        compiler_params=pltpu.CompilerParams(vmem_limit_bytes=16 * MIB),
        cost_estimate=pl.CostEstimate(
            flops=2 * total * q_tokens * p_count * p_tokens * depth,
            bytes_accessed=2 * p_count * p_tokens * depth,
            transcendentals=0,
        ),
        name="score_memory",
    )(*packed, in_hbm(memory))


def batch_kernel(query_ref, *refs):
    passage_refs, (out_ref, best_ref) = refs[:-2], refs[-2:]
    _, queries, q_tokens, depth = query_ref.shape
    count = passage_refs[0].shape[1]
    if len(passage_refs) * count < best_ref.shape[0]:
        best_ref[...] = jnp.zeros_like(best_ref)
    tokens = query_ref[0].reshape(queries * q_tokens, depth)
    for chip, passage_ref in enumerate(passage_refs):
        best_ref[chip * count : (chip + 1) * count, :] = token_max(passage_ref[0], tokens)
    out_ref[...] = token_sum(best_ref[...], queries)


def score_batch(queries, positives):
    _, q_count, q_tokens, depth = queries.shape
    _, p_count, p_tokens, _ = positives[0].shape
    chips = len(positives)
    lanes = -(-chips * p_count // LANES) * LANES
    return pl.pallas_call(
        batch_kernel,
        out_shape=jax.ShapeDtypeStruct((q_count, lanes), jnp.float32),
        scratch_shapes=[pltpu.VMEM((lanes, q_count * q_tokens), jnp.float32)],
        compiler_params=pltpu.CompilerParams(vmem_limit_bytes=16 * MIB),
        cost_estimate=pl.CostEstimate(
            flops=2 * chips * q_count * q_tokens * p_count * p_tokens * depth,
            bytes_accessed=2 * chips * p_count * p_tokens * depth,
            transcendentals=0,
        ),
        name="score_batch",
    )(queries, *positives)


def loss_kernel(shards, own_batch, mate_batch, *refs):
    pairs = shards // 2 - 1
    far_refs, near_refs, hop_refs = refs[:pairs], refs[pairs : pairs + 2], refs[pairs + 2 : shards]
    candidate_ref, count_ref, batch_ref, memory_ref, loss_ref = refs[shards:]
    memory_refs = [near_refs[0].at[0], near_refs[1].at[1]]
    for far_ref, hop_ref in zip(far_refs, hop_refs):
        memory_refs += [far_ref.at[0], hop_ref.at[1]]
    group, shard = lax.axis_index("group"), lax.axis_index("memory")
    chip, core = group // 2, group % 2
    _, q_count, slots = candidate_ref.shape
    p_count = memory_refs[0].shape[1]
    columns = batch_ref.shape[2]

    parts = []
    for first in range(0, columns, LANES):
        lane = lax.broadcasted_iota(jnp.int32, (q_count, LANES), 1) + first
        owner = lane // q_count
        source = (((owner // 2) ^ chip) * q_count + lane % q_count) % LANES
        own = jnp.take_along_axis(own_batch[...], source, axis=1)
        mate = jnp.take_along_axis(mate_batch[...], source, axis=1)
        parts.append(jnp.where(owner % 2 == core, own, mate))
    batch = jnp.concatenate(parts, axis=1)[:, :columns]
    batch_ref[0] = batch

    ids = candidate_ref[0]
    padded = jnp.concatenate([ids, jnp.zeros((q_count, p_count - slots), jnp.int32)], axis=1)
    holder, local = padded // p_count, padded % p_count
    picked = jnp.zeros((q_count, p_count), jnp.float32)
    for step in range(shards):
        found = jnp.take_along_axis(memory_refs[step][...], local, axis=1)
        picked = jnp.where(holder == (shard ^ step), found, picked)

    valid = lax.broadcasted_iota(jnp.int32, (q_count, p_count), 1) < column_of(count_ref[...])
    memory_ref[0] = jnp.where(valid, picked, 0.0)[:, :slots]

    top = jnp.maximum(
        jnp.max(batch, axis=1, keepdims=True),
        jnp.max(jnp.where(valid, picked, -jnp.inf), axis=1, keepdims=True),
    )
    total = jnp.sum(jnp.exp(batch - top), axis=1, keepdims=True) + jnp.sum(
        jnp.where(valid, jnp.exp(picked - top), 0.0), axis=1, keepdims=True
    )
    column = lax.broadcasted_iota(jnp.int32, batch.shape, 1)
    own = group * q_count + lax.broadcasted_iota(jnp.int32, batch.shape, 0)
    target_score = jnp.sum(jnp.where(column == own, batch, 0.0), axis=1, keepdims=True)
    loss_ref[...] = row_of(top + jnp.log(total) - target_score)


def finish(own_batch, mate_batch, near, far, hops, candidates, counts, columns):
    _, q_count, slots = candidates.shape
    memory_parts = far + near + hops
    return pl.pallas_call(
        functools.partial(loss_kernel, len(memory_parts)),
        out_shape=[
            jax.ShapeDtypeStruct((1, q_count, columns), jnp.float32),
            jax.ShapeDtypeStruct((1, q_count, slots), jnp.float32),
            jax.ShapeDtypeStruct((1, q_count), jnp.float32),
        ],
        compiler_params=pltpu.CompilerParams(vmem_limit_bytes=4 * MIB),
        name="finish",
    )(own_batch, mate_batch, *memory_parts, candidates, counts)


def body(queries, positives, memory, candidates, counts):
    shards = lax.axis_size("memory")
    groups = lax.axis_size("group")
    chips = groups // 2
    q_count = queries.shape[1]
    slots = candidates.shape[2] // 2

    def to_shard(array, step):
        return lax.ppermute(array, "memory", [(i, i ^ step) for i in range(shards)])

    def to_group(array, step):
        return lax.ppermute(array, "group", [(i, i ^ step) for i in range(groups)])

    own = pack(queries, candidates, counts, memory.shape[1])
    packed = [to_shard(own, step) for step in range(shards - 1, 0, -1)] + [own]
    sent_positives, sent_queries, _ = lax.optimization_barrier((positives, queries, own))
    row = [positives] + [to_group(sent_positives, 2 * step) for step in range(1, chips)]
    mate_queries = to_group(sent_queries, 1)

    near, *pairs = score_memory(packed, memory, slots)[::-1]
    far = [to_shard(pair, 2 * index) for index, pair in enumerate(pairs, start=1)]
    mate_queries, _ = lax.optimization_barrier((mate_queries, near))
    mate_scores = score_batch(mate_queries, row)
    near = [near, to_shard(lax.optimization_barrier((near, mate_scores))[0], 1)]
    mate_batch = to_group(mate_scores, 1)
    own_queries, _ = lax.optimization_barrier((queries, mate_scores))
    own_batch = score_batch(own_queries, row)
    passed = lax.optimization_barrier((far, own_batch))[0]
    hops = [to_shard(pair, 1) for pair in passed]
    columns = groups * q_count
    return finish(own_batch, mate_batch, near, far, hops, candidates, counts, columns)


def solution(mesh):
    in_specs = (
        P("group", "memory", None, None),
        P("group", "memory", None, None),
        P("group", "memory", None, None),
        P("group", "memory", None),
        P("group", "memory"),
    )
    out_specs = (P("group", "memory", None), P("group", "memory", None), P("group", "memory"))
    return jax.shard_map(body, mesh=mesh, in_specs=in_specs, out_specs=out_specs, check_vma=False)
```

```python
import functools

import jax
import jax.numpy as jnp
from jax import lax
from jax.experimental import pallas as pl
from jax.experimental.pallas import tpu as pltpu
from jax.sharding import PartitionSpec as P

LANES = 128
MIB = 1024 * 1024
SLOTS = 8
CHUNK = 32
LIST_ROWS = 16


def in_hbm(array):
    return pltpu.with_memory_space_constraint(array, pltpu.HBM)


def token_max(passages, tokens):
    count, width, depth = passages.shape
    product = lax.dot_general(
        passages.reshape(count * width, depth),
        tokens,
        (((1,), (1,)), ((), ())),
        preferred_element_type=jnp.float32,
    )
    return jnp.max(product.reshape(count, width, tokens.shape[0]), axis=1)


def token_sum(best, queries):
    tokens = best.shape[1]
    per_query = tokens // queries
    row = lax.broadcasted_iota(jnp.int32, (queries, tokens), 0)
    col = lax.broadcasted_iota(jnp.int32, (queries, tokens), 1)
    own = (col // per_query == row).astype(jnp.float32)
    return lax.dot_general(
        own,
        best,
        (((1,), (1,)), ((), ())),
        precision=lax.Precision.HIGHEST,
        preferred_element_type=jnp.float32,
    )


def column_of(row):
    size = row.shape[1]
    square = (size, size)
    diagonal = lax.broadcasted_iota(jnp.int32, square, 0) == lax.broadcasted_iota(
        jnp.int32, square, 1
    )
    return jnp.sum(jnp.where(diagonal, jnp.broadcast_to(row, square), 0), axis=1, keepdims=True)


def row_of(column):
    size = column.shape[0]
    square = (size, size)
    diagonal = lax.broadcasted_iota(jnp.int32, square, 0) == lax.broadcasted_iota(
        jnp.int32, square, 1
    )
    return jnp.sum(jnp.where(diagonal, jnp.broadcast_to(column, square), 0), axis=0, keepdims=True)


def split_ids(p_count, candidate_ref, count_ref):
    ids = candidate_ref[0]
    row = lax.broadcasted_iota(jnp.int32, ids.shape, 0)
    valid_count = jnp.zeros(ids.shape, jnp.int32)
    for index in range(ids.shape[0]):
        valid_count = jnp.where(row == index, count_ref[0, index], valid_count)
    valid = lax.broadcasted_iota(jnp.int32, ids.shape, 1) < valid_count
    holder = jnp.where(valid, ids // p_count, -1)
    return (ids % p_count).astype(jnp.float32), holder.astype(jnp.float32)


def pack_kernel(p_count, query_ref, candidate_ref, count_ref, out_ref):
    _, q_count, slots = candidate_ref.shape
    _, _, q_tokens, depth = query_ref.shape
    tokens = q_count * q_tokens
    out_ref[:tokens] = query_ref[0].reshape(tokens, depth)
    planes = jnp.concatenate(split_ids(p_count, candidate_ref, count_ref), axis=0)
    empty = jnp.zeros((2 * q_count, depth - slots), jnp.float32)
    out_ref[tokens:] = jnp.concatenate([planes, empty], axis=1).astype(out_ref.dtype)


def pack(queries, candidates, counts, p_count):
    _, q_count, q_tokens, depth = queries.shape
    vmem = pl.BlockSpec(memory_space=pltpu.VMEM)
    return pl.pallas_call(
        functools.partial(pack_kernel, p_count),
        in_specs=[vmem, vmem, pl.BlockSpec(memory_space=pltpu.SMEM)],
        out_shape=jax.ShapeDtypeStruct((q_count * (q_tokens + 2), depth), queries.dtype),
        compiler_params=pltpu.CompilerParams(vmem_limit_bytes=4 * MIB),
        name="pack",
    )(in_hbm(queries), in_hbm(candidates), in_hbm(counts))


def memory_kernel(shards, slots, *refs):
    packed_refs, memory_ref = refs[:shards], refs[shards]
    out_refs = refs[shards + 1 : 2 * shards + 1]
    passage_ref, query_ref, rank_ref, best_ref, list_ref, scalar_ref, copy_sems, list_sem = refs[
        2 * shards + 1 :
    ]
    q_count = out_refs[0].shape[0]
    p_count = passage_ref.shape[0]
    total, q_tokens, depth = query_ref.shape
    chunks = p_count // CHUNK

    def fetch(chunk):
        rows = pl.ds(pl.multiple_of(chunk * CHUNK, CHUNK), CHUNK)
        return pltpu.make_async_copy(
            memory_ref.at[0, rows], passage_ref.at[rows], copy_sems.at[chunk]
        )

    for chunk in range(chunks):
        fetch(chunk).start()

    me = lax.axis_index("memory").astype(jnp.float32)
    keys = []
    for index, packed_ref in enumerate(packed_refs):
        tokens = packed_ref[: q_count * q_tokens].reshape(q_count, q_tokens, depth)
        query_ref[index * q_count : (index + 1) * q_count] = tokens
        planes = packed_ref[q_count * q_tokens :].astype(jnp.float32)
        local, holder = planes[:q_count], planes[q_count:]
        keys.append(jnp.where(holder == me, local, -1.0))
    keys = jnp.concatenate(keys, axis=0)
    passage = lax.broadcasted_iota(jnp.int32, (total, p_count), 1).astype(jnp.float32)
    named = jnp.zeros((total, p_count), jnp.float32)
    for slot in range(slots):
        named = jnp.where(keys[:, slot : slot + 1] == passage, 1.0, named)

    square = (total, total)
    earlier = lax.broadcasted_iota(jnp.int32, square, 1) < lax.broadcasted_iota(
        jnp.int32, square, 0
    )
    before = jnp.dot(earlier.astype(jnp.float32), named, preferred_element_type=jnp.float32)
    rank_ref[...] = jnp.where(named > 0.0, before, -1.0)
    counts = jnp.sum(named, axis=0, keepdims=True)
    most = jnp.broadcast_to(jnp.max(counts, axis=1, keepdims=True), counts.shape)

    def left_over(first):
        left = jnp.where(rank_ref[...] == first, 1.0, 0.0)
        left = jnp.sum(left, axis=0, keepdims=True)
        square = (p_count, p_count)
        row = lax.broadcasted_iota(jnp.int32, square, 0).astype(jnp.float32)
        column = lax.broadcasted_iota(jnp.int32, square, 1).astype(jnp.float32)
        place = jnp.dot(left, (row < column).astype(jnp.float32), preferred_element_type=jnp.float32)
        mine = jnp.where((place == row) & (left > 0.0), column, 0.0)
        index = jnp.sum(mine, axis=1, keepdims=True)
        index = jnp.sum(jnp.where(row == column, index, 0.0), axis=0, keepdims=True)
        return [index, jnp.broadcast_to(jnp.sum(left, axis=1, keepdims=True), left.shape)]

    def write_list(first, extra):
        asker = lax.broadcasted_iota(jnp.int32, (total, p_count), 0).astype(jnp.float32)
        rank = rank_ref[...] - first
        rows = [
            jnp.sum(jnp.where(rank == float(slot), asker, 0.0), axis=0, keepdims=True)
            for slot in range(SLOTS)
        ]
        rest = jnp.zeros((LIST_ROWS - SLOTS - len(extra), p_count), jnp.float32)
        list_ref[...] = jnp.concatenate(rows + extra + [rest], axis=0).astype(jnp.int32)
        copy = pltpu.make_async_copy(list_ref, scalar_ref, list_sem)
        copy.start()
        copy.wait()

    def unit(index):
        tokens = [query_ref[scalar_ref[slot, index]] for slot in range(SLOTS)]
        return token_max(passage_ref[pl.ds(index, 1)], jnp.concatenate(tokens, axis=0))

    def add_scores(first):
        sums = token_sum(best_ref[...], SLOTS)
        for index, out_ref in enumerate(out_refs):
            rank = rank_ref[index * q_count : (index + 1) * q_count] - first
            for slot in range(SLOTS):
                out_ref[...] = jnp.where(rank == float(slot), sums[slot : slot + 1], out_ref[...])

    for out_ref in out_refs:
        out_ref[...] = jnp.zeros_like(out_ref)
    write_list(0.0, [most])
    rounds = (scalar_ref[SLOTS, 0] + SLOTS - 1) // SLOTS

    @pl.loop(0, chunks)
    def _(chunk):
        fetch(chunk).wait()
        for start in range(0, CHUNK, 8):
            first = pl.multiple_of(chunk * CHUNK + start, 8)
            rows = [unit(first + offset) for offset in range(8)]
            best_ref[pl.ds(first, 8), :] = jnp.concatenate(rows, axis=0)

    add_scores(0.0)

    @pl.loop(1, rounds)
    def _(turn):
        done = (turn * SLOTS).astype(jnp.float32)
        write_list(done, left_over(done))

        @pl.loop(0, scalar_ref[SLOTS + 1, 0])
        def _(place):
            index = scalar_ref[SLOTS, place]
            best_ref[pl.ds(index, 1), :] = unit(index)

        add_scores(done)


def score_memory(packed, memory, q_count, slots):
    shards = len(packed)
    q_tokens = packed[0].shape[0] // q_count - 2
    _, p_count, p_tokens, depth = memory.shape
    total = shards * q_count
    vmem = pl.BlockSpec(memory_space=pltpu.VMEM)
    return pl.pallas_call(
        functools.partial(memory_kernel, shards, slots),
        in_specs=[vmem] * shards + [pl.BlockSpec(memory_space=pltpu.HBM)],
        out_specs=[vmem] * shards,
        out_shape=[jax.ShapeDtypeStruct((q_count, p_count), jnp.float32)] * shards,
        scratch_shapes=[
            pltpu.VMEM((p_count, p_tokens, depth), memory.dtype),
            pltpu.VMEM((total, q_tokens, depth), memory.dtype),
            pltpu.VMEM((total, p_count), jnp.float32),
            pltpu.VMEM((p_count, SLOTS * q_tokens), jnp.float32),
            pltpu.VMEM((LIST_ROWS, p_count), jnp.int32),
            pltpu.SMEM((LIST_ROWS, p_count), jnp.int32),
            pltpu.SemaphoreType.DMA((p_count // CHUNK,)),
            pltpu.SemaphoreType.DMA,
        ],
        compiler_params=pltpu.CompilerParams(vmem_limit_bytes=16 * MIB),
        cost_estimate=pl.CostEstimate(
            flops=2 * total * q_tokens * p_count * p_tokens * depth,
            bytes_accessed=2 * p_count * p_tokens * depth,
            transcendentals=0,
        ),
        name="score_memory",
    )(*packed, in_hbm(memory))


def batch_kernel(query_ref, *refs):
    passage_refs, (out_ref, best_ref) = refs[:-2], refs[-2:]
    _, queries, q_tokens, depth = query_ref.shape
    count = passage_refs[0].shape[1]
    if len(passage_refs) * count < best_ref.shape[0]:
        best_ref[...] = jnp.zeros_like(best_ref)
    tokens = query_ref[0].reshape(queries * q_tokens, depth)
    for chip, passage_ref in enumerate(passage_refs):
        best_ref[chip * count : (chip + 1) * count, :] = token_max(passage_ref[0], tokens)
    out_ref[...] = token_sum(best_ref[...], queries)


def score_batch(queries, positives):
    _, q_count, q_tokens, depth = queries.shape
    _, p_count, p_tokens, _ = positives[0].shape
    chips = len(positives)
    lanes = -(-chips * p_count // LANES) * LANES
    return pl.pallas_call(
        batch_kernel,
        out_shape=jax.ShapeDtypeStruct((q_count, lanes), jnp.float32),
        scratch_shapes=[pltpu.VMEM((lanes, q_count * q_tokens), jnp.float32)],
        compiler_params=pltpu.CompilerParams(vmem_limit_bytes=16 * MIB),
        cost_estimate=pl.CostEstimate(
            flops=2 * chips * q_count * q_tokens * p_count * p_tokens * depth,
            bytes_accessed=2 * chips * p_count * p_tokens * depth,
            transcendentals=0,
        ),
        name="score_batch",
    )(queries, *positives)


def loss_kernel(shards, own_batch, mate_batch, *refs):
    memory_refs = refs[:shards]
    candidate_ref, count_ref, batch_ref, memory_ref, loss_ref = refs[shards:]
    group, shard = lax.axis_index("group"), lax.axis_index("memory")
    chip, core = group // 2, group % 2
    _, q_count, slots = candidate_ref.shape
    p_count = memory_refs[0].shape[1]
    columns = batch_ref.shape[2]

    parts = []
    for first in range(0, columns, LANES):
        lane = lax.broadcasted_iota(jnp.int32, (q_count, LANES), 1) + first
        owner = lane // q_count
        source = (((owner // 2) ^ chip) * q_count + lane % q_count) % LANES
        own = jnp.take_along_axis(own_batch[...], source, axis=1)
        mate = jnp.take_along_axis(mate_batch[...], source, axis=1)
        parts.append(jnp.where(owner % 2 == core, own, mate))
    batch = jnp.concatenate(parts, axis=1)[:, :columns]
    batch_ref[0] = batch

    ids = candidate_ref[0]
    padded = jnp.concatenate([ids, jnp.zeros((q_count, p_count - slots), jnp.int32)], axis=1)
    holder, local = padded // p_count, padded % p_count
    picked = jnp.zeros((q_count, p_count), jnp.float32)
    for step in range(shards):
        found = jnp.take_along_axis(memory_refs[-step][...], local, axis=1)
        picked = jnp.where(holder == (shard ^ step), found, picked)

    valid = lax.broadcasted_iota(jnp.int32, (q_count, p_count), 1) < column_of(count_ref[...])
    memory_ref[0] = jnp.where(valid, picked, 0.0)[:, :slots]

    top = jnp.maximum(
        jnp.max(batch, axis=1, keepdims=True),
        jnp.max(jnp.where(valid, picked, -jnp.inf), axis=1, keepdims=True),
    )
    total = jnp.sum(jnp.exp(batch - top), axis=1, keepdims=True) + jnp.sum(
        jnp.where(valid, jnp.exp(picked - top), 0.0), axis=1, keepdims=True
    )
    column = lax.broadcasted_iota(jnp.int32, batch.shape, 1)
    own = group * q_count + lax.broadcasted_iota(jnp.int32, batch.shape, 0)
    target_score = jnp.sum(jnp.where(column == own, batch, 0.0), axis=1, keepdims=True)
    loss_ref[...] = row_of(top + jnp.log(total) - target_score)


def finish(own_batch, mate_batch, memory_parts, candidates, counts, columns):
    _, q_count, slots = candidates.shape
    return pl.pallas_call(
        functools.partial(loss_kernel, len(memory_parts)),
        out_shape=[
            jax.ShapeDtypeStruct((1, q_count, columns), jnp.float32),
            jax.ShapeDtypeStruct((1, q_count, slots), jnp.float32),
            jax.ShapeDtypeStruct((1, q_count), jnp.float32),
        ],
        compiler_params=pltpu.CompilerParams(vmem_limit_bytes=4 * MIB),
        name="finish",
    )(own_batch, mate_batch, *memory_parts, candidates, counts)


def body(queries, positives, memory, candidates, counts):
    shards = lax.axis_size("memory")
    groups = lax.axis_size("group")
    chips = groups // 2
    q_count = queries.shape[1]
    slots = candidates.shape[2] // 2

    def to_shard(array, step):
        return lax.ppermute(array, "memory", [(i, i ^ step) for i in range(shards)])

    def to_group(array, step):
        return lax.ppermute(array, "group", [(i, i ^ step) for i in range(groups)])

    own = pack(queries, candidates, counts, memory.shape[1])
    packed = [own] + [to_shard(own, step) for step in range(1, shards)]
    sent_positives, sent_queries, _ = lax.optimization_barrier((positives, queries, own))
    row = [positives] + [to_group(sent_positives, 2 * step) for step in range(1, chips)]
    mate_queries = to_group(sent_queries, 1)

    scores = score_memory(packed, memory, q_count, slots)
    returned = [to_shard(scores[step], step) for step in range(shards - 1, 0, -1)]
    mate_queries, _ = lax.optimization_barrier((mate_queries, scores[0]))
    mate_scores = score_batch(mate_queries, row)
    mate_batch = to_group(mate_scores, 1)
    own_queries, _ = lax.optimization_barrier((queries, mate_scores))
    own_batch = score_batch(own_queries, row)
    columns = groups * q_count
    return finish(
        own_batch, mate_batch, [scores[0]] + returned, candidates, counts, columns
    )


def solution(mesh):
    in_specs = (
        P("group", "memory", None, None),
        P("group", "memory", None, None),
        P("group", "memory", None, None),
        P("group", "memory", None),
        P("group", "memory"),
    )
    out_specs = (P("group", "memory", None), P("group", "memory", None), P("group", "memory"))
    return jax.shard_map(body, mesh=mesh, in_specs=in_specs, out_specs=out_specs, check_vma=False)
```

```python
import functools

import jax
import jax.numpy as jnp
from jax import lax
from jax.experimental import pallas as pl
from jax.experimental.pallas import tpu as pltpu
from jax.sharding import PartitionSpec as P

LANES = 128
MIB = 1024 * 1024
SLOTS = 4
CHUNK = 32
LIST_ROWS = 8
STEP = 8


def in_hbm(array):
    return pltpu.with_memory_space_constraint(array, pltpu.HBM)


def token_max(passages, tokens):
    count, width, depth = passages.shape
    product = lax.dot_general(
        passages.reshape(count * width, depth),
        tokens,
        (((1,), (1,)), ((), ())),
        preferred_element_type=jnp.float32,
    )
    return jnp.max(product.reshape(count, width, tokens.shape[0]), axis=1)


def token_sum(best, queries):
    tokens = best.shape[1]
    per_query = tokens // queries
    row = lax.broadcasted_iota(jnp.int32, (max(queries, 8), tokens), 0)
    col = lax.broadcasted_iota(jnp.int32, (max(queries, 8), tokens), 1)
    own = (col // per_query == row).astype(jnp.float32)
    return lax.dot_general(
        own,
        best,
        (((1,), (1,)), ((), ())),
        precision=lax.Precision.HIGHEST,
        preferred_element_type=jnp.float32,
    )


def column_of(row):
    size = row.shape[1]
    square = (size, size)
    diagonal = lax.broadcasted_iota(jnp.int32, square, 0) == lax.broadcasted_iota(
        jnp.int32, square, 1
    )
    return jnp.sum(jnp.where(diagonal, jnp.broadcast_to(row, square), 0), axis=1, keepdims=True)


def row_of(column):
    size = column.shape[0]
    square = (size, size)
    diagonal = lax.broadcasted_iota(jnp.int32, square, 0) == lax.broadcasted_iota(
        jnp.int32, square, 1
    )
    return jnp.sum(jnp.where(diagonal, jnp.broadcast_to(column, square), 0), axis=0, keepdims=True)


def split_ids(p_count, candidate_ref, count_ref):
    ids = candidate_ref[0]
    row = lax.broadcasted_iota(jnp.int32, ids.shape, 0)
    valid_count = jnp.zeros(ids.shape, jnp.int32)
    for index in range(ids.shape[0]):
        valid_count = jnp.where(row == index, count_ref[0, index], valid_count)
    valid = lax.broadcasted_iota(jnp.int32, ids.shape, 1) < valid_count
    holder = jnp.where(valid, ids // p_count, -1)
    return (ids % p_count).astype(jnp.float32), holder.astype(jnp.float32)


def pack_kernel(p_count, query_ref, candidate_ref, count_ref, out_ref):
    _, q_count, slots = candidate_ref.shape
    _, _, q_tokens, depth = query_ref.shape
    tokens = q_count * q_tokens
    out_ref[:tokens] = query_ref[0].reshape(tokens, depth)
    planes = jnp.concatenate(split_ids(p_count, candidate_ref, count_ref), axis=0)
    empty = jnp.zeros((2 * q_count, depth - slots), jnp.float32)
    out_ref[tokens:] = jnp.concatenate([planes, empty], axis=1).astype(out_ref.dtype)


def pack(queries, candidates, counts, p_count):
    _, q_count, q_tokens, depth = queries.shape
    vmem = pl.BlockSpec(memory_space=pltpu.VMEM)
    return pl.pallas_call(
        functools.partial(pack_kernel, p_count),
        in_specs=[vmem, vmem, pl.BlockSpec(memory_space=pltpu.SMEM)],
        out_shape=jax.ShapeDtypeStruct((q_count * (q_tokens + 2), depth), queries.dtype),
        compiler_params=pltpu.CompilerParams(vmem_limit_bytes=4 * MIB),
        name="pack",
    )(in_hbm(queries), in_hbm(candidates), in_hbm(counts))


def memory_kernel(shards, slots, *refs):
    packed_refs, memory_ref = refs[:shards], refs[shards]
    out_refs = refs[shards + 1 : 2 * shards + 1]
    passage_ref, query_ref, rank_ref, best_ref, left_best_ref, *refs = refs[2 * shards + 1 :]
    list_ref, scalar_ref, left_ref, left_scalar_ref, copy_sems, list_sems = refs
    q_count = out_refs[0].shape[0]
    p_count = passage_ref.shape[0]
    total, q_tokens, depth = query_ref.shape
    chunks = p_count // CHUNK

    def fetch(chunk):
        rows = pl.ds(pl.multiple_of(chunk * CHUNK, CHUNK), CHUNK)
        return pltpu.make_async_copy(
            memory_ref.at[0, rows], passage_ref.at[rows], copy_sems.at[chunk]
        )

    for chunk in range(chunks):
        fetch(chunk).start()

    me = lax.axis_index("memory").astype(jnp.float32)
    keys = []
    for index, packed_ref in enumerate(packed_refs):
        tokens = packed_ref[: q_count * q_tokens].reshape(q_count, q_tokens, depth)
        query_ref[index * q_count : (index + 1) * q_count] = tokens
        planes = packed_ref[q_count * q_tokens :].astype(jnp.float32)
        local, holder = planes[:q_count], planes[q_count:]
        keys.append(jnp.where(holder == me, local, -1.0))
    keys = jnp.concatenate(keys, axis=0)
    passage = lax.broadcasted_iota(jnp.int32, (total, p_count), 1).astype(jnp.float32)
    named = jnp.zeros((total, p_count), jnp.float32)
    for slot in range(slots):
        named = jnp.where(keys[:, slot : slot + 1] == passage, 1.0, named)

    square = (total, total)
    earlier = lax.broadcasted_iota(jnp.int32, square, 1) < lax.broadcasted_iota(
        jnp.int32, square, 0
    )
    before = jnp.dot(earlier.astype(jnp.float32), named, preferred_element_type=jnp.float32)
    rank_ref[...] = jnp.where(named > 0.0, before, -1.0)
    counts = jnp.sum(named, axis=0, keepdims=True)
    most = jnp.broadcast_to(jnp.max(counts, axis=1, keepdims=True), counts.shape)

    asker = lax.broadcasted_iota(jnp.int32, (total, p_count), 0).astype(jnp.float32)

    def ids_from(first):
        rank = rank_ref[...] - first
        return [
            jnp.sum(jnp.where(rank == float(slot), asker, 0.0), axis=0, keepdims=True)
            for slot in range(SLOTS)
        ]

    list_copy = pltpu.make_async_copy(list_ref, scalar_ref, list_sems.at[0])
    left_copy = pltpu.make_async_copy(left_ref, left_scalar_ref, list_sems.at[1])

    def write_list():
        rest = jnp.zeros((LIST_ROWS - SLOTS - 1, p_count), jnp.float32)
        rows = ids_from(0.0) + [most, rest]
        list_ref[...] = jnp.concatenate(rows, axis=0).astype(jnp.int32)

    def write_left(first):
        left = jnp.where(rank_ref[...] == first, 1.0, 0.0)
        left = jnp.sum(left, axis=0, keepdims=True)
        square = (p_count, p_count)
        row = lax.broadcasted_iota(jnp.int32, square, 0).astype(jnp.float32)
        column = lax.broadcasted_iota(jnp.int32, square, 1).astype(jnp.float32)
        before = (row < column).astype(jnp.float32)
        place = jnp.dot(left, before, preferred_element_type=jnp.float32)
        chosen = jnp.where((place == row) & (left > 0.0), 1.0, 0.0)
        rest = jnp.zeros((LIST_ROWS - SLOTS - 1, p_count), jnp.float32)
        spread = jnp.concatenate(ids_from(first) + [column[:1], rest], axis=0)
        close = lax.dot_general(
            spread, chosen, (((1,), (1,)), ((), ())), preferred_element_type=jnp.float32
        )
        number = jnp.broadcast_to(jnp.sum(left, axis=1, keepdims=True), left.shape)
        rows = [close[: SLOTS + 1], number, rest[1:]]
        left_ref[...] = jnp.concatenate(rows, axis=0).astype(jnp.int32)

    def unit(index, ids_ref, place):
        tokens = [query_ref[ids_ref[slot, place]] for slot in range(SLOTS)]
        return token_max(passage_ref[pl.ds(index, 1)], jnp.concatenate(tokens, axis=0))

    def add_scores(best, first):
        sums = token_sum(best, SLOTS)
        for index, out_ref in enumerate(out_refs):
            rank = rank_ref[index * q_count : (index + 1) * q_count] - first
            scores = out_ref[...]
            for slot in range(SLOTS):
                scores = jnp.where(rank == float(slot), sums[slot : slot + 1], scores)
            out_ref[...] = scores

    for out_ref in out_refs:
        out_ref[...] = jnp.zeros_like(out_ref)
    write_list()
    list_copy.start()
    write_left(float(SLOTS))
    left_copy.start()
    list_copy.wait()

    @pl.loop(0, chunks)
    def _(chunk):
        fetch(chunk).wait()
        for start in range(0, CHUNK, 8):
            first = pl.multiple_of(chunk * CHUNK + start, 8)
            rows = [unit(first + offset, scalar_ref, first + offset) for offset in range(8)]
            best_ref[pl.ds(first, 8), :] = jnp.concatenate(rows, axis=0)

    left_copy.wait()
    add_scores(best_ref[...], 0.0)

    @pl.loop(1, (scalar_ref[SLOTS, 0] + SLOTS - 1) // SLOTS)
    def _(turn):
        done = (turn * SLOTS).astype(jnp.float32)

        @pl.when(turn > 1)
        def _():
            write_left(done)
            left_copy.start()
            left_copy.wait()

        number = left_scalar_ref[SLOTS + 1, 0]

        @pl.loop(0, (number + STEP - 1) // STEP)
        def _(block):
            rows = []
            for offset in range(STEP):
                place = block * STEP + offset
                index = left_scalar_ref[SLOTS, place]
                rows.append((place, index, unit(index, left_scalar_ref, place)))
            for place, index, row in rows:
                kept = jnp.where(place < number, index, p_count)
                left_best_ref[pl.ds(kept, 1), :] = row

        add_scores(left_best_ref[:p_count], done)


def score_memory(packed, memory, q_count, slots):
    shards = len(packed)
    q_tokens = packed[0].shape[0] // q_count - 2
    _, p_count, p_tokens, depth = memory.shape
    total = shards * q_count
    vmem = pl.BlockSpec(memory_space=pltpu.VMEM)
    return pl.pallas_call(
        functools.partial(memory_kernel, shards, slots),
        in_specs=[vmem] * shards + [pl.BlockSpec(memory_space=pltpu.HBM)],
        out_specs=[vmem] * shards,
        out_shape=[jax.ShapeDtypeStruct((q_count, p_count), jnp.float32)] * shards,
        scratch_shapes=[
            pltpu.VMEM((p_count, p_tokens, depth), memory.dtype),
            pltpu.VMEM((total, q_tokens, depth), memory.dtype),
            pltpu.VMEM((total, p_count), jnp.float32),
            pltpu.VMEM((p_count, SLOTS * q_tokens), jnp.float32),
            pltpu.VMEM((p_count + 8, SLOTS * q_tokens), jnp.float32),
            pltpu.VMEM((LIST_ROWS, p_count), jnp.int32),
            pltpu.SMEM((LIST_ROWS, p_count), jnp.int32),
            pltpu.VMEM((LIST_ROWS, p_count), jnp.int32),
            pltpu.SMEM((LIST_ROWS, p_count), jnp.int32),
            pltpu.SemaphoreType.DMA((p_count // CHUNK,)),
            pltpu.SemaphoreType.DMA((2,)),
        ],
        compiler_params=pltpu.CompilerParams(vmem_limit_bytes=16 * MIB),
        cost_estimate=pl.CostEstimate(
            flops=2 * total * q_tokens * p_count * p_tokens * depth,
            bytes_accessed=2 * p_count * p_tokens * depth,
            transcendentals=0,
        ),
        name="score_memory",
    )(*packed, in_hbm(memory))


def batch_kernel(query_ref, *refs):
    passage_refs, (out_ref, best_ref) = refs[:-2], refs[-2:]
    _, queries, q_tokens, depth = query_ref.shape
    count = passage_refs[0].shape[1]
    if len(passage_refs) * count < best_ref.shape[0]:
        best_ref[...] = jnp.zeros_like(best_ref)
    tokens = query_ref[0].reshape(queries * q_tokens, depth)
    for chip, passage_ref in enumerate(passage_refs):
        best_ref[chip * count : (chip + 1) * count, :] = token_max(passage_ref[0], tokens)
    out_ref[...] = token_sum(best_ref[...], queries)


def score_batch(queries, positives):
    _, q_count, q_tokens, depth = queries.shape
    _, p_count, p_tokens, _ = positives[0].shape
    chips = len(positives)
    lanes = -(-chips * p_count // LANES) * LANES
    return pl.pallas_call(
        batch_kernel,
        out_shape=jax.ShapeDtypeStruct((q_count, lanes), jnp.float32),
        scratch_shapes=[pltpu.VMEM((lanes, q_count * q_tokens), jnp.float32)],
        compiler_params=pltpu.CompilerParams(vmem_limit_bytes=16 * MIB),
        cost_estimate=pl.CostEstimate(
            flops=2 * chips * q_count * q_tokens * p_count * p_tokens * depth,
            bytes_accessed=2 * chips * p_count * p_tokens * depth,
            transcendentals=0,
        ),
        name="score_batch",
    )(queries, *positives)


def loss_kernel(shards, own_batch, mate_batch, *refs):
    memory_refs = refs[:shards]
    candidate_ref, count_ref, batch_ref, memory_ref, loss_ref = refs[shards:]
    group, shard = lax.axis_index("group"), lax.axis_index("memory")
    chip, core = group // 2, group % 2
    _, q_count, slots = candidate_ref.shape
    p_count = memory_refs[0].shape[1]
    columns = batch_ref.shape[2]

    parts = []
    for first in range(0, columns, LANES):
        lane = lax.broadcasted_iota(jnp.int32, (q_count, LANES), 1) + first
        owner = lane // q_count
        source = (((owner // 2) ^ chip) * q_count + lane % q_count) % LANES
        own = jnp.take_along_axis(own_batch[...], source, axis=1)
        mate = jnp.take_along_axis(mate_batch[...], source, axis=1)
        parts.append(jnp.where(owner % 2 == core, own, mate))
    batch = jnp.concatenate(parts, axis=1)[:, :columns]
    batch_ref[0] = batch

    ids = candidate_ref[0]
    padded = jnp.concatenate([ids, jnp.zeros((q_count, p_count - slots), jnp.int32)], axis=1)
    holder, local = padded // p_count, padded % p_count
    picked = jnp.zeros((q_count, p_count), jnp.float32)
    for step in range(shards):
        found = jnp.take_along_axis(memory_refs[-step][...], local, axis=1)
        picked = jnp.where(holder == (shard ^ step), found, picked)

    valid = lax.broadcasted_iota(jnp.int32, (q_count, p_count), 1) < column_of(count_ref[...])
    memory_ref[0] = jnp.where(valid, picked, 0.0)[:, :slots]

    top = jnp.maximum(
        jnp.max(batch, axis=1, keepdims=True),
        jnp.max(jnp.where(valid, picked, -jnp.inf), axis=1, keepdims=True),
    )
    total = jnp.sum(jnp.exp(batch - top), axis=1, keepdims=True) + jnp.sum(
        jnp.where(valid, jnp.exp(picked - top), 0.0), axis=1, keepdims=True
    )
    column = lax.broadcasted_iota(jnp.int32, batch.shape, 1)
    own = group * q_count + lax.broadcasted_iota(jnp.int32, batch.shape, 0)
    target_score = jnp.sum(jnp.where(column == own, batch, 0.0), axis=1, keepdims=True)
    loss_ref[...] = row_of(top + jnp.log(total) - target_score)


def finish(own_batch, mate_batch, memory_parts, candidates, counts, columns):
    _, q_count, slots = candidates.shape
    return pl.pallas_call(
        functools.partial(loss_kernel, len(memory_parts)),
        out_shape=[
            jax.ShapeDtypeStruct((1, q_count, columns), jnp.float32),
            jax.ShapeDtypeStruct((1, q_count, slots), jnp.float32),
            jax.ShapeDtypeStruct((1, q_count), jnp.float32),
        ],
        compiler_params=pltpu.CompilerParams(vmem_limit_bytes=4 * MIB),
        name="finish",
    )(own_batch, mate_batch, *memory_parts, candidates, counts)


def body(queries, positives, memory, candidates, counts):
    shards = lax.axis_size("memory")
    groups = lax.axis_size("group")
    chips = groups // 2
    q_count = queries.shape[1]
    slots = candidates.shape[2] // 2

    def to_shard(array, step):
        return lax.ppermute(array, "memory", [(i, i ^ step) for i in range(shards)])

    def to_group(array, step):
        return lax.ppermute(array, "group", [(i, i ^ step) for i in range(groups)])

    own = pack(queries, candidates, counts, memory.shape[1])
    packed = [own] + [to_shard(own, step) for step in range(1, shards)]
    sent_positives, sent_queries, _ = lax.optimization_barrier((positives, queries, own))
    row = [positives] + [to_group(sent_positives, 2 * step) for step in range(1, chips)]
    mate_queries = to_group(sent_queries, 1)

    scores = score_memory(packed, memory, q_count, slots)
    returned = [to_shard(scores[step], step) for step in range(shards - 1, 0, -1)]
    mate_queries, _ = lax.optimization_barrier((mate_queries, scores[0]))
    mate_scores = score_batch(mate_queries, row)
    mate_batch = to_group(mate_scores, 1)
    own_queries, _ = lax.optimization_barrier((queries, mate_scores))
    own_batch = score_batch(own_queries, row)
    columns = groups * q_count
    return finish(
        own_batch, mate_batch, [scores[0]] + returned, candidates, counts, columns
    )


def solution(mesh):
    in_specs = (
        P("group", "memory", None, None),
        P("group", "memory", None, None),
        P("group", "memory", None, None),
        P("group", "memory", None),
        P("group", "memory"),
    )
    out_specs = (P("group", "memory", None), P("group", "memory", None), P("group", "memory"))
    return jax.shard_map(body, mesh=mesh, in_specs=in_specs, out_specs=out_specs, check_vma=False)
```

```python
import functools

import jax
import jax.numpy as jnp
from jax import lax
from jax.experimental import pallas as pl
from jax.experimental.pallas import tpu as pltpu
from jax.sharding import PartitionSpec as P

LANES = 128
MIB = 1024 * 1024
SLOTS = 8
CHUNK = 32
LIST_ROWS = 16
STEP = 4


def in_hbm(array):
    return pltpu.with_memory_space_constraint(array, pltpu.HBM)


def token_max(passages, tokens):
    count, width, depth = passages.shape
    product = lax.dot_general(
        passages.reshape(count * width, depth),
        tokens,
        (((1,), (1,)), ((), ())),
        preferred_element_type=jnp.float32,
    )
    return jnp.max(product.reshape(count, width, tokens.shape[0]), axis=1)


def token_sum(best, queries):
    tokens = best.shape[1]
    per_query = tokens // queries
    row = lax.broadcasted_iota(jnp.int32, (max(queries, 8), tokens), 0)
    col = lax.broadcasted_iota(jnp.int32, (max(queries, 8), tokens), 1)
    own = (col // per_query == row).astype(jnp.float32)
    return lax.dot_general(
        own,
        best,
        (((1,), (1,)), ((), ())),
        precision=lax.Precision.HIGHEST,
        preferred_element_type=jnp.float32,
    )


def column_of(row):
    size = row.shape[1]
    square = (size, size)
    diagonal = lax.broadcasted_iota(jnp.int32, square, 0) == lax.broadcasted_iota(
        jnp.int32, square, 1
    )
    return jnp.sum(jnp.where(diagonal, jnp.broadcast_to(row, square), 0), axis=1, keepdims=True)


def row_of(column):
    size = column.shape[0]
    square = (size, size)
    diagonal = lax.broadcasted_iota(jnp.int32, square, 0) == lax.broadcasted_iota(
        jnp.int32, square, 1
    )
    return jnp.sum(jnp.where(diagonal, jnp.broadcast_to(column, square), 0), axis=0, keepdims=True)


def other_half(row):
    half = row.shape[1] // 2
    return jnp.concatenate([row[:, half:], row[:, :half]], axis=1)


def split_ids(p_count, candidate_ref, count_ref):
    ids = candidate_ref[0]
    row = lax.broadcasted_iota(jnp.int32, ids.shape, 0)
    valid_count = jnp.zeros(ids.shape, jnp.int32)
    for index in range(ids.shape[0]):
        valid_count = jnp.where(row == index, count_ref[0, index], valid_count)
    valid = lax.broadcasted_iota(jnp.int32, ids.shape, 1) < valid_count
    holder = jnp.where(valid, ids // p_count, -1)
    return (ids % p_count).astype(jnp.float32), holder.astype(jnp.float32)


def pack_kernel(p_count, query_ref, candidate_ref, count_ref, out_ref):
    _, q_count, slots = candidate_ref.shape
    _, _, q_tokens, depth = query_ref.shape
    tokens = q_count * q_tokens
    out_ref[:tokens] = query_ref[0].reshape(tokens, depth)
    planes = jnp.concatenate(split_ids(p_count, candidate_ref, count_ref), axis=0)
    empty = jnp.zeros((2 * q_count, depth - slots), jnp.float32)
    out_ref[tokens:] = jnp.concatenate([planes, empty], axis=1).astype(out_ref.dtype)


def pack(queries, candidates, counts, p_count):
    _, q_count, q_tokens, depth = queries.shape
    vmem = pl.BlockSpec(memory_space=pltpu.VMEM)
    return pl.pallas_call(
        functools.partial(pack_kernel, p_count),
        in_specs=[vmem, vmem, pl.BlockSpec(memory_space=pltpu.SMEM)],
        out_shape=jax.ShapeDtypeStruct((q_count * (q_tokens + 2), depth), queries.dtype),
        compiler_params=pltpu.CompilerParams(vmem_limit_bytes=4 * MIB),
        name="pack",
    )(in_hbm(queries), in_hbm(candidates), in_hbm(counts))


def memory_kernel(shards, slots, *refs):
    packed_refs, memory_ref = refs[:shards], refs[shards]
    out_refs = refs[shards + 1 : 2 * shards + 1]
    passage_ref, query_ref, rank_ref, best_ref, left_best_ref, *refs = refs[2 * shards + 1 :]
    list_ref, scalar_ref, left_ref, left_scalar_ref, copy_sems, list_sems = refs
    q_count = out_refs[0].shape[0]
    p_count = passage_ref.shape[0]
    total, q_tokens, depth = (size // parts for size, parts in zip(query_ref.shape, (2, 1, 2)))
    half = p_count // 2
    chunks = half // CHUNK

    def fetch(chunk, side):
        rows = pl.ds(pl.multiple_of(side * half + chunk * CHUNK, CHUNK), CHUNK)
        return pltpu.make_async_copy(
            memory_ref.at[0, rows], passage_ref.at[rows], copy_sems.at[chunk, side]
        )

    for chunk in range(chunks):
        for side in range(2):
            fetch(chunk, side).start()

    me = lax.axis_index("memory").astype(jnp.float32)
    keys = []
    for index, packed_ref in enumerate(packed_refs):
        tokens = packed_ref[: q_count * q_tokens].reshape(q_count, q_tokens, depth)
        rows = slice(index * q_count, (index + 1) * q_count)
        query_ref[rows] = jnp.concatenate([tokens, jnp.zeros_like(tokens)], axis=2)
        query_ref[index * q_count + total : (index + 1) * q_count + total] = jnp.concatenate([jnp.zeros_like(tokens), tokens], axis=2)
        planes = packed_ref[q_count * q_tokens :].astype(jnp.float32)
        local, holder = planes[:q_count], planes[q_count:]
        keys.append(jnp.where(holder == me, local, -1.0))
    keys = jnp.concatenate(keys, axis=0)
    passage = lax.broadcasted_iota(jnp.int32, (total, p_count), 1).astype(jnp.float32)
    named = jnp.zeros((total, p_count), jnp.float32)
    for slot in range(slots):
        named = jnp.where(keys[:, slot : slot + 1] == passage, 1.0, named)

    square = (total, total)
    earlier = lax.broadcasted_iota(jnp.int32, square, 1) < lax.broadcasted_iota(
        jnp.int32, square, 0
    )
    before = jnp.dot(earlier.astype(jnp.float32), named, preferred_element_type=jnp.float32)
    counts = jnp.sum(named, axis=0, keepdims=True)
    upper = passage >= half
    before = before + jnp.where(upper, other_half(counts), 0.0)
    rank_ref[...] = jnp.where(named > 0.0, before, -1.0)
    both = counts + other_half(counts)
    most = jnp.broadcast_to(jnp.max(both, axis=1, keepdims=True), counts.shape)

    asker = lax.broadcasted_iota(jnp.int32, (total, p_count), 0).astype(jnp.float32)
    asker = jnp.where(upper, asker + total, asker)

    def ids_from(first):
        rank = rank_ref[...] - first
        rows = [
            jnp.sum(jnp.where(rank == float(slot), asker, 0.0), axis=0, keepdims=True)
            for slot in range(SLOTS)
        ]
        return [row + other_half(row) for row in rows]

    list_copy = pltpu.make_async_copy(list_ref, scalar_ref, list_sems.at[0])
    left_copy = pltpu.make_async_copy(left_ref, left_scalar_ref, list_sems.at[1])

    def write_list():
        rest = jnp.zeros((LIST_ROWS - SLOTS - 1, p_count), jnp.float32)
        rows = ids_from(0.0) + [most, rest]
        list_ref[...] = jnp.concatenate(rows, axis=0).astype(jnp.int32)

    def write_left(first):
        left = jnp.where(rank_ref[...] == first, 1.0, 0.0)
        left = jnp.sum(left, axis=0, keepdims=True)
        left = jnp.where(upper[:1], 0.0, left + other_half(left))
        square = (p_count, p_count)
        row = lax.broadcasted_iota(jnp.int32, square, 0).astype(jnp.float32)
        column = lax.broadcasted_iota(jnp.int32, square, 1).astype(jnp.float32)
        before = (row < column).astype(jnp.float32)
        place = jnp.dot(left, before, preferred_element_type=jnp.float32)
        chosen = jnp.where((place == row) & (left > 0.0), 1.0, 0.0)
        rest = jnp.zeros((LIST_ROWS - SLOTS - 1, p_count), jnp.float32)
        spread = jnp.concatenate(ids_from(first) + [column[:1], rest], axis=0)
        close = lax.dot_general(
            spread, chosen, (((1,), (1,)), ((), ())), preferred_element_type=jnp.float32
        )
        number = jnp.broadcast_to(jnp.sum(left, axis=1, keepdims=True), left.shape)
        rows = [close[: SLOTS + 1], number, rest[1:]]
        left_ref[...] = jnp.concatenate(rows, axis=0).astype(jnp.int32)

    def unit(index, ids_ref, place):
        tokens = [query_ref[ids_ref[slot, place]] for slot in range(SLOTS)]
        pair = [passage_ref[pl.ds(index + side * half, 1)] for side in range(2)]
        return token_max(jnp.concatenate(pair, axis=2), jnp.concatenate(tokens, axis=0))

    def add_scores(best, first):
        sums = token_sum(best, SLOTS)
        sums = jnp.concatenate([sums, sums], axis=1)
        for index, out_ref in enumerate(out_refs):
            rank = rank_ref[index * q_count : (index + 1) * q_count] - first
            scores = out_ref[...]
            for slot in range(SLOTS):
                scores = jnp.where(rank == float(slot), sums[slot : slot + 1], scores)
            out_ref[...] = scores

    for out_ref in out_refs:
        out_ref[...] = jnp.zeros_like(out_ref)
    write_list()
    list_copy.start()
    write_left(float(SLOTS))
    left_copy.start()
    list_copy.wait()

    @pl.loop(0, chunks)
    def _(chunk):
        for side in range(2):
            fetch(chunk, side).wait()
        for start in range(0, CHUNK, 8):
            first = pl.multiple_of(chunk * CHUNK + start, 8)
            rows = [unit(first + offset, scalar_ref, first + offset) for offset in range(8)]
            best_ref[pl.ds(first, 8), :] = jnp.concatenate(rows, axis=0)

    left_copy.wait()
    add_scores(best_ref[...], 0.0)

    @pl.loop(1, (scalar_ref[SLOTS, 0] + SLOTS - 1) // SLOTS)
    def _(turn):
        done = (turn * SLOTS).astype(jnp.float32)

        @pl.when(turn > 1)
        def _():
            write_left(done)
            left_copy.start()
            left_copy.wait()

        number = left_scalar_ref[SLOTS + 1, 0]

        @pl.loop(0, (number + STEP - 1) // STEP)
        def _(block):
            rows = []
            for offset in range(STEP):
                place = block * STEP + offset
                index = left_scalar_ref[SLOTS, place]
                rows.append((place, index, unit(index, left_scalar_ref, place)))
            for place, index, row in rows:
                kept = jnp.where(place < number, index, half)
                left_best_ref[pl.ds(kept, 1), :] = row

        add_scores(left_best_ref[:half], done)


def score_memory(packed, memory, q_count, slots):
    shards = len(packed)
    q_tokens = packed[0].shape[0] // q_count - 2
    _, p_count, p_tokens, depth = memory.shape
    total = shards * q_count
    vmem = pl.BlockSpec(memory_space=pltpu.VMEM)
    return pl.pallas_call(
        functools.partial(memory_kernel, shards, slots),
        in_specs=[vmem] * shards + [pl.BlockSpec(memory_space=pltpu.HBM)],
        out_specs=[vmem] * shards,
        out_shape=[jax.ShapeDtypeStruct((q_count, p_count), jnp.float32)] * shards,
        scratch_shapes=[
            pltpu.VMEM((p_count, p_tokens, depth), memory.dtype),
            pltpu.VMEM((2 * total, q_tokens, 2 * depth), memory.dtype),
            pltpu.VMEM((total, p_count), jnp.float32),
            pltpu.VMEM((p_count // 2, SLOTS * q_tokens), jnp.float32),
            pltpu.VMEM((p_count // 2 + 8, SLOTS * q_tokens), jnp.float32),
            pltpu.VMEM((LIST_ROWS, p_count), jnp.int32),
            pltpu.SMEM((LIST_ROWS, p_count), jnp.int32),
            pltpu.VMEM((LIST_ROWS, p_count), jnp.int32),
            pltpu.SMEM((LIST_ROWS, p_count), jnp.int32),
            pltpu.SemaphoreType.DMA((p_count // 2 // CHUNK, 2)),
            pltpu.SemaphoreType.DMA((2,)),
        ],
        compiler_params=pltpu.CompilerParams(vmem_limit_bytes=20 * MIB),
        cost_estimate=pl.CostEstimate(
            flops=2 * total * q_tokens * p_count * p_tokens * depth,
            bytes_accessed=2 * p_count * p_tokens * depth,
            transcendentals=0,
        ),
        name="score_memory",
    )(*packed, in_hbm(memory))


def batch_kernel(query_ref, *refs):
    passage_refs, (out_ref, best_ref) = refs[:-2], refs[-2:]
    _, queries, q_tokens, depth = query_ref.shape
    count = passage_refs[0].shape[1]
    if len(passage_refs) * count < best_ref.shape[0]:
        best_ref[...] = jnp.zeros_like(best_ref)
    tokens = query_ref[0].reshape(queries * q_tokens, depth)
    for chip, passage_ref in enumerate(passage_refs):
        best_ref[chip * count : (chip + 1) * count, :] = token_max(passage_ref[0], tokens)
    out_ref[...] = token_sum(best_ref[...], queries)


def score_batch(queries, positives):
    _, q_count, q_tokens, depth = queries.shape
    _, p_count, p_tokens, _ = positives[0].shape
    chips = len(positives)
    lanes = -(-chips * p_count // LANES) * LANES
    return pl.pallas_call(
        batch_kernel,
        out_shape=jax.ShapeDtypeStruct((q_count, lanes), jnp.float32),
        scratch_shapes=[pltpu.VMEM((lanes, q_count * q_tokens), jnp.float32)],
        compiler_params=pltpu.CompilerParams(vmem_limit_bytes=16 * MIB),
        cost_estimate=pl.CostEstimate(
            flops=2 * chips * q_count * q_tokens * p_count * p_tokens * depth,
            bytes_accessed=2 * chips * p_count * p_tokens * depth,
            transcendentals=0,
        ),
        name="score_batch",
    )(queries, *positives)


def loss_kernel(shards, own_batch, mate_batch, *refs):
    memory_refs = refs[:shards]
    candidate_ref, count_ref, batch_ref, memory_ref, loss_ref = refs[shards:]
    group, shard = lax.axis_index("group"), lax.axis_index("memory")
    chip, core = group // 2, group % 2
    _, q_count, slots = candidate_ref.shape
    p_count = memory_refs[0].shape[1]
    columns = batch_ref.shape[2]

    parts = []
    for first in range(0, columns, LANES):
        lane = lax.broadcasted_iota(jnp.int32, (q_count, LANES), 1) + first
        owner = lane // q_count
        source = (((owner // 2) ^ chip) * q_count + lane % q_count) % LANES
        own = jnp.take_along_axis(own_batch[...], source, axis=1)
        mate = jnp.take_along_axis(mate_batch[...], source, axis=1)
        parts.append(jnp.where(owner % 2 == core, own, mate))
    batch = jnp.concatenate(parts, axis=1)[:, :columns]
    batch_ref[0] = batch

    ids = candidate_ref[0]
    padded = jnp.concatenate([ids, jnp.zeros((q_count, p_count - slots), jnp.int32)], axis=1)
    holder, local = padded // p_count, padded % p_count
    picked = jnp.zeros((q_count, p_count), jnp.float32)
    for step in range(shards):
        found = jnp.take_along_axis(memory_refs[-step][...], local, axis=1)
        picked = jnp.where(holder == (shard ^ step), found, picked)

    valid = lax.broadcasted_iota(jnp.int32, (q_count, p_count), 1) < column_of(count_ref[...])
    memory_ref[0] = jnp.where(valid, picked, 0.0)[:, :slots]

    top = jnp.maximum(
        jnp.max(batch, axis=1, keepdims=True),
        jnp.max(jnp.where(valid, picked, -jnp.inf), axis=1, keepdims=True),
    )
    total = jnp.sum(jnp.exp(batch - top), axis=1, keepdims=True) + jnp.sum(
        jnp.where(valid, jnp.exp(picked - top), 0.0), axis=1, keepdims=True
    )
    column = lax.broadcasted_iota(jnp.int32, batch.shape, 1)
    own = group * q_count + lax.broadcasted_iota(jnp.int32, batch.shape, 0)
    target_score = jnp.sum(jnp.where(column == own, batch, 0.0), axis=1, keepdims=True)
    loss_ref[...] = row_of(top + jnp.log(total) - target_score)


def finish(own_batch, mate_batch, memory_parts, candidates, counts, columns):
    _, q_count, slots = candidates.shape
    return pl.pallas_call(
        functools.partial(loss_kernel, len(memory_parts)),
        out_shape=[
            jax.ShapeDtypeStruct((1, q_count, columns), jnp.float32),
            jax.ShapeDtypeStruct((1, q_count, slots), jnp.float32),
            jax.ShapeDtypeStruct((1, q_count), jnp.float32),
        ],
        compiler_params=pltpu.CompilerParams(vmem_limit_bytes=4 * MIB),
        name="finish",
    )(own_batch, mate_batch, *memory_parts, candidates, counts)


def body(queries, positives, memory, candidates, counts):
    shards = lax.axis_size("memory")
    groups = lax.axis_size("group")
    chips = groups // 2
    q_count = queries.shape[1]
    slots = candidates.shape[2] // 2

    def to_shard(array, step):
        return lax.ppermute(array, "memory", [(i, i ^ step) for i in range(shards)])

    def to_group(array, step):
        return lax.ppermute(array, "group", [(i, i ^ step) for i in range(groups)])

    own = pack(queries, candidates, counts, memory.shape[1])
    packed = [own] + [to_shard(own, step) for step in range(1, shards)]
    sent_positives, sent_queries, _ = lax.optimization_barrier((positives, queries, own))
    row = [positives] + [to_group(sent_positives, 2 * step) for step in range(1, chips)]
    mate_queries = to_group(sent_queries, 1)

    scores = score_memory(packed, memory, q_count, slots)
    returned = [to_shard(scores[step], step) for step in range(shards - 1, 0, -1)]
    mate_queries, _ = lax.optimization_barrier((mate_queries, scores[0]))
    mate_scores = score_batch(mate_queries, row)
    mate_batch = to_group(mate_scores, 1)
    own_queries, _ = lax.optimization_barrier((queries, mate_scores))
    own_batch = score_batch(own_queries, row)
    columns = groups * q_count
    return finish(
        own_batch, mate_batch, [scores[0]] + returned, candidates, counts, columns
    )


def solution(mesh):
    in_specs = (
        P("group", "memory", None, None),
        P("group", "memory", None, None),
        P("group", "memory", None, None),
        P("group", "memory", None),
        P("group", "memory"),
    )
    out_specs = (P("group", "memory", None), P("group", "memory", None), P("group", "memory"))
    return jax.shard_map(body, mesh=mesh, in_specs=in_specs, out_specs=out_specs, check_vma=False)
```

```python
import functools

import jax
import jax.numpy as jnp
from jax import lax
from jax.experimental import pallas as pl
from jax.experimental.pallas import tpu as pltpu
from jax.sharding import PartitionSpec as P

LANES = 128
MIB = 1024 * 1024
SLOTS = 8
LOW = 256
CHUNK = 32


def in_hbm(array):
    return pltpu.with_memory_space_constraint(array, pltpu.HBM)


def token_max(passages, tokens):
    count, width, depth = passages.shape
    product = lax.dot_general(
        passages.reshape(count * width, depth),
        tokens,
        (((1,), (1,)), ((), ())),
        preferred_element_type=jnp.float32,
    )
    return jnp.max(product.reshape(count, width, tokens.shape[0]), axis=1)


def token_sum(best, queries):
    tokens = best.shape[1]
    per_query = tokens // queries
    row = lax.broadcasted_iota(jnp.int32, (queries, tokens), 0)
    col = lax.broadcasted_iota(jnp.int32, (queries, tokens), 1)
    own = (col // per_query == row).astype(jnp.bfloat16)
    high = best.astype(jnp.bfloat16)
    rest = best - high.astype(jnp.float32)
    middle = rest.astype(jnp.bfloat16)
    low = (rest - middle.astype(jnp.float32)).astype(jnp.bfloat16)
    return lax.dot_general(
        jnp.concatenate([own] * 3, axis=1),
        jnp.concatenate([high, middle, low], axis=1),
        (((1,), (1,)), ((), ())),
        preferred_element_type=jnp.float32,
    )


def column_of(row):
    size = row.shape[1]
    square = (size, size)
    diagonal = lax.broadcasted_iota(jnp.int32, square, 0) == lax.broadcasted_iota(
        jnp.int32, square, 1
    )
    return jnp.sum(jnp.where(diagonal, jnp.broadcast_to(row, square), 0), axis=1, keepdims=True)


def row_of(column):
    size = column.shape[0]
    square = (size, size)
    diagonal = lax.broadcasted_iota(jnp.int32, square, 0) == lax.broadcasted_iota(
        jnp.int32, square, 1
    )
    return jnp.sum(jnp.where(diagonal, jnp.broadcast_to(column, square), 0), axis=0, keepdims=True)


def split_ids(p_count, candidate_ref, count_ref):
    ids = candidate_ref[0]
    row = lax.broadcasted_iota(jnp.int32, ids.shape, 0)
    valid_count = jnp.zeros(ids.shape, jnp.int32)
    for index in range(ids.shape[0]):
        valid_count = jnp.where(row == index, count_ref[0, index], valid_count)
    valid = lax.broadcasted_iota(jnp.int32, ids.shape, 1) < valid_count
    holder = jnp.where(valid, ids // p_count, -1)
    return (ids % p_count).astype(jnp.float32), holder.astype(jnp.float32)


def pack_kernel(p_count, query_ref, candidate_ref, count_ref, out_ref):
    _, q_count, slots = candidate_ref.shape
    _, _, q_tokens, depth = query_ref.shape
    tokens = q_count * q_tokens
    out_ref[:tokens] = query_ref[0].reshape(tokens, depth)
    planes = jnp.concatenate(split_ids(p_count, candidate_ref, count_ref), axis=0)
    empty = jnp.zeros((2 * q_count, depth - slots), jnp.float32)
    out_ref[tokens:] = jnp.concatenate([planes, empty], axis=1).astype(out_ref.dtype)


def pack(queries, candidates, counts, p_count):
    _, q_count, q_tokens, depth = queries.shape
    vmem = pl.BlockSpec(memory_space=pltpu.VMEM)
    return pl.pallas_call(
        functools.partial(pack_kernel, p_count),
        in_specs=[vmem, vmem, pl.BlockSpec(memory_space=pltpu.SMEM)],
        out_shape=jax.ShapeDtypeStruct((q_count * (q_tokens + 2), depth), queries.dtype),
        compiler_params=pltpu.CompilerParams(vmem_limit_bytes=4 * MIB),
        name="pack",
    )(in_hbm(queries), in_hbm(candidates), in_hbm(counts))


def memory_kernel(shards, slots, *refs):
    packed_refs, memory_ref = refs[:shards], refs[shards]
    out_refs = refs[shards + 1 : 2 * shards + 1]
    passage_ref, query_ref, rank_ref, best_ref, list_ref, scalar_ref, copy_sems, list_sem = refs[
        2 * shards + 1 :
    ]
    q_count = out_refs[0].shape[0]
    p_count = passage_ref.shape[0]
    total, q_tokens, depth = query_ref.shape
    chunks = p_count // CHUNK

    def fetch(chunk):
        rows = pl.ds(pl.multiple_of(chunk * CHUNK, CHUNK), CHUNK)
        return pltpu.make_async_copy(
            memory_ref.at[0, rows], passage_ref.at[rows], copy_sems.at[chunk]
        )

    for chunk in range(chunks):
        fetch(chunk).start()

    me = lax.axis_index("memory").astype(jnp.float32)
    keys = []
    for index, packed_ref in enumerate(packed_refs):
        tokens = packed_ref[: q_count * q_tokens].reshape(q_count, q_tokens, depth)
        query_ref[index * q_count : (index + 1) * q_count] = tokens
        planes = packed_ref[q_count * q_tokens :].astype(jnp.float32)
        local, holder = planes[:q_count], planes[q_count:]
        keys.append(jnp.where(holder == me, local, -1.0))
    keys = jnp.concatenate(keys, axis=0)
    passage = lax.broadcasted_iota(jnp.int32, (total, p_count), 1).astype(jnp.float32)
    named = jnp.zeros((total, p_count), jnp.float32)
    for slot in range(slots):
        named = jnp.where(keys[:, slot : slot + 1] == passage, 1.0, named)

    square = (total, total)
    earlier = lax.broadcasted_iota(jnp.int32, square, 1) < lax.broadcasted_iota(
        jnp.int32, square, 0
    )
    before = jnp.dot(earlier.astype(jnp.float32), named, preferred_element_type=jnp.float32)
    rank_ref[...] = jnp.where(named > 0.0, before, -1.0)
    counts = jnp.sum(named, axis=0, keepdims=True)
    most = jnp.broadcast_to(jnp.max(counts, axis=1, keepdims=True), counts.shape)

    def left_over(first):
        left = jnp.where(rank_ref[...] == first, 1.0, 0.0)
        left = jnp.sum(left, axis=0, keepdims=True)
        square = (p_count, p_count)
        row = lax.broadcasted_iota(jnp.int32, square, 0).astype(jnp.float32)
        column = lax.broadcasted_iota(jnp.int32, square, 1).astype(jnp.float32)
        place = jnp.dot(left, (row < column).astype(jnp.float32), preferred_element_type=jnp.float32)
        mine = jnp.where((place == row) & (left > 0.0), column, 0.0)
        index = jnp.sum(mine, axis=1, keepdims=True)
        index = jnp.sum(jnp.where(row == column, index, 0.0), axis=0, keepdims=True)
        return [index, jnp.broadcast_to(jnp.sum(left, axis=1, keepdims=True), left.shape)]

    def write_list(first, extra):
        asker = lax.broadcasted_iota(jnp.int32, (total, p_count), 0).astype(jnp.float32)
        rank = rank_ref[...] - first
        rows = [
            jnp.sum(jnp.where(rank == float(slot), asker, 0.0), axis=0, keepdims=True)
            for slot in range(SLOTS)
        ]
        for slot, above in enumerate(extra):
            rows[slot] = rows[slot] + LOW * above
        list_ref[...] = jnp.concatenate(rows, axis=0).astype(jnp.int32)
        copy = pltpu.make_async_copy(list_ref, scalar_ref, list_sem)
        copy.start()
        copy.wait()

    def unit(index):
        tokens = [query_ref[scalar_ref[slot, index] & (LOW - 1)] for slot in range(SLOTS)]
        return token_max(passage_ref[pl.ds(index, 1)], jnp.concatenate(tokens, axis=0))

    def add_scores(first, scores):
        sums = token_sum(best_ref[...], SLOTS)
        for index, out_ref in enumerate(out_refs):
            rank = rank_ref[index * q_count : (index + 1) * q_count] - first
            total_scores = scores[index]
            for slot in range(SLOTS):
                total_scores = jnp.where(rank == float(slot), sums[slot : slot + 1], total_scores)
            out_ref[...] = total_scores

    write_list(0.0, [most])
    rounds = (scalar_ref[0, 0] // LOW + SLOTS - 1) // SLOTS

    @pl.loop(0, chunks)
    def _(chunk):
        fetch(chunk).wait()
        for start in range(0, CHUNK, 8):
            first = pl.multiple_of(chunk * CHUNK + start, 8)
            rows = [unit(first + offset) for offset in range(8)]
            best_ref[pl.ds(first, 8), :] = jnp.concatenate(rows, axis=0)

    add_scores(0.0, [jnp.zeros((q_count, p_count), jnp.float32)] * shards)

    @pl.loop(1, rounds)
    def _(turn):
        done = (turn * SLOTS).astype(jnp.float32)
        write_list(done, left_over(done))

        @pl.loop(0, scalar_ref[1, 0] // LOW)
        def _(place):
            index = scalar_ref[0, place] // LOW
            best_ref[pl.ds(index, 1), :] = unit(index)

        add_scores(done, [out_ref[...] for out_ref in out_refs])


def score_memory(packed, memory, q_count, slots):
    shards = len(packed)
    q_tokens = packed[0].shape[0] // q_count - 2
    _, p_count, p_tokens, depth = memory.shape
    total = shards * q_count
    vmem = pl.BlockSpec(memory_space=pltpu.VMEM)
    return pl.pallas_call(
        functools.partial(memory_kernel, shards, slots),
        in_specs=[vmem] * shards + [pl.BlockSpec(memory_space=pltpu.HBM)],
        out_specs=[vmem] * shards,
        out_shape=[jax.ShapeDtypeStruct((q_count, p_count), jnp.float32)] * shards,
        scratch_shapes=[
            pltpu.VMEM((p_count, p_tokens, depth), memory.dtype),
            pltpu.VMEM((total, q_tokens, depth), memory.dtype),
            pltpu.VMEM((total, p_count), jnp.float32),
            pltpu.VMEM((p_count, SLOTS * q_tokens), jnp.float32),
            pltpu.VMEM((SLOTS, p_count), jnp.int32),
            pltpu.SMEM((SLOTS, p_count), jnp.int32),
            pltpu.SemaphoreType.DMA((p_count // CHUNK,)),
            pltpu.SemaphoreType.DMA,
        ],
        compiler_params=pltpu.CompilerParams(vmem_limit_bytes=16 * MIB),
        cost_estimate=pl.CostEstimate(
            flops=2 * total * q_tokens * p_count * p_tokens * depth,
            bytes_accessed=2 * p_count * p_tokens * depth,
            transcendentals=0,
        ),
        name="score_memory",
    )(*packed, in_hbm(memory))


def batch_kernel(query_ref, *refs):
    passage_refs, (out_ref, best_ref) = refs[:-2], refs[-2:]
    _, queries, q_tokens, depth = query_ref.shape
    count = passage_refs[0].shape[1]
    tokens = query_ref[0].reshape(queries * q_tokens, depth)
    for chip, passage_ref in enumerate(passage_refs):
        best_ref[chip * count : (chip + 1) * count, :] = token_max(passage_ref[0], tokens)
    sums = token_sum(best_ref[...], queries)
    empty = jnp.zeros((queries, out_ref.shape[1] - sums.shape[1]), jnp.float32)
    out_ref[...] = jnp.concatenate([sums, empty], axis=1) if empty.size else sums


def score_batch(queries, positives):
    _, q_count, q_tokens, depth = queries.shape
    _, p_count, p_tokens, _ = positives[0].shape
    chips = len(positives)
    lanes = -(-chips * p_count // LANES) * LANES
    return pl.pallas_call(
        batch_kernel,
        out_shape=jax.ShapeDtypeStruct((q_count, lanes), jnp.float32),
        scratch_shapes=[pltpu.VMEM((chips * p_count, q_count * q_tokens), jnp.float32)],
        compiler_params=pltpu.CompilerParams(vmem_limit_bytes=16 * MIB),
        cost_estimate=pl.CostEstimate(
            flops=2 * chips * q_count * q_tokens * p_count * p_tokens * depth,
            bytes_accessed=2 * chips * p_count * p_tokens * depth,
            transcendentals=0,
        ),
        name="score_batch",
    )(queries, *positives)


def loss_kernel(shards, own_batch, mate_batch, *refs):
    memory_refs = refs[:shards]
    candidate_ref, count_ref, batch_ref, memory_ref, loss_ref = refs[shards:]
    group, shard = lax.axis_index("group"), lax.axis_index("memory")
    chip, core = group // 2, group % 2
    _, q_count, slots = candidate_ref.shape
    p_count = memory_refs[0].shape[1]
    columns = batch_ref.shape[2]

    parts = []
    for first in range(0, columns, LANES):
        lane = lax.broadcasted_iota(jnp.int32, (q_count, LANES), 1) + first
        owner = lane // q_count
        source = (((owner // 2) ^ chip) * q_count + lane % q_count) % LANES
        own = jnp.take_along_axis(own_batch[...], source, axis=1)
        mate = jnp.take_along_axis(mate_batch[...], source, axis=1)
        parts.append(jnp.where(owner % 2 == core, own, mate))
    batch = jnp.concatenate(parts, axis=1)[:, :columns]
    batch_ref[0] = batch

    ids = candidate_ref[0]
    padded = jnp.concatenate([ids, jnp.zeros((q_count, p_count - slots), jnp.int32)], axis=1)
    holder, local = padded // p_count, padded % p_count
    picked = jnp.zeros((q_count, p_count), jnp.float32)
    for step in range(shards):
        found = jnp.take_along_axis(memory_refs[-step][...], local, axis=1)
        picked = jnp.where(holder == (shard ^ step), found, picked)

    valid = lax.broadcasted_iota(jnp.int32, (q_count, p_count), 1) < column_of(count_ref[...])
    memory_ref[0] = jnp.where(valid, picked, 0.0)[:, :slots]

    top = jnp.maximum(
        jnp.max(batch, axis=1, keepdims=True),
        jnp.max(jnp.where(valid, picked, -jnp.inf), axis=1, keepdims=True),
    )
    total = jnp.sum(jnp.exp(batch - top), axis=1, keepdims=True) + jnp.sum(
        jnp.where(valid, jnp.exp(picked - top), 0.0), axis=1, keepdims=True
    )
    column = lax.broadcasted_iota(jnp.int32, batch.shape, 1)
    own = group * q_count + lax.broadcasted_iota(jnp.int32, batch.shape, 0)
    target_score = jnp.sum(jnp.where(column == own, batch, 0.0), axis=1, keepdims=True)
    loss_ref[...] = row_of(top + jnp.log(total) - target_score)


def finish(own_batch, mate_batch, memory_parts, candidates, counts, columns):
    _, q_count, slots = candidates.shape
    return pl.pallas_call(
        functools.partial(loss_kernel, len(memory_parts)),
        out_shape=[
            jax.ShapeDtypeStruct((1, q_count, columns), jnp.float32),
            jax.ShapeDtypeStruct((1, q_count, slots), jnp.float32),
            jax.ShapeDtypeStruct((1, q_count), jnp.float32),
        ],
        compiler_params=pltpu.CompilerParams(vmem_limit_bytes=4 * MIB),
        name="finish",
    )(own_batch, mate_batch, *memory_parts, candidates, counts)


def body(queries, positives, memory, candidates, counts):
    shards = lax.axis_size("memory")
    groups = lax.axis_size("group")
    chips = groups // 2
    q_count = queries.shape[1]
    slots = candidates.shape[2] // 2

    def to_shard(array, step):
        return lax.ppermute(array, "memory", [(i, i ^ step) for i in range(shards)])

    def to_group(array, step):
        return lax.ppermute(array, "group", [(i, i ^ step) for i in range(groups)])

    own = pack(queries, candidates, counts, memory.shape[1])
    packed = [own] + [to_shard(own, step) for step in range(1, shards)]
    sent_positives, sent_queries, _ = lax.optimization_barrier((positives, queries, own))
    row = [positives] + [to_group(sent_positives, 2 * step) for step in range(1, chips)]
    mate_queries = to_group(sent_queries, 1)

    scores = score_memory(packed, memory, q_count, slots)
    returned = [to_shard(scores[step], step) for step in range(shards - 1, 0, -1)]
    mate_queries, _ = lax.optimization_barrier((mate_queries, scores[0]))
    mate_scores = score_batch(mate_queries, row)
    mate_batch = to_group(mate_scores, 1)
    own_queries, _ = lax.optimization_barrier((queries, mate_scores))
    own_batch = score_batch(own_queries, row)
    columns = groups * q_count
    return finish(
        own_batch, mate_batch, [scores[0]] + returned, candidates, counts, columns
    )


def solution(mesh):
    in_specs = (
        P("group", "memory", None, None),
        P("group", "memory", None, None),
        P("group", "memory", None, None),
        P("group", "memory", None),
        P("group", "memory"),
    )
    out_specs = (P("group", "memory", None), P("group", "memory", None), P("group", "memory"))
    return jax.shard_map(body, mesh=mesh, in_specs=in_specs, out_specs=out_specs, check_vma=False)
```

```python
import functools

import jax
import jax.numpy as jnp
from jax import lax
from jax.experimental import pallas as pl
from jax.experimental.pallas import tpu as pltpu
from jax.sharding import PartitionSpec as P

LANES = 128
MIB = 1024 * 1024
SLOTS = 8
LOW = 256
PACK_FLOPS = 10**10
PACK_BYTES = 2**24
CHUNK = 32


def in_hbm(array):
    return pltpu.with_memory_space_constraint(array, pltpu.HBM)


def token_max(passages, tokens):
    count, width, depth = passages.shape
    product = lax.dot_general(
        passages.reshape(count * width, depth),
        tokens,
        (((1,), (1,)), ((), ())),
        preferred_element_type=jnp.float32,
    )
    return jnp.max(product.reshape(count, width, tokens.shape[0]), axis=1)


def token_sum(best, queries):
    tokens = best.shape[1]
    per_query = tokens // queries
    row = lax.broadcasted_iota(jnp.int32, (queries, tokens), 0)
    col = lax.broadcasted_iota(jnp.int32, (queries, tokens), 1)
    own = (col // per_query == row).astype(jnp.bfloat16)
    high = best.astype(jnp.bfloat16)
    rest = best - high.astype(jnp.float32)
    middle = rest.astype(jnp.bfloat16)
    low = (rest - middle.astype(jnp.float32)).astype(jnp.bfloat16)
    return lax.dot_general(
        jnp.concatenate([own] * 3, axis=1),
        jnp.concatenate([high, middle, low], axis=1),
        (((1,), (1,)), ((), ())),
        preferred_element_type=jnp.float32,
    )


def column_of(row):
    size = row.shape[1]
    square = (size, size)
    diagonal = lax.broadcasted_iota(jnp.int32, square, 0) == lax.broadcasted_iota(
        jnp.int32, square, 1
    )
    return jnp.sum(jnp.where(diagonal, jnp.broadcast_to(row, square), 0), axis=1, keepdims=True)


def row_of(column):
    size = column.shape[0]
    square = (size, size)
    diagonal = lax.broadcasted_iota(jnp.int32, square, 0) == lax.broadcasted_iota(
        jnp.int32, square, 1
    )
    return jnp.sum(jnp.where(diagonal, jnp.broadcast_to(column, square), 0), axis=0, keepdims=True)


def split_ids(p_count, candidate_ref, count_ref):
    ids = candidate_ref[0]
    row = lax.broadcasted_iota(jnp.int32, ids.shape, 0)
    valid_count = jnp.zeros(ids.shape, jnp.int32)
    for index in range(ids.shape[0]):
        valid_count = jnp.where(row == index, count_ref[0, index], valid_count)
    valid = lax.broadcasted_iota(jnp.int32, ids.shape, 1) < valid_count
    holder = jnp.where(valid, ids // p_count, -1)
    return (ids % p_count).astype(jnp.float32), holder.astype(jnp.float32)


def pack_kernel(p_count, query_ref, candidate_ref, count_ref, out_ref):
    _, q_count, slots = candidate_ref.shape
    _, _, q_tokens, depth = query_ref.shape
    tokens = q_count * q_tokens
    out_ref[:tokens] = query_ref[0].reshape(tokens, depth)
    planes = jnp.concatenate(split_ids(p_count, candidate_ref, count_ref), axis=0)
    empty = jnp.zeros((2 * q_count, depth - slots), jnp.float32)
    out_ref[tokens:] = jnp.concatenate([planes, empty], axis=1).astype(out_ref.dtype)


def pack(queries, candidates, counts, p_count):
    _, q_count, q_tokens, depth = queries.shape
    vmem = pl.BlockSpec(memory_space=pltpu.VMEM)
    return pl.pallas_call(
        functools.partial(pack_kernel, p_count),
        in_specs=[vmem, vmem, pl.BlockSpec(memory_space=pltpu.SMEM)],
        out_shape=jax.ShapeDtypeStruct((q_count * (q_tokens + 2), depth), queries.dtype),
        compiler_params=pltpu.CompilerParams(vmem_limit_bytes=4 * MIB),
        cost_estimate=pl.CostEstimate(
            flops=PACK_FLOPS, bytes_accessed=PACK_BYTES, transcendentals=0
        ),
        name="pack",
    )(in_hbm(queries), in_hbm(candidates), in_hbm(counts))


def memory_kernel(shards, slots, *refs):
    packed_refs, passage_ref = refs[:shards], refs[shards].at[0]
    out_refs = refs[shards + 1 : 2 * shards + 1]
    query_ref, rank_ref, best_ref, list_ref, scalar_ref, list_sem = refs[2 * shards + 1 :]
    q_count = out_refs[0].shape[0]
    p_count = passage_ref.shape[0]
    total, q_tokens, depth = query_ref.shape
    chunks = p_count // CHUNK

    me = lax.axis_index("memory").astype(jnp.float32)
    keys = []
    for index, packed_ref in enumerate(packed_refs):
        tokens = packed_ref[: q_count * q_tokens].reshape(q_count, q_tokens, depth)
        query_ref[index * q_count : (index + 1) * q_count] = tokens
        planes = packed_ref[q_count * q_tokens :].astype(jnp.float32)
        local, holder = planes[:q_count], planes[q_count:]
        keys.append(jnp.where(holder == me, local, -1.0))
    keys = jnp.concatenate(keys, axis=0)
    passage = lax.broadcasted_iota(jnp.int32, (total, p_count), 1).astype(jnp.float32)
    named = jnp.zeros((total, p_count), jnp.float32)
    for slot in range(slots):
        named = jnp.where(keys[:, slot : slot + 1] == passage, 1.0, named)

    square = (total, total)
    earlier = lax.broadcasted_iota(jnp.int32, square, 1) < lax.broadcasted_iota(
        jnp.int32, square, 0
    )
    before = jnp.dot(earlier.astype(jnp.float32), named, preferred_element_type=jnp.float32)
    rank_ref[...] = jnp.where(named > 0.0, before, -1.0)
    counts = jnp.sum(named, axis=0, keepdims=True)
    most = jnp.broadcast_to(jnp.max(counts, axis=1, keepdims=True), counts.shape)

    def left_over(first):
        left = jnp.where(rank_ref[...] == first, 1.0, 0.0)
        left = jnp.sum(left, axis=0, keepdims=True)
        square = (p_count, p_count)
        row = lax.broadcasted_iota(jnp.int32, square, 0).astype(jnp.float32)
        column = lax.broadcasted_iota(jnp.int32, square, 1).astype(jnp.float32)
        place = jnp.dot(left, (row < column).astype(jnp.float32), preferred_element_type=jnp.float32)
        mine = jnp.where((place == row) & (left > 0.0), column, 0.0)
        index = jnp.sum(mine, axis=1, keepdims=True)
        index = jnp.sum(jnp.where(row == column, index, 0.0), axis=0, keepdims=True)
        return [index, jnp.broadcast_to(jnp.sum(left, axis=1, keepdims=True), left.shape)]

    def write_list(first, extra):
        asker = lax.broadcasted_iota(jnp.int32, (total, p_count), 0).astype(jnp.float32)
        rank = rank_ref[...] - first
        rows = [
            jnp.sum(jnp.where(rank == float(slot), asker, 0.0), axis=0, keepdims=True)
            for slot in range(SLOTS)
        ]
        for slot, above in enumerate(extra):
            rows[slot] = rows[slot] + LOW * above
        list_ref[...] = jnp.concatenate(rows, axis=0).astype(jnp.int32)
        copy = pltpu.make_async_copy(list_ref, scalar_ref, list_sem)
        copy.start()
        copy.wait()

    def unit(index):
        tokens = [query_ref[scalar_ref[slot, index] & (LOW - 1)] for slot in range(SLOTS)]
        return token_max(passage_ref[pl.ds(index, 1)], jnp.concatenate(tokens, axis=0))

    def add_scores(first, scores):
        sums = token_sum(best_ref[...], SLOTS)
        for index, out_ref in enumerate(out_refs):
            rank = rank_ref[index * q_count : (index + 1) * q_count] - first
            total_scores = scores[index]
            for slot in range(SLOTS):
                total_scores = jnp.where(rank == float(slot), sums[slot : slot + 1], total_scores)
            out_ref[...] = total_scores

    write_list(0.0, [most])
    rounds = (scalar_ref[0, 0] // LOW + SLOTS - 1) // SLOTS

    @pl.loop(0, chunks)
    def _(chunk):
        for start in range(0, CHUNK, 8):
            first = pl.multiple_of(chunk * CHUNK + start, 8)
            rows = [unit(first + offset) for offset in range(8)]
            best_ref[pl.ds(first, 8), :] = jnp.concatenate(rows, axis=0)

    add_scores(0.0, [jnp.zeros((q_count, p_count), jnp.float32)] * shards)

    @pl.loop(1, rounds)
    def _(turn):
        done = (turn * SLOTS).astype(jnp.float32)
        write_list(done, left_over(done))

        @pl.loop(0, scalar_ref[1, 0] // LOW)
        def _(place):
            index = scalar_ref[0, place] // LOW
            best_ref[pl.ds(index, 1), :] = unit(index)

        add_scores(done, [out_ref[...] for out_ref in out_refs])


def score_memory(packed, memory, q_count, slots):
    shards = len(packed)
    q_tokens = packed[0].shape[0] // q_count - 2
    _, p_count, p_tokens, depth = memory.shape
    total = shards * q_count
    vmem = pl.BlockSpec(memory_space=pltpu.VMEM)
    return pl.pallas_call(
        functools.partial(memory_kernel, shards, slots),
        in_specs=[vmem] * (shards + 1),
        out_specs=[vmem] * shards,
        out_shape=[jax.ShapeDtypeStruct((q_count, p_count), jnp.float32)] * shards,
        scratch_shapes=[
            pltpu.VMEM((total, q_tokens, depth), memory.dtype),
            pltpu.VMEM((total, p_count), jnp.float32),
            pltpu.VMEM((p_count, SLOTS * q_tokens), jnp.float32),
            pltpu.VMEM((SLOTS, p_count), jnp.int32),
            pltpu.SMEM((SLOTS, p_count), jnp.int32),
            pltpu.SemaphoreType.DMA,
        ],
        compiler_params=pltpu.CompilerParams(vmem_limit_bytes=16 * MIB),
        cost_estimate=pl.CostEstimate(
            flops=2 * total * q_tokens * p_count * p_tokens * depth,
            bytes_accessed=2 * p_count * p_tokens * depth,
            transcendentals=0,
        ),
        name="score_memory",
    )(*packed, memory)


def batch_kernel(query_ref, *refs):
    passage_refs, (out_ref, best_ref) = refs[:-2], refs[-2:]
    _, queries, q_tokens, depth = query_ref.shape
    count = passage_refs[0].shape[1]
    tokens = query_ref[0].reshape(queries * q_tokens, depth)
    for chip, passage_ref in enumerate(passage_refs):
        best_ref[chip * count : (chip + 1) * count, :] = token_max(passage_ref[0], tokens)
    sums = token_sum(best_ref[...], queries)
    empty = jnp.zeros((queries, out_ref.shape[1] - sums.shape[1]), jnp.float32)
    out_ref[...] = jnp.concatenate([sums, empty], axis=1) if empty.size else sums


def score_batch(queries, positives):
    _, q_count, q_tokens, depth = queries.shape
    _, p_count, p_tokens, _ = positives[0].shape
    chips = len(positives)
    lanes = -(-chips * p_count // LANES) * LANES
    return pl.pallas_call(
        batch_kernel,
        out_shape=jax.ShapeDtypeStruct((q_count, lanes), jnp.float32),
        scratch_shapes=[pltpu.VMEM((chips * p_count, q_count * q_tokens), jnp.float32)],
        compiler_params=pltpu.CompilerParams(vmem_limit_bytes=16 * MIB),
        cost_estimate=pl.CostEstimate(
            flops=2 * chips * q_count * q_tokens * p_count * p_tokens * depth,
            bytes_accessed=2 * chips * p_count * p_tokens * depth,
            transcendentals=0,
        ),
        name="score_batch",
    )(queries, *positives)


def loss_kernel(shards, own_batch, mate_batch, *refs):
    memory_refs = refs[:shards]
    candidate_ref, count_ref, batch_ref, memory_ref, loss_ref = refs[shards:]
    group, shard = lax.axis_index("group"), lax.axis_index("memory")
    chip, core = group // 2, group % 2
    _, q_count, slots = candidate_ref.shape
    p_count = memory_refs[0].shape[1]
    columns = batch_ref.shape[2]

    parts = []
    for first in range(0, columns, LANES):
        lane = lax.broadcasted_iota(jnp.int32, (q_count, LANES), 1) + first
        owner = lane // q_count
        source = (((owner // 2) ^ chip) * q_count + lane % q_count) % LANES
        own = jnp.take_along_axis(own_batch[...], source, axis=1)
        mate = jnp.take_along_axis(mate_batch[...], source, axis=1)
        parts.append(jnp.where(owner % 2 == core, own, mate))
    batch = jnp.concatenate(parts, axis=1)[:, :columns]
    batch_ref[0] = batch

    ids = candidate_ref[0]
    padded = jnp.concatenate([ids, jnp.zeros((q_count, p_count - slots), jnp.int32)], axis=1)
    holder, local = padded // p_count, padded % p_count
    picked = jnp.zeros((q_count, p_count), jnp.float32)
    for step in range(shards):
        found = jnp.take_along_axis(memory_refs[-step][...], local, axis=1)
        picked = jnp.where(holder == (shard ^ step), found, picked)

    valid = lax.broadcasted_iota(jnp.int32, (q_count, p_count), 1) < column_of(count_ref[...])
    memory_ref[0] = jnp.where(valid, picked, 0.0)[:, :slots]

    top = jnp.maximum(
        jnp.max(batch, axis=1, keepdims=True),
        jnp.max(jnp.where(valid, picked, -jnp.inf), axis=1, keepdims=True),
    )
    total = jnp.sum(jnp.exp(batch - top), axis=1, keepdims=True) + jnp.sum(
        jnp.where(valid, jnp.exp(picked - top), 0.0), axis=1, keepdims=True
    )
    column = lax.broadcasted_iota(jnp.int32, batch.shape, 1)
    own = group * q_count + lax.broadcasted_iota(jnp.int32, batch.shape, 0)
    target_score = jnp.sum(jnp.where(column == own, batch, 0.0), axis=1, keepdims=True)
    loss_ref[...] = row_of(top + jnp.log(total) - target_score)


def finish(own_batch, mate_batch, memory_parts, candidates, counts, columns):
    _, q_count, slots = candidates.shape
    return pl.pallas_call(
        functools.partial(loss_kernel, len(memory_parts)),
        out_shape=[
            jax.ShapeDtypeStruct((1, q_count, columns), jnp.float32),
            jax.ShapeDtypeStruct((1, q_count, slots), jnp.float32),
            jax.ShapeDtypeStruct((1, q_count), jnp.float32),
        ],
        compiler_params=pltpu.CompilerParams(vmem_limit_bytes=4 * MIB),
        name="finish",
    )(own_batch, mate_batch, *memory_parts, candidates, counts)


def body(queries, positives, memory, candidates, counts):
    shards = lax.axis_size("memory")
    groups = lax.axis_size("group")
    chips = groups // 2
    q_count = queries.shape[1]
    slots = candidates.shape[2] // 2

    def to_shard(array, step):
        return lax.ppermute(array, "memory", [(i, i ^ step) for i in range(shards)])

    def to_group(array, step):
        return lax.ppermute(array, "group", [(i, i ^ step) for i in range(groups)])

    own = pack(queries, candidates, counts, memory.shape[1])
    packed = [own] + [to_shard(own, step) for step in range(1, shards)]
    sent_positives, sent_queries, _ = lax.optimization_barrier((positives, queries, own))
    row = [positives] + [to_group(sent_positives, 2 * step) for step in range(1, chips)]
    mate_queries = to_group(sent_queries, 1)

    scores = score_memory(packed, memory, q_count, slots)
    returned = [to_shard(scores[step], step) for step in range(shards - 1, 0, -1)]
    mate_queries, _ = lax.optimization_barrier((mate_queries, scores[0]))
    mate_scores = score_batch(mate_queries, row)
    mate_batch = to_group(mate_scores, 1)
    own_queries, _ = lax.optimization_barrier((queries, mate_scores))
    own_batch = score_batch(own_queries, row)
    columns = groups * q_count
    return finish(
        own_batch, mate_batch, [scores[0]] + returned, candidates, counts, columns
    )


def solution(mesh):
    in_specs = (
        P("group", "memory", None, None),
        P("group", "memory", None, None),
        P("group", "memory", None, None),
        P("group", "memory", None),
        P("group", "memory"),
    )
    out_specs = (P("group", "memory", None), P("group", "memory", None), P("group", "memory"))
    return jax.shard_map(body, mesh=mesh, in_specs=in_specs, out_specs=out_specs, check_vma=False)
```

```python
import functools

import jax
import jax.numpy as jnp
from jax import lax
from jax.experimental import pallas as pl
from jax.experimental.pallas import tpu as pltpu
from jax.sharding import PartitionSpec as P

LANES = 128
MIB = 1024 * 1024
SLOTS = 8
LOW = 256
PACK_FLOPS = 10**10
PACK_BYTES = 2**24
CHUNK = 32


def in_hbm(array):
    return pltpu.with_memory_space_constraint(array, pltpu.HBM)


def token_max(passages, tokens):
    count, width, depth = passages.shape
    product = lax.dot_general(
        passages.reshape(count * width, depth),
        tokens,
        (((1,), (1,)), ((), ())),
        preferred_element_type=jnp.float32,
    )
    return jnp.max(product.reshape(count, width, tokens.shape[0]), axis=1)


def token_sum(best, queries):
    tokens = best.shape[1]
    per_query = tokens // queries
    row = lax.broadcasted_iota(jnp.int32, (queries, tokens), 0)
    col = lax.broadcasted_iota(jnp.int32, (queries, tokens), 1)
    own = (col // per_query == row).astype(jnp.bfloat16)
    high = best.astype(jnp.bfloat16)
    rest = best - high.astype(jnp.float32)
    middle = rest.astype(jnp.bfloat16)
    low = (rest - middle.astype(jnp.float32)).astype(jnp.bfloat16)
    return lax.dot_general(
        jnp.concatenate([own] * 3, axis=1),
        jnp.concatenate([high, middle, low], axis=1),
        (((1,), (1,)), ((), ())),
        preferred_element_type=jnp.float32,
    )


def column_of(row):
    size = row.shape[1]
    square = (size, size)
    diagonal = lax.broadcasted_iota(jnp.int32, square, 0) == lax.broadcasted_iota(
        jnp.int32, square, 1
    )
    return jnp.sum(jnp.where(diagonal, jnp.broadcast_to(row, square), 0), axis=1, keepdims=True)


def row_of(column):
    size = column.shape[0]
    square = (size, size)
    diagonal = lax.broadcasted_iota(jnp.int32, square, 0) == lax.broadcasted_iota(
        jnp.int32, square, 1
    )
    return jnp.sum(jnp.where(diagonal, jnp.broadcast_to(column, square), 0), axis=0, keepdims=True)


def split_ids(p_count, candidate_ref, count_ref):
    ids = candidate_ref[0]
    row = lax.broadcasted_iota(jnp.int32, ids.shape, 0)
    valid_count = jnp.zeros(ids.shape, jnp.int32)
    for index in range(ids.shape[0]):
        valid_count = jnp.where(row == index, count_ref[0, index], valid_count)
    valid = lax.broadcasted_iota(jnp.int32, ids.shape, 1) < valid_count
    holder = jnp.where(valid, ids // p_count, -1)
    return (ids % p_count).astype(jnp.float32), holder.astype(jnp.float32)


def pack_kernel(p_count, query_ref, candidate_ref, count_ref, out_ref):
    _, q_count, slots = candidate_ref.shape
    _, _, q_tokens, depth = query_ref.shape
    tokens = q_count * q_tokens
    out_ref[:tokens] = query_ref[0].reshape(tokens, depth)
    planes = jnp.concatenate(split_ids(p_count, candidate_ref, count_ref), axis=0)
    empty = jnp.zeros((2 * q_count, depth - slots), jnp.float32)
    out_ref[tokens:] = jnp.concatenate([planes, empty], axis=1).astype(out_ref.dtype)


def pack(queries, candidates, counts, p_count):
    _, q_count, q_tokens, depth = queries.shape
    vmem = pl.BlockSpec(memory_space=pltpu.VMEM)
    return pl.pallas_call(
        functools.partial(pack_kernel, p_count),
        in_specs=[vmem, vmem, pl.BlockSpec(memory_space=pltpu.SMEM)],
        out_shape=jax.ShapeDtypeStruct((q_count * (q_tokens + 2), depth), queries.dtype),
        compiler_params=pltpu.CompilerParams(vmem_limit_bytes=4 * MIB),
        cost_estimate=pl.CostEstimate(
            flops=PACK_FLOPS, bytes_accessed=PACK_BYTES, transcendentals=0
        ),
        name="pack",
    )(in_hbm(queries), in_hbm(candidates), in_hbm(counts))


def memory_kernel(shards, slots, *refs):
    packed_refs, passage_ref = refs[:shards], refs[shards].at[0]
    score_ref, query_ref, rank_ref, best_ref, list_ref, scalar_ref, list_sem = refs[shards + 1 :]
    place = lax.axis_index("memory")
    out_refs = [score_ref.at[place ^ step] for step in range(shards)]
    q_count = score_ref.shape[1]
    p_count = passage_ref.shape[0]
    total, q_tokens, depth = query_ref.shape
    chunks = p_count // CHUNK

    me = place.astype(jnp.float32)
    keys = []
    for index, packed_ref in enumerate(packed_refs):
        tokens = packed_ref[: q_count * q_tokens].reshape(q_count, q_tokens, depth)
        query_ref[index * q_count : (index + 1) * q_count] = tokens
        planes = packed_ref[q_count * q_tokens :].astype(jnp.float32)
        local, holder = planes[:q_count], planes[q_count:]
        keys.append(jnp.where(holder == me, local, -1.0))
    keys = jnp.concatenate(keys, axis=0)
    passage = lax.broadcasted_iota(jnp.int32, (total, p_count), 1).astype(jnp.float32)
    named = jnp.zeros((total, p_count), jnp.float32)
    for slot in range(slots):
        named = jnp.where(keys[:, slot : slot + 1] == passage, 1.0, named)

    square = (total, total)
    earlier = lax.broadcasted_iota(jnp.int32, square, 1) < lax.broadcasted_iota(
        jnp.int32, square, 0
    )
    before = jnp.dot(earlier.astype(jnp.float32), named, preferred_element_type=jnp.float32)
    rank_ref[...] = jnp.where(named > 0.0, before, -1.0)
    counts = jnp.sum(named, axis=0, keepdims=True)
    most = jnp.broadcast_to(jnp.max(counts, axis=1, keepdims=True), counts.shape)

    def left_over(first):
        left = jnp.where(rank_ref[...] == first, 1.0, 0.0)
        left = jnp.sum(left, axis=0, keepdims=True)
        square = (p_count, p_count)
        row = lax.broadcasted_iota(jnp.int32, square, 0).astype(jnp.float32)
        column = lax.broadcasted_iota(jnp.int32, square, 1).astype(jnp.float32)
        place = jnp.dot(left, (row < column).astype(jnp.float32), preferred_element_type=jnp.float32)
        mine = jnp.where((place == row) & (left > 0.0), column, 0.0)
        index = jnp.sum(mine, axis=1, keepdims=True)
        index = jnp.sum(jnp.where(row == column, index, 0.0), axis=0, keepdims=True)
        return [index, jnp.broadcast_to(jnp.sum(left, axis=1, keepdims=True), left.shape)]

    def write_list(first, extra):
        asker = lax.broadcasted_iota(jnp.int32, (total, p_count), 0).astype(jnp.float32)
        rank = rank_ref[...] - first
        rows = [
            jnp.sum(jnp.where(rank == float(slot), asker, 0.0), axis=0, keepdims=True)
            for slot in range(SLOTS)
        ]
        for slot, above in enumerate(extra):
            rows[slot] = rows[slot] + LOW * above
        list_ref[...] = jnp.concatenate(rows, axis=0).astype(jnp.int32)
        copy = pltpu.make_async_copy(list_ref, scalar_ref, list_sem)
        copy.start()
        copy.wait()

    def unit(index):
        tokens = [query_ref[scalar_ref[slot, index] & (LOW - 1)] for slot in range(SLOTS)]
        return token_max(passage_ref[pl.ds(index, 1)], jnp.concatenate(tokens, axis=0))

    def add_scores(first, scores):
        sums = token_sum(best_ref[...], SLOTS)
        for index, out_ref in enumerate(out_refs):
            rank = rank_ref[index * q_count : (index + 1) * q_count] - first
            total_scores = scores[index]
            for slot in range(SLOTS):
                total_scores = jnp.where(rank == float(slot), sums[slot : slot + 1], total_scores)
            out_ref[...] = total_scores

    write_list(0.0, [most])
    rounds = (scalar_ref[0, 0] // LOW + SLOTS - 1) // SLOTS

    @pl.loop(0, chunks)
    def _(chunk):
        for start in range(0, CHUNK, 8):
            first = pl.multiple_of(chunk * CHUNK + start, 8)
            rows = [unit(first + offset) for offset in range(8)]
            best_ref[pl.ds(first, 8), :] = jnp.concatenate(rows, axis=0)

    add_scores(0.0, [jnp.zeros((q_count, p_count), jnp.float32)] * shards)

    @pl.loop(1, rounds)
    def _(turn):
        done = (turn * SLOTS).astype(jnp.float32)
        write_list(done, left_over(done))

        @pl.loop(0, scalar_ref[1, 0] // LOW)
        def _(place):
            index = scalar_ref[0, place] // LOW
            best_ref[pl.ds(index, 1), :] = unit(index)

        add_scores(done, [out_ref[...] for out_ref in out_refs])


def score_memory(packed, memory, q_count, slots):
    shards = len(packed)
    q_tokens = packed[0].shape[0] // q_count - 2
    _, p_count, p_tokens, depth = memory.shape
    total = shards * q_count
    vmem = pl.BlockSpec(memory_space=pltpu.VMEM)
    return pl.pallas_call(
        functools.partial(memory_kernel, shards, slots),
        in_specs=[vmem] * (shards + 1),
        out_specs=vmem,
        out_shape=jax.ShapeDtypeStruct((shards, q_count, p_count), jnp.float32),
        scratch_shapes=[
            pltpu.VMEM((total, q_tokens, depth), memory.dtype),
            pltpu.VMEM((total, p_count), jnp.float32),
            pltpu.VMEM((p_count, SLOTS * q_tokens), jnp.float32),
            pltpu.VMEM((SLOTS, p_count), jnp.int32),
            pltpu.SMEM((SLOTS, p_count), jnp.int32),
            pltpu.SemaphoreType.DMA,
        ],
        compiler_params=pltpu.CompilerParams(vmem_limit_bytes=16 * MIB),
        cost_estimate=pl.CostEstimate(
            flops=2 * total * q_tokens * p_count * p_tokens * depth,
            bytes_accessed=2 * p_count * p_tokens * depth,
            transcendentals=0,
        ),
        name="score_memory",
    )(*packed, memory)


def batch_kernel(query_ref, *refs):
    passage_refs, (out_ref, best_ref) = refs[:-2], refs[-2:]
    _, queries, q_tokens, depth = query_ref.shape
    count = passage_refs[0].shape[1]
    tokens = query_ref[0].reshape(queries * q_tokens, depth)
    for chip, passage_ref in enumerate(passage_refs):
        best_ref[chip * count : (chip + 1) * count, :] = token_max(passage_ref[0], tokens)
    sums = token_sum(best_ref[...], queries)
    empty = jnp.zeros((queries, out_ref.shape[1] - sums.shape[1]), jnp.float32)
    out_ref[...] = jnp.concatenate([sums, empty], axis=1) if empty.size else sums


def score_batch(queries, positives):
    _, q_count, q_tokens, depth = queries.shape
    _, p_count, p_tokens, _ = positives[0].shape
    chips = len(positives)
    lanes = -(-chips * p_count // LANES) * LANES
    return pl.pallas_call(
        batch_kernel,
        out_shape=jax.ShapeDtypeStruct((q_count, lanes), jnp.float32),
        scratch_shapes=[pltpu.VMEM((chips * p_count, q_count * q_tokens), jnp.float32)],
        compiler_params=pltpu.CompilerParams(vmem_limit_bytes=16 * MIB),
        cost_estimate=pl.CostEstimate(
            flops=2 * chips * q_count * q_tokens * p_count * p_tokens * depth,
            bytes_accessed=2 * chips * p_count * p_tokens * depth,
            transcendentals=0,
        ),
        name="score_batch",
    )(queries, *positives)


def loss_kernel(own_batch, mate_batch, part_ref, candidate_ref, count_ref, *out_refs):
    batch_ref, memory_ref, loss_ref = out_refs
    group = lax.axis_index("group")
    chip, core = group // 2, group % 2
    _, q_count, slots = candidate_ref.shape
    shards, _, p_count = part_ref.shape
    columns = batch_ref.shape[2]

    parts = []
    for first in range(0, columns, LANES):
        lane = lax.broadcasted_iota(jnp.int32, (q_count, LANES), 1) + first
        owner = lane // q_count
        source = (((owner // 2) ^ chip) * q_count + lane % q_count) % LANES
        own = jnp.take_along_axis(own_batch[...], source, axis=1)
        mate = jnp.take_along_axis(mate_batch[...], source, axis=1)
        parts.append(jnp.where(owner % 2 == core, own, mate))
    batch = jnp.concatenate(parts, axis=1)[:, :columns]
    batch_ref[0] = batch

    ids = candidate_ref[0]
    padded = jnp.concatenate([ids, jnp.zeros((q_count, p_count - slots), jnp.int32)], axis=1)
    holder, local = padded // p_count, padded % p_count
    picked = jnp.zeros((q_count, p_count), jnp.float32)
    for shard in range(shards):
        found = jnp.take_along_axis(part_ref[shard], local, axis=1)
        picked = jnp.where(holder == shard, found, picked)

    valid = lax.broadcasted_iota(jnp.int32, (q_count, p_count), 1) < column_of(count_ref[...])
    memory_ref[0] = jnp.where(valid, picked, 0.0)[:, :slots]

    top = jnp.maximum(
        jnp.max(batch, axis=1, keepdims=True),
        jnp.max(jnp.where(valid, picked, -jnp.inf), axis=1, keepdims=True),
    )
    total = jnp.sum(jnp.exp(batch - top), axis=1, keepdims=True) + jnp.sum(
        jnp.where(valid, jnp.exp(picked - top), 0.0), axis=1, keepdims=True
    )
    column = lax.broadcasted_iota(jnp.int32, batch.shape, 1)
    own = group * q_count + lax.broadcasted_iota(jnp.int32, batch.shape, 0)
    target_score = jnp.sum(jnp.where(column == own, batch, 0.0), axis=1, keepdims=True)
    loss_ref[...] = row_of(top + jnp.log(total) - target_score)


def finish(own_batch, mate_batch, memory_parts, candidates, counts, columns):
    _, q_count, slots = candidates.shape
    return pl.pallas_call(
        loss_kernel,
        out_shape=[
            jax.ShapeDtypeStruct((1, q_count, columns), jnp.float32),
            jax.ShapeDtypeStruct((1, q_count, slots), jnp.float32),
            jax.ShapeDtypeStruct((1, q_count), jnp.float32),
        ],
        compiler_params=pltpu.CompilerParams(vmem_limit_bytes=4 * MIB),
        name="finish",
    )(own_batch, mate_batch, memory_parts, candidates, counts)


def body(queries, positives, memory, candidates, counts):
    shards = lax.axis_size("memory")
    groups = lax.axis_size("group")
    chips = groups // 2
    q_count = queries.shape[1]
    slots = candidates.shape[2] // 2

    def to_shard(array, step):
        return lax.ppermute(array, "memory", [(i, i ^ step) for i in range(shards)])

    def to_group(array, step):
        return lax.ppermute(array, "group", [(i, i ^ step) for i in range(groups)])

    own = pack(queries, candidates, counts, memory.shape[1])
    packed = [own] + [to_shard(own, step) for step in range(1, shards)]
    sent_positives, sent_queries, _ = lax.optimization_barrier((positives, queries, own))
    row = [positives] + [to_group(sent_positives, 2 * step) for step in range(1, chips)]
    mate_queries = to_group(sent_queries, 1)

    scores = score_memory(packed, memory, q_count, slots)
    returned = lax.all_to_all(scores, "memory", split_axis=0, concat_axis=0, tiled=True)
    mate_queries, _ = lax.optimization_barrier((mate_queries, scores))
    mate_scores = score_batch(mate_queries, row)
    mate_batch = to_group(mate_scores, 1)
    own_queries, _ = lax.optimization_barrier((queries, mate_scores))
    own_batch = score_batch(own_queries, row)
    columns = groups * q_count
    return finish(own_batch, mate_batch, returned, candidates, counts, columns)


def solution(mesh):
    in_specs = (
        P("group", "memory", None, None),
        P("group", "memory", None, None),
        P("group", "memory", None, None),
        P("group", "memory", None),
        P("group", "memory"),
    )
    out_specs = (P("group", "memory", None), P("group", "memory", None), P("group", "memory"))
    return jax.shard_map(body, mesh=mesh, in_specs=in_specs, out_specs=out_specs, check_vma=False)
```

```python
import functools

import jax
import jax.numpy as jnp
from jax import lax
from jax.experimental import pallas as pl
from jax.experimental.pallas import tpu as pltpu
from jax.sharding import PartitionSpec as P

LANES = 128
MIB = 1024 * 1024
SLOTS = 8
CHUNK = 32
LIST_ROWS = 16
STEP = 4
PACK_FLOPS = 10**10
PACK_BYTES = 2**24


def in_hbm(array):
    return pltpu.with_memory_space_constraint(array, pltpu.HBM)


def token_max(passages, tokens):
    count, width, depth = passages.shape
    product = lax.dot_general(
        passages.reshape(count * width, depth),
        tokens,
        (((1,), (1,)), ((), ())),
        preferred_element_type=jnp.float32,
    )
    return jnp.max(product.reshape(count, width, tokens.shape[0]), axis=1)


def token_sum(best, queries):
    tokens = best.shape[1]
    per_query = tokens // queries
    row = lax.broadcasted_iota(jnp.int32, (queries, tokens), 0)
    col = lax.broadcasted_iota(jnp.int32, (queries, tokens), 1)
    own = (col // per_query == row).astype(jnp.bfloat16)
    high = best.astype(jnp.bfloat16)
    rest = best - high.astype(jnp.float32)
    middle = rest.astype(jnp.bfloat16)
    low = (rest - middle.astype(jnp.float32)).astype(jnp.bfloat16)
    return lax.dot_general(
        jnp.concatenate([own] * 3, axis=1),
        jnp.concatenate([high, middle, low], axis=1),
        (((1,), (1,)), ((), ())),
        preferred_element_type=jnp.float32,
    )


def column_of(row):
    size = row.shape[1]
    square = (size, size)
    diagonal = lax.broadcasted_iota(jnp.int32, square, 0) == lax.broadcasted_iota(
        jnp.int32, square, 1
    )
    return jnp.sum(jnp.where(diagonal, jnp.broadcast_to(row, square), 0), axis=1, keepdims=True)


def row_of(column):
    size = column.shape[0]
    square = (size, size)
    diagonal = lax.broadcasted_iota(jnp.int32, square, 0) == lax.broadcasted_iota(
        jnp.int32, square, 1
    )
    return jnp.sum(jnp.where(diagonal, jnp.broadcast_to(column, square), 0), axis=0, keepdims=True)


def other_half(row):
    half = row.shape[1] // 2
    return jnp.concatenate([row[:, half:], row[:, :half]], axis=1)


def split_ids(p_count, candidate_ref, count_ref):
    ids = candidate_ref[0]
    row = lax.broadcasted_iota(jnp.int32, ids.shape, 0)
    valid_count = jnp.zeros(ids.shape, jnp.int32)
    for index in range(ids.shape[0]):
        valid_count = jnp.where(row == index, count_ref[0, index], valid_count)
    valid = lax.broadcasted_iota(jnp.int32, ids.shape, 1) < valid_count
    holder = jnp.where(valid, ids // p_count, -1)
    return (ids % p_count).astype(jnp.float32), holder.astype(jnp.float32)


def pack_kernel(p_count, query_ref, candidate_ref, count_ref, out_ref):
    _, q_count, slots = candidate_ref.shape
    _, _, q_tokens, depth = query_ref.shape
    tokens = q_count * q_tokens
    out_ref[:tokens] = query_ref[0].reshape(tokens, depth)
    planes = jnp.concatenate(split_ids(p_count, candidate_ref, count_ref), axis=0)
    empty = jnp.zeros((2 * q_count, depth - slots), jnp.float32)
    out_ref[tokens:] = jnp.concatenate([planes, empty], axis=1).astype(out_ref.dtype)


def pack(queries, candidates, counts, p_count):
    _, q_count, q_tokens, depth = queries.shape
    vmem = pl.BlockSpec(memory_space=pltpu.VMEM)
    return pl.pallas_call(
        functools.partial(pack_kernel, p_count),
        in_specs=[vmem, vmem, pl.BlockSpec(memory_space=pltpu.SMEM)],
        out_shape=jax.ShapeDtypeStruct((q_count * (q_tokens + 2), depth), queries.dtype),
        compiler_params=pltpu.CompilerParams(vmem_limit_bytes=4 * MIB),
        cost_estimate=pl.CostEstimate(
            flops=PACK_FLOPS, bytes_accessed=PACK_BYTES, transcendentals=0
        ),
        name="pack",
    )(in_hbm(queries), in_hbm(candidates), in_hbm(counts))


def memory_kernel(shards, slots, *refs):
    packed_refs, passage_ref = refs[:shards], refs[shards].at[0]
    out_refs = refs[shards + 1 : 2 * shards + 1]
    query_ref, rank_ref, best_ref, left_best_ref, *refs = refs[2 * shards + 1 :]
    list_ref, scalar_ref, left_ref, left_scalar_ref, list_sems = refs
    q_count = out_refs[0].shape[0]
    p_count = passage_ref.shape[0]
    total, q_tokens, depth = (size // parts for size, parts in zip(query_ref.shape, (2, 1, 2)))
    half = p_count // 2
    chunks = half // CHUNK

    me = lax.axis_index("memory").astype(jnp.float32)
    keys = []
    for index, packed_ref in enumerate(packed_refs):
        tokens = packed_ref[: q_count * q_tokens].reshape(q_count, q_tokens, depth)
        rows = slice(index * q_count, (index + 1) * q_count)
        query_ref[rows] = jnp.concatenate([tokens, jnp.zeros_like(tokens)], axis=2)
        query_ref[index * q_count + total : (index + 1) * q_count + total] = jnp.concatenate([jnp.zeros_like(tokens), tokens], axis=2)
        planes = packed_ref[q_count * q_tokens :].astype(jnp.float32)
        local, holder = planes[:q_count], planes[q_count:]
        keys.append(jnp.where(holder == me, local, -1.0))
    keys = jnp.concatenate(keys, axis=0)
    passage = lax.broadcasted_iota(jnp.int32, (total, p_count), 1).astype(jnp.float32)
    named = jnp.zeros((total, p_count), jnp.float32)
    for slot in range(slots):
        named = jnp.where(keys[:, slot : slot + 1] == passage, 1.0, named)

    square = (total, total)
    earlier = lax.broadcasted_iota(jnp.int32, square, 1) < lax.broadcasted_iota(
        jnp.int32, square, 0
    )
    before = jnp.dot(earlier.astype(jnp.float32), named, preferred_element_type=jnp.float32)
    counts = jnp.sum(named, axis=0, keepdims=True)
    upper = passage >= half
    before = before + jnp.where(upper, other_half(counts), 0.0)
    rank_ref[...] = jnp.where(named > 0.0, before, -1.0)
    both = counts + other_half(counts)
    most = jnp.broadcast_to(jnp.max(both, axis=1, keepdims=True), counts.shape)

    asker = lax.broadcasted_iota(jnp.int32, (total, p_count), 0).astype(jnp.float32)
    asker = jnp.where(upper, asker + total, asker)

    def ids_from(first):
        rank = rank_ref[...] - first
        rows = [
            jnp.sum(jnp.where(rank == float(slot), asker, 0.0), axis=0, keepdims=True)
            for slot in range(SLOTS)
        ]
        return [row + other_half(row) for row in rows]

    list_copy = pltpu.make_async_copy(list_ref, scalar_ref, list_sems.at[0])
    left_copy = pltpu.make_async_copy(left_ref, left_scalar_ref, list_sems.at[1])

    def write_list():
        rest = jnp.zeros((LIST_ROWS - SLOTS - 1, p_count), jnp.float32)
        rows = ids_from(0.0) + [most, rest]
        list_ref[...] = jnp.concatenate(rows, axis=0).astype(jnp.int32)

    def write_left(first):
        left = jnp.where(rank_ref[...] == first, 1.0, 0.0)
        left = jnp.sum(left, axis=0, keepdims=True)
        left = jnp.where(upper[:1], 0.0, left + other_half(left))
        square = (p_count, p_count)
        row = lax.broadcasted_iota(jnp.int32, square, 0).astype(jnp.float32)
        column = lax.broadcasted_iota(jnp.int32, square, 1).astype(jnp.float32)
        before = (row < column).astype(jnp.float32)
        place = jnp.dot(left, before, preferred_element_type=jnp.float32)
        chosen = jnp.where((place == row) & (left > 0.0), 1.0, 0.0)
        rest = jnp.zeros((LIST_ROWS - SLOTS - 1, p_count), jnp.float32)
        spread = jnp.concatenate(ids_from(first) + [column[:1], rest], axis=0)
        close = lax.dot_general(
            spread, chosen, (((1,), (1,)), ((), ())), preferred_element_type=jnp.float32
        )
        number = jnp.broadcast_to(jnp.sum(left, axis=1, keepdims=True), left.shape)
        rows = [close[: SLOTS + 1], number, rest[1:]]
        left_ref[...] = jnp.concatenate(rows, axis=0).astype(jnp.int32)

    def unit(index, ids_ref, place):
        tokens = [query_ref[ids_ref[slot, place]] for slot in range(SLOTS)]
        pair = [passage_ref[pl.ds(index + side * half, 1)] for side in range(2)]
        return token_max(jnp.concatenate(pair, axis=2), jnp.concatenate(tokens, axis=0))

    def add_scores(best, first):
        sums = token_sum(best, SLOTS)
        sums = jnp.concatenate([sums, sums], axis=1)
        for index, out_ref in enumerate(out_refs):
            rank = rank_ref[index * q_count : (index + 1) * q_count] - first
            scores = out_ref[...]
            for slot in range(SLOTS):
                scores = jnp.where(rank == float(slot), sums[slot : slot + 1], scores)
            out_ref[...] = scores

    for out_ref in out_refs:
        out_ref[...] = jnp.zeros_like(out_ref)
    write_list()
    list_copy.start()
    write_left(float(SLOTS))
    left_copy.start()
    list_copy.wait()

    @pl.loop(0, chunks)
    def _(chunk):
        for start in range(0, CHUNK, 8):
            first = pl.multiple_of(chunk * CHUNK + start, 8)
            rows = [unit(first + offset, scalar_ref, first + offset) for offset in range(8)]
            best_ref[pl.ds(first, 8), :] = jnp.concatenate(rows, axis=0)

    left_copy.wait()
    add_scores(best_ref[...], 0.0)

    @pl.loop(1, (scalar_ref[SLOTS, 0] + SLOTS - 1) // SLOTS)
    def _(turn):
        done = (turn * SLOTS).astype(jnp.float32)

        @pl.when(turn > 1)
        def _():
            write_left(done)
            left_copy.start()
            left_copy.wait()

        number = left_scalar_ref[SLOTS + 1, 0]

        @pl.loop(0, (number + STEP - 1) // STEP)
        def _(block):
            rows = []
            for offset in range(STEP):
                place = block * STEP + offset
                index = left_scalar_ref[SLOTS, place]
                rows.append((place, index, unit(index, left_scalar_ref, place)))
            for place, index, row in rows:
                kept = jnp.where(place < number, index, half)
                left_best_ref[pl.ds(kept, 1), :] = row

        add_scores(left_best_ref[:half], done)


def score_memory(packed, memory, q_count, slots):
    shards = len(packed)
    q_tokens = packed[0].shape[0] // q_count - 2
    _, p_count, p_tokens, depth = memory.shape
    total = shards * q_count
    vmem = pl.BlockSpec(memory_space=pltpu.VMEM)
    return pl.pallas_call(
        functools.partial(memory_kernel, shards, slots),
        in_specs=[vmem] * (shards + 1),
        out_specs=[vmem] * shards,
        out_shape=[jax.ShapeDtypeStruct((q_count, p_count), jnp.float32)] * shards,
        scratch_shapes=[
            pltpu.VMEM((2 * total, q_tokens, 2 * depth), memory.dtype),
            pltpu.VMEM((total, p_count), jnp.float32),
            pltpu.VMEM((p_count // 2, SLOTS * q_tokens), jnp.float32),
            pltpu.VMEM((p_count // 2 + 8, SLOTS * q_tokens), jnp.float32),
            pltpu.VMEM((LIST_ROWS, p_count), jnp.int32),
            pltpu.SMEM((LIST_ROWS, p_count), jnp.int32),
            pltpu.VMEM((LIST_ROWS, p_count), jnp.int32),
            pltpu.SMEM((LIST_ROWS, p_count), jnp.int32),
            pltpu.SemaphoreType.DMA((2,)),
        ],
        compiler_params=pltpu.CompilerParams(vmem_limit_bytes=16 * MIB),
        cost_estimate=pl.CostEstimate(
            flops=2 * total * q_tokens * p_count * p_tokens * depth,
            bytes_accessed=2 * p_count * p_tokens * depth,
            transcendentals=0,
        ),
        name="score_memory",
    )(*packed, memory)


def batch_kernel(query_ref, *refs):
    passage_refs, (out_ref, best_ref) = refs[:-2], refs[-2:]
    _, queries, q_tokens, depth = query_ref.shape
    count = passage_refs[0].shape[1]
    tokens = query_ref[0].reshape(queries * q_tokens, depth)
    for chip, passage_ref in enumerate(passage_refs):
        best_ref[chip * count : (chip + 1) * count, :] = token_max(passage_ref[0], tokens)
    sums = token_sum(best_ref[...], queries)
    empty = jnp.zeros((queries, out_ref.shape[1] - sums.shape[1]), jnp.float32)
    out_ref[...] = jnp.concatenate([sums, empty], axis=1) if empty.size else sums


def score_batch(queries, positives):
    _, q_count, q_tokens, depth = queries.shape
    _, p_count, p_tokens, _ = positives[0].shape
    chips = len(positives)
    lanes = -(-chips * p_count // LANES) * LANES
    return pl.pallas_call(
        batch_kernel,
        out_shape=jax.ShapeDtypeStruct((q_count, lanes), jnp.float32),
        scratch_shapes=[pltpu.VMEM((chips * p_count, q_count * q_tokens), jnp.float32)],
        compiler_params=pltpu.CompilerParams(vmem_limit_bytes=16 * MIB),
        cost_estimate=pl.CostEstimate(
            flops=2 * chips * q_count * q_tokens * p_count * p_tokens * depth,
            bytes_accessed=2 * chips * p_count * p_tokens * depth,
            transcendentals=0,
        ),
        name="score_batch",
    )(queries, *positives)


def loss_kernel(shards, own_batch, mate_batch, *refs):
    memory_refs = refs[:shards]
    candidate_ref, count_ref, batch_ref, memory_ref, loss_ref = refs[shards:]
    group, shard = lax.axis_index("group"), lax.axis_index("memory")
    chip, core = group // 2, group % 2
    _, q_count, slots = candidate_ref.shape
    p_count = memory_refs[0].shape[1]
    columns = batch_ref.shape[2]

    parts = []
    for first in range(0, columns, LANES):
        lane = lax.broadcasted_iota(jnp.int32, (q_count, LANES), 1) + first
        owner = lane // q_count
        source = (((owner // 2) ^ chip) * q_count + lane % q_count) % LANES
        own = jnp.take_along_axis(own_batch[...], source, axis=1)
        mate = jnp.take_along_axis(mate_batch[...], source, axis=1)
        parts.append(jnp.where(owner % 2 == core, own, mate))
    batch = jnp.concatenate(parts, axis=1)[:, :columns]
    batch_ref[0] = batch

    ids = candidate_ref[0]
    padded = jnp.concatenate([ids, jnp.zeros((q_count, p_count - slots), jnp.int32)], axis=1)
    holder, local = padded // p_count, padded % p_count
    picked = jnp.zeros((q_count, p_count), jnp.float32)
    for step in range(shards):
        found = jnp.take_along_axis(memory_refs[-step][...], local, axis=1)
        picked = jnp.where(holder == (shard ^ step), found, picked)

    valid = lax.broadcasted_iota(jnp.int32, (q_count, p_count), 1) < column_of(count_ref[...])
    memory_ref[0] = jnp.where(valid, picked, 0.0)[:, :slots]

    top = jnp.maximum(
        jnp.max(batch, axis=1, keepdims=True),
        jnp.max(jnp.where(valid, picked, -jnp.inf), axis=1, keepdims=True),
    )
    total = jnp.sum(jnp.exp(batch - top), axis=1, keepdims=True) + jnp.sum(
        jnp.where(valid, jnp.exp(picked - top), 0.0), axis=1, keepdims=True
    )
    column = lax.broadcasted_iota(jnp.int32, batch.shape, 1)
    own = group * q_count + lax.broadcasted_iota(jnp.int32, batch.shape, 0)
    target_score = jnp.sum(jnp.where(column == own, batch, 0.0), axis=1, keepdims=True)
    loss_ref[...] = row_of(top + jnp.log(total) - target_score)


def finish(own_batch, mate_batch, memory_parts, candidates, counts, columns):
    _, q_count, slots = candidates.shape
    return pl.pallas_call(
        functools.partial(loss_kernel, len(memory_parts)),
        out_shape=[
            jax.ShapeDtypeStruct((1, q_count, columns), jnp.float32),
            jax.ShapeDtypeStruct((1, q_count, slots), jnp.float32),
            jax.ShapeDtypeStruct((1, q_count), jnp.float32),
        ],
        compiler_params=pltpu.CompilerParams(vmem_limit_bytes=4 * MIB),
        name="finish",
    )(own_batch, mate_batch, *memory_parts, candidates, counts)


def body(queries, positives, memory, candidates, counts):
    shards = lax.axis_size("memory")
    groups = lax.axis_size("group")
    chips = groups // 2
    q_count = queries.shape[1]
    slots = candidates.shape[2] // 2

    def to_shard(array, step):
        return lax.ppermute(array, "memory", [(i, i ^ step) for i in range(shards)])

    def to_group(array, step):
        return lax.ppermute(array, "group", [(i, i ^ step) for i in range(groups)])

    own = pack(queries, candidates, counts, memory.shape[1])
    packed = [own] + [to_shard(own, step) for step in range(1, shards)]
    sent_positives, sent_queries, _ = lax.optimization_barrier((positives, queries, own))
    row = [positives] + [to_group(sent_positives, 2 * step) for step in range(1, chips)]
    mate_queries = to_group(sent_queries, 1)

    scores = score_memory(packed, memory, q_count, slots)
    returned = [to_shard(scores[step], step) for step in range(shards - 1, 0, -1)]
    mate_queries, _ = lax.optimization_barrier((mate_queries, scores[0]))
    mate_scores = score_batch(mate_queries, row)
    mate_batch = to_group(mate_scores, 1)
    own_queries, _ = lax.optimization_barrier((queries, mate_scores))
    own_batch = score_batch(own_queries, row)
    columns = groups * q_count
    return finish(
        own_batch, mate_batch, [scores[0]] + returned, candidates, counts, columns
    )


def solution(mesh):
    in_specs = (
        P("group", "memory", None, None),
        P("group", "memory", None, None),
        P("group", "memory", None, None),
        P("group", "memory", None),
        P("group", "memory"),
    )
    out_specs = (P("group", "memory", None), P("group", "memory", None), P("group", "memory"))
    return jax.shard_map(body, mesh=mesh, in_specs=in_specs, out_specs=out_specs, check_vma=False)
```

```python
import functools

import jax
import jax.numpy as jnp
from jax import lax
from jax.experimental import pallas as pl
from jax.experimental.pallas import tpu as pltpu
from jax.sharding import PartitionSpec as P

LANES = 128
MIB = 1024 * 1024
SLOTS = 8
LOW = 256
PACK_FLOPS = 10**10
PACK_BYTES = 2**24
CHUNK = 32


def in_hbm(array):
    return pltpu.with_memory_space_constraint(array, pltpu.HBM)


def token_max(passages, tokens):
    count, width, depth = passages.shape
    product = lax.dot_general(
        passages.reshape(count * width, depth),
        tokens,
        (((1,), (1,)), ((), ())),
        preferred_element_type=jnp.float32,
    )
    return jnp.max(product.reshape(count, width, tokens.shape[0]), axis=1)


def token_sum(best, queries):
    tokens = best.shape[1]
    per_query = tokens // queries
    row = lax.broadcasted_iota(jnp.int32, (queries, tokens), 0)
    col = lax.broadcasted_iota(jnp.int32, (queries, tokens), 1)
    own = (col // per_query == row).astype(jnp.bfloat16)
    high = best.astype(jnp.bfloat16)
    rest = best - high.astype(jnp.float32)
    middle = rest.astype(jnp.bfloat16)
    low = (rest - middle.astype(jnp.float32)).astype(jnp.bfloat16)
    return lax.dot_general(
        jnp.concatenate([own] * 3, axis=1),
        jnp.concatenate([high, middle, low], axis=1),
        (((1,), (1,)), ((), ())),
        preferred_element_type=jnp.float32,
    )


def column_of(row):
    size = row.shape[1]
    square = (size, size)
    diagonal = lax.broadcasted_iota(jnp.int32, square, 0) == lax.broadcasted_iota(
        jnp.int32, square, 1
    )
    return jnp.sum(jnp.where(diagonal, jnp.broadcast_to(row, square), 0), axis=1, keepdims=True)


def row_of(column):
    size = column.shape[0]
    square = (size, size)
    diagonal = lax.broadcasted_iota(jnp.int32, square, 0) == lax.broadcasted_iota(
        jnp.int32, square, 1
    )
    return jnp.sum(jnp.where(diagonal, jnp.broadcast_to(column, square), 0), axis=0, keepdims=True)


def split_ids(p_count, candidate_ref, count_ref):
    ids = candidate_ref[0]
    row = lax.broadcasted_iota(jnp.int32, ids.shape, 0)
    valid_count = jnp.zeros(ids.shape, jnp.int32)
    for index in range(ids.shape[0]):
        valid_count = jnp.where(row == index, count_ref[0, index], valid_count)
    valid = lax.broadcasted_iota(jnp.int32, ids.shape, 1) < valid_count
    holder = jnp.where(valid, ids // p_count, -1)
    return (ids % p_count).astype(jnp.float32), holder.astype(jnp.float32)


def pack_kernel(p_count, query_ref, candidate_ref, count_ref, out_ref):
    _, q_count, slots = candidate_ref.shape
    _, _, q_tokens, depth = query_ref.shape
    tokens = q_count * q_tokens
    out_ref[:tokens] = query_ref[0].reshape(tokens, depth)
    planes = jnp.concatenate(split_ids(p_count, candidate_ref, count_ref), axis=0)
    empty = jnp.zeros((2 * q_count, depth - slots), jnp.float32)
    out_ref[tokens:] = jnp.concatenate([planes, empty], axis=1).astype(out_ref.dtype)


def pack(queries, candidates, counts, p_count):
    _, q_count, q_tokens, depth = queries.shape
    vmem = pl.BlockSpec(memory_space=pltpu.VMEM)
    return pl.pallas_call(
        functools.partial(pack_kernel, p_count),
        in_specs=[vmem, vmem, pl.BlockSpec(memory_space=pltpu.SMEM)],
        out_shape=jax.ShapeDtypeStruct((q_count * (q_tokens + 2), depth), queries.dtype),
        compiler_params=pltpu.CompilerParams(vmem_limit_bytes=4 * MIB),
        cost_estimate=pl.CostEstimate(
            flops=PACK_FLOPS, bytes_accessed=PACK_BYTES, transcendentals=0
        ),
        name="pack",
    )(in_hbm(queries), in_hbm(candidates), in_hbm(counts))


def memory_kernel(shards, slots, *refs):
    packed_refs, passage_ref = refs[shards - 1 :: -1], refs[shards].at[0]
    pairs = shards // 2
    pair_refs = refs[shards + pairs : shards : -1]
    query_ref, rank_ref, best_ref, list_ref, scalar_ref, list_sem = refs[shards + 1 + pairs :]
    out_refs = [pair_ref.at[index] for pair_ref in pair_refs for index in range(2)]
    q_count = pair_refs[0].shape[1]
    p_count = passage_ref.shape[0]
    total, q_tokens, depth = query_ref.shape
    chunks = p_count // CHUNK

    me = lax.axis_index("memory").astype(jnp.float32)
    keys = []
    for index, packed_ref in enumerate(packed_refs):
        tokens = packed_ref[: q_count * q_tokens].reshape(q_count, q_tokens, depth)
        query_ref[index * q_count : (index + 1) * q_count] = tokens
        planes = packed_ref[q_count * q_tokens :].astype(jnp.float32)
        local, holder = planes[:q_count], planes[q_count:]
        keys.append(jnp.where(holder == me, local, -1.0))
    keys = jnp.concatenate(keys, axis=0)
    passage = lax.broadcasted_iota(jnp.int32, (total, p_count), 1).astype(jnp.float32)
    named = jnp.zeros((total, p_count), jnp.float32)
    for slot in range(slots):
        named = jnp.where(keys[:, slot : slot + 1] == passage, 1.0, named)

    square = (total, total)
    earlier = lax.broadcasted_iota(jnp.int32, square, 1) < lax.broadcasted_iota(
        jnp.int32, square, 0
    )
    before = jnp.dot(earlier.astype(jnp.float32), named, preferred_element_type=jnp.float32)
    rank_ref[...] = jnp.where(named > 0.0, before, -1.0)
    counts = jnp.sum(named, axis=0, keepdims=True)
    most = jnp.broadcast_to(jnp.max(counts, axis=1, keepdims=True), counts.shape)

    def left_over(first):
        left = jnp.where(rank_ref[...] == first, 1.0, 0.0)
        left = jnp.sum(left, axis=0, keepdims=True)
        square = (p_count, p_count)
        row = lax.broadcasted_iota(jnp.int32, square, 0).astype(jnp.float32)
        column = lax.broadcasted_iota(jnp.int32, square, 1).astype(jnp.float32)
        place = jnp.dot(left, (row < column).astype(jnp.float32), preferred_element_type=jnp.float32)
        mine = jnp.where((place == row) & (left > 0.0), column, 0.0)
        index = jnp.sum(mine, axis=1, keepdims=True)
        index = jnp.sum(jnp.where(row == column, index, 0.0), axis=0, keepdims=True)
        return [index, jnp.broadcast_to(jnp.sum(left, axis=1, keepdims=True), left.shape)]

    def write_list(first, extra):
        asker = lax.broadcasted_iota(jnp.int32, (total, p_count), 0).astype(jnp.float32)
        rank = rank_ref[...] - first
        rows = [
            jnp.sum(jnp.where(rank == float(slot), asker, 0.0), axis=0, keepdims=True)
            for slot in range(SLOTS)
        ]
        for slot, above in enumerate(extra):
            rows[slot] = rows[slot] + LOW * above
        list_ref[...] = jnp.concatenate(rows, axis=0).astype(jnp.int32)
        copy = pltpu.make_async_copy(list_ref, scalar_ref, list_sem)
        copy.start()
        copy.wait()

    def unit(index):
        tokens = [query_ref[scalar_ref[slot, index] & (LOW - 1)] for slot in range(SLOTS)]
        return token_max(passage_ref[pl.ds(index, 1)], jnp.concatenate(tokens, axis=0))

    def add_scores(first, scores):
        sums = token_sum(best_ref[...], SLOTS)
        for index, out_ref in enumerate(out_refs):
            rank = rank_ref[index * q_count : (index + 1) * q_count] - first
            total_scores = scores[index]
            for slot in range(SLOTS):
                total_scores = jnp.where(rank == float(slot), sums[slot : slot + 1], total_scores)
            out_ref[...] = total_scores

    write_list(0.0, [most])
    rounds = (scalar_ref[0, 0] // LOW + SLOTS - 1) // SLOTS

    @pl.loop(0, chunks)
    def _(chunk):
        for start in range(0, CHUNK, 8):
            first = pl.multiple_of(chunk * CHUNK + start, 8)
            rows = [unit(first + offset) for offset in range(8)]
            best_ref[pl.ds(first, 8), :] = jnp.concatenate(rows, axis=0)

    add_scores(0.0, [jnp.zeros((q_count, p_count), jnp.float32)] * shards)

    @pl.loop(1, rounds)
    def _(turn):
        done = (turn * SLOTS).astype(jnp.float32)
        write_list(done, left_over(done))

        @pl.loop(0, scalar_ref[1, 0] // LOW)
        def _(place):
            index = scalar_ref[0, place] // LOW
            best_ref[pl.ds(index, 1), :] = unit(index)

        add_scores(done, [out_ref[...] for out_ref in out_refs])


def score_memory(packed, memory, q_count, slots):
    shards = len(packed)
    q_tokens = packed[0].shape[0] // q_count - 2
    _, p_count, p_tokens, depth = memory.shape
    total = shards * q_count
    vmem = pl.BlockSpec(memory_space=pltpu.VMEM)
    return pl.pallas_call(
        functools.partial(memory_kernel, shards, slots),
        in_specs=[vmem] * (shards + 1),
        out_specs=[vmem] * (shards // 2),
        out_shape=[jax.ShapeDtypeStruct((2, q_count, p_count), jnp.float32)] * (shards // 2),
        scratch_shapes=[
            pltpu.VMEM((total, q_tokens, depth), memory.dtype),
            pltpu.VMEM((total, p_count), jnp.float32),
            pltpu.VMEM((p_count, SLOTS * q_tokens), jnp.float32),
            pltpu.VMEM((SLOTS, p_count), jnp.int32),
            pltpu.SMEM((SLOTS, p_count), jnp.int32),
            pltpu.SemaphoreType.DMA,
        ],
        compiler_params=pltpu.CompilerParams(vmem_limit_bytes=16 * MIB),
        cost_estimate=pl.CostEstimate(
            flops=2 * total * q_tokens * p_count * p_tokens * depth,
            bytes_accessed=2 * p_count * p_tokens * depth,
            transcendentals=0,
        ),
        name="score_memory",
    )(*packed, memory)


def batch_kernel(query_ref, *refs):
    passage_refs, (out_ref, best_ref) = refs[:-2], refs[-2:]
    _, queries, q_tokens, depth = query_ref.shape
    count = passage_refs[0].shape[1]
    tokens = query_ref[0].reshape(queries * q_tokens, depth)
    for chip, passage_ref in enumerate(passage_refs):
        best_ref[chip * count : (chip + 1) * count, :] = token_max(passage_ref[0], tokens)
    sums = token_sum(best_ref[...], queries)
    empty = jnp.zeros((queries, out_ref.shape[1] - sums.shape[1]), jnp.float32)
    out_ref[...] = jnp.concatenate([sums, empty], axis=1) if empty.size else sums


def score_batch(queries, positives):
    _, q_count, q_tokens, depth = queries.shape
    _, p_count, p_tokens, _ = positives[0].shape
    chips = len(positives)
    lanes = -(-chips * p_count // LANES) * LANES
    return pl.pallas_call(
        batch_kernel,
        out_shape=jax.ShapeDtypeStruct((q_count, lanes), jnp.float32),
        scratch_shapes=[pltpu.VMEM((chips * p_count, q_count * q_tokens), jnp.float32)],
        compiler_params=pltpu.CompilerParams(vmem_limit_bytes=16 * MIB),
        cost_estimate=pl.CostEstimate(
            flops=2 * chips * q_count * q_tokens * p_count * p_tokens * depth,
            bytes_accessed=2 * chips * p_count * p_tokens * depth,
            transcendentals=0,
        ),
        name="score_batch",
    )(queries, *positives)


def loss_kernel(shards, own_batch, mate_batch, *refs):
    pairs = shards // 2 - 1
    far_refs, near_refs, hop_refs = refs[:pairs], refs[pairs : pairs + 2], refs[pairs + 2 : shards]
    candidate_ref, count_ref, batch_ref, memory_ref, loss_ref = refs[shards:]
    memory_refs = [near_refs[0].at[0], near_refs[1].at[1]]
    for far_ref, hop_ref in zip(far_refs, hop_refs):
        memory_refs += [far_ref.at[0], hop_ref.at[1]]
    group, shard = lax.axis_index("group"), lax.axis_index("memory")
    chip, core = group // 2, group % 2
    _, q_count, slots = candidate_ref.shape
    p_count = memory_refs[0].shape[1]
    columns = batch_ref.shape[2]

    parts = []
    for first in range(0, columns, LANES):
        lane = lax.broadcasted_iota(jnp.int32, (q_count, LANES), 1) + first
        owner = lane // q_count
        source = (((owner // 2) ^ chip) * q_count + lane % q_count) % LANES
        own = jnp.take_along_axis(own_batch[...], source, axis=1)
        mate = jnp.take_along_axis(mate_batch[...], source, axis=1)
        parts.append(jnp.where(owner % 2 == core, own, mate))
    batch = jnp.concatenate(parts, axis=1)[:, :columns]
    batch_ref[0] = batch

    ids = candidate_ref[0]
    padded = jnp.concatenate([ids, jnp.zeros((q_count, p_count - slots), jnp.int32)], axis=1)
    holder, local = padded // p_count, padded % p_count
    picked = jnp.zeros((q_count, p_count), jnp.float32)
    for step in range(shards):
        found = jnp.take_along_axis(memory_refs[step][...], local, axis=1)
        picked = jnp.where(holder == (shard ^ step), found, picked)

    valid = lax.broadcasted_iota(jnp.int32, (q_count, p_count), 1) < column_of(count_ref[...])
    memory_ref[0] = jnp.where(valid, picked, 0.0)[:, :slots]

    top = jnp.maximum(
        jnp.max(batch, axis=1, keepdims=True),
        jnp.max(jnp.where(valid, picked, -jnp.inf), axis=1, keepdims=True),
    )
    total = jnp.sum(jnp.exp(batch - top), axis=1, keepdims=True) + jnp.sum(
        jnp.where(valid, jnp.exp(picked - top), 0.0), axis=1, keepdims=True
    )
    column = lax.broadcasted_iota(jnp.int32, batch.shape, 1)
    own = group * q_count + lax.broadcasted_iota(jnp.int32, batch.shape, 0)
    target_score = jnp.sum(jnp.where(column == own, batch, 0.0), axis=1, keepdims=True)
    loss_ref[...] = row_of(top + jnp.log(total) - target_score)


def finish(own_batch, mate_batch, memory_parts, candidates, counts, columns):
    _, q_count, slots = candidates.shape
    return pl.pallas_call(
        functools.partial(loss_kernel, len(memory_parts)),
        out_shape=[
            jax.ShapeDtypeStruct((1, q_count, columns), jnp.float32),
            jax.ShapeDtypeStruct((1, q_count, slots), jnp.float32),
            jax.ShapeDtypeStruct((1, q_count), jnp.float32),
        ],
        compiler_params=pltpu.CompilerParams(vmem_limit_bytes=4 * MIB),
        name="finish",
    )(own_batch, mate_batch, *memory_parts, candidates, counts)


def body(queries, positives, memory, candidates, counts):
    shards = lax.axis_size("memory")
    groups = lax.axis_size("group")
    chips = groups // 2
    q_count = queries.shape[1]
    slots = candidates.shape[2] // 2

    def to_shard(array, step):
        return lax.ppermute(array, "memory", [(i, i ^ step) for i in range(shards)])

    def to_group(array, step):
        return lax.ppermute(array, "group", [(i, i ^ step) for i in range(groups)])

    own = pack(queries, candidates, counts, memory.shape[1])
    packed = [to_shard(own, step) for step in range(shards - 1, 0, -1)] + [own]
    sent_positives, sent_queries, _ = lax.optimization_barrier((positives, queries, own))
    row = [positives] + [to_group(sent_positives, 2 * step) for step in range(1, chips)]
    mate_queries = to_group(sent_queries, 1)

    near, *pairs = score_memory(packed, memory, q_count, slots)[::-1]
    far = [to_shard(pair, 2 * index) for index, pair in enumerate(pairs, start=1)]
    near = [near, to_shard(near, 1)]
    hops = [to_shard(pair, 1) for pair in far]
    mate_queries, _ = lax.optimization_barrier((mate_queries, far))
    mate_scores = score_batch(mate_queries, row)
    mate_batch = to_group(mate_scores, 1)
    own_queries, _ = lax.optimization_barrier((queries, mate_scores))
    own_batch = score_batch(own_queries, row)
    columns = groups * q_count
    parts = far + near + hops
    return finish(own_batch, mate_batch, parts, candidates, counts, columns)


def solution(mesh):
    in_specs = (
        P("group", "memory", None, None),
        P("group", "memory", None, None),
        P("group", "memory", None, None),
        P("group", "memory", None),
        P("group", "memory"),
    )
    out_specs = (P("group", "memory", None), P("group", "memory", None), P("group", "memory"))
    return jax.shard_map(body, mesh=mesh, in_specs=in_specs, out_specs=out_specs, check_vma=False)
```

```python
import functools

import jax
import jax.numpy as jnp
from jax import lax
from jax.experimental import pallas as pl
from jax.experimental.pallas import tpu as pltpu
from jax.sharding import PartitionSpec as P

LANES = 128
MIB = 1024 * 1024
SLOTS = 8
LOW = 256
PACK_FLOPS = 10**10
PACK_BYTES = 2**24
CHUNK = 32


def send_order(count):
    return [0, 1] + list(range(count - 1, 1, -1))


def in_hbm(array):
    return pltpu.with_memory_space_constraint(array, pltpu.HBM)


def token_max(passages, tokens):
    count, width, depth = passages.shape
    product = lax.dot_general(
        passages.reshape(count * width, depth),
        tokens,
        (((1,), (1,)), ((), ())),
        preferred_element_type=jnp.float32,
    )
    return jnp.max(product.reshape(count, width, tokens.shape[0]), axis=1)


def token_sum(best, queries):
    tokens = best.shape[1]
    per_query = tokens // queries
    row = lax.broadcasted_iota(jnp.int32, (queries, tokens), 0)
    col = lax.broadcasted_iota(jnp.int32, (queries, tokens), 1)
    own = (col // per_query == row).astype(jnp.bfloat16)
    high = best.astype(jnp.bfloat16)
    rest = best - high.astype(jnp.float32)
    middle = rest.astype(jnp.bfloat16)
    low = (rest - middle.astype(jnp.float32)).astype(jnp.bfloat16)
    return lax.dot_general(
        jnp.concatenate([own] * 3, axis=1),
        jnp.concatenate([high, middle, low], axis=1),
        (((1,), (1,)), ((), ())),
        preferred_element_type=jnp.float32,
    )


def column_of(row):
    size = row.shape[1]
    square = (size, size)
    diagonal = lax.broadcasted_iota(jnp.int32, square, 0) == lax.broadcasted_iota(
        jnp.int32, square, 1
    )
    return jnp.sum(jnp.where(diagonal, jnp.broadcast_to(row, square), 0), axis=1, keepdims=True)


def row_of(column):
    size = column.shape[0]
    square = (size, size)
    diagonal = lax.broadcasted_iota(jnp.int32, square, 0) == lax.broadcasted_iota(
        jnp.int32, square, 1
    )
    return jnp.sum(jnp.where(diagonal, jnp.broadcast_to(column, square), 0), axis=0, keepdims=True)


def split_ids(p_count, candidate_ref, count_ref):
    ids = candidate_ref[0]
    row = lax.broadcasted_iota(jnp.int32, ids.shape, 0)
    valid_count = jnp.zeros(ids.shape, jnp.int32)
    for index in range(ids.shape[0]):
        valid_count = jnp.where(row == index, count_ref[0, index], valid_count)
    valid = lax.broadcasted_iota(jnp.int32, ids.shape, 1) < valid_count
    holder = jnp.where(valid, ids // p_count, -1)
    return (ids % p_count).astype(jnp.float32), holder.astype(jnp.float32)


def pack_kernel(p_count, query_ref, candidate_ref, count_ref, out_ref):
    _, q_count, slots = candidate_ref.shape
    _, _, q_tokens, depth = query_ref.shape
    tokens = q_count * q_tokens
    out_ref[:tokens] = query_ref[0].reshape(tokens, depth)
    planes = jnp.concatenate(split_ids(p_count, candidate_ref, count_ref), axis=0)
    empty = jnp.zeros((2 * q_count, depth - slots), jnp.float32)
    out_ref[tokens:] = jnp.concatenate([planes, empty], axis=1).astype(out_ref.dtype)


def pack(queries, candidates, counts, p_count):
    _, q_count, q_tokens, depth = queries.shape
    vmem = pl.BlockSpec(memory_space=pltpu.VMEM)
    return pl.pallas_call(
        functools.partial(pack_kernel, p_count),
        in_specs=[vmem, vmem, pl.BlockSpec(memory_space=pltpu.SMEM)],
        out_shape=jax.ShapeDtypeStruct((q_count * (q_tokens + 2), depth), queries.dtype),
        compiler_params=pltpu.CompilerParams(vmem_limit_bytes=4 * MIB),
        cost_estimate=pl.CostEstimate(
            flops=PACK_FLOPS, bytes_accessed=PACK_BYTES, transcendentals=0
        ),
        name="pack",
    )(in_hbm(queries), in_hbm(candidates), in_hbm(counts))


def memory_kernel(shards, slots, *refs):
    passage_ref = refs[shards].at[0]
    packed_refs = [None] * shards
    for step, packed_ref in zip(send_order(shards), refs):
        packed_refs[step] = packed_ref
    out_refs = refs[shards + 1 : 2 * shards + 1]
    query_ref, rank_ref, best_ref, list_ref, scalar_ref, list_sem = refs[2 * shards + 1 :]
    q_count = out_refs[0].shape[0]
    p_count = passage_ref.shape[0]
    total, q_tokens, depth = query_ref.shape
    chunks = p_count // CHUNK

    me = lax.axis_index("memory").astype(jnp.float32)
    keys = []
    for index, packed_ref in enumerate(packed_refs):
        tokens = packed_ref[: q_count * q_tokens].reshape(q_count, q_tokens, depth)
        query_ref[index * q_count : (index + 1) * q_count] = tokens
        planes = packed_ref[q_count * q_tokens :].astype(jnp.float32)
        local, holder = planes[:q_count], planes[q_count:]
        keys.append(jnp.where(holder == me, local, -1.0))
    keys = jnp.concatenate(keys, axis=0)
    passage = lax.broadcasted_iota(jnp.int32, (total, p_count), 1).astype(jnp.float32)
    named = jnp.zeros((total, p_count), jnp.float32)
    for slot in range(slots):
        named = jnp.where(keys[:, slot : slot + 1] == passage, 1.0, named)

    square = (total, total)
    earlier = lax.broadcasted_iota(jnp.int32, square, 1) < lax.broadcasted_iota(
        jnp.int32, square, 0
    )
    before = jnp.dot(earlier.astype(jnp.float32), named, preferred_element_type=jnp.float32)
    rank_ref[...] = jnp.where(named > 0.0, before, -1.0)
    counts = jnp.sum(named, axis=0, keepdims=True)
    most = jnp.broadcast_to(jnp.max(counts, axis=1, keepdims=True), counts.shape)

    def left_over(first):
        left = jnp.where(rank_ref[...] == first, 1.0, 0.0)
        left = jnp.sum(left, axis=0, keepdims=True)
        square = (p_count, p_count)
        row = lax.broadcasted_iota(jnp.int32, square, 0).astype(jnp.float32)
        column = lax.broadcasted_iota(jnp.int32, square, 1).astype(jnp.float32)
        place = jnp.dot(left, (row < column).astype(jnp.float32), preferred_element_type=jnp.float32)
        mine = jnp.where((place == row) & (left > 0.0), column, 0.0)
        index = jnp.sum(mine, axis=1, keepdims=True)
        index = jnp.sum(jnp.where(row == column, index, 0.0), axis=0, keepdims=True)
        return [index, jnp.broadcast_to(jnp.sum(left, axis=1, keepdims=True), left.shape)]

    def write_list(first, extra):
        asker = lax.broadcasted_iota(jnp.int32, (total, p_count), 0).astype(jnp.float32)
        rank = rank_ref[...] - first
        rows = [
            jnp.sum(jnp.where(rank == float(slot), asker, 0.0), axis=0, keepdims=True)
            for slot in range(SLOTS)
        ]
        for slot, above in enumerate(extra):
            rows[slot] = rows[slot] + LOW * above
        list_ref[...] = jnp.concatenate(rows, axis=0).astype(jnp.int32)
        copy = pltpu.make_async_copy(list_ref, scalar_ref, list_sem)
        copy.start()
        copy.wait()

    def unit(index):
        tokens = [query_ref[scalar_ref[slot, index] & (LOW - 1)] for slot in range(SLOTS)]
        return token_max(passage_ref[pl.ds(index, 1)], jnp.concatenate(tokens, axis=0))

    def add_scores(first, scores):
        sums = token_sum(best_ref[...], SLOTS)
        for index, out_ref in enumerate(out_refs):
            rank = rank_ref[index * q_count : (index + 1) * q_count] - first
            total_scores = scores[index]
            for slot in range(SLOTS):
                total_scores = jnp.where(rank == float(slot), sums[slot : slot + 1], total_scores)
            out_ref[...] = total_scores

    write_list(0.0, [most])
    rounds = (scalar_ref[0, 0] // LOW + SLOTS - 1) // SLOTS

    @pl.loop(0, chunks)
    def _(chunk):
        for start in range(0, CHUNK, 8):
            first = pl.multiple_of(chunk * CHUNK + start, 8)
            rows = [unit(first + offset) for offset in range(8)]
            best_ref[pl.ds(first, 8), :] = jnp.concatenate(rows, axis=0)

    add_scores(0.0, [jnp.zeros((q_count, p_count), jnp.float32)] * shards)

    @pl.loop(1, rounds)
    def _(turn):
        done = (turn * SLOTS).astype(jnp.float32)
        write_list(done, left_over(done))

        @pl.loop(0, scalar_ref[1, 0] // LOW)
        def _(place):
            index = scalar_ref[0, place] // LOW
            best_ref[pl.ds(index, 1), :] = unit(index)

        add_scores(done, [out_ref[...] for out_ref in out_refs])


def score_memory(packed, memory, q_count, slots):
    shards = len(packed)
    q_tokens = packed[0].shape[0] // q_count - 2
    _, p_count, p_tokens, depth = memory.shape
    total = shards * q_count
    vmem = pl.BlockSpec(memory_space=pltpu.VMEM)
    return pl.pallas_call(
        functools.partial(memory_kernel, shards, slots),
        in_specs=[vmem] * (shards + 1),
        out_specs=[vmem] * shards,
        out_shape=[jax.ShapeDtypeStruct((q_count, p_count), jnp.float32)] * shards,
        scratch_shapes=[
            pltpu.VMEM((total, q_tokens, depth), memory.dtype),
            pltpu.VMEM((total, p_count), jnp.float32),
            pltpu.VMEM((p_count, SLOTS * q_tokens), jnp.float32),
            pltpu.VMEM((SLOTS, p_count), jnp.int32),
            pltpu.SMEM((SLOTS, p_count), jnp.int32),
            pltpu.SemaphoreType.DMA,
        ],
        compiler_params=pltpu.CompilerParams(vmem_limit_bytes=16 * MIB),
        cost_estimate=pl.CostEstimate(
            flops=2 * total * q_tokens * p_count * p_tokens * depth,
            bytes_accessed=2 * p_count * p_tokens * depth,
            transcendentals=0,
        ),
        name="score_memory",
    )(*packed, memory)


def batch_kernel(query_ref, *refs):
    passage_refs, (out_ref, best_ref) = refs[:-2], refs[-2:]
    _, queries, q_tokens, depth = query_ref.shape
    count = passage_refs[0].shape[1]
    tokens = query_ref[0].reshape(queries * q_tokens, depth)
    for chip, passage_ref in zip(send_order(len(passage_refs)), passage_refs):
        best_ref[chip * count : (chip + 1) * count, :] = token_max(passage_ref[0], tokens)
    sums = token_sum(best_ref[...], queries)
    empty = jnp.zeros((queries, out_ref.shape[1] - sums.shape[1]), jnp.float32)
    out_ref[...] = jnp.concatenate([sums, empty], axis=1) if empty.size else sums


def score_batch(queries, positives):
    _, q_count, q_tokens, depth = queries.shape
    _, p_count, p_tokens, _ = positives[0].shape
    chips = len(positives)
    lanes = -(-chips * p_count // LANES) * LANES
    return pl.pallas_call(
        batch_kernel,
        out_shape=jax.ShapeDtypeStruct((q_count, lanes), jnp.float32),
        scratch_shapes=[pltpu.VMEM((chips * p_count, q_count * q_tokens), jnp.float32)],
        compiler_params=pltpu.CompilerParams(vmem_limit_bytes=16 * MIB),
        cost_estimate=pl.CostEstimate(
            flops=2 * chips * q_count * q_tokens * p_count * p_tokens * depth,
            bytes_accessed=2 * chips * p_count * p_tokens * depth,
            transcendentals=0,
        ),
        name="score_batch",
    )(queries, *positives)


def loss_kernel(shards, own_batch, mate_batch, *refs):
    memory_refs = refs[:shards]
    candidate_ref, count_ref, batch_ref, memory_ref, loss_ref = refs[shards:]
    group, shard = lax.axis_index("group"), lax.axis_index("memory")
    chip, core = group // 2, group % 2
    _, q_count, slots = candidate_ref.shape
    p_count = memory_refs[0].shape[1]
    columns = batch_ref.shape[2]

    parts = []
    for first in range(0, columns, LANES):
        lane = lax.broadcasted_iota(jnp.int32, (q_count, LANES), 1) + first
        owner = lane // q_count
        source = (((owner // 2) ^ chip) * q_count + lane % q_count) % LANES
        own = jnp.take_along_axis(own_batch[...], source, axis=1)
        mate = jnp.take_along_axis(mate_batch[...], source, axis=1)
        parts.append(jnp.where(owner % 2 == core, own, mate))
    batch = jnp.concatenate(parts, axis=1)[:, :columns]
    batch_ref[0] = batch

    ids = candidate_ref[0]
    padded = jnp.concatenate([ids, jnp.zeros((q_count, p_count - slots), jnp.int32)], axis=1)
    holder, local = padded // p_count, padded % p_count
    picked = jnp.zeros((q_count, p_count), jnp.float32)
    for step in range(shards):
        found = jnp.take_along_axis(memory_refs[-step][...], local, axis=1)
        picked = jnp.where(holder == (shard ^ step), found, picked)

    valid = lax.broadcasted_iota(jnp.int32, (q_count, p_count), 1) < column_of(count_ref[...])
    memory_ref[0] = jnp.where(valid, picked, 0.0)[:, :slots]

    top = jnp.maximum(
        jnp.max(batch, axis=1, keepdims=True),
        jnp.max(jnp.where(valid, picked, -jnp.inf), axis=1, keepdims=True),
    )
    total = jnp.sum(jnp.exp(batch - top), axis=1, keepdims=True) + jnp.sum(
        jnp.where(valid, jnp.exp(picked - top), 0.0), axis=1, keepdims=True
    )
    column = lax.broadcasted_iota(jnp.int32, batch.shape, 1)
    own = group * q_count + lax.broadcasted_iota(jnp.int32, batch.shape, 0)
    target_score = jnp.sum(jnp.where(column == own, batch, 0.0), axis=1, keepdims=True)
    loss_ref[...] = row_of(top + jnp.log(total) - target_score)


def finish(own_batch, mate_batch, memory_parts, candidates, counts, columns):
    _, q_count, slots = candidates.shape
    return pl.pallas_call(
        functools.partial(loss_kernel, len(memory_parts)),
        out_shape=[
            jax.ShapeDtypeStruct((1, q_count, columns), jnp.float32),
            jax.ShapeDtypeStruct((1, q_count, slots), jnp.float32),
            jax.ShapeDtypeStruct((1, q_count), jnp.float32),
        ],
        compiler_params=pltpu.CompilerParams(vmem_limit_bytes=4 * MIB),
        name="finish",
    )(own_batch, mate_batch, *memory_parts, candidates, counts)


def body(queries, positives, memory, candidates, counts):
    shards = lax.axis_size("memory")
    groups = lax.axis_size("group")
    chips = groups // 2
    q_count = queries.shape[1]
    slots = candidates.shape[2] // 2

    def to_shard(array, step):
        return lax.ppermute(array, "memory", [(i, i ^ step) for i in range(shards)])

    def to_group(array, step):
        return lax.ppermute(array, "group", [(i, i ^ step) for i in range(groups)])

    own = pack(queries, candidates, counts, memory.shape[1])
    packed = [to_shard(own, step) if step else own for step in send_order(shards)]
    sent_positives, sent_queries, _ = lax.optimization_barrier((positives, queries, own))
    row = [
        to_group(sent_positives, 2 * step) if step else positives for step in send_order(chips)
    ]
    mate_queries = to_group(sent_queries, 1)

    scores = score_memory(packed, memory, q_count, slots)
    returned = [to_shard(scores[step], step) for step in range(shards - 1, 0, -1)]
    mate_queries, _ = lax.optimization_barrier((mate_queries, scores[0]))
    mate_scores = score_batch(mate_queries, row)
    mate_batch = to_group(mate_scores, 1)
    own_queries, _ = lax.optimization_barrier((queries, mate_scores))
    own_batch = score_batch(own_queries, row)
    columns = groups * q_count
    return finish(
        own_batch, mate_batch, [scores[0]] + returned, candidates, counts, columns
    )


def solution(mesh):
    in_specs = (
        P("group", "memory", None, None),
        P("group", "memory", None, None),
        P("group", "memory", None, None),
        P("group", "memory", None),
        P("group", "memory"),
    )
    out_specs = (P("group", "memory", None), P("group", "memory", None), P("group", "memory"))
    return jax.shard_map(body, mesh=mesh, in_specs=in_specs, out_specs=out_specs, check_vma=False)
```

```python
import functools

import jax
import jax.numpy as jnp
from jax import lax
from jax.experimental import pallas as pl
from jax.experimental.pallas import tpu as pltpu
from jax.sharding import PartitionSpec as P

LANES = 128
MIB = 1024 * 1024
SLOTS = 4
CHUNK = 32
LIST_ROWS = 8
STEP = 16
PACK_FLOPS = 10**10
PACK_BYTES = 2**24


def in_hbm(array):
    return pltpu.with_memory_space_constraint(array, pltpu.HBM)


def token_max(passages, tokens):
    count, width, depth = passages.shape
    product = lax.dot_general(
        passages.reshape(count * width, depth),
        tokens,
        (((1,), (1,)), ((), ())),
        preferred_element_type=jnp.float32,
    )
    return jnp.max(product.reshape(count, width, tokens.shape[0]), axis=1)


def token_sum(best, queries):
    tokens = best.shape[1]
    per_query = tokens // queries
    row = lax.broadcasted_iota(jnp.int32, (queries, tokens), 0)
    col = lax.broadcasted_iota(jnp.int32, (queries, tokens), 1)
    own = (col // per_query == row).astype(jnp.bfloat16)
    high = best.astype(jnp.bfloat16)
    rest = best - high.astype(jnp.float32)
    middle = rest.astype(jnp.bfloat16)
    low = (rest - middle.astype(jnp.float32)).astype(jnp.bfloat16)
    return lax.dot_general(
        jnp.concatenate([own] * 3, axis=1),
        jnp.concatenate([high, middle, low], axis=1),
        (((1,), (1,)), ((), ())),
        preferred_element_type=jnp.float32,
    )


def column_of(row):
    size = row.shape[1]
    square = (size, size)
    diagonal = lax.broadcasted_iota(jnp.int32, square, 0) == lax.broadcasted_iota(
        jnp.int32, square, 1
    )
    return jnp.sum(jnp.where(diagonal, jnp.broadcast_to(row, square), 0), axis=1, keepdims=True)


def row_of(column):
    size = column.shape[0]
    square = (size, size)
    diagonal = lax.broadcasted_iota(jnp.int32, square, 0) == lax.broadcasted_iota(
        jnp.int32, square, 1
    )
    return jnp.sum(jnp.where(diagonal, jnp.broadcast_to(column, square), 0), axis=0, keepdims=True)


def split_ids(p_count, candidate_ref, count_ref):
    ids = candidate_ref[0]
    row = lax.broadcasted_iota(jnp.int32, ids.shape, 0)
    valid_count = jnp.zeros(ids.shape, jnp.int32)
    for index in range(ids.shape[0]):
        valid_count = jnp.where(row == index, count_ref[0, index], valid_count)
    valid = lax.broadcasted_iota(jnp.int32, ids.shape, 1) < valid_count
    holder = jnp.where(valid, ids // p_count, -1)
    return (ids % p_count).astype(jnp.float32), holder.astype(jnp.float32)


def pack_kernel(p_count, query_ref, candidate_ref, count_ref, out_ref):
    _, q_count, slots = candidate_ref.shape
    _, _, q_tokens, depth = query_ref.shape
    tokens = q_count * q_tokens
    out_ref[:tokens] = query_ref[0].reshape(tokens, depth)
    planes = jnp.concatenate(split_ids(p_count, candidate_ref, count_ref), axis=0)
    empty = jnp.zeros((2 * q_count, depth - slots), jnp.float32)
    out_ref[tokens:] = jnp.concatenate([planes, empty], axis=1).astype(out_ref.dtype)


def pack(queries, candidates, counts, p_count):
    _, q_count, q_tokens, depth = queries.shape
    vmem = pl.BlockSpec(memory_space=pltpu.VMEM)
    return pl.pallas_call(
        functools.partial(pack_kernel, p_count),
        in_specs=[vmem, vmem, pl.BlockSpec(memory_space=pltpu.SMEM)],
        out_shape=jax.ShapeDtypeStruct((q_count * (q_tokens + 2), depth), queries.dtype),
        compiler_params=pltpu.CompilerParams(vmem_limit_bytes=4 * MIB),
        cost_estimate=pl.CostEstimate(
            flops=PACK_FLOPS, bytes_accessed=PACK_BYTES, transcendentals=0
        ),
        name="pack",
    )(in_hbm(queries), in_hbm(candidates), in_hbm(counts))


def memory_kernel(shards, slots, *refs):
    packed_refs, passage_ref = refs[:shards], refs[shards].at[0]
    out_refs = refs[shards + 1 : 2 * shards + 1]
    query_ref, rank_ref, best_ref, left_best_ref, *refs = refs[2 * shards + 1 :]
    list_ref, scalar_ref, left_ref, left_scalar_ref, list_sems = refs
    q_count = out_refs[0].shape[0]
    p_count = passage_ref.shape[0]
    total, q_tokens, depth = query_ref.shape
    chunks = p_count // CHUNK

    me = lax.axis_index("memory").astype(jnp.float32)
    keys = []
    for index, packed_ref in enumerate(packed_refs):
        tokens = packed_ref[: q_count * q_tokens].reshape(q_count, q_tokens, depth)
        query_ref[index * q_count : (index + 1) * q_count] = tokens
        planes = packed_ref[q_count * q_tokens :].astype(jnp.float32)
        local, holder = planes[:q_count], planes[q_count:]
        keys.append(jnp.where(holder == me, local, -1.0))
    keys = jnp.concatenate(keys, axis=0)
    passage = lax.broadcasted_iota(jnp.int32, (total, p_count), 1).astype(jnp.float32)
    named = jnp.zeros((total, p_count), jnp.float32)
    for slot in range(slots):
        named = jnp.where(keys[:, slot : slot + 1] == passage, 1.0, named)

    square = (total, total)
    earlier = lax.broadcasted_iota(jnp.int32, square, 1) < lax.broadcasted_iota(
        jnp.int32, square, 0
    )
    before = jnp.dot(earlier.astype(jnp.float32), named, preferred_element_type=jnp.float32)
    rank_ref[...] = jnp.where(named > 0.0, before, -1.0)
    counts = jnp.sum(named, axis=0, keepdims=True)
    most = jnp.broadcast_to(jnp.max(counts, axis=1, keepdims=True), counts.shape)

    asker = lax.broadcasted_iota(jnp.int32, (total, p_count), 0).astype(jnp.float32)

    def ids_from(first):
        rank = rank_ref[...] - first
        return [
            jnp.sum(jnp.where(rank == float(slot), asker, 0.0), axis=0, keepdims=True)
            for slot in range(SLOTS)
        ]

    list_copy = pltpu.make_async_copy(list_ref, scalar_ref, list_sems.at[0])
    left_copy = pltpu.make_async_copy(left_ref, left_scalar_ref, list_sems.at[1])

    def write_list():
        rest = jnp.zeros((LIST_ROWS - SLOTS - 1, p_count), jnp.float32)
        rows = ids_from(0.0) + [most, rest]
        list_ref[...] = jnp.concatenate(rows, axis=0).astype(jnp.int32)

    def write_left(first):
        left = jnp.where(rank_ref[...] == first, 1.0, 0.0)
        left = jnp.sum(left, axis=0, keepdims=True)
        square = (p_count, p_count)
        row = lax.broadcasted_iota(jnp.int32, square, 0).astype(jnp.float32)
        column = lax.broadcasted_iota(jnp.int32, square, 1).astype(jnp.float32)
        before = (row < column).astype(jnp.float32)
        place = jnp.dot(left, before, preferred_element_type=jnp.float32)
        chosen = jnp.where((place == row) & (left > 0.0), 1.0, 0.0)
        rest = jnp.zeros((LIST_ROWS - SLOTS - 1, p_count), jnp.float32)
        spread = jnp.concatenate(ids_from(first) + [column[:1], rest], axis=0)
        close = lax.dot_general(
            spread, chosen, (((1,), (1,)), ((), ())), preferred_element_type=jnp.float32
        )
        number = jnp.broadcast_to(jnp.sum(left, axis=1, keepdims=True), left.shape)
        rows = [close[: SLOTS + 1], number, rest[1:]]
        left_ref[...] = jnp.concatenate(rows, axis=0).astype(jnp.int32)

    def unit(index, ids_ref, place):
        tokens = [query_ref[ids_ref[slot, place]] for slot in range(SLOTS)]
        return token_max(passage_ref[pl.ds(index, 1)], jnp.concatenate(tokens, axis=0))

    def score_chunk(chunk):
        for start in range(0, CHUNK, 8):
            first = pl.multiple_of(chunk * CHUNK + start, 8)
            rows = [unit(first + offset, scalar_ref, first + offset) for offset in range(8)]
            best_ref[pl.ds(first, 8), :] = jnp.concatenate(rows, axis=0)

    def score_left(block):
        number = left_scalar_ref[SLOTS + 1, 0]
        for offset in range(STEP):
            place = block * STEP + offset
            index = left_scalar_ref[SLOTS, place]
            kept = jnp.where(place < number, index, p_count)
            left_best_ref[pl.ds(kept, 1), :] = unit(index, left_scalar_ref, place)

    def add_scores(scores, best, first):
        sums = token_sum(best, SLOTS)
        for index in range(shards):
            rank = rank_ref[index * q_count : (index + 1) * q_count] - first
            for slot in range(SLOTS):
                row = sums[slot : slot + 1]
                scores[index] = jnp.where(rank == float(slot), row, scores[index])
        return scores

    write_list()
    list_copy.start()
    write_left(float(SLOTS))
    left_copy.start()
    list_copy.wait()

    @pl.loop(0, chunks - 1)
    def _(chunk):
        score_chunk(chunk)

    left_copy.wait()
    score_chunk(chunks - 1)
    score_left(0)
    scores = [jnp.zeros((q_count, p_count), jnp.float32)] * shards
    scores = add_scores(scores, best_ref[...], 0.0)
    scores = add_scores(scores, left_best_ref[:p_count], float(SLOTS))
    for out_ref, score in zip(out_refs, scores):
        out_ref[...] = score

    largest, number = scalar_ref[SLOTS, 0], left_scalar_ref[SLOTS + 1, 0]

    @pl.when((largest > 2 * SLOTS) | (number > STEP))
    def _():
        @pl.loop(1, (largest + SLOTS - 1) // SLOTS)
        def _(turn):
            done = (turn * SLOTS).astype(jnp.float32)
            write_left(done)
            left_copy.start()
            left_copy.wait()

            @pl.loop(0, (left_scalar_ref[SLOTS + 1, 0] + STEP - 1) // STEP)
            def _(block):
                score_left(block)

            scores = [out_ref[...] for out_ref in out_refs]
            scores = add_scores(scores, left_best_ref[:p_count], done)
            for out_ref, score in zip(out_refs, scores):
                out_ref[...] = score


def score_memory(packed, memory, q_count, slots):
    shards = len(packed)
    q_tokens = packed[0].shape[0] // q_count - 2
    _, p_count, p_tokens, depth = memory.shape
    total = shards * q_count
    vmem = pl.BlockSpec(memory_space=pltpu.VMEM)
    return pl.pallas_call(
        functools.partial(memory_kernel, shards, slots),
        in_specs=[vmem] * (shards + 1),
        out_specs=[vmem] * shards,
        out_shape=[jax.ShapeDtypeStruct((q_count, p_count), jnp.float32)] * shards,
        scratch_shapes=[
            pltpu.VMEM((total, q_tokens, depth), memory.dtype),
            pltpu.VMEM((total, p_count), jnp.float32),
            pltpu.VMEM((p_count, SLOTS * q_tokens), jnp.float32),
            pltpu.VMEM((p_count + 8, SLOTS * q_tokens), jnp.float32),
            pltpu.VMEM((LIST_ROWS, p_count), jnp.int32),
            pltpu.SMEM((LIST_ROWS, p_count), jnp.int32),
            pltpu.VMEM((LIST_ROWS, p_count), jnp.int32),
            pltpu.SMEM((LIST_ROWS, p_count), jnp.int32),
            pltpu.SemaphoreType.DMA((2,)),
        ],
        compiler_params=pltpu.CompilerParams(vmem_limit_bytes=16 * MIB),
        cost_estimate=pl.CostEstimate(
            flops=2 * total * q_tokens * p_count * p_tokens * depth,
            bytes_accessed=2 * p_count * p_tokens * depth,
            transcendentals=0,
        ),
        name="score_memory",
    )(*packed, memory)


def batch_kernel(query_ref, *refs):
    passage_refs, (out_ref, best_ref) = refs[:-2], refs[-2:]
    _, queries, q_tokens, depth = query_ref.shape
    count = passage_refs[0].shape[1]
    tokens = query_ref[0].reshape(queries * q_tokens, depth)
    for chip, passage_ref in enumerate(passage_refs):
        best_ref[chip * count : (chip + 1) * count, :] = token_max(passage_ref[0], tokens)
    sums = token_sum(best_ref[...], queries)
    empty = jnp.zeros((queries, out_ref.shape[1] - sums.shape[1]), jnp.float32)
    out_ref[...] = jnp.concatenate([sums, empty], axis=1) if empty.size else sums


def score_batch(queries, positives):
    _, q_count, q_tokens, depth = queries.shape
    _, p_count, p_tokens, _ = positives[0].shape
    chips = len(positives)
    lanes = -(-chips * p_count // LANES) * LANES
    return pl.pallas_call(
        batch_kernel,
        out_shape=jax.ShapeDtypeStruct((q_count, lanes), jnp.float32),
        scratch_shapes=[pltpu.VMEM((chips * p_count, q_count * q_tokens), jnp.float32)],
        compiler_params=pltpu.CompilerParams(vmem_limit_bytes=16 * MIB),
        cost_estimate=pl.CostEstimate(
            flops=2 * chips * q_count * q_tokens * p_count * p_tokens * depth,
            bytes_accessed=2 * chips * p_count * p_tokens * depth,
            transcendentals=0,
        ),
        name="score_batch",
    )(queries, *positives)


def loss_kernel(shards, own_batch, mate_batch, *refs):
    memory_refs = refs[:shards]
    candidate_ref, count_ref, batch_ref, memory_ref, loss_ref = refs[shards:]
    group, shard = lax.axis_index("group"), lax.axis_index("memory")
    chip, core = group // 2, group % 2
    _, q_count, slots = candidate_ref.shape
    p_count = memory_refs[0].shape[1]
    columns = batch_ref.shape[2]

    parts = []
    for first in range(0, columns, LANES):
        lane = lax.broadcasted_iota(jnp.int32, (q_count, LANES), 1) + first
        owner = lane // q_count
        source = (((owner // 2) ^ chip) * q_count + lane % q_count) % LANES
        own = jnp.take_along_axis(own_batch[...], source, axis=1)
        mate = jnp.take_along_axis(mate_batch[...], source, axis=1)
        parts.append(jnp.where(owner % 2 == core, own, mate))
    batch = jnp.concatenate(parts, axis=1)[:, :columns]
    batch_ref[0] = batch

    ids = candidate_ref[0]
    padded = jnp.concatenate([ids, jnp.zeros((q_count, p_count - slots), jnp.int32)], axis=1)
    holder, local = padded // p_count, padded % p_count
    picked = jnp.zeros((q_count, p_count), jnp.float32)
    for step in range(shards):
        found = jnp.take_along_axis(memory_refs[-step][...], local, axis=1)
        picked = jnp.where(holder == (shard ^ step), found, picked)

    valid = lax.broadcasted_iota(jnp.int32, (q_count, p_count), 1) < column_of(count_ref[...])
    memory_ref[0] = jnp.where(valid, picked, 0.0)[:, :slots]

    top = jnp.maximum(
        jnp.max(batch, axis=1, keepdims=True),
        jnp.max(jnp.where(valid, picked, -jnp.inf), axis=1, keepdims=True),
    )
    total = jnp.sum(jnp.exp(batch - top), axis=1, keepdims=True) + jnp.sum(
        jnp.where(valid, jnp.exp(picked - top), 0.0), axis=1, keepdims=True
    )
    column = lax.broadcasted_iota(jnp.int32, batch.shape, 1)
    own = group * q_count + lax.broadcasted_iota(jnp.int32, batch.shape, 0)
    target_score = jnp.sum(jnp.where(column == own, batch, 0.0), axis=1, keepdims=True)
    loss_ref[...] = row_of(top + jnp.log(total) - target_score)


def finish(own_batch, mate_batch, memory_parts, candidates, counts, columns):
    _, q_count, slots = candidates.shape
    return pl.pallas_call(
        functools.partial(loss_kernel, len(memory_parts)),
        out_shape=[
            jax.ShapeDtypeStruct((1, q_count, columns), jnp.float32),
            jax.ShapeDtypeStruct((1, q_count, slots), jnp.float32),
            jax.ShapeDtypeStruct((1, q_count), jnp.float32),
        ],
        compiler_params=pltpu.CompilerParams(vmem_limit_bytes=4 * MIB),
        name="finish",
    )(own_batch, mate_batch, *memory_parts, candidates, counts)


def body(queries, positives, memory, candidates, counts):
    shards = lax.axis_size("memory")
    groups = lax.axis_size("group")
    chips = groups // 2
    q_count = queries.shape[1]
    slots = candidates.shape[2] // 2

    def to_shard(array, step):
        return lax.ppermute(array, "memory", [(i, i ^ step) for i in range(shards)])

    def to_group(array, step):
        return lax.ppermute(array, "group", [(i, i ^ step) for i in range(groups)])

    own = pack(queries, candidates, counts, memory.shape[1])
    packed = [own] + [to_shard(own, step) for step in range(1, shards)]
    sent_positives, sent_queries, _ = lax.optimization_barrier((positives, queries, own))
    row = [positives] + [to_group(sent_positives, 2 * step) for step in range(1, chips)]
    mate_queries = to_group(sent_queries, 1)

    scores = score_memory(packed, memory, q_count, slots)
    returned = [to_shard(scores[step], step) for step in range(shards - 1, 0, -1)]
    mate_queries, _ = lax.optimization_barrier((mate_queries, scores[0]))
    mate_scores = score_batch(mate_queries, row)
    mate_batch = to_group(mate_scores, 1)
    own_queries, _ = lax.optimization_barrier((queries, mate_scores))
    own_batch = score_batch(own_queries, row)
    columns = groups * q_count
    return finish(
        own_batch, mate_batch, [scores[0]] + returned, candidates, counts, columns
    )


def solution(mesh):
    in_specs = (
        P("group", "memory", None, None),
        P("group", "memory", None, None),
        P("group", "memory", None, None),
        P("group", "memory", None),
        P("group", "memory"),
    )
    out_specs = (P("group", "memory", None), P("group", "memory", None), P("group", "memory"))
    return jax.shard_map(body, mesh=mesh, in_specs=in_specs, out_specs=out_specs, check_vma=False)
```

```python
import functools

import jax
import jax.numpy as jnp
from jax import lax
from jax.experimental import pallas as pl
from jax.experimental.pallas import tpu as pltpu
from jax.sharding import PartitionSpec as P

LANES = 128
MIB = 1024 * 1024
SLOTS = 8
LOW = 256
PACK_FLOPS = 10**10
PACK_BYTES = 2**24
CHUNK = 32


def return_order(shards):
    return list(range(2, shards)) + [1]


def in_hbm(array):
    return pltpu.with_memory_space_constraint(array, pltpu.HBM)


def token_max(passages, tokens):
    count, width, depth = passages.shape
    product = lax.dot_general(
        passages.reshape(count * width, depth),
        tokens,
        (((1,), (1,)), ((), ())),
        preferred_element_type=jnp.float32,
    )
    return jnp.max(product.reshape(count, width, tokens.shape[0]), axis=1)


def token_sum(best, queries):
    tokens = best.shape[1]
    per_query = tokens // queries
    row = lax.broadcasted_iota(jnp.int32, (queries, tokens), 0)
    col = lax.broadcasted_iota(jnp.int32, (queries, tokens), 1)
    own = (col // per_query == row).astype(jnp.bfloat16)
    high = best.astype(jnp.bfloat16)
    rest = best - high.astype(jnp.float32)
    middle = rest.astype(jnp.bfloat16)
    low = (rest - middle.astype(jnp.float32)).astype(jnp.bfloat16)
    return lax.dot_general(
        jnp.concatenate([own] * 3, axis=1),
        jnp.concatenate([high, middle, low], axis=1),
        (((1,), (1,)), ((), ())),
        preferred_element_type=jnp.float32,
    )


def column_of(row):
    size = row.shape[1]
    square = (size, size)
    diagonal = lax.broadcasted_iota(jnp.int32, square, 0) == lax.broadcasted_iota(
        jnp.int32, square, 1
    )
    return jnp.sum(jnp.where(diagonal, jnp.broadcast_to(row, square), 0), axis=1, keepdims=True)


def row_of(column):
    size = column.shape[0]
    square = (size, size)
    diagonal = lax.broadcasted_iota(jnp.int32, square, 0) == lax.broadcasted_iota(
        jnp.int32, square, 1
    )
    return jnp.sum(jnp.where(diagonal, jnp.broadcast_to(column, square), 0), axis=0, keepdims=True)


def split_ids(p_count, candidate_ref, count_ref):
    ids = candidate_ref[0]
    row = lax.broadcasted_iota(jnp.int32, ids.shape, 0)
    valid_count = jnp.zeros(ids.shape, jnp.int32)
    for index in range(ids.shape[0]):
        valid_count = jnp.where(row == index, count_ref[0, index], valid_count)
    valid = lax.broadcasted_iota(jnp.int32, ids.shape, 1) < valid_count
    holder = jnp.where(valid, ids // p_count, -1)
    return (ids % p_count).astype(jnp.float32), holder.astype(jnp.float32)


def pack_kernel(p_count, query_ref, candidate_ref, count_ref, out_ref):
    _, q_count, slots = candidate_ref.shape
    _, _, q_tokens, depth = query_ref.shape
    tokens = q_count * q_tokens
    out_ref[:tokens] = query_ref[0].reshape(tokens, depth)
    planes = jnp.concatenate(split_ids(p_count, candidate_ref, count_ref), axis=0)
    empty = jnp.zeros((2 * q_count, depth - slots), jnp.float32)
    out_ref[tokens:] = jnp.concatenate([planes, empty], axis=1).astype(out_ref.dtype)


def pack(queries, candidates, counts, p_count):
    _, q_count, q_tokens, depth = queries.shape
    vmem = pl.BlockSpec(memory_space=pltpu.VMEM)
    return pl.pallas_call(
        functools.partial(pack_kernel, p_count),
        in_specs=[vmem, vmem, pl.BlockSpec(memory_space=pltpu.SMEM)],
        out_shape=jax.ShapeDtypeStruct((q_count * (q_tokens + 2), depth), queries.dtype),
        compiler_params=pltpu.CompilerParams(vmem_limit_bytes=4 * MIB),
        cost_estimate=pl.CostEstimate(
            flops=PACK_FLOPS, bytes_accessed=PACK_BYTES, transcendentals=0
        ),
        name="pack",
    )(in_hbm(queries), in_hbm(candidates), in_hbm(counts))


def memory_kernel(shards, slots, *refs):
    packed_refs, passage_ref = refs[:shards], refs[shards].at[0]
    out_refs = refs[shards + 1 : 2 * shards + 1]
    query_ref, rank_ref, best_ref, list_ref, scalar_ref, list_sem = refs[2 * shards + 1 :]
    q_count = out_refs[0].shape[0]
    p_count = passage_ref.shape[0]
    total, q_tokens, depth = query_ref.shape
    chunks = p_count // CHUNK

    me = lax.axis_index("memory").astype(jnp.float32)
    keys = []
    for index, packed_ref in enumerate(packed_refs):
        tokens = packed_ref[: q_count * q_tokens].reshape(q_count, q_tokens, depth)
        query_ref[index * q_count : (index + 1) * q_count] = tokens
        planes = packed_ref[q_count * q_tokens :].astype(jnp.float32)
        local, holder = planes[:q_count], planes[q_count:]
        keys.append(jnp.where(holder == me, local, -1.0))
    keys = jnp.concatenate(keys, axis=0)
    passage = lax.broadcasted_iota(jnp.int32, (total, p_count), 1).astype(jnp.float32)
    named = jnp.zeros((total, p_count), jnp.float32)
    for slot in range(slots):
        named = jnp.where(keys[:, slot : slot + 1] == passage, 1.0, named)

    square = (total, total)
    earlier = lax.broadcasted_iota(jnp.int32, square, 1) < lax.broadcasted_iota(
        jnp.int32, square, 0
    )
    before = jnp.dot(earlier.astype(jnp.float32), named, preferred_element_type=jnp.float32)
    rank_ref[...] = jnp.where(named > 0.0, before, -1.0)
    counts = jnp.sum(named, axis=0, keepdims=True)
    most = jnp.broadcast_to(jnp.max(counts, axis=1, keepdims=True), counts.shape)

    def left_over(first):
        left = jnp.where(rank_ref[...] == first, 1.0, 0.0)
        left = jnp.sum(left, axis=0, keepdims=True)
        square = (p_count, p_count)
        row = lax.broadcasted_iota(jnp.int32, square, 0).astype(jnp.float32)
        column = lax.broadcasted_iota(jnp.int32, square, 1).astype(jnp.float32)
        place = jnp.dot(left, (row < column).astype(jnp.float32), preferred_element_type=jnp.float32)
        mine = jnp.where((place == row) & (left > 0.0), column, 0.0)
        index = jnp.sum(mine, axis=1, keepdims=True)
        index = jnp.sum(jnp.where(row == column, index, 0.0), axis=0, keepdims=True)
        return [index, jnp.broadcast_to(jnp.sum(left, axis=1, keepdims=True), left.shape)]

    def write_list(first, extra):
        asker = lax.broadcasted_iota(jnp.int32, (total, p_count), 0).astype(jnp.float32)
        rank = rank_ref[...] - first
        rows = [
            jnp.sum(jnp.where(rank == float(slot), asker, 0.0), axis=0, keepdims=True)
            for slot in range(SLOTS)
        ]
        for slot, above in enumerate(extra):
            rows[slot] = rows[slot] + LOW * above
        list_ref[...] = jnp.concatenate(rows, axis=0).astype(jnp.int32)
        copy = pltpu.make_async_copy(list_ref, scalar_ref, list_sem)
        copy.start()
        copy.wait()

    def unit(index):
        tokens = [query_ref[scalar_ref[slot, index] & (LOW - 1)] for slot in range(SLOTS)]
        return token_max(passage_ref[pl.ds(index, 1)], jnp.concatenate(tokens, axis=0))

    def add_scores(first, scores):
        sums = token_sum(best_ref[...], SLOTS)
        for index, out_ref in enumerate(out_refs):
            rank = rank_ref[index * q_count : (index + 1) * q_count] - first
            total_scores = scores[index]
            for slot in range(SLOTS):
                total_scores = jnp.where(rank == float(slot), sums[slot : slot + 1], total_scores)
            out_ref[...] = total_scores

    write_list(0.0, [most])
    rounds = (scalar_ref[0, 0] // LOW + SLOTS - 1) // SLOTS

    @pl.loop(0, chunks)
    def _(chunk):
        for start in range(0, CHUNK, 8):
            first = pl.multiple_of(chunk * CHUNK + start, 8)
            rows = [unit(first + offset) for offset in range(8)]
            best_ref[pl.ds(first, 8), :] = jnp.concatenate(rows, axis=0)

    add_scores(0.0, [jnp.zeros((q_count, p_count), jnp.float32)] * shards)

    @pl.loop(1, rounds)
    def _(turn):
        done = (turn * SLOTS).astype(jnp.float32)
        write_list(done, left_over(done))

        @pl.loop(0, scalar_ref[1, 0] // LOW)
        def _(place):
            index = scalar_ref[0, place] // LOW
            best_ref[pl.ds(index, 1), :] = unit(index)

        add_scores(done, [out_ref[...] for out_ref in out_refs])


def score_memory(packed, memory, q_count, slots):
    shards = len(packed)
    q_tokens = packed[0].shape[0] // q_count - 2
    _, p_count, p_tokens, depth = memory.shape
    total = shards * q_count
    vmem = pl.BlockSpec(memory_space=pltpu.VMEM)
    return pl.pallas_call(
        functools.partial(memory_kernel, shards, slots),
        in_specs=[vmem] * (shards + 1),
        out_specs=[vmem] * shards,
        out_shape=[jax.ShapeDtypeStruct((q_count, p_count), jnp.float32)] * shards,
        scratch_shapes=[
            pltpu.VMEM((total, q_tokens, depth), memory.dtype),
            pltpu.VMEM((total, p_count), jnp.float32),
            pltpu.VMEM((p_count, SLOTS * q_tokens), jnp.float32),
            pltpu.VMEM((SLOTS, p_count), jnp.int32),
            pltpu.SMEM((SLOTS, p_count), jnp.int32),
            pltpu.SemaphoreType.DMA,
        ],
        compiler_params=pltpu.CompilerParams(vmem_limit_bytes=16 * MIB),
        cost_estimate=pl.CostEstimate(
            flops=2 * total * q_tokens * p_count * p_tokens * depth,
            bytes_accessed=2 * p_count * p_tokens * depth,
            transcendentals=0,
        ),
        name="score_memory",
    )(*packed, memory)


def batch_kernel(query_ref, *refs):
    passage_refs, (out_ref, best_ref) = refs[:-2], refs[-2:]
    _, queries, q_tokens, depth = query_ref.shape
    count = passage_refs[0].shape[1]
    tokens = query_ref[0].reshape(queries * q_tokens, depth)
    for chip, passage_ref in enumerate(passage_refs):
        best_ref[chip * count : (chip + 1) * count, :] = token_max(passage_ref[0], tokens)
    sums = token_sum(best_ref[...], queries)
    empty = jnp.zeros((queries, out_ref.shape[1] - sums.shape[1]), jnp.float32)
    out_ref[...] = jnp.concatenate([sums, empty], axis=1) if empty.size else sums


def score_batch(queries, positives):
    _, q_count, q_tokens, depth = queries.shape
    _, p_count, p_tokens, _ = positives[0].shape
    chips = len(positives)
    lanes = -(-chips * p_count // LANES) * LANES
    return pl.pallas_call(
        batch_kernel,
        out_shape=jax.ShapeDtypeStruct((q_count, lanes), jnp.float32),
        scratch_shapes=[pltpu.VMEM((chips * p_count, q_count * q_tokens), jnp.float32)],
        compiler_params=pltpu.CompilerParams(vmem_limit_bytes=16 * MIB),
        cost_estimate=pl.CostEstimate(
            flops=2 * chips * q_count * q_tokens * p_count * p_tokens * depth,
            bytes_accessed=2 * chips * p_count * p_tokens * depth,
            transcendentals=0,
        ),
        name="score_batch",
    )(queries, *positives)


def loss_kernel(shards, own_batch, mate_batch, *refs):
    memory_refs = refs[:shards]
    candidate_ref, count_ref, batch_ref, memory_ref, loss_ref = refs[shards:]
    group, shard = lax.axis_index("group"), lax.axis_index("memory")
    chip, core = group // 2, group % 2
    _, q_count, slots = candidate_ref.shape
    p_count = memory_refs[0].shape[1]
    columns = batch_ref.shape[2]

    parts = []
    for first in range(0, columns, LANES):
        lane = lax.broadcasted_iota(jnp.int32, (q_count, LANES), 1) + first
        owner = lane // q_count
        source = (((owner // 2) ^ chip) * q_count + lane % q_count) % LANES
        own = jnp.take_along_axis(own_batch[...], source, axis=1)
        mate = jnp.take_along_axis(mate_batch[...], source, axis=1)
        parts.append(jnp.where(owner % 2 == core, own, mate))
    batch = jnp.concatenate(parts, axis=1)[:, :columns]
    batch_ref[0] = batch

    ids = candidate_ref[0]
    padded = jnp.concatenate([ids, jnp.zeros((q_count, p_count - slots), jnp.int32)], axis=1)
    holder, local = padded // p_count, padded % p_count
    picked = jnp.zeros((q_count, p_count), jnp.float32)
    for step, part_ref in zip([0] + return_order(shards), memory_refs):
        found = jnp.take_along_axis(part_ref[...], local, axis=1)
        picked = jnp.where(holder == (shard ^ step), found, picked)

    valid = lax.broadcasted_iota(jnp.int32, (q_count, p_count), 1) < column_of(count_ref[...])
    memory_ref[0] = jnp.where(valid, picked, 0.0)[:, :slots]

    top = jnp.maximum(
        jnp.max(batch, axis=1, keepdims=True),
        jnp.max(jnp.where(valid, picked, -jnp.inf), axis=1, keepdims=True),
    )
    total = jnp.sum(jnp.exp(batch - top), axis=1, keepdims=True) + jnp.sum(
        jnp.where(valid, jnp.exp(picked - top), 0.0), axis=1, keepdims=True
    )
    column = lax.broadcasted_iota(jnp.int32, batch.shape, 1)
    own = group * q_count + lax.broadcasted_iota(jnp.int32, batch.shape, 0)
    target_score = jnp.sum(jnp.where(column == own, batch, 0.0), axis=1, keepdims=True)
    loss_ref[...] = row_of(top + jnp.log(total) - target_score)


def finish(own_batch, mate_batch, memory_parts, candidates, counts, columns):
    _, q_count, slots = candidates.shape
    return pl.pallas_call(
        functools.partial(loss_kernel, len(memory_parts)),
        out_shape=[
            jax.ShapeDtypeStruct((1, q_count, columns), jnp.float32),
            jax.ShapeDtypeStruct((1, q_count, slots), jnp.float32),
            jax.ShapeDtypeStruct((1, q_count), jnp.float32),
        ],
        compiler_params=pltpu.CompilerParams(vmem_limit_bytes=4 * MIB),
        name="finish",
    )(own_batch, mate_batch, *memory_parts, candidates, counts)


def body(queries, positives, memory, candidates, counts):
    shards = lax.axis_size("memory")
    groups = lax.axis_size("group")
    chips = groups // 2
    q_count = queries.shape[1]
    slots = candidates.shape[2] // 2

    def to_shard(array, step):
        return lax.ppermute(array, "memory", [(i, i ^ step) for i in range(shards)])

    def to_group(array, step):
        return lax.ppermute(array, "group", [(i, i ^ step) for i in range(groups)])

    own = pack(queries, candidates, counts, memory.shape[1])
    packed = [own] + [to_shard(own, step) for step in range(1, shards)]
    sent_positives, sent_queries, _ = lax.optimization_barrier((positives, queries, own))
    row = [positives] + [to_group(sent_positives, 2 * step) for step in range(1, chips)]
    mate_queries = to_group(sent_queries, 1)

    scores = score_memory(packed, memory, q_count, slots)
    returned = [to_shard(scores[step], step) for step in return_order(shards)]
    mate_queries, _ = lax.optimization_barrier((mate_queries, scores[0]))
    mate_scores = score_batch(mate_queries, row)
    mate_batch = to_group(mate_scores, 1)
    own_queries, _ = lax.optimization_barrier((queries, mate_scores))
    own_batch = score_batch(own_queries, row)
    columns = groups * q_count
    return finish(
        own_batch, mate_batch, [scores[0]] + returned, candidates, counts, columns
    )


def solution(mesh):
    in_specs = (
        P("group", "memory", None, None),
        P("group", "memory", None, None),
        P("group", "memory", None, None),
        P("group", "memory", None),
        P("group", "memory"),
    )
    out_specs = (P("group", "memory", None), P("group", "memory", None), P("group", "memory"))
    return jax.shard_map(body, mesh=mesh, in_specs=in_specs, out_specs=out_specs, check_vma=False)
```

```python
import functools

import jax
import jax.numpy as jnp
from jax import lax
from jax.experimental import pallas as pl
from jax.experimental.pallas import tpu as pltpu
from jax.sharding import PartitionSpec as P

LANES = 128
MIB = 1024 * 1024
SLOTS = 8
LOW = 256
PACK_FLOPS = 10**10
PACK_BYTES = 2**24


def in_hbm(array):
    return pltpu.with_memory_space_constraint(array, pltpu.HBM)


def token_max(passages, tokens):
    count, width, depth = passages.shape
    product = lax.dot_general(
        passages.reshape(count * width, depth),
        tokens,
        (((1,), (1,)), ((), ())),
        preferred_element_type=jnp.float32,
    )
    return jnp.max(product.reshape(count, width, tokens.shape[0]), axis=1)


def token_sum(best, queries):
    tokens = best.shape[1]
    per_query = tokens // queries
    row = lax.broadcasted_iota(jnp.int32, (queries, tokens), 0)
    col = lax.broadcasted_iota(jnp.int32, (queries, tokens), 1)
    own = (col // per_query == row).astype(jnp.bfloat16)
    high = best.astype(jnp.bfloat16)
    rest = best - high.astype(jnp.float32)
    middle = rest.astype(jnp.bfloat16)
    low = (rest - middle.astype(jnp.float32)).astype(jnp.bfloat16)
    return lax.dot_general(
        jnp.concatenate([own] * 3, axis=1),
        jnp.concatenate([high, middle, low], axis=1),
        (((1,), (1,)), ((), ())),
        preferred_element_type=jnp.float32,
    )


def column_of(row):
    size = row.shape[1]
    square = (size, size)
    diagonal = lax.broadcasted_iota(jnp.int32, square, 0) == lax.broadcasted_iota(
        jnp.int32, square, 1
    )
    return jnp.sum(jnp.where(diagonal, jnp.broadcast_to(row, square), 0), axis=1, keepdims=True)


def row_of(column):
    size = column.shape[0]
    square = (size, size)
    diagonal = lax.broadcasted_iota(jnp.int32, square, 0) == lax.broadcasted_iota(
        jnp.int32, square, 1
    )
    return jnp.sum(jnp.where(diagonal, jnp.broadcast_to(column, square), 0), axis=0, keepdims=True)


def split_ids(p_count, candidate_ref, count_ref):
    ids = candidate_ref[0]
    row = lax.broadcasted_iota(jnp.int32, ids.shape, 0)
    valid_count = jnp.zeros(ids.shape, jnp.int32)
    for index in range(ids.shape[0]):
        valid_count = jnp.where(row == index, count_ref[0, index], valid_count)
    valid = lax.broadcasted_iota(jnp.int32, ids.shape, 1) < valid_count
    holder = jnp.where(valid, ids // p_count, -1)
    return (ids % p_count).astype(jnp.float32), holder.astype(jnp.float32)


def pack_kernel(p_count, query_ref, candidate_ref, count_ref, out_ref):
    _, q_count, slots = candidate_ref.shape
    _, _, q_tokens, depth = query_ref.shape
    tokens = q_count * q_tokens
    out_ref[:tokens] = query_ref[0].reshape(tokens, depth)
    planes = jnp.concatenate(split_ids(p_count, candidate_ref, count_ref), axis=0)
    empty = jnp.zeros((2 * q_count, depth - slots), jnp.float32)
    out_ref[tokens:] = jnp.concatenate([planes, empty], axis=1).astype(out_ref.dtype)


def pack(queries, candidates, counts, p_count):
    _, q_count, q_tokens, depth = queries.shape
    vmem = pl.BlockSpec(memory_space=pltpu.VMEM)
    return pl.pallas_call(
        functools.partial(pack_kernel, p_count),
        in_specs=[vmem, vmem, pl.BlockSpec(memory_space=pltpu.SMEM)],
        out_shape=jax.ShapeDtypeStruct((q_count * (q_tokens + 2), depth), queries.dtype),
        compiler_params=pltpu.CompilerParams(vmem_limit_bytes=4 * MIB),
        cost_estimate=pl.CostEstimate(
            flops=PACK_FLOPS, bytes_accessed=PACK_BYTES, transcendentals=0
        ),
        name="pack",
    )(in_hbm(queries), in_hbm(candidates), in_hbm(counts))


def memory_kernel(shards, slots, *refs):
    packed_refs, passage_ref = refs[:shards], refs[shards].at[0]
    out_refs = refs[shards + 1 : 2 * shards + 1]
    query_ref, rank_ref, best_ref, list_ref, scalar_ref, *refs = refs[2 * shards + 1 :]
    most_ref, rounds_ref, list_sems = refs
    q_count = out_refs[0].shape[0]
    p_count = passage_ref.shape[0]
    total, q_tokens, depth = query_ref.shape

    me = lax.axis_index("memory").astype(jnp.float32)
    keys = []
    for index, packed_ref in enumerate(packed_refs):
        tokens = packed_ref[: q_count * q_tokens].reshape(q_count, q_tokens, depth)
        query_ref[index * q_count : (index + 1) * q_count] = tokens
        planes = packed_ref[q_count * q_tokens :].astype(jnp.float32)
        local, holder = planes[:q_count], planes[q_count:]
        keys.append(jnp.where(holder == me, local, -1.0))
    keys = jnp.concatenate(keys, axis=0)
    passage = lax.broadcasted_iota(jnp.int32, (total, p_count), 1).astype(jnp.float32)
    named = jnp.zeros((total, p_count), jnp.float32)
    for slot in range(slots):
        named = jnp.where(keys[:, slot : slot + 1] == passage, 1.0, named)

    square = (total, total)
    earlier = lax.broadcasted_iota(jnp.int32, square, 1) < lax.broadcasted_iota(
        jnp.int32, square, 0
    )
    before = jnp.dot(
        earlier.astype(jnp.bfloat16),
        named.astype(jnp.bfloat16),
        preferred_element_type=jnp.float32,
    )
    rank_ref[...] = jnp.where(named > 0.0, before, -1.0)
    def left_over(first):
        left = jnp.where(rank_ref[...] == first, 1.0, 0.0)
        left = jnp.sum(left, axis=0, keepdims=True)
        square = (p_count, p_count)
        row = lax.broadcasted_iota(jnp.int32, square, 0).astype(jnp.float32)
        column = lax.broadcasted_iota(jnp.int32, square, 1).astype(jnp.float32)
        place = jnp.dot(left, (row < column).astype(jnp.float32), preferred_element_type=jnp.float32)
        mine = jnp.where((place == row) & (left > 0.0), column, 0.0)
        index = jnp.sum(mine, axis=1, keepdims=True)
        index = jnp.sum(jnp.where(row == column, index, 0.0), axis=0, keepdims=True)
        return [index, jnp.broadcast_to(jnp.sum(left, axis=1, keepdims=True), left.shape)]

    def write_list(first, extra):
        asker = lax.broadcasted_iota(jnp.int32, (total, p_count), 0).astype(jnp.float32)
        rank = rank_ref[...] - first
        rows = [
            jnp.sum(jnp.where(rank == float(slot), asker, 0.0), axis=0, keepdims=True)
            for slot in range(SLOTS)
        ]
        for slot, above in enumerate(extra):
            rows[slot] = rows[slot] + LOW * above
        list_ref[...] = jnp.concatenate(rows, axis=0).astype(jnp.int32)
        copy = pltpu.make_async_copy(list_ref, scalar_ref, list_sems.at[0])
        copy.start()
        return copy

    def unit(index):
        tokens = [query_ref[scalar_ref[slot, index] & (LOW - 1)] for slot in range(SLOTS)]
        return token_max(passage_ref[pl.ds(index, 1)], jnp.concatenate(tokens, axis=0))

    def add_scores(first, scores):
        sums = token_sum(best_ref[...], SLOTS)
        for index, out_ref in enumerate(out_refs):
            rank = rank_ref[index * q_count : (index + 1) * q_count] - first
            total_scores = scores[index]
            for slot in range(SLOTS):
                total_scores = jnp.where(rank == float(slot), sums[slot : slot + 1], total_scores)
            out_ref[...] = total_scores

    list_copy = write_list(0.0, [])
    counts = jnp.sum(named, axis=0, keepdims=True)
    most = jnp.broadcast_to(jnp.max(counts, axis=1, keepdims=True), most_ref.shape)
    most_ref[...] = most.astype(jnp.int32)
    most_copy = pltpu.make_async_copy(most_ref, rounds_ref, list_sems.at[1])
    most_copy.start()
    list_copy.wait()

    for first in range(0, p_count, 8):
        rows = [unit(first + offset) for offset in range(8)]
        best_ref[first : first + 8, :] = jnp.concatenate(rows, axis=0)

    most_copy.wait()
    rounds = (rounds_ref[0, 0] + SLOTS - 1) // SLOTS
    add_scores(0.0, [jnp.zeros((q_count, p_count), jnp.float32)] * shards)

    @pl.loop(1, rounds)
    def _(turn):
        done = (turn * SLOTS).astype(jnp.float32)
        write_list(done, left_over(done)).wait()

        @pl.loop(0, scalar_ref[1, 0] // LOW)
        def _(place):
            index = scalar_ref[0, place] // LOW
            best_ref[pl.ds(index, 1), :] = unit(index)

        add_scores(done, [out_ref[...] for out_ref in out_refs])


def score_memory(packed, memory, q_count, slots):
    shards = len(packed)
    q_tokens = packed[0].shape[0] // q_count - 2
    _, p_count, p_tokens, depth = memory.shape
    total = shards * q_count
    vmem = pl.BlockSpec(memory_space=pltpu.VMEM)
    return pl.pallas_call(
        functools.partial(memory_kernel, shards, slots),
        in_specs=[vmem] * (shards + 1),
        out_specs=[vmem] * shards,
        out_shape=[jax.ShapeDtypeStruct((q_count, p_count), jnp.float32)] * shards,
        scratch_shapes=[
            pltpu.VMEM((total, q_tokens, depth), memory.dtype),
            pltpu.VMEM((total, p_count), jnp.float32),
            pltpu.VMEM((p_count, SLOTS * q_tokens), jnp.float32),
            pltpu.VMEM((SLOTS, p_count), jnp.int32),
            pltpu.SMEM((SLOTS, p_count), jnp.int32),
            pltpu.VMEM((8, LANES), jnp.int32),
            pltpu.SMEM((8, LANES), jnp.int32),
            pltpu.SemaphoreType.DMA((2,)),
        ],
        compiler_params=pltpu.CompilerParams(vmem_limit_bytes=16 * MIB),
        cost_estimate=pl.CostEstimate(
            flops=2 * total * q_tokens * p_count * p_tokens * depth,
            bytes_accessed=2 * p_count * p_tokens * depth,
            transcendentals=0,
        ),
        name="score_memory",
    )(*packed, memory)


def batch_kernel(query_ref, *refs):
    passage_refs, (out_ref, best_ref) = refs[:-2], refs[-2:]
    _, queries, q_tokens, depth = query_ref.shape
    count = passage_refs[0].shape[1]
    tokens = query_ref[0].reshape(queries * q_tokens, depth)
    for chip, passage_ref in enumerate(passage_refs):
        best_ref[chip * count : (chip + 1) * count, :] = token_max(passage_ref[0], tokens)
    sums = token_sum(best_ref[...], queries)
    empty = jnp.zeros((queries, out_ref.shape[1] - sums.shape[1]), jnp.float32)
    out_ref[...] = jnp.concatenate([sums, empty], axis=1) if empty.size else sums


def score_batch(queries, positives):
    _, q_count, q_tokens, depth = queries.shape
    _, p_count, p_tokens, _ = positives[0].shape
    chips = len(positives)
    lanes = -(-chips * p_count // LANES) * LANES
    return pl.pallas_call(
        batch_kernel,
        out_shape=jax.ShapeDtypeStruct((q_count, lanes), jnp.float32),
        scratch_shapes=[pltpu.VMEM((chips * p_count, q_count * q_tokens), jnp.float32)],
        compiler_params=pltpu.CompilerParams(vmem_limit_bytes=16 * MIB),
        cost_estimate=pl.CostEstimate(
            flops=2 * chips * q_count * q_tokens * p_count * p_tokens * depth,
            bytes_accessed=2 * chips * p_count * p_tokens * depth,
            transcendentals=0,
        ),
        name="score_batch",
    )(queries, *positives)


def loss_kernel(shards, own_batch, mate_batch, *refs):
    memory_refs = refs[:shards]
    candidate_ref, count_ref, batch_ref, memory_ref, loss_ref = refs[shards:]
    group, shard = lax.axis_index("group"), lax.axis_index("memory")
    chip, core = group // 2, group % 2
    _, q_count, slots = candidate_ref.shape
    p_count = memory_refs[0].shape[1]
    columns = batch_ref.shape[2]

    parts = []
    for first in range(0, columns, LANES):
        lane = lax.broadcasted_iota(jnp.int32, (q_count, LANES), 1) + first
        owner = lane // q_count
        source = (((owner // 2) ^ chip) * q_count + lane % q_count) % LANES
        own = jnp.take_along_axis(own_batch[...], source, axis=1)
        mate = jnp.take_along_axis(mate_batch[...], source, axis=1)
        parts.append(jnp.where(owner % 2 == core, own, mate))
    batch = jnp.concatenate(parts, axis=1)[:, :columns]
    batch_ref[0] = batch

    ids = candidate_ref[0]
    padded = jnp.concatenate([ids, jnp.zeros((q_count, p_count - slots), jnp.int32)], axis=1)
    holder, local = padded // p_count, padded % p_count
    picked = jnp.zeros((q_count, p_count), jnp.float32)
    for step in range(shards):
        found = jnp.take_along_axis(memory_refs[-step][...], local, axis=1)
        picked = jnp.where(holder == (shard ^ step), found, picked)

    valid = lax.broadcasted_iota(jnp.int32, (q_count, p_count), 1) < column_of(count_ref[...])
    memory_ref[0] = jnp.where(valid, picked, 0.0)[:, :slots]

    top = jnp.maximum(
        jnp.max(batch, axis=1, keepdims=True),
        jnp.max(jnp.where(valid, picked, -jnp.inf), axis=1, keepdims=True),
    )
    total = jnp.sum(jnp.exp(batch - top), axis=1, keepdims=True) + jnp.sum(
        jnp.where(valid, jnp.exp(picked - top), 0.0), axis=1, keepdims=True
    )
    column = lax.broadcasted_iota(jnp.int32, batch.shape, 1)
    own = group * q_count + lax.broadcasted_iota(jnp.int32, batch.shape, 0)
    target_score = jnp.sum(jnp.where(column == own, batch, 0.0), axis=1, keepdims=True)
    loss_ref[...] = row_of(top + jnp.log(total) - target_score)


def finish(own_batch, mate_batch, memory_parts, candidates, counts, columns):
    _, q_count, slots = candidates.shape
    return pl.pallas_call(
        functools.partial(loss_kernel, len(memory_parts)),
        out_shape=[
            jax.ShapeDtypeStruct((1, q_count, columns), jnp.float32),
            jax.ShapeDtypeStruct((1, q_count, slots), jnp.float32),
            jax.ShapeDtypeStruct((1, q_count), jnp.float32),
        ],
        compiler_params=pltpu.CompilerParams(vmem_limit_bytes=4 * MIB),
        name="finish",
    )(own_batch, mate_batch, *memory_parts, candidates, counts)


def body(queries, positives, memory, candidates, counts):
    shards = lax.axis_size("memory")
    groups = lax.axis_size("group")
    chips = groups // 2
    q_count = queries.shape[1]
    slots = candidates.shape[2] // 2

    def to_shard(array, step):
        return lax.ppermute(array, "memory", [(i, i ^ step) for i in range(shards)])

    def to_group(array, step):
        return lax.ppermute(array, "group", [(i, i ^ step) for i in range(groups)])

    own = pack(queries, candidates, counts, memory.shape[1])
    packed = [own] + [to_shard(own, step) for step in range(1, shards)]
    sent_positives, sent_queries, _ = lax.optimization_barrier((positives, queries, own))
    row = [positives] + [to_group(sent_positives, 2 * step) for step in range(1, chips)]
    mate_queries = to_group(sent_queries, 1)

    scores = score_memory(packed, memory, q_count, slots)
    returned = [to_shard(scores[step], step) for step in range(shards - 1, 0, -1)]
    mate_queries, _ = lax.optimization_barrier((mate_queries, scores[0]))
    mate_scores = score_batch(mate_queries, row)
    mate_batch = to_group(mate_scores, 1)
    own_queries, _ = lax.optimization_barrier((queries, mate_scores))
    own_batch = score_batch(own_queries, row)
    columns = groups * q_count
    return finish(
        own_batch, mate_batch, [scores[0]] + returned, candidates, counts, columns
    )


def solution(mesh):
    in_specs = (
        P("group", "memory", None, None),
        P("group", "memory", None, None),
        P("group", "memory", None, None),
        P("group", "memory", None),
        P("group", "memory"),
    )
    out_specs = (P("group", "memory", None), P("group", "memory", None), P("group", "memory"))
    return jax.shard_map(body, mesh=mesh, in_specs=in_specs, out_specs=out_specs, check_vma=False)
```

```python
import functools

import jax
import jax.numpy as jnp
from jax import lax
from jax.experimental import pallas as pl
from jax.experimental.pallas import tpu as pltpu
from jax.sharding import PartitionSpec as P

LANES = 128
MIB = 1024 * 1024
SLOTS = 8
LOW = 256
HALF = 64
PACK_FLOPS = 10**10
PACK_BYTES = 2**24


def in_hbm(array):
    return pltpu.with_memory_space_constraint(array, pltpu.HBM)


def token_max(passages, tokens):
    count, width, depth = passages.shape
    product = lax.dot_general(
        passages.reshape(count * width, depth),
        tokens,
        (((1,), (1,)), ((), ())),
        preferred_element_type=jnp.float32,
    )
    return jnp.max(product.reshape(count, width, tokens.shape[0]), axis=1)


def token_sum(best, queries):
    tokens = best.shape[1]
    per_query = tokens // queries
    row = lax.broadcasted_iota(jnp.int32, (queries, tokens), 0)
    col = lax.broadcasted_iota(jnp.int32, (queries, tokens), 1)
    own = (col // per_query == row).astype(jnp.bfloat16)
    high = best.astype(jnp.bfloat16)
    rest = best - high.astype(jnp.float32)
    middle = rest.astype(jnp.bfloat16)
    low = (rest - middle.astype(jnp.float32)).astype(jnp.bfloat16)
    return lax.dot_general(
        jnp.concatenate([own] * 3, axis=1),
        jnp.concatenate([high, middle, low], axis=1),
        (((1,), (1,)), ((), ())),
        preferred_element_type=jnp.float32,
    )


def column_of(row):
    size = row.shape[1]
    square = (size, size)
    diagonal = lax.broadcasted_iota(jnp.int32, square, 0) == lax.broadcasted_iota(
        jnp.int32, square, 1
    )
    return jnp.sum(jnp.where(diagonal, jnp.broadcast_to(row, square), 0), axis=1, keepdims=True)


def row_of(column):
    size = column.shape[0]
    square = (size, size)
    diagonal = lax.broadcasted_iota(jnp.int32, square, 0) == lax.broadcasted_iota(
        jnp.int32, square, 1
    )
    return jnp.sum(jnp.where(diagonal, jnp.broadcast_to(column, square), 0), axis=0, keepdims=True)


def split_ids(p_count, candidate_ref, count_ref):
    ids = candidate_ref[0]
    row = lax.broadcasted_iota(jnp.int32, ids.shape, 0)
    valid_count = jnp.zeros(ids.shape, jnp.int32)
    for index in range(ids.shape[0]):
        valid_count = jnp.where(row == index, count_ref[0, index], valid_count)
    valid = lax.broadcasted_iota(jnp.int32, ids.shape, 1) < valid_count
    holder = jnp.where(valid, ids // p_count, -1)
    return (ids % p_count).astype(jnp.float32), holder.astype(jnp.float32)


def pack_kernel(p_count, query_ref, candidate_ref, count_ref, out_ref):
    _, q_count, slots = candidate_ref.shape
    _, _, q_tokens, depth = query_ref.shape
    tokens = q_count * q_tokens
    out_ref[:tokens] = query_ref[0].reshape(tokens, depth)
    planes = jnp.concatenate(split_ids(p_count, candidate_ref, count_ref), axis=0)
    empty = jnp.zeros((2 * q_count, depth - slots), jnp.float32)
    out_ref[tokens:] = jnp.concatenate([planes, empty], axis=1).astype(out_ref.dtype)


def pack(queries, candidates, counts, p_count):
    _, q_count, q_tokens, depth = queries.shape
    vmem = pl.BlockSpec(memory_space=pltpu.VMEM)
    return pl.pallas_call(
        functools.partial(pack_kernel, p_count),
        in_specs=[vmem, vmem, pl.BlockSpec(memory_space=pltpu.SMEM)],
        out_shape=jax.ShapeDtypeStruct((q_count * (q_tokens + 2), depth), queries.dtype),
        compiler_params=pltpu.CompilerParams(vmem_limit_bytes=4 * MIB),
        cost_estimate=pl.CostEstimate(
            flops=PACK_FLOPS, bytes_accessed=PACK_BYTES, transcendentals=0
        ),
        name="pack",
    )(in_hbm(queries), in_hbm(candidates), in_hbm(counts))


def memory_kernel(shards, slots, *refs):
    packed_refs, passage_ref = refs[:shards], refs[shards].at[0]
    out_refs = refs[shards + 1 : 2 * shards + 1]
    query_ref, rank_ref, best_ref, list_ref, scalar_ref, *refs = refs[2 * shards + 1 :]
    most_ref, rounds_ref, list_sems = refs
    q_count = out_refs[0].shape[0]
    p_count = passage_ref.shape[0]
    total, q_tokens, depth = query_ref.shape

    me = lax.axis_index("memory").astype(jnp.float32)
    keys = []
    for index, packed_ref in enumerate(packed_refs):
        tokens = packed_ref[: q_count * q_tokens].reshape(q_count, q_tokens, depth)
        query_ref[index * q_count : (index + 1) * q_count] = tokens
        planes = packed_ref[q_count * q_tokens :].astype(jnp.float32)
        local, holder = planes[:q_count], planes[q_count:]
        keys.append(jnp.where(holder == me, local, -1.0))
    keys = jnp.concatenate(keys, axis=0)
    passage = lax.broadcasted_iota(jnp.int32, (total, p_count), 1).astype(jnp.float32)
    named = jnp.zeros((total, p_count), jnp.float32)
    for slot in range(slots):
        named = jnp.where(keys[:, slot : slot + 1] == passage, 1.0, named)

    square = (total, total)
    earlier = lax.broadcasted_iota(jnp.int32, square, 1) < lax.broadcasted_iota(
        jnp.int32, square, 0
    )
    before = jnp.dot(
        earlier.astype(jnp.bfloat16),
        named.astype(jnp.bfloat16),
        preferred_element_type=jnp.float32,
    )
    rank_ref[...] = jnp.where(named > 0.0, before, -1.0)
    def left_over(first):
        left = jnp.where(rank_ref[...] == first, 1.0, 0.0)
        left = jnp.sum(left, axis=0, keepdims=True)
        square = (p_count, p_count)
        row = lax.broadcasted_iota(jnp.int32, square, 0).astype(jnp.float32)
        column = lax.broadcasted_iota(jnp.int32, square, 1).astype(jnp.float32)
        place = jnp.dot(left, (row < column).astype(jnp.float32), preferred_element_type=jnp.float32)
        mine = jnp.where((place == row) & (left > 0.0), column, 0.0)
        index = jnp.sum(mine, axis=1, keepdims=True)
        index = jnp.sum(jnp.where(row == column, index, 0.0), axis=0, keepdims=True)
        return [index, jnp.broadcast_to(jnp.sum(left, axis=1, keepdims=True), left.shape)]

    def write_list(first, extra):
        asker = lax.broadcasted_iota(jnp.int32, (total, p_count), 0).astype(jnp.float32)
        rank = rank_ref[...] - first
        rows = [
            jnp.sum(jnp.where(rank == float(slot), asker, 0.0), axis=0, keepdims=True)
            for slot in range(SLOTS)
        ]
        for slot, above in enumerate(extra):
            rows[slot] = rows[slot] + LOW * above
        list_ref[...] = jnp.concatenate(rows, axis=0).astype(jnp.int32)
        copy = pltpu.make_async_copy(list_ref, scalar_ref, list_sems.at[0])
        copy.start()
        return copy

    def unit(index):
        tokens = [query_ref[scalar_ref[slot, index] & (LOW - 1)] for slot in range(SLOTS)]
        return token_max(passage_ref[pl.ds(index, 1)], jnp.concatenate(tokens, axis=0))

    def add_scores(first, scores, sums):
        for index, out_ref in enumerate(out_refs):
            rank = rank_ref[index * q_count : (index + 1) * q_count] - first
            total_scores = scores[index]
            for slot in range(SLOTS):
                total_scores = jnp.where(rank == float(slot), sums[slot : slot + 1], total_scores)
            out_ref[...] = total_scores

    list_copy = write_list(0.0, [])
    counts = jnp.sum(named, axis=0, keepdims=True)
    most = jnp.broadcast_to(jnp.max(counts, axis=1, keepdims=True), most_ref.shape)
    most_ref[...] = most.astype(jnp.int32)
    most_copy = pltpu.make_async_copy(most_ref, rounds_ref, list_sems.at[1])
    most_copy.start()
    list_copy.wait()

    sums = []
    for first in range(0, p_count, HALF):
        rows = [unit(index) for index in range(first, first + HALF)]
        sums.append(token_sum(jnp.concatenate(rows, axis=0), SLOTS))

    most_copy.wait()
    rounds = (rounds_ref[0, 0] + SLOTS - 1) // SLOTS
    nothing = [jnp.zeros((q_count, p_count), jnp.float32)] * shards
    add_scores(0.0, nothing, jnp.concatenate(sums, axis=1))

    @pl.loop(1, rounds)
    def _(turn):
        done = (turn * SLOTS).astype(jnp.float32)
        write_list(done, left_over(done)).wait()

        @pl.loop(0, scalar_ref[1, 0] // LOW)
        def _(place):
            index = scalar_ref[0, place] // LOW
            best_ref[pl.ds(index, 1), :] = unit(index)

        scores = [out_ref[...] for out_ref in out_refs]
        add_scores(done, scores, token_sum(best_ref[...], SLOTS))


def score_memory(packed, memory, q_count, slots):
    shards = len(packed)
    q_tokens = packed[0].shape[0] // q_count - 2
    _, p_count, p_tokens, depth = memory.shape
    total = shards * q_count
    vmem = pl.BlockSpec(memory_space=pltpu.VMEM)
    return pl.pallas_call(
        functools.partial(memory_kernel, shards, slots),
        in_specs=[vmem] * (shards + 1),
        out_specs=[vmem] * shards,
        out_shape=[jax.ShapeDtypeStruct((q_count, p_count), jnp.float32)] * shards,
        scratch_shapes=[
            pltpu.VMEM((total, q_tokens, depth), memory.dtype),
            pltpu.VMEM((total, p_count), jnp.float32),
            pltpu.VMEM((p_count, SLOTS * q_tokens), jnp.float32),
            pltpu.VMEM((SLOTS, p_count), jnp.int32),
            pltpu.SMEM((SLOTS, p_count), jnp.int32),
            pltpu.VMEM((8, LANES), jnp.int32),
            pltpu.SMEM((8, LANES), jnp.int32),
            pltpu.SemaphoreType.DMA((2,)),
        ],
        compiler_params=pltpu.CompilerParams(vmem_limit_bytes=16 * MIB),
        cost_estimate=pl.CostEstimate(
            flops=2 * total * q_tokens * p_count * p_tokens * depth,
            bytes_accessed=2 * p_count * p_tokens * depth,
            transcendentals=0,
        ),
        name="score_memory",
    )(*packed, memory)


def batch_kernel(query_ref, *refs):
    passage_refs, (out_ref, best_ref) = refs[:-2], refs[-2:]
    _, queries, q_tokens, depth = query_ref.shape
    count = passage_refs[0].shape[1]
    tokens = query_ref[0].reshape(queries * q_tokens, depth)
    for chip, passage_ref in enumerate(passage_refs):
        best_ref[chip * count : (chip + 1) * count, :] = token_max(passage_ref[0], tokens)
    sums = token_sum(best_ref[...], queries)
    empty = jnp.zeros((queries, out_ref.shape[1] - sums.shape[1]), jnp.float32)
    out_ref[...] = jnp.concatenate([sums, empty], axis=1) if empty.size else sums


def score_batch(queries, positives):
    _, q_count, q_tokens, depth = queries.shape
    _, p_count, p_tokens, _ = positives[0].shape
    chips = len(positives)
    lanes = -(-chips * p_count // LANES) * LANES
    return pl.pallas_call(
        batch_kernel,
        out_shape=jax.ShapeDtypeStruct((q_count, lanes), jnp.float32),
        scratch_shapes=[pltpu.VMEM((chips * p_count, q_count * q_tokens), jnp.float32)],
        compiler_params=pltpu.CompilerParams(vmem_limit_bytes=16 * MIB),
        cost_estimate=pl.CostEstimate(
            flops=2 * chips * q_count * q_tokens * p_count * p_tokens * depth,
            bytes_accessed=2 * chips * p_count * p_tokens * depth,
            transcendentals=0,
        ),
        name="score_batch",
    )(queries, *positives)


def loss_kernel(shards, own_batch, mate_batch, *refs):
    memory_refs = refs[:shards]
    candidate_ref, count_ref, batch_ref, memory_ref, loss_ref = refs[shards:]
    group, shard = lax.axis_index("group"), lax.axis_index("memory")
    chip, core = group // 2, group % 2
    _, q_count, slots = candidate_ref.shape
    p_count = memory_refs[0].shape[1]
    columns = batch_ref.shape[2]

    parts = []
    for first in range(0, columns, LANES):
        lane = lax.broadcasted_iota(jnp.int32, (q_count, LANES), 1) + first
        owner = lane // q_count
        source = (((owner // 2) ^ chip) * q_count + lane % q_count) % LANES
        own = jnp.take_along_axis(own_batch[...], source, axis=1)
        mate = jnp.take_along_axis(mate_batch[...], source, axis=1)
        parts.append(jnp.where(owner % 2 == core, own, mate))
    batch = jnp.concatenate(parts, axis=1)[:, :columns]
    batch_ref[0] = batch

    ids = candidate_ref[0]
    padded = jnp.concatenate([ids, jnp.zeros((q_count, p_count - slots), jnp.int32)], axis=1)
    holder, local = padded // p_count, padded % p_count
    picked = jnp.zeros((q_count, p_count), jnp.float32)
    for step in range(shards):
        found = jnp.take_along_axis(memory_refs[-step][...], local, axis=1)
        picked = jnp.where(holder == (shard ^ step), found, picked)

    valid = lax.broadcasted_iota(jnp.int32, (q_count, p_count), 1) < column_of(count_ref[...])
    memory_ref[0] = jnp.where(valid, picked, 0.0)[:, :slots]

    top = jnp.maximum(
        jnp.max(batch, axis=1, keepdims=True),
        jnp.max(jnp.where(valid, picked, -jnp.inf), axis=1, keepdims=True),
    )
    total = jnp.sum(jnp.exp(batch - top), axis=1, keepdims=True) + jnp.sum(
        jnp.where(valid, jnp.exp(picked - top), 0.0), axis=1, keepdims=True
    )
    column = lax.broadcasted_iota(jnp.int32, batch.shape, 1)
    own = group * q_count + lax.broadcasted_iota(jnp.int32, batch.shape, 0)
    target_score = jnp.sum(jnp.where(column == own, batch, 0.0), axis=1, keepdims=True)
    loss_ref[...] = row_of(top + jnp.log(total) - target_score)


def finish(own_batch, mate_batch, memory_parts, candidates, counts, columns):
    _, q_count, slots = candidates.shape
    return pl.pallas_call(
        functools.partial(loss_kernel, len(memory_parts)),
        out_shape=[
            jax.ShapeDtypeStruct((1, q_count, columns), jnp.float32),
            jax.ShapeDtypeStruct((1, q_count, slots), jnp.float32),
            jax.ShapeDtypeStruct((1, q_count), jnp.float32),
        ],
        compiler_params=pltpu.CompilerParams(vmem_limit_bytes=4 * MIB),
        name="finish",
    )(own_batch, mate_batch, *memory_parts, candidates, counts)


def body(queries, positives, memory, candidates, counts):
    shards = lax.axis_size("memory")
    groups = lax.axis_size("group")
    chips = groups // 2
    q_count = queries.shape[1]
    slots = candidates.shape[2] // 2

    def to_shard(array, step):
        return lax.ppermute(array, "memory", [(i, i ^ step) for i in range(shards)])

    def to_group(array, step):
        return lax.ppermute(array, "group", [(i, i ^ step) for i in range(groups)])

    own = pack(queries, candidates, counts, memory.shape[1])
    packed = [own] + [to_shard(own, step) for step in range(1, shards)]
    sent_positives, sent_queries, _ = lax.optimization_barrier((positives, queries, own))
    row = [positives] + [to_group(sent_positives, 2 * step) for step in range(1, chips)]
    mate_queries = to_group(sent_queries, 1)

    scores = score_memory(packed, memory, q_count, slots)
    returned = [to_shard(scores[step], step) for step in range(shards - 1, 0, -1)]
    mate_queries, _ = lax.optimization_barrier((mate_queries, scores[0]))
    mate_scores = score_batch(mate_queries, row)
    mate_batch = to_group(mate_scores, 1)
    own_queries, _ = lax.optimization_barrier((queries, mate_scores))
    own_batch = score_batch(own_queries, row)
    columns = groups * q_count
    return finish(
        own_batch, mate_batch, [scores[0]] + returned, candidates, counts, columns
    )


def solution(mesh):
    in_specs = (
        P("group", "memory", None, None),
        P("group", "memory", None, None),
        P("group", "memory", None, None),
        P("group", "memory", None),
        P("group", "memory"),
    )
    out_specs = (P("group", "memory", None), P("group", "memory", None), P("group", "memory"))
    return jax.shard_map(body, mesh=mesh, in_specs=in_specs, out_specs=out_specs, check_vma=False)
```

```python
import functools

import jax
import jax.numpy as jnp
from jax import lax
from jax.experimental import pallas as pl
from jax.experimental.pallas import tpu as pltpu
from jax.sharding import PartitionSpec as P

LANES = 128
MIB = 1024 * 1024
SLOTS = 8
LOW = 256
UP, DOWN = 1, -1
PACK_FLOPS = 10**10
PACK_BYTES = 2**24


def in_hbm(array):
    return pltpu.with_memory_space_constraint(array, pltpu.HBM)


def token_max(passages, tokens):
    count, width, depth = passages.shape
    product = lax.dot_general(
        passages.reshape(count * width, depth),
        tokens,
        (((1,), (1,)), ((), ())),
        preferred_element_type=jnp.float32,
    )
    return jnp.max(product.reshape(count, width, tokens.shape[0]), axis=1)


def token_sum(best, queries):
    tokens = best.shape[1]
    per_query = tokens // queries
    row = lax.broadcasted_iota(jnp.int32, (queries, tokens), 0)
    col = lax.broadcasted_iota(jnp.int32, (queries, tokens), 1)
    own = (col // per_query == row).astype(jnp.bfloat16)
    high = best.astype(jnp.bfloat16)
    rest = best - high.astype(jnp.float32)
    middle = rest.astype(jnp.bfloat16)
    low = (rest - middle.astype(jnp.float32)).astype(jnp.bfloat16)
    return lax.dot_general(
        jnp.concatenate([own] * 3, axis=1),
        jnp.concatenate([high, middle, low], axis=1),
        (((1,), (1,)), ((), ())),
        preferred_element_type=jnp.float32,
    )


def column_of(row):
    size = row.shape[1]
    square = (size, size)
    diagonal = lax.broadcasted_iota(jnp.int32, square, 0) == lax.broadcasted_iota(
        jnp.int32, square, 1
    )
    return jnp.sum(jnp.where(diagonal, jnp.broadcast_to(row, square), 0), axis=1, keepdims=True)


def row_of(column):
    size = column.shape[0]
    square = (size, size)
    diagonal = lax.broadcasted_iota(jnp.int32, square, 0) == lax.broadcasted_iota(
        jnp.int32, square, 1
    )
    return jnp.sum(jnp.where(diagonal, jnp.broadcast_to(column, square), 0), axis=0, keepdims=True)


def split_ids(p_count, candidate_ref, count_ref):
    ids = candidate_ref[0]
    row = lax.broadcasted_iota(jnp.int32, ids.shape, 0)
    valid_count = jnp.zeros(ids.shape, jnp.int32)
    for index in range(ids.shape[0]):
        valid_count = jnp.where(row == index, count_ref[0, index], valid_count)
    valid = lax.broadcasted_iota(jnp.int32, ids.shape, 1) < valid_count
    holder = jnp.where(valid, ids // p_count, -1)
    return (ids % p_count).astype(jnp.float32), holder.astype(jnp.float32)


def pack_kernel(p_count, query_ref, candidate_ref, count_ref, out_ref):
    _, q_count, slots = candidate_ref.shape
    _, _, q_tokens, depth = query_ref.shape
    tokens = q_count * q_tokens
    out_ref[:tokens] = query_ref[0].reshape(tokens, depth)
    planes = jnp.concatenate(split_ids(p_count, candidate_ref, count_ref), axis=0)
    empty = jnp.zeros((2 * q_count, depth - slots), jnp.float32)
    out_ref[tokens:] = jnp.concatenate([planes, empty], axis=1).astype(out_ref.dtype)


def pack(queries, candidates, counts, p_count):
    _, q_count, q_tokens, depth = queries.shape
    vmem = pl.BlockSpec(memory_space=pltpu.VMEM)
    return pl.pallas_call(
        functools.partial(pack_kernel, p_count),
        in_specs=[vmem, vmem, pl.BlockSpec(memory_space=pltpu.SMEM)],
        out_shape=jax.ShapeDtypeStruct((q_count * (q_tokens + 2), depth), queries.dtype),
        compiler_params=pltpu.CompilerParams(vmem_limit_bytes=4 * MIB),
        cost_estimate=pl.CostEstimate(
            flops=PACK_FLOPS, bytes_accessed=PACK_BYTES, transcendentals=0
        ),
        name="pack",
    )(in_hbm(queries), in_hbm(candidates), in_hbm(counts))


def memory_kernel(shards, slots, *refs):
    packed_refs, passage_ref = refs[shards - 1 :: -1], refs[shards].at[0]
    out_refs = refs[shards + 1 : 2 * shards + 1]
    query_ref, rank_ref, best_ref, list_ref, scalar_ref, *refs = refs[2 * shards + 1 :]
    most_ref, rounds_ref, list_sems = refs
    q_count = out_refs[0].shape[0]
    p_count = passage_ref.shape[0]
    total, q_tokens, depth = query_ref.shape

    me = lax.axis_index("memory").astype(jnp.float32)
    keys = []
    for index, packed_ref in enumerate(packed_refs):
        tokens = packed_ref[: q_count * q_tokens].reshape(q_count, q_tokens, depth)
        query_ref[index * q_count : (index + 1) * q_count] = tokens
        planes = packed_ref[q_count * q_tokens :].astype(jnp.float32)
        local, holder = planes[:q_count], planes[q_count:]
        keys.append(jnp.where(holder == me, local, -1.0))
    keys = jnp.concatenate(keys, axis=0)
    passage = lax.broadcasted_iota(jnp.int32, (total, p_count), 1).astype(jnp.float32)
    named = jnp.zeros((total, p_count), jnp.float32)
    for slot in range(slots):
        named = jnp.where(keys[:, slot : slot + 1] == passage, 1.0, named)

    square = (total, total)
    earlier = lax.broadcasted_iota(jnp.int32, square, 1) < lax.broadcasted_iota(
        jnp.int32, square, 0
    )
    before = jnp.dot(
        earlier.astype(jnp.bfloat16),
        named.astype(jnp.bfloat16),
        preferred_element_type=jnp.float32,
    )
    rank_ref[...] = jnp.where(named > 0.0, before, -1.0)
    def left_over(first):
        left = jnp.where(rank_ref[...] == first, 1.0, 0.0)
        left = jnp.sum(left, axis=0, keepdims=True)
        square = (p_count, p_count)
        row = lax.broadcasted_iota(jnp.int32, square, 0).astype(jnp.float32)
        column = lax.broadcasted_iota(jnp.int32, square, 1).astype(jnp.float32)
        place = jnp.dot(left, (row < column).astype(jnp.float32), preferred_element_type=jnp.float32)
        mine = jnp.where((place == row) & (left > 0.0), column, 0.0)
        index = jnp.sum(mine, axis=1, keepdims=True)
        index = jnp.sum(jnp.where(row == column, index, 0.0), axis=0, keepdims=True)
        return [index, jnp.broadcast_to(jnp.sum(left, axis=1, keepdims=True), left.shape)]

    def write_list(first, extra):
        asker = lax.broadcasted_iota(jnp.int32, (total, p_count), 0).astype(jnp.float32)
        rank = rank_ref[...] - first
        rows = [
            jnp.sum(jnp.where(rank == float(slot), asker, 0.0), axis=0, keepdims=True)
            for slot in range(SLOTS)
        ]
        for slot, above in enumerate(extra):
            rows[slot] = rows[slot] + LOW * above
        list_ref[...] = jnp.concatenate(rows, axis=0).astype(jnp.int32)
        copy = pltpu.make_async_copy(list_ref, scalar_ref, list_sems.at[0])
        copy.start()
        return copy

    def unit(index):
        tokens = [query_ref[scalar_ref[slot, index] & (LOW - 1)] for slot in range(SLOTS)]
        return token_max(passage_ref[pl.ds(index, 1)], jnp.concatenate(tokens, axis=0))

    def add_scores(first, scores):
        sums = token_sum(best_ref[...], SLOTS)
        for index, out_ref in enumerate(out_refs):
            rank = rank_ref[index * q_count : (index + 1) * q_count] - first
            total_scores = scores[index]
            for slot in range(SLOTS):
                total_scores = jnp.where(rank == float(slot), sums[slot : slot + 1], total_scores)
            out_ref[...] = total_scores

    list_copy = write_list(0.0, [])
    counts = jnp.sum(named, axis=0, keepdims=True)
    most = jnp.broadcast_to(jnp.max(counts, axis=1, keepdims=True), most_ref.shape)
    most_ref[...] = most.astype(jnp.int32)
    most_copy = pltpu.make_async_copy(most_ref, rounds_ref, list_sems.at[1])
    most_copy.start()
    list_copy.wait()

    for first in range(0, p_count, 8):
        rows = [unit(first + offset) for offset in range(8)]
        best_ref[first : first + 8, :] = jnp.concatenate(rows, axis=0)

    most_copy.wait()
    rounds = (rounds_ref[0, 0] + SLOTS - 1) // SLOTS
    add_scores(0.0, [jnp.zeros((q_count, p_count), jnp.float32)] * shards)

    @pl.loop(1, rounds)
    def _(turn):
        done = (turn * SLOTS).astype(jnp.float32)
        write_list(done, left_over(done)).wait()

        @pl.loop(0, scalar_ref[1, 0] // LOW)
        def _(place):
            index = scalar_ref[0, place] // LOW
            best_ref[pl.ds(index, 1), :] = unit(index)

        add_scores(done, [out_ref[...] for out_ref in out_refs])


def score_memory(packed, memory, q_count, slots):
    shards = len(packed)
    q_tokens = packed[0].shape[0] // q_count - 2
    _, p_count, p_tokens, depth = memory.shape
    total = shards * q_count
    vmem = pl.BlockSpec(memory_space=pltpu.VMEM)
    return pl.pallas_call(
        functools.partial(memory_kernel, shards, slots),
        in_specs=[vmem] * (shards + 1),
        out_specs=[vmem] * shards,
        out_shape=[jax.ShapeDtypeStruct((q_count, p_count), jnp.float32)] * shards,
        scratch_shapes=[
            pltpu.VMEM((total, q_tokens, depth), memory.dtype),
            pltpu.VMEM((total, p_count), jnp.float32),
            pltpu.VMEM((p_count, SLOTS * q_tokens), jnp.float32),
            pltpu.VMEM((SLOTS, p_count), jnp.int32),
            pltpu.SMEM((SLOTS, p_count), jnp.int32),
            pltpu.VMEM((8, LANES), jnp.int32),
            pltpu.SMEM((8, LANES), jnp.int32),
            pltpu.SemaphoreType.DMA((2,)),
        ],
        compiler_params=pltpu.CompilerParams(vmem_limit_bytes=16 * MIB),
        cost_estimate=pl.CostEstimate(
            flops=2 * total * q_tokens * p_count * p_tokens * depth,
            bytes_accessed=2 * p_count * p_tokens * depth,
            transcendentals=0,
        ),
        name="score_memory",
    )(*packed, memory)


def batch_kernel(query_ref, *refs):
    passage_refs, (out_ref, best_ref) = refs[:-2], refs[-2:]
    _, queries, q_tokens, depth = query_ref.shape
    count = passage_refs[0].shape[1]
    tokens = query_ref[0].reshape(queries * q_tokens, depth)
    for chip, passage_ref in enumerate(passage_refs):
        best_ref[chip * count : (chip + 1) * count, :] = token_max(passage_ref[0], tokens)
    sums = token_sum(best_ref[...], queries)
    empty = jnp.zeros((queries, out_ref.shape[1] - sums.shape[1]), jnp.float32)
    out_ref[...] = jnp.concatenate([sums, empty], axis=1) if empty.size else sums


def score_batch(queries, positives):
    _, q_count, q_tokens, depth = queries.shape
    _, p_count, p_tokens, _ = positives[0].shape
    chips = len(positives)
    lanes = -(-chips * p_count // LANES) * LANES
    return pl.pallas_call(
        batch_kernel,
        out_shape=jax.ShapeDtypeStruct((q_count, lanes), jnp.float32),
        scratch_shapes=[pltpu.VMEM((chips * p_count, q_count * q_tokens), jnp.float32)],
        compiler_params=pltpu.CompilerParams(vmem_limit_bytes=16 * MIB),
        cost_estimate=pl.CostEstimate(
            flops=2 * chips * q_count * q_tokens * p_count * p_tokens * depth,
            bytes_accessed=2 * chips * p_count * p_tokens * depth,
            transcendentals=0,
        ),
        name="score_batch",
    )(queries, *positives)


def loss_kernel(shards, own_batch, mate_batch, *refs):
    group, shard = lax.axis_index("group"), lax.axis_index("memory")
    far = shards - 2
    memory_parts = [refs[0][...], refs[1 + far][...]]
    for step in range(2, shards):
        down_ref, up_ref = refs[step - 1], refs[step + far]
        memory_parts.append(jnp.where(shard < (shard ^ step), down_ref[...], up_ref[...]))
    candidate_ref, count_ref, batch_ref, memory_ref, loss_ref = refs[2 + 2 * far :]
    chip, core = group // 2, group % 2
    _, q_count, slots = candidate_ref.shape
    p_count = memory_parts[0].shape[1]
    columns = batch_ref.shape[2]

    parts = []
    for first in range(0, columns, LANES):
        lane = lax.broadcasted_iota(jnp.int32, (q_count, LANES), 1) + first
        owner = lane // q_count
        source = (((owner // 2) ^ chip) * q_count + lane % q_count) % LANES
        own = jnp.take_along_axis(own_batch[...], source, axis=1)
        mate = jnp.take_along_axis(mate_batch[...], source, axis=1)
        parts.append(jnp.where(owner % 2 == core, own, mate))
    batch = jnp.concatenate(parts, axis=1)[:, :columns]
    batch_ref[0] = batch

    ids = candidate_ref[0]
    padded = jnp.concatenate([ids, jnp.zeros((q_count, p_count - slots), jnp.int32)], axis=1)
    holder, local = padded // p_count, padded % p_count
    picked = jnp.zeros((q_count, p_count), jnp.float32)
    for step in range(shards):
        found = jnp.take_along_axis(memory_parts[step], local, axis=1)
        picked = jnp.where(holder == (shard ^ step), found, picked)

    valid = lax.broadcasted_iota(jnp.int32, (q_count, p_count), 1) < column_of(count_ref[...])
    memory_ref[0] = jnp.where(valid, picked, 0.0)[:, :slots]

    top = jnp.maximum(
        jnp.max(batch, axis=1, keepdims=True),
        jnp.max(jnp.where(valid, picked, -jnp.inf), axis=1, keepdims=True),
    )
    total = jnp.sum(jnp.exp(batch - top), axis=1, keepdims=True) + jnp.sum(
        jnp.where(valid, jnp.exp(picked - top), 0.0), axis=1, keepdims=True
    )
    column = lax.broadcasted_iota(jnp.int32, batch.shape, 1)
    own = group * q_count + lax.broadcasted_iota(jnp.int32, batch.shape, 0)
    target_score = jnp.sum(jnp.where(column == own, batch, 0.0), axis=1, keepdims=True)
    loss_ref[...] = row_of(top + jnp.log(total) - target_score)


def finish(own_batch, mate_batch, memory_parts, candidates, counts, columns):
    _, q_count, slots = candidates.shape
    return pl.pallas_call(
        functools.partial(loss_kernel, len(memory_parts) // 2 + 1),
        out_shape=[
            jax.ShapeDtypeStruct((1, q_count, columns), jnp.float32),
            jax.ShapeDtypeStruct((1, q_count, slots), jnp.float32),
            jax.ShapeDtypeStruct((1, q_count), jnp.float32),
        ],
        compiler_params=pltpu.CompilerParams(vmem_limit_bytes=4 * MIB),
        name="finish",
    )(own_batch, mate_batch, *memory_parts, candidates, counts)


def body(queries, positives, memory, candidates, counts):
    shards = lax.axis_size("memory")
    groups = lax.axis_size("group")
    chips = groups // 2
    q_count = queries.shape[1]
    slots = candidates.shape[2] // 2

    def to_shard(array, step, way=0):
        pairs = [(i, i ^ step) for i in range(shards)]
        pairs = [(i, j) for i, j in pairs if way == 0 or way * (j - i) > 0]
        return lax.ppermute(array, "memory", pairs)

    def to_group(array, step):
        return lax.ppermute(array, "group", [(i, i ^ step) for i in range(groups)])

    own = pack(queries, candidates, counts, memory.shape[1])
    packed = [to_shard(own, step) for step in range(shards - 1, 0, -1)] + [own]
    sent_positives, sent_queries, _ = lax.optimization_barrier((positives, queries, own))
    row = [positives] + [to_group(sent_positives, 2 * step) for step in range(1, chips)]
    mate_queries = to_group(sent_queries, 1)

    scores = score_memory(packed, memory, q_count, slots)
    returned = [to_shard(scores[step], step, DOWN) for step in range(2, shards)]
    later, returned = lax.optimization_barrier((scores, returned))
    returned = [*returned, to_shard(scores[1], 1)]
    returned += [to_shard(later[step], step, UP) for step in range(2, shards)]
    mate_queries, _ = lax.optimization_barrier((mate_queries, scores[0]))
    mate_scores = score_batch(mate_queries, row)
    mate_batch = to_group(mate_scores, 1)
    own_queries, _ = lax.optimization_barrier((queries, mate_scores))
    own_batch = score_batch(own_queries, row)
    columns = groups * q_count
    return finish(
        own_batch, mate_batch, [scores[0]] + returned, candidates, counts, columns
    )


def solution(mesh):
    in_specs = (
        P("group", "memory", None, None),
        P("group", "memory", None, None),
        P("group", "memory", None, None),
        P("group", "memory", None),
        P("group", "memory"),
    )
    out_specs = (P("group", "memory", None), P("group", "memory", None), P("group", "memory"))
    return jax.shard_map(body, mesh=mesh, in_specs=in_specs, out_specs=out_specs, check_vma=False)
```

```python
import functools

import jax
import jax.numpy as jnp
from jax import lax
from jax.experimental import pallas as pl
from jax.experimental.pallas import tpu as pltpu
from jax.sharding import PartitionSpec as P

LANES = 128
MIB = 1024 * 1024
SLOTS = 8
LOW = 256
PACK_FLOPS = 10**10
PACK_BYTES = 2**24


def in_hbm(array):
    return pltpu.with_memory_space_constraint(array, pltpu.HBM)


def token_max(passages, tokens):
    count, width, depth = passages.shape
    product = lax.dot_general(
        passages.reshape(count * width, depth),
        tokens,
        (((1,), (1,)), ((), ())),
        preferred_element_type=jnp.float32,
    )
    return jnp.max(product.reshape(count, width, tokens.shape[0]), axis=1)


def token_sum(best, queries):
    tokens = best.shape[1]
    per_query = tokens // queries
    row = lax.broadcasted_iota(jnp.int32, (queries, tokens), 0)
    col = lax.broadcasted_iota(jnp.int32, (queries, tokens), 1)
    own = (col // per_query == row).astype(jnp.bfloat16)
    high = best.astype(jnp.bfloat16)
    rest = best - high.astype(jnp.float32)
    middle = rest.astype(jnp.bfloat16)
    low = (rest - middle.astype(jnp.float32)).astype(jnp.bfloat16)
    return lax.dot_general(
        jnp.concatenate([own] * 3, axis=1),
        jnp.concatenate([high, middle, low], axis=1),
        (((1,), (1,)), ((), ())),
        preferred_element_type=jnp.float32,
    )


def column_of(row):
    size = row.shape[1]
    square = (size, size)
    diagonal = lax.broadcasted_iota(jnp.int32, square, 0) == lax.broadcasted_iota(
        jnp.int32, square, 1
    )
    return jnp.sum(jnp.where(diagonal, jnp.broadcast_to(row, square), 0), axis=1, keepdims=True)


def row_of(column):
    size = column.shape[0]
    square = (size, size)
    diagonal = lax.broadcasted_iota(jnp.int32, square, 0) == lax.broadcasted_iota(
        jnp.int32, square, 1
    )
    return jnp.sum(jnp.where(diagonal, jnp.broadcast_to(column, square), 0), axis=0, keepdims=True)


def split_ids(p_count, candidate_ref, count_ref):
    ids = candidate_ref[0]
    row = lax.broadcasted_iota(jnp.int32, ids.shape, 0)
    valid_count = jnp.zeros(ids.shape, jnp.int32)
    for index in range(ids.shape[0]):
        valid_count = jnp.where(row == index, count_ref[0, index], valid_count)
    valid = lax.broadcasted_iota(jnp.int32, ids.shape, 1) < valid_count
    holder = jnp.where(valid, ids // p_count, -1)
    return (ids % p_count).astype(jnp.float32), holder.astype(jnp.float32)


def pack_kernel(p_count, query_ref, candidate_ref, count_ref, out_ref):
    _, q_count, slots = candidate_ref.shape
    _, _, q_tokens, depth = query_ref.shape
    tokens = q_count * q_tokens
    out_ref[:tokens] = query_ref[0].reshape(tokens, depth)
    planes = jnp.concatenate(split_ids(p_count, candidate_ref, count_ref), axis=0)
    empty = jnp.zeros((2 * q_count, depth - slots), jnp.float32)
    out_ref[tokens:] = jnp.concatenate([planes, empty], axis=1).astype(out_ref.dtype)


def pack(queries, candidates, counts, p_count):
    _, q_count, q_tokens, depth = queries.shape
    vmem = pl.BlockSpec(memory_space=pltpu.VMEM)
    return pl.pallas_call(
        functools.partial(pack_kernel, p_count),
        in_specs=[vmem, vmem, pl.BlockSpec(memory_space=pltpu.SMEM)],
        out_shape=jax.ShapeDtypeStruct((q_count * (q_tokens + 2), depth), queries.dtype),
        compiler_params=pltpu.CompilerParams(vmem_limit_bytes=4 * MIB),
        cost_estimate=pl.CostEstimate(
            flops=PACK_FLOPS, bytes_accessed=PACK_BYTES, transcendentals=0
        ),
        name="pack",
    )(in_hbm(queries), in_hbm(candidates), in_hbm(counts))


def memory_kernel(shards, slots, *refs):
    packed_refs, passage_ref = refs[:shards], refs[shards].at[0]
    out_refs = refs[shards + 1 : 2 * shards + 1]
    query_ref, rank_ref, best_ref, list_ref, scalar_ref, *refs = refs[2 * shards + 1 :]
    most_ref, rounds_ref, list_sems = refs
    q_count = out_refs[0].shape[0]
    p_count = passage_ref.shape[0]
    total, q_tokens, depth = query_ref.shape

    me = lax.axis_index("memory").astype(jnp.float32)
    keys = []
    for packed_ref in packed_refs:
        planes = packed_ref[q_count * q_tokens :].astype(jnp.float32)
        local, holder = planes[:q_count], planes[q_count:]
        keys.append(jnp.where(holder == me, local, -1.0))
    keys = jnp.concatenate(keys, axis=0)
    passage = lax.broadcasted_iota(jnp.int32, (total, p_count), 1).astype(jnp.float32)
    named = jnp.zeros((total, p_count), jnp.float32)
    for slot in range(slots):
        named = jnp.where(keys[:, slot : slot + 1] == passage, 1.0, named)

    square = (total, total)
    earlier = lax.broadcasted_iota(jnp.int32, square, 1) < lax.broadcasted_iota(
        jnp.int32, square, 0
    )
    before = jnp.dot(
        earlier.astype(jnp.bfloat16),
        named.astype(jnp.bfloat16),
        preferred_element_type=jnp.float32,
    )
    rank_ref[...] = jnp.where(named > 0.0, before, -1.0)
    def left_over(first):
        left = jnp.where(rank_ref[...] == first, 1.0, 0.0)
        left = jnp.sum(left, axis=0, keepdims=True)
        square = (p_count, p_count)
        row = lax.broadcasted_iota(jnp.int32, square, 0).astype(jnp.float32)
        column = lax.broadcasted_iota(jnp.int32, square, 1).astype(jnp.float32)
        place = jnp.dot(left, (row < column).astype(jnp.float32), preferred_element_type=jnp.float32)
        mine = jnp.where((place == row) & (left > 0.0), column, 0.0)
        index = jnp.sum(mine, axis=1, keepdims=True)
        index = jnp.sum(jnp.where(row == column, index, 0.0), axis=0, keepdims=True)
        return [index, jnp.broadcast_to(jnp.sum(left, axis=1, keepdims=True), left.shape)]

    def write_list(first, extra):
        asker = lax.broadcasted_iota(jnp.int32, (total, p_count), 0).astype(jnp.float32)
        rank = rank_ref[...] - first
        rows = [
            jnp.sum(jnp.where(rank == float(slot), asker, 0.0), axis=0, keepdims=True)
            for slot in range(SLOTS)
        ]
        for slot, above in enumerate(extra):
            rows[slot] = rows[slot] + LOW * above
        list_ref[...] = jnp.concatenate(rows, axis=0).astype(jnp.int32)
        copy = pltpu.make_async_copy(list_ref, scalar_ref, list_sems.at[0])
        copy.start()
        return copy

    def unit(index):
        tokens = [query_ref[scalar_ref[slot, index] & (LOW - 1)] for slot in range(SLOTS)]
        return token_max(passage_ref[pl.ds(index, 1)], jnp.concatenate(tokens, axis=0))

    def add_scores(first, scores):
        sums = token_sum(best_ref[...], SLOTS)
        for index, out_ref in enumerate(out_refs):
            rank = rank_ref[index * q_count : (index + 1) * q_count] - first
            total_scores = scores[index]
            for slot in range(SLOTS):
                total_scores = jnp.where(rank == float(slot), sums[slot : slot + 1], total_scores)
            out_ref[...] = total_scores

    list_copy = write_list(0.0, [])
    for index, packed_ref in enumerate(packed_refs):
        tokens = packed_ref[: q_count * q_tokens].reshape(q_count, q_tokens, depth)
        query_ref[index * q_count : (index + 1) * q_count] = tokens
    counts = jnp.sum(named, axis=0, keepdims=True)
    most = jnp.broadcast_to(jnp.max(counts, axis=1, keepdims=True), most_ref.shape)
    most_ref[...] = most.astype(jnp.int32)
    most_copy = pltpu.make_async_copy(most_ref, rounds_ref, list_sems.at[1])
    most_copy.start()
    list_copy.wait()

    for first in range(0, p_count, 8):
        rows = [unit(first + offset) for offset in range(8)]
        best_ref[first : first + 8, :] = jnp.concatenate(rows, axis=0)

    most_copy.wait()
    rounds = (rounds_ref[0, 0] + SLOTS - 1) // SLOTS
    add_scores(0.0, [jnp.zeros((q_count, p_count), jnp.float32)] * shards)

    @pl.loop(1, rounds)
    def _(turn):
        done = (turn * SLOTS).astype(jnp.float32)
        write_list(done, left_over(done)).wait()

        @pl.loop(0, scalar_ref[1, 0] // LOW)
        def _(place):
            index = scalar_ref[0, place] // LOW
            best_ref[pl.ds(index, 1), :] = unit(index)

        add_scores(done, [out_ref[...] for out_ref in out_refs])


def score_memory(packed, memory, q_count, slots):
    shards = len(packed)
    q_tokens = packed[0].shape[0] // q_count - 2
    _, p_count, p_tokens, depth = memory.shape
    total = shards * q_count
    vmem = pl.BlockSpec(memory_space=pltpu.VMEM)
    return pl.pallas_call(
        functools.partial(memory_kernel, shards, slots),
        in_specs=[vmem] * (shards + 1),
        out_specs=[vmem] * shards,
        out_shape=[jax.ShapeDtypeStruct((q_count, p_count), jnp.float32)] * shards,
        scratch_shapes=[
            pltpu.VMEM((total, q_tokens, depth), memory.dtype),
            pltpu.VMEM((total, p_count), jnp.float32),
            pltpu.VMEM((p_count, SLOTS * q_tokens), jnp.float32),
            pltpu.VMEM((SLOTS, p_count), jnp.int32),
            pltpu.SMEM((SLOTS, p_count), jnp.int32),
            pltpu.VMEM((8, LANES), jnp.int32),
            pltpu.SMEM((8, LANES), jnp.int32),
            pltpu.SemaphoreType.DMA((2,)),
        ],
        compiler_params=pltpu.CompilerParams(vmem_limit_bytes=16 * MIB),
        cost_estimate=pl.CostEstimate(
            flops=2 * total * q_tokens * p_count * p_tokens * depth,
            bytes_accessed=2 * p_count * p_tokens * depth,
            transcendentals=0,
        ),
        name="score_memory",
    )(*packed, memory)


def batch_kernel(query_ref, *refs):
    passage_refs, (out_ref, best_ref) = refs[:-2], refs[-2:]
    _, queries, q_tokens, depth = query_ref.shape
    count = passage_refs[0].shape[1]
    tokens = query_ref[0].reshape(queries * q_tokens, depth)
    for chip, passage_ref in enumerate(passage_refs):
        rows = [token_max(passage_ref[0, index : index + 1], tokens) for index in range(count)]
        best_ref[chip * count : (chip + 1) * count, :] = jnp.concatenate(rows, axis=0)
    sums = token_sum(best_ref[...], queries)
    empty = jnp.zeros((queries, out_ref.shape[1] - sums.shape[1]), jnp.float32)
    out_ref[...] = jnp.concatenate([sums, empty], axis=1) if empty.size else sums


def score_batch(queries, positives):
    _, q_count, q_tokens, depth = queries.shape
    _, p_count, p_tokens, _ = positives[0].shape
    chips = len(positives)
    lanes = -(-chips * p_count // LANES) * LANES
    return pl.pallas_call(
        batch_kernel,
        out_shape=jax.ShapeDtypeStruct((q_count, lanes), jnp.float32),
        scratch_shapes=[pltpu.VMEM((chips * p_count, q_count * q_tokens), jnp.float32)],
        compiler_params=pltpu.CompilerParams(vmem_limit_bytes=16 * MIB),
        cost_estimate=pl.CostEstimate(
            flops=2 * chips * q_count * q_tokens * p_count * p_tokens * depth,
            bytes_accessed=2 * chips * p_count * p_tokens * depth,
            transcendentals=0,
        ),
        name="score_batch",
    )(queries, *positives)


def loss_kernel(shards, own_batch, mate_batch, *refs):
    memory_refs = refs[:shards]
    candidate_ref, count_ref, batch_ref, memory_ref, loss_ref = refs[shards:]
    group, shard = lax.axis_index("group"), lax.axis_index("memory")
    chip, core = group // 2, group % 2
    _, q_count, slots = candidate_ref.shape
    p_count = memory_refs[0].shape[1]
    columns = batch_ref.shape[2]

    parts = []
    for first in range(0, columns, LANES):
        lane = lax.broadcasted_iota(jnp.int32, (q_count, LANES), 1) + first
        owner = lane // q_count
        source = (((owner // 2) ^ chip) * q_count + lane % q_count) % LANES
        own = jnp.take_along_axis(own_batch[...], source, axis=1)
        mate = jnp.take_along_axis(mate_batch[...], source, axis=1)
        parts.append(jnp.where(owner % 2 == core, own, mate))
    batch = jnp.concatenate(parts, axis=1)[:, :columns]
    batch_ref[0] = batch

    ids = candidate_ref[0]
    padded = jnp.concatenate([ids, jnp.zeros((q_count, p_count - slots), jnp.int32)], axis=1)
    holder, local = padded // p_count, padded % p_count
    picked = jnp.zeros((q_count, p_count), jnp.float32)
    for step in range(shards):
        found = jnp.take_along_axis(memory_refs[-step][...], local, axis=1)
        picked = jnp.where(holder == (shard ^ step), found, picked)

    valid = lax.broadcasted_iota(jnp.int32, (q_count, p_count), 1) < column_of(count_ref[...])
    memory_ref[0] = jnp.where(valid, picked, 0.0)[:, :slots]

    top = jnp.maximum(
        jnp.max(batch, axis=1, keepdims=True),
        jnp.max(jnp.where(valid, picked, -jnp.inf), axis=1, keepdims=True),
    )
    total = jnp.sum(jnp.exp(batch - top), axis=1, keepdims=True) + jnp.sum(
        jnp.where(valid, jnp.exp(picked - top), 0.0), axis=1, keepdims=True
    )
    column = lax.broadcasted_iota(jnp.int32, batch.shape, 1)
    own = group * q_count + lax.broadcasted_iota(jnp.int32, batch.shape, 0)
    target_score = jnp.sum(jnp.where(column == own, batch, 0.0), axis=1, keepdims=True)
    loss_ref[...] = row_of(top + jnp.log(total) - target_score)


def finish(own_batch, mate_batch, memory_parts, candidates, counts, columns):
    _, q_count, slots = candidates.shape
    return pl.pallas_call(
        functools.partial(loss_kernel, len(memory_parts)),
        out_shape=[
            jax.ShapeDtypeStruct((1, q_count, columns), jnp.float32),
            jax.ShapeDtypeStruct((1, q_count, slots), jnp.float32),
            jax.ShapeDtypeStruct((1, q_count), jnp.float32),
        ],
        compiler_params=pltpu.CompilerParams(vmem_limit_bytes=4 * MIB),
        name="finish",
    )(own_batch, mate_batch, *memory_parts, candidates, counts)


def body(queries, positives, memory, candidates, counts):
    shards = lax.axis_size("memory")
    groups = lax.axis_size("group")
    chips = groups // 2
    q_count = queries.shape[1]
    slots = candidates.shape[2] // 2

    def to_shard(array, step):
        return lax.ppermute(array, "memory", [(i, i ^ step) for i in range(shards)])

    def to_group(array, step):
        return lax.ppermute(array, "group", [(i, i ^ step) for i in range(groups)])

    own = pack(queries, candidates, counts, memory.shape[1])
    packed = [own] + [to_shard(own, step) for step in range(1, shards)]
    sent_positives, sent_queries, _ = lax.optimization_barrier((positives, queries, own))
    row = [positives] + [to_group(sent_positives, 2 * step) for step in range(1, chips)]
    mate_queries = to_group(sent_queries, 1)

    scores = score_memory(packed, memory, q_count, slots)
    returned = [to_shard(scores[step], step) for step in range(shards - 1, 0, -1)]
    mate_queries, _ = lax.optimization_barrier((mate_queries, scores[0]))
    mate_scores = score_batch(mate_queries, row)
    mate_batch = to_group(mate_scores, 1)
    own_queries, _ = lax.optimization_barrier((queries, mate_scores))
    own_batch = score_batch(own_queries, row)
    columns = groups * q_count
    return finish(
        own_batch, mate_batch, [scores[0]] + returned, candidates, counts, columns
    )


def solution(mesh):
    in_specs = (
        P("group", "memory", None, None),
        P("group", "memory", None, None),
        P("group", "memory", None, None),
        P("group", "memory", None),
        P("group", "memory"),
    )
    out_specs = (P("group", "memory", None), P("group", "memory", None), P("group", "memory"))
    return jax.shard_map(body, mesh=mesh, in_specs=in_specs, out_specs=out_specs, check_vma=False)
```

```python
import functools

import jax
import jax.numpy as jnp
from jax import lax
from jax.experimental import pallas as pl
from jax.experimental.pallas import tpu as pltpu
from jax.sharding import PartitionSpec as P

LANES = 128
MIB = 1024 * 1024
SLOTS = 8
LOW = 256
PACK_FLOPS = 10**10
PACK_BYTES = 2**24


def in_hbm(array):
    return pltpu.with_memory_space_constraint(array, pltpu.HBM)


def token_max(passages, tokens):
    count, width, depth = passages.shape
    product = lax.dot_general(
        passages.reshape(count * width, depth),
        tokens,
        (((1,), (1,)), ((), ())),
        preferred_element_type=jnp.float32,
    )
    return jnp.max(product.reshape(count, width, tokens.shape[0]), axis=1)


def token_sum(best, queries):
    tokens = best.shape[1]
    per_query = tokens // queries
    row = lax.broadcasted_iota(jnp.int32, (queries, tokens), 0)
    col = lax.broadcasted_iota(jnp.int32, (queries, tokens), 1)
    own = (col // per_query == row).astype(jnp.bfloat16)
    high = best.astype(jnp.bfloat16)
    rest = best - high.astype(jnp.float32)
    middle = rest.astype(jnp.bfloat16)
    low = (rest - middle.astype(jnp.float32)).astype(jnp.bfloat16)
    return lax.dot_general(
        jnp.concatenate([own] * 3, axis=1),
        jnp.concatenate([high, middle, low], axis=1),
        (((1,), (1,)), ((), ())),
        preferred_element_type=jnp.float32,
    )


def column_of(row):
    size = row.shape[1]
    square = (size, size)
    diagonal = lax.broadcasted_iota(jnp.int32, square, 0) == lax.broadcasted_iota(
        jnp.int32, square, 1
    )
    return jnp.sum(jnp.where(diagonal, jnp.broadcast_to(row, square), 0), axis=1, keepdims=True)


def row_of(column):
    size = column.shape[0]
    square = (size, size)
    diagonal = lax.broadcasted_iota(jnp.int32, square, 0) == lax.broadcasted_iota(
        jnp.int32, square, 1
    )
    return jnp.sum(jnp.where(diagonal, jnp.broadcast_to(column, square), 0), axis=0, keepdims=True)


def split_ids(p_count, candidate_ref, count_ref):
    ids = candidate_ref[0]
    row = lax.broadcasted_iota(jnp.int32, ids.shape, 0)
    valid_count = jnp.zeros(ids.shape, jnp.int32)
    for index in range(ids.shape[0]):
        valid_count = jnp.where(row == index, count_ref[0, index], valid_count)
    valid = lax.broadcasted_iota(jnp.int32, ids.shape, 1) < valid_count
    holder = jnp.where(valid, ids // p_count, -1)
    return (ids % p_count).astype(jnp.float32), holder.astype(jnp.float32)


def pack_kernel(p_count, query_ref, candidate_ref, count_ref, out_ref):
    _, q_count, slots = candidate_ref.shape
    _, _, q_tokens, depth = query_ref.shape
    tokens = q_count * q_tokens
    out_ref[:tokens] = query_ref[0].reshape(tokens, depth)
    planes = jnp.concatenate(split_ids(p_count, candidate_ref, count_ref), axis=0)
    empty = jnp.zeros((2 * q_count, depth - slots), jnp.float32)
    out_ref[tokens:] = jnp.concatenate([planes, empty], axis=1).astype(out_ref.dtype)


def pack(queries, candidates, counts, p_count):
    _, q_count, q_tokens, depth = queries.shape
    vmem = pl.BlockSpec(memory_space=pltpu.VMEM)
    return pl.pallas_call(
        functools.partial(pack_kernel, p_count),
        in_specs=[vmem, vmem, pl.BlockSpec(memory_space=pltpu.SMEM)],
        out_shape=jax.ShapeDtypeStruct((q_count * (q_tokens + 2), depth), queries.dtype),
        compiler_params=pltpu.CompilerParams(vmem_limit_bytes=4 * MIB),
        cost_estimate=pl.CostEstimate(
            flops=PACK_FLOPS, bytes_accessed=PACK_BYTES, transcendentals=0
        ),
        name="pack",
    )(in_hbm(queries), in_hbm(candidates), in_hbm(counts))


def memory_kernel(shards, slots, *refs):
    packed_refs, passage_ref = refs[:shards], refs[shards].at[0]
    out_refs = refs[shards + 1 : 2 * shards + 1]
    query_ref, rank_ref, best_ref, list_ref, scalar_ref, *refs = refs[2 * shards + 1 :]
    most_ref, rounds_ref, list_sems = refs
    q_count = out_refs[0].shape[0]
    p_count = passage_ref.shape[0]
    total, q_tokens, depth = query_ref.shape

    me = lax.axis_index("memory").astype(jnp.float32)
    keys = []
    for packed_ref in packed_refs:
        planes = packed_ref[q_count * q_tokens :].astype(jnp.float32)
        local, holder = planes[:q_count], planes[q_count:]
        keys.append(jnp.where(holder == me, local, -1.0))
    keys = jnp.concatenate(keys, axis=0)
    passage = lax.broadcasted_iota(jnp.int32, (total, p_count), 1).astype(jnp.float32)
    named = jnp.zeros((total, p_count), jnp.float32)
    for slot in range(slots):
        named = jnp.where(keys[:, slot : slot + 1] == passage, 1.0, named)

    square = (total, total)
    earlier = lax.broadcasted_iota(jnp.int32, square, 1) < lax.broadcasted_iota(
        jnp.int32, square, 0
    )
    before = jnp.dot(
        earlier.astype(jnp.bfloat16),
        named.astype(jnp.bfloat16),
        preferred_element_type=jnp.float32,
    )
    rank_ref[...] = jnp.where(named > 0.0, before, -1.0)
    def left_over(first):
        left = jnp.where(rank_ref[...] == first, 1.0, 0.0)
        left = jnp.sum(left, axis=0, keepdims=True)
        square = (p_count, p_count)
        row = lax.broadcasted_iota(jnp.int32, square, 0).astype(jnp.float32)
        column = lax.broadcasted_iota(jnp.int32, square, 1).astype(jnp.float32)
        place = jnp.dot(left, (row < column).astype(jnp.float32), preferred_element_type=jnp.float32)
        mine = jnp.where((place == row) & (left > 0.0), column, 0.0)
        index = jnp.sum(mine, axis=1, keepdims=True)
        index = jnp.sum(jnp.where(row == column, index, 0.0), axis=0, keepdims=True)
        return [index, jnp.broadcast_to(jnp.sum(left, axis=1, keepdims=True), left.shape)]

    def write_list(first, extra):
        asker = lax.broadcasted_iota(jnp.int32, (total, p_count), 0).astype(jnp.float32)
        rank = rank_ref[...] - first
        rows = [
            jnp.sum(jnp.where(rank == float(slot), asker, 0.0), axis=0, keepdims=True)
            for slot in range(SLOTS)
        ]
        for slot, above in enumerate(extra):
            rows[slot] = rows[slot] + LOW * above
        list_ref[...] = jnp.concatenate(rows, axis=0).astype(jnp.int32)
        copy = pltpu.make_async_copy(list_ref, scalar_ref, list_sems.at[0])
        copy.start()
        return copy

    def unit(index, mask):
        numbers = [scalar_ref[slot, index] for slot in range(SLOTS)]
        if mask:
            numbers = [number & (LOW - 1) for number in numbers]
        tokens = [query_ref[number] for number in numbers]
        return token_max(passage_ref[pl.ds(index, 1)], jnp.concatenate(tokens, axis=0))

    def add_scores(first, scores):
        sums = token_sum(best_ref[...], SLOTS)
        for index, out_ref in enumerate(out_refs):
            rank = rank_ref[index * q_count : (index + 1) * q_count] - first
            total_scores = scores[index]
            for slot in range(SLOTS):
                total_scores = jnp.where(rank == float(slot), sums[slot : slot + 1], total_scores)
            out_ref[...] = total_scores

    list_copy = write_list(0.0, [])
    for index, packed_ref in enumerate(packed_refs):
        tokens = packed_ref[: q_count * q_tokens].reshape(q_count, q_tokens, depth)
        query_ref[index * q_count : (index + 1) * q_count] = tokens
    counts = jnp.sum(named, axis=0, keepdims=True)
    most = jnp.broadcast_to(jnp.max(counts, axis=1, keepdims=True), most_ref.shape)
    most_ref[...] = most.astype(jnp.int32)
    most_copy = pltpu.make_async_copy(most_ref, rounds_ref, list_sems.at[1])
    most_copy.start()
    list_copy.wait()

    for first in range(0, p_count, 8):
        rows = [unit(first + offset, False) for offset in range(8)]
        best_ref[first : first + 8, :] = jnp.concatenate(rows, axis=0)

    most_copy.wait()
    rounds = (rounds_ref[0, 0] + SLOTS - 1) // SLOTS
    add_scores(0.0, [jnp.zeros((q_count, p_count), jnp.float32)] * shards)

    @pl.loop(1, rounds)
    def _(turn):
        done = (turn * SLOTS).astype(jnp.float32)
        write_list(done, left_over(done)).wait()

        @pl.loop(0, scalar_ref[1, 0] // LOW)
        def _(place):
            index = scalar_ref[0, place] // LOW
            best_ref[pl.ds(index, 1), :] = unit(index, True)

        add_scores(done, [out_ref[...] for out_ref in out_refs])


def score_memory(packed, memory, q_count, slots):
    shards = len(packed)
    q_tokens = packed[0].shape[0] // q_count - 2
    _, p_count, p_tokens, depth = memory.shape
    total = shards * q_count
    vmem = pl.BlockSpec(memory_space=pltpu.VMEM)
    return pl.pallas_call(
        functools.partial(memory_kernel, shards, slots),
        in_specs=[vmem] * (shards + 1),
        out_specs=[vmem] * shards,
        out_shape=[jax.ShapeDtypeStruct((q_count, p_count), jnp.float32)] * shards,
        scratch_shapes=[
            pltpu.VMEM((total, q_tokens, depth), memory.dtype),
            pltpu.VMEM((total, p_count), jnp.float32),
            pltpu.VMEM((p_count, SLOTS * q_tokens), jnp.float32),
            pltpu.VMEM((SLOTS, p_count), jnp.int32),
            pltpu.SMEM((SLOTS, p_count), jnp.int32),
            pltpu.VMEM((8, LANES), jnp.int32),
            pltpu.SMEM((8, LANES), jnp.int32),
            pltpu.SemaphoreType.DMA((2,)),
        ],
        compiler_params=pltpu.CompilerParams(vmem_limit_bytes=16 * MIB),
        cost_estimate=pl.CostEstimate(
            flops=2 * total * q_tokens * p_count * p_tokens * depth,
            bytes_accessed=2 * p_count * p_tokens * depth,
            transcendentals=0,
        ),
        name="score_memory",
    )(*packed, memory)


def batch_kernel(query_ref, *refs):
    passage_refs, (out_ref, best_ref) = refs[:-2], refs[-2:]
    _, queries, q_tokens, depth = query_ref.shape
    count = passage_refs[0].shape[1]
    tokens = query_ref[0].reshape(queries * q_tokens, depth)
    for chip, passage_ref in enumerate(passage_refs):
        rows = [token_max(passage_ref[0, index : index + 1], tokens) for index in range(count)]
        best_ref[chip * count : (chip + 1) * count, :] = jnp.concatenate(rows, axis=0)
    sums = token_sum(best_ref[...], queries)
    empty = jnp.zeros((queries, out_ref.shape[1] - sums.shape[1]), jnp.float32)
    out_ref[...] = jnp.concatenate([sums, empty], axis=1) if empty.size else sums


def score_batch(queries, positives):
    _, q_count, q_tokens, depth = queries.shape
    _, p_count, p_tokens, _ = positives[0].shape
    chips = len(positives)
    lanes = -(-chips * p_count // LANES) * LANES
    return pl.pallas_call(
        batch_kernel,
        out_shape=jax.ShapeDtypeStruct((q_count, lanes), jnp.float32),
        scratch_shapes=[pltpu.VMEM((chips * p_count, q_count * q_tokens), jnp.float32)],
        compiler_params=pltpu.CompilerParams(vmem_limit_bytes=16 * MIB),
        cost_estimate=pl.CostEstimate(
            flops=2 * chips * q_count * q_tokens * p_count * p_tokens * depth,
            bytes_accessed=2 * chips * p_count * p_tokens * depth,
            transcendentals=0,
        ),
        name="score_batch",
    )(queries, *positives)


def loss_kernel(shards, own_batch, mate_batch, *refs):
    memory_refs = refs[:shards]
    candidate_ref, count_ref, batch_ref, memory_ref, loss_ref = refs[shards:]
    group, shard = lax.axis_index("group"), lax.axis_index("memory")
    chip, core = group // 2, group % 2
    _, q_count, slots = candidate_ref.shape
    p_count = memory_refs[0].shape[1]
    columns = batch_ref.shape[2]

    parts = []
    for first in range(0, columns, LANES):
        lane = lax.broadcasted_iota(jnp.int32, (q_count, LANES), 1) + first
        owner = lane // q_count
        source = (((owner // 2) ^ chip) * q_count + lane % q_count) % LANES
        own = jnp.take_along_axis(own_batch[...], source, axis=1)
        mate = jnp.take_along_axis(mate_batch[...], source, axis=1)
        parts.append(jnp.where(owner % 2 == core, own, mate))
    batch = jnp.concatenate(parts, axis=1)[:, :columns]
    batch_ref[0] = batch

    ids = candidate_ref[0]
    padded = jnp.concatenate([ids, jnp.zeros((q_count, p_count - slots), jnp.int32)], axis=1)
    holder, local = padded // p_count, padded % p_count
    picked = jnp.zeros((q_count, p_count), jnp.float32)
    for step in range(shards):
        found = jnp.take_along_axis(memory_refs[-step][...], local, axis=1)
        picked = jnp.where(holder == (shard ^ step), found, picked)

    valid = lax.broadcasted_iota(jnp.int32, (q_count, p_count), 1) < column_of(count_ref[...])
    memory_ref[0] = jnp.where(valid, picked, 0.0)[:, :slots]

    top = jnp.maximum(
        jnp.max(batch, axis=1, keepdims=True),
        jnp.max(jnp.where(valid, picked, -jnp.inf), axis=1, keepdims=True),
    )
    total = jnp.sum(jnp.exp(batch - top), axis=1, keepdims=True) + jnp.sum(
        jnp.where(valid, jnp.exp(picked - top), 0.0), axis=1, keepdims=True
    )
    column = lax.broadcasted_iota(jnp.int32, batch.shape, 1)
    own = group * q_count + lax.broadcasted_iota(jnp.int32, batch.shape, 0)
    target_score = jnp.sum(jnp.where(column == own, batch, 0.0), axis=1, keepdims=True)
    loss_ref[...] = row_of(top + jnp.log(total) - target_score)


def finish(own_batch, mate_batch, memory_parts, candidates, counts, columns):
    _, q_count, slots = candidates.shape
    return pl.pallas_call(
        functools.partial(loss_kernel, len(memory_parts)),
        out_shape=[
            jax.ShapeDtypeStruct((1, q_count, columns), jnp.float32),
            jax.ShapeDtypeStruct((1, q_count, slots), jnp.float32),
            jax.ShapeDtypeStruct((1, q_count), jnp.float32),
        ],
        compiler_params=pltpu.CompilerParams(vmem_limit_bytes=4 * MIB),
        name="finish",
    )(own_batch, mate_batch, *memory_parts, candidates, counts)


def body(queries, positives, memory, candidates, counts):
    shards = lax.axis_size("memory")
    groups = lax.axis_size("group")
    chips = groups // 2
    q_count = queries.shape[1]
    slots = candidates.shape[2] // 2

    def to_shard(array, step):
        return lax.ppermute(array, "memory", [(i, i ^ step) for i in range(shards)])

    def to_group(array, step):
        return lax.ppermute(array, "group", [(i, i ^ step) for i in range(groups)])

    own = pack(queries, candidates, counts, memory.shape[1])
    packed = [own] + [to_shard(own, step) for step in range(1, shards)]
    sent_positives, sent_queries, _ = lax.optimization_barrier((positives, queries, own))
    row = [positives] + [to_group(sent_positives, 2 * step) for step in range(1, chips)]
    mate_queries = to_group(sent_queries, 1)

    scores = score_memory(packed, memory, q_count, slots)
    returned = [to_shard(scores[step], step) for step in range(shards - 1, 0, -1)]
    mate_queries, _ = lax.optimization_barrier((mate_queries, scores[0]))
    mate_scores = score_batch(mate_queries, row)
    mate_batch = to_group(mate_scores, 1)
    own_queries, _ = lax.optimization_barrier((queries, mate_scores))
    own_batch = score_batch(own_queries, row)
    columns = groups * q_count
    return finish(
        own_batch, mate_batch, [scores[0]] + returned, candidates, counts, columns
    )


def solution(mesh):
    in_specs = (
        P("group", "memory", None, None),
        P("group", "memory", None, None),
        P("group", "memory", None, None),
        P("group", "memory", None),
        P("group", "memory"),
    )
    out_specs = (P("group", "memory", None), P("group", "memory", None), P("group", "memory"))
    return jax.shard_map(body, mesh=mesh, in_specs=in_specs, out_specs=out_specs, check_vma=False)
```

```python
import functools

import jax
import jax.numpy as jnp
from jax import lax
from jax.experimental import pallas as pl
from jax.experimental.pallas import tpu as pltpu
from jax.sharding import PartitionSpec as P

LANES = 128
MIB = 1024 * 1024
SLOTS = 8
LOW = 256
PACK_FLOPS = 10**10
PACK_BYTES = 2**24


def in_hbm(array):
    return pltpu.with_memory_space_constraint(array, pltpu.HBM)


def token_max(passages, tokens):
    count, width, depth = passages.shape
    product = lax.dot_general(
        passages.reshape(count * width, depth),
        tokens,
        (((1,), (1,)), ((), ())),
        preferred_element_type=jnp.float32,
    )
    return jnp.max(product.reshape(count, width, tokens.shape[0]), axis=1)


def token_sum(best, queries):
    tokens = best.shape[1]
    per_query = tokens // queries
    row = lax.broadcasted_iota(jnp.int32, (queries, tokens), 0)
    col = lax.broadcasted_iota(jnp.int32, (queries, tokens), 1)
    own = (col // per_query == row).astype(jnp.bfloat16)
    high = best.astype(jnp.bfloat16)
    rest = best - high.astype(jnp.float32)
    middle = rest.astype(jnp.bfloat16)
    low = (rest - middle.astype(jnp.float32)).astype(jnp.bfloat16)
    return lax.dot_general(
        jnp.concatenate([own] * 3, axis=1),
        jnp.concatenate([high, middle, low], axis=1),
        (((1,), (1,)), ((), ())),
        preferred_element_type=jnp.float32,
    )


def column_of(row):
    size = row.shape[1]
    square = (size, size)
    diagonal = lax.broadcasted_iota(jnp.int32, square, 0) == lax.broadcasted_iota(
        jnp.int32, square, 1
    )
    return jnp.sum(jnp.where(diagonal, jnp.broadcast_to(row, square), 0), axis=1, keepdims=True)


def row_of(column):
    size = column.shape[0]
    square = (size, size)
    diagonal = lax.broadcasted_iota(jnp.int32, square, 0) == lax.broadcasted_iota(
        jnp.int32, square, 1
    )
    return jnp.sum(jnp.where(diagonal, jnp.broadcast_to(column, square), 0), axis=0, keepdims=True)


def split_ids(p_count, candidate_ref, count_ref):
    ids = candidate_ref[0]
    row = lax.broadcasted_iota(jnp.int32, ids.shape, 0)
    valid_count = jnp.zeros(ids.shape, jnp.int32)
    for index in range(ids.shape[0]):
        valid_count = jnp.where(row == index, count_ref[0, index], valid_count)
    valid = lax.broadcasted_iota(jnp.int32, ids.shape, 1) < valid_count
    holder = jnp.where(valid, ids // p_count, -1)
    return (ids % p_count).astype(jnp.float32), holder.astype(jnp.float32)


def pack_kernel(p_count, query_ref, candidate_ref, count_ref, out_ref, sems):
    _, q_count, slots = candidate_ref.shape
    _, _, q_tokens, depth = query_ref.shape
    tokens = q_count * q_tokens
    copies = [
        pltpu.make_async_copy(
            query_ref.at[0, index],
            out_ref.at[pl.ds(index * q_tokens, q_tokens)],
            sems.at[index],
        )
        for index in range(q_count)
    ]
    for copy in copies:
        copy.start()
    planes = jnp.concatenate(split_ids(p_count, candidate_ref, count_ref), axis=0)
    empty = jnp.zeros((2 * q_count, depth - slots), jnp.float32)
    out_ref[tokens:] = jnp.concatenate([planes, empty], axis=1).astype(out_ref.dtype)
    for copy in copies:
        copy.wait()


def pack(queries, candidates, counts, p_count):
    _, q_count, q_tokens, depth = queries.shape
    vmem = pl.BlockSpec(memory_space=pltpu.VMEM)
    return pl.pallas_call(
        functools.partial(pack_kernel, p_count),
        in_specs=[
            pl.BlockSpec(memory_space=pltpu.HBM),
            vmem,
            pl.BlockSpec(memory_space=pltpu.SMEM),
        ],
        scratch_shapes=[pltpu.SemaphoreType.DMA((q_count,))],
        out_shape=jax.ShapeDtypeStruct((q_count * (q_tokens + 2), depth), queries.dtype),
        compiler_params=pltpu.CompilerParams(vmem_limit_bytes=4 * MIB),
        cost_estimate=pl.CostEstimate(
            flops=PACK_FLOPS, bytes_accessed=PACK_BYTES, transcendentals=0
        ),
        name="pack",
    )(in_hbm(queries), in_hbm(candidates), in_hbm(counts))


def memory_kernel(shards, slots, *refs):
    packed_refs, passage_ref = refs[:shards], refs[shards].at[0]
    out_refs = refs[shards + 1 : 2 * shards + 1]
    query_ref, rank_ref, best_ref, list_ref, scalar_ref, *refs = refs[2 * shards + 1 :]
    most_ref, rounds_ref, list_sems = refs
    q_count = out_refs[0].shape[0]
    p_count = passage_ref.shape[0]
    total, q_tokens, depth = query_ref.shape

    me = lax.axis_index("memory").astype(jnp.float32)
    keys = []
    for packed_ref in packed_refs:
        planes = packed_ref[q_count * q_tokens :].astype(jnp.float32)
        local, holder = planes[:q_count], planes[q_count:]
        keys.append(jnp.where(holder == me, local, -1.0))
    keys = jnp.concatenate(keys, axis=0)
    passage = lax.broadcasted_iota(jnp.int32, (total, p_count), 1).astype(jnp.float32)
    named = jnp.zeros((total, p_count), jnp.float32)
    for slot in range(slots):
        named = jnp.where(keys[:, slot : slot + 1] == passage, 1.0, named)

    square = (total, total)
    earlier = lax.broadcasted_iota(jnp.int32, square, 1) < lax.broadcasted_iota(
        jnp.int32, square, 0
    )
    before = jnp.dot(
        earlier.astype(jnp.bfloat16),
        named.astype(jnp.bfloat16),
        preferred_element_type=jnp.float32,
    )
    rank_ref[...] = jnp.where(named > 0.0, before, -1.0)
    def left_over(first):
        left = jnp.where(rank_ref[...] == first, 1.0, 0.0)
        left = jnp.sum(left, axis=0, keepdims=True)
        square = (p_count, p_count)
        row = lax.broadcasted_iota(jnp.int32, square, 0).astype(jnp.float32)
        column = lax.broadcasted_iota(jnp.int32, square, 1).astype(jnp.float32)
        place = jnp.dot(left, (row < column).astype(jnp.float32), preferred_element_type=jnp.float32)
        mine = jnp.where((place == row) & (left > 0.0), column, 0.0)
        index = jnp.sum(mine, axis=1, keepdims=True)
        index = jnp.sum(jnp.where(row == column, index, 0.0), axis=0, keepdims=True)
        return [index, jnp.broadcast_to(jnp.sum(left, axis=1, keepdims=True), left.shape)]

    def write_list(first, extra):
        asker = lax.broadcasted_iota(jnp.int32, (total, p_count), 0).astype(jnp.float32)
        rank = rank_ref[...] - first
        rows = [
            jnp.sum(jnp.where(rank == float(slot), asker, 0.0), axis=0, keepdims=True)
            for slot in range(SLOTS)
        ]
        for slot, above in enumerate(extra):
            rows[slot] = rows[slot] + LOW * above
        list_ref[...] = jnp.concatenate(rows, axis=0).astype(jnp.int32)
        copy = pltpu.make_async_copy(list_ref, scalar_ref, list_sems.at[0])
        copy.start()
        return copy

    def unit(index):
        tokens = [query_ref[scalar_ref[slot, index] & (LOW - 1)] for slot in range(SLOTS)]
        return token_max(passage_ref[pl.ds(index, 1)], jnp.concatenate(tokens, axis=0))

    def add_scores(first, scores):
        sums = token_sum(best_ref[...], SLOTS)
        for index, out_ref in enumerate(out_refs):
            rank = rank_ref[index * q_count : (index + 1) * q_count] - first
            total_scores = scores[index]
            for slot in range(SLOTS):
                total_scores = jnp.where(rank == float(slot), sums[slot : slot + 1], total_scores)
            out_ref[...] = total_scores

    list_copy = write_list(0.0, [])
    for index, packed_ref in enumerate(packed_refs):
        tokens = packed_ref[: q_count * q_tokens].reshape(q_count, q_tokens, depth)
        query_ref[index * q_count : (index + 1) * q_count] = tokens
    counts = jnp.sum(named, axis=0, keepdims=True)
    most = jnp.broadcast_to(jnp.max(counts, axis=1, keepdims=True), most_ref.shape)
    most_ref[...] = most.astype(jnp.int32)
    most_copy = pltpu.make_async_copy(most_ref, rounds_ref, list_sems.at[1])
    most_copy.start()
    list_copy.wait()

    for first in range(0, p_count, 8):
        rows = [unit(first + offset) for offset in range(8)]
        best_ref[first : first + 8, :] = jnp.concatenate(rows, axis=0)

    most_copy.wait()
    rounds = (rounds_ref[0, 0] + SLOTS - 1) // SLOTS
    add_scores(0.0, [jnp.zeros((q_count, p_count), jnp.float32)] * shards)

    @pl.loop(1, rounds)
    def _(turn):
        done = (turn * SLOTS).astype(jnp.float32)
        write_list(done, left_over(done)).wait()

        @pl.loop(0, scalar_ref[1, 0] // LOW)
        def _(place):
            index = scalar_ref[0, place] // LOW
            best_ref[pl.ds(index, 1), :] = unit(index)

        add_scores(done, [out_ref[...] for out_ref in out_refs])


def score_memory(packed, memory, q_count, slots):
    shards = len(packed)
    q_tokens = packed[0].shape[0] // q_count - 2
    _, p_count, p_tokens, depth = memory.shape
    total = shards * q_count
    vmem = pl.BlockSpec(memory_space=pltpu.VMEM)
    return pl.pallas_call(
        functools.partial(memory_kernel, shards, slots),
        in_specs=[vmem] * (shards + 1),
        out_specs=[vmem] * shards,
        out_shape=[jax.ShapeDtypeStruct((q_count, p_count), jnp.float32)] * shards,
        scratch_shapes=[
            pltpu.VMEM((total, q_tokens, depth), memory.dtype),
            pltpu.VMEM((total, p_count), jnp.float32),
            pltpu.VMEM((p_count, SLOTS * q_tokens), jnp.float32),
            pltpu.VMEM((SLOTS, p_count), jnp.int32),
            pltpu.SMEM((SLOTS, p_count), jnp.int32),
            pltpu.VMEM((8, LANES), jnp.int32),
            pltpu.SMEM((8, LANES), jnp.int32),
            pltpu.SemaphoreType.DMA((2,)),
        ],
        compiler_params=pltpu.CompilerParams(vmem_limit_bytes=16 * MIB),
        cost_estimate=pl.CostEstimate(
            flops=2 * total * q_tokens * p_count * p_tokens * depth,
            bytes_accessed=2 * p_count * p_tokens * depth,
            transcendentals=0,
        ),
        name="score_memory",
    )(*packed, memory)


def batch_kernel(query_ref, *refs):
    passage_refs, (out_ref, best_ref) = refs[:-2], refs[-2:]
    _, queries, q_tokens, depth = query_ref.shape
    count = passage_refs[0].shape[1]
    tokens = query_ref[0].reshape(queries * q_tokens, depth)
    for chip, passage_ref in enumerate(passage_refs):
        rows = [token_max(passage_ref[0, index : index + 1], tokens) for index in range(count)]
        best_ref[chip * count : (chip + 1) * count, :] = jnp.concatenate(rows, axis=0)
    sums = token_sum(best_ref[...], queries)
    empty = jnp.zeros((queries, out_ref.shape[1] - sums.shape[1]), jnp.float32)
    out_ref[...] = jnp.concatenate([sums, empty], axis=1) if empty.size else sums


def score_batch(queries, positives):
    _, q_count, q_tokens, depth = queries.shape
    _, p_count, p_tokens, _ = positives[0].shape
    chips = len(positives)
    lanes = -(-chips * p_count // LANES) * LANES
    return pl.pallas_call(
        batch_kernel,
        out_shape=jax.ShapeDtypeStruct((q_count, lanes), jnp.float32),
        scratch_shapes=[pltpu.VMEM((chips * p_count, q_count * q_tokens), jnp.float32)],
        compiler_params=pltpu.CompilerParams(vmem_limit_bytes=16 * MIB),
        cost_estimate=pl.CostEstimate(
            flops=2 * chips * q_count * q_tokens * p_count * p_tokens * depth,
            bytes_accessed=2 * chips * p_count * p_tokens * depth,
            transcendentals=0,
        ),
        name="score_batch",
    )(queries, *positives)


def loss_kernel(shards, own_batch, mate_batch, *refs):
    memory_refs = refs[:shards]
    candidate_ref, count_ref, batch_ref, memory_ref, loss_ref = refs[shards:]
    group, shard = lax.axis_index("group"), lax.axis_index("memory")
    chip, core = group // 2, group % 2
    _, q_count, slots = candidate_ref.shape
    p_count = memory_refs[0].shape[1]
    columns = batch_ref.shape[2]

    parts = []
    for first in range(0, columns, LANES):
        lane = lax.broadcasted_iota(jnp.int32, (q_count, LANES), 1) + first
        owner = lane // q_count
        source = (((owner // 2) ^ chip) * q_count + lane % q_count) % LANES
        own = jnp.take_along_axis(own_batch[...], source, axis=1)
        mate = jnp.take_along_axis(mate_batch[...], source, axis=1)
        parts.append(jnp.where(owner % 2 == core, own, mate))
    batch = jnp.concatenate(parts, axis=1)[:, :columns]
    batch_ref[0] = batch

    ids = candidate_ref[0]
    padded = jnp.concatenate([ids, jnp.zeros((q_count, p_count - slots), jnp.int32)], axis=1)
    holder, local = padded // p_count, padded % p_count
    picked = jnp.zeros((q_count, p_count), jnp.float32)
    for step in range(shards):
        found = jnp.take_along_axis(memory_refs[-step][...], local, axis=1)
        picked = jnp.where(holder == (shard ^ step), found, picked)

    valid = lax.broadcasted_iota(jnp.int32, (q_count, p_count), 1) < column_of(count_ref[...])
    memory_ref[0] = jnp.where(valid, picked, 0.0)[:, :slots]

    top = jnp.maximum(
        jnp.max(batch, axis=1, keepdims=True),
        jnp.max(jnp.where(valid, picked, -jnp.inf), axis=1, keepdims=True),
    )
    total = jnp.sum(jnp.exp(batch - top), axis=1, keepdims=True) + jnp.sum(
        jnp.where(valid, jnp.exp(picked - top), 0.0), axis=1, keepdims=True
    )
    column = lax.broadcasted_iota(jnp.int32, batch.shape, 1)
    own = group * q_count + lax.broadcasted_iota(jnp.int32, batch.shape, 0)
    target_score = jnp.sum(jnp.where(column == own, batch, 0.0), axis=1, keepdims=True)
    loss_ref[...] = row_of(top + jnp.log(total) - target_score)


def finish(own_batch, mate_batch, memory_parts, candidates, counts, columns):
    _, q_count, slots = candidates.shape
    return pl.pallas_call(
        functools.partial(loss_kernel, len(memory_parts)),
        out_shape=[
            jax.ShapeDtypeStruct((1, q_count, columns), jnp.float32),
            jax.ShapeDtypeStruct((1, q_count, slots), jnp.float32),
            jax.ShapeDtypeStruct((1, q_count), jnp.float32),
        ],
        compiler_params=pltpu.CompilerParams(vmem_limit_bytes=4 * MIB),
        name="finish",
    )(own_batch, mate_batch, *memory_parts, candidates, counts)


def body(queries, positives, memory, candidates, counts):
    shards = lax.axis_size("memory")
    groups = lax.axis_size("group")
    chips = groups // 2
    q_count = queries.shape[1]
    slots = candidates.shape[2] // 2

    def to_shard(array, step):
        return lax.ppermute(array, "memory", [(i, i ^ step) for i in range(shards)])

    def to_group(array, step):
        return lax.ppermute(array, "group", [(i, i ^ step) for i in range(groups)])

    own = pack(queries, candidates, counts, memory.shape[1])
    packed = [own] + [to_shard(own, step) for step in range(1, shards)]
    sent_positives, sent_queries, _ = lax.optimization_barrier((positives, queries, own))
    row = [positives] + [to_group(sent_positives, 2 * step) for step in range(1, chips)]
    mate_queries = to_group(sent_queries, 1)

    scores = score_memory(packed, memory, q_count, slots)
    returned = [to_shard(scores[step], step) for step in range(shards - 1, 0, -1)]
    mate_queries, _ = lax.optimization_barrier((mate_queries, scores[0]))
    mate_scores = score_batch(mate_queries, row)
    mate_batch = to_group(mate_scores, 1)
    own_queries, _ = lax.optimization_barrier((queries, mate_scores))
    own_batch = score_batch(own_queries, row)
    columns = groups * q_count
    return finish(
        own_batch, mate_batch, [scores[0]] + returned, candidates, counts, columns
    )


def solution(mesh):
    in_specs = (
        P("group", "memory", None, None),
        P("group", "memory", None, None),
        P("group", "memory", None, None),
        P("group", "memory", None),
        P("group", "memory"),
    )
    out_specs = (P("group", "memory", None), P("group", "memory", None), P("group", "memory"))
    return jax.shard_map(body, mesh=mesh, in_specs=in_specs, out_specs=out_specs, check_vma=False)
```
